32 devices in a mesh: groups: 2 (over x), replica: 8 (over z, y), tensor: 2 (over core).
Axes of the slice: x: 2, y: 2, z: 4, core: 2. Of those that a mesh axis runs over, the one named last changes fastest.
Arguments:
- hidden_in: bfloat16 [64, 8192], P(('groups', 'replica'), 'tensor'), parts along dimension 0, may hold values from -0.0625 to 0.0625
- queries: bfloat16 [64, 4096], P(('groups', 'replica'), 'tensor'), parts along dimension 0, may hold values from -5.5 to 5.5
- stored_keys: bfloat16 [64, 1024, 512], P(('groups', 'replica'), None, 'tensor'), parts along dimension 0, may hold values from -5.5 to 5.5
- stored_values: bfloat16 [64, 1024, 512], P(('groups', 'replica'), None, 'tensor'), parts along dimension 0, may hold values from -6 to 6
- fresh_token_key: bfloat16 [64, 512], P(('groups', 'replica'), 'tensor'), parts along dimension 0, may hold values from -5.5 to 5.5
- lengths: int32 [64], P(('groups', 'replica')), parts along dimension 0, may hold values from 1 to 1024, as said below
- served_value_weight: bfloat16 [8192, 512], P(None, 'tensor'), may hold values from -6 to 6
- adapter_in: bfloat16 [128, 8192], P('groups', 'replica'), parts along dimension 0, may hold values from -6 to 6
- adapter_out: bfloat16 [128, 512], P(('groups', 'replica'), 'tensor'), parts along dimension 0, may hold values from -0.75 to 0.75
- owner_rank: int32 [16], P('groups'), parts along dimension 0, may hold values from 0 to 7, each once
Outputs:
- merged: bfloat16 [16384, 512], P('groups', 'tensor'), parts along dimension 0
- fresh_token_value: bfloat16 [64, 512], P(('groups', 'replica'), 'tensor'), parts along dimension 0
- attended: bfloat16 [64, 4096], P(('groups', 'replica'), 'tensor'), parts along dimension 0
The draws below stay inside these ranges and needn't reach their ends.
There are 2 independent parts, one for each index of `groups`. The reference program is written for one: setup_inputs(seed, part) draws one part's arguments, and reference() takes and returns one part's arrays. A program takes and returns all parts, laid end to end along the dimension named above; an argument that names none is the same for every part. Nothing has to cross between parts.
Inputs may be any that keep to these rules, and one draw needn't show every extreme that they name: Row lengths; some row has exactly 1024. `owner_rank`: each slot named once.
All inputs are finite; a program needn't handle non-finite values.
Results may differ from the reference program's by a relative error of at most 0.0054.
Values may be sent and summed in bfloat16 or wider, within the bound.
No kernel may reach another device: no remote copies, remote signals or barrier semaphores. Data moves between devices by JAX's collectives and lax.ppermute only.
A program may use at most 64 MiB of HBM per device.

```python
import jax
import jax.numpy as jnp
from jax import lax

D = 8192
HEAD_SIZE = 128
QUERY_HEADS = 32
KEY_VALUE_HEADS = 4
R = 64
CACHE_ROOM = 1024
TOTAL_ROWS = 32
KVW = 512
N_REPLICA = 8


def draw_queries(key, part):
    key = jax.random.fold_in(key, 1)
    values = jnp.clip(jax.random.normal(key, (TOTAL_ROWS, QUERY_HEADS * HEAD_SIZE), jnp.float32), -4.0, 4.0)
    return values.astype(jnp.bfloat16)


def draw_stored_keys(key, part):
    key = jax.random.fold_in(key, 2)
    values = jnp.clip(jax.random.normal(key, (TOTAL_ROWS, CACHE_ROOM, KVW), jnp.float32), -4.0, 4.0)
    return values.astype(jnp.bfloat16)


def draw_fresh_token_key(key, part):
    key = jax.random.fold_in(key, 3)
    values = jnp.clip(jax.random.normal(key, (TOTAL_ROWS, KVW), jnp.float32), -4.0, 4.0)
    return values.astype(jnp.bfloat16)


def draw_lengths(key, part):
    key = jax.random.fold_in(key, 4)
    ceiling_key = jax.random.fold_in(key, 1)
    length_key = jax.random.fold_in(key, 2)
    spot_key = jax.random.fold_in(key, 3)
    ceiling = jax.random.randint(ceiling_key, (TOTAL_ROWS,), 2, CACHE_ROOM + 2)
    drawn = jax.random.randint(length_key, (TOTAL_ROWS,), 1, ceiling)
    spot = jax.random.randint(spot_key, (), 0, TOTAL_ROWS)
    return jnp.where(jnp.arange(TOTAL_ROWS, dtype=jnp.int32) == spot, CACHE_ROOM, drawn).astype(jnp.int32)


def block_levels(stream_key, dims, split, least, top_value):
    loudness = 1.0
    for dim, blocks in split:
        heights = jax.random.uniform(jax.random.fold_in(jax.random.fold_in(stream_key, 6), dim), (blocks,), jnp.float32, least / len(split), top_value / len(split))
        loudness = loudness * jnp.repeat(jnp.exp(heights), dims[dim] // blocks).reshape((-1,) + (1,) * (len(dims) - 1 - dim))
    return loudness


def bell_draw(stream_key, extent, deviation, limit, split=(), kind=jnp.bfloat16):
    loudness = block_levels(stream_key, extent, split, -0.22, 0.18) if split else 1.0
    values = jax.random.normal(stream_key, extent, jnp.float32) * deviation * loudness
    return jnp.minimum(jnp.maximum(values, -limit), limit).astype(kind)


def setup_inputs(seed: int = 0, part: int = 0) -> dict:
    key_list = jax.random.split(jax.random.key(seed), 11)
    part_keys = jax.random.split(jax.random.fold_in(key_list[10], part), 11)
    return {
        "hidden_in": bell_draw(part_keys[0], (TOTAL_ROWS, D), D ** -0.5, 0.0625, ((0, 8), (1, 2))),
        "queries": draw_queries(jax.random.fold_in(jax.random.fold_in(key_list[10], part), 71), part),
        "stored_keys": draw_stored_keys(jax.random.fold_in(jax.random.fold_in(key_list[10], part), 71), part),
        "stored_values": bell_draw(part_keys[3], (TOTAL_ROWS, CACHE_ROOM, KVW), 1.0, 6.0, ((0, 8), (2, 2))),
        "fresh_token_key": draw_fresh_token_key(jax.random.fold_in(jax.random.fold_in(key_list[10], part), 71), part),
        "lengths": draw_lengths(jax.random.fold_in(jax.random.fold_in(key_list[10], part), 71), part),
        "served_value_weight": bell_draw(key_list[6], (D, KVW), 1.0, 6.0, ((1, 2),)),
        "adapter_in": bell_draw(part_keys[7], (R, D), 1.0, 6.0, ((1, 8),)),
        "adapter_out": bell_draw(part_keys[8], (R, KVW), 0.05, 0.75, ((0, 8), (1, 2))),
        "owner_rank": jax.random.permutation(part_keys[9], N_REPLICA).astype(jnp.int32),
    }


adapter_scale = 2.0


def reference(hidden_in, queries, stored_keys, stored_values, fresh_token_key, lengths, served_value_weight, adapter_in, adapter_out, owner_rank):
    shard_width = D // N_REPLICA
    split_blocks = adapter_in.reshape(R, N_REPLICA, shard_width)
    factor_full = jnp.take(split_blocks, owner_rank, axis=1).reshape(R, D)
    weight_update = lax.dot_general(factor_full, adapter_out, (((0,), (0,)), ((), ())), preferred_element_type=jnp.float32)
    merged = (served_value_weight.astype(jnp.float32) + adapter_scale * weight_update).astype(jnp.bfloat16)
    fresh_token_value = jnp.dot(hidden_in, merged, preferred_element_type=jnp.float32).astype(jnp.bfloat16)
    query_group_size = QUERY_HEADS // KEY_VALUE_HEADS
    scaling = 1.0 / (HEAD_SIZE ** 0.5)
    head_queries = queries.reshape(TOTAL_ROWS, KEY_VALUE_HEADS, query_group_size, HEAD_SIZE).astype(jnp.float32)
    head_keys = stored_keys.reshape(TOTAL_ROWS, CACHE_ROOM, KEY_VALUE_HEADS, HEAD_SIZE).astype(jnp.float32)
    head_values = stored_values.reshape(TOTAL_ROWS, CACHE_ROOM, KEY_VALUE_HEADS, HEAD_SIZE).astype(jnp.float32)
    self_key = fresh_token_key.reshape(TOTAL_ROWS, KEY_VALUE_HEADS, HEAD_SIZE).astype(jnp.float32)
    self_value = fresh_token_value.reshape(TOTAL_ROWS, KEY_VALUE_HEADS, HEAD_SIZE).astype(jnp.float32)
    scores = jnp.einsum("rhgd,rlhd->rhgl", head_queries, head_keys) * scaling
    own_score = jnp.einsum("rhgd,rhd->rhg", head_queries, self_key) * scaling
    valid = jnp.arange(CACHE_ROOM, dtype=jnp.int32)[None, :] < lengths[:, None]
    valid = valid[:, None, None, :]
    masked = jnp.where(valid, scores, -1e30)
    largest = jnp.maximum(jnp.max(masked, axis=-1), own_score)
    cached_exp = jnp.where(valid, jnp.exp(masked - largest[..., None]), 0.0)
    own_exp = jnp.exp(own_score - largest)
    normaliser = jnp.sum(cached_exp, axis=-1) + own_exp
    weights_cached = (cached_exp / normaliser[..., None]).astype(jnp.bfloat16)
    weight_own = (own_exp / normaliser).astype(jnp.bfloat16)
    context = jnp.einsum("rhgl,rlhd->rhgd", weights_cached.astype(jnp.float32), head_values)
    context = context + weight_own.astype(jnp.float32)[..., None] * self_value[:, :, None, :]
    attended = context.reshape(TOTAL_ROWS, QUERY_HEADS * HEAD_SIZE).astype(jnp.bfloat16)
    return merged, fresh_token_value, attended
```

```python
import functools

import jax
import jax.numpy as jnp
from jax import lax
from jax.experimental import pallas as pl
from jax.experimental.pallas import tpu as pltpu
from jax.sharding import PartitionSpec as P

HEAD_SIZE = 128
ADAPTER_SCALE = 2.0


def attend_kernel(lengths_ref, q_ref, k_ref, v_ref, own_k_ref, context_ref, own_weight_ref):
    row = pl.program_id(0)
    length = lengths_ref[row]
    q = q_ref[0]
    heads = q.shape[0]
    local_heads = k_ref.shape[2] // HEAD_SIZE
    group = heads // local_heads
    cache_len = k_ref.shape[1]
    scaling = 1.0 / HEAD_SIZE**0.5
    head_of = lax.broadcasted_iota(jnp.int32, (heads, HEAD_SIZE), 0) // group
    q32 = q.astype(jnp.float32)
    spread = jnp.concatenate(
        [jnp.where(head_of == h, q32, 0.0) for h in range(local_heads)], axis=1
    )
    scores = (
        lax.dot_general(
            spread.astype(jnp.bfloat16), k_ref[0], (((1,), (1,)), ((), ())),
            preferred_element_type=jnp.float32,
        )
        * scaling
    )
    own_key = own_k_ref[pl.ds(row, 1), :]
    own = jnp.sum(spread * own_key, axis=1, keepdims=True) * scaling
    valid = lax.broadcasted_iota(jnp.int32, (heads, cache_len), 1) < length
    masked = jnp.where(valid, scores, -1e30)
    largest = jnp.maximum(jnp.max(masked, axis=1, keepdims=True), own)
    cached_exp = jnp.where(valid, jnp.exp(masked - largest), 0.0)
    own_exp = jnp.exp(own - largest)
    normaliser = jnp.sum(cached_exp, axis=1, keepdims=True) + own_exp
    weights = (cached_exp / normaliser).astype(jnp.bfloat16)
    weight_own = (own_exp / normaliser).astype(jnp.bfloat16).astype(jnp.float32)
    wide = jnp.dot(weights, v_ref[0], preferred_element_type=jnp.float32)
    context = wide[:, :HEAD_SIZE]
    for h in range(1, local_heads):
        context = jnp.where(
            head_of == h, wide[:, h * HEAD_SIZE : (h + 1) * HEAD_SIZE], context
        )
    context_ref[0] = context
    own_weight_ref[0] = jnp.broadcast_to(weight_own, (heads, HEAD_SIZE))


def attend(queries, stored_keys, stored_values, fresh_token_key, lengths):
    rows, cache_len, width = stored_keys.shape
    heads = queries.shape[1] // HEAD_SIZE
    out = jax.ShapeDtypeStruct((rows, heads, HEAD_SIZE), jnp.float32)
    spec = pl.BlockSpec((1, heads, HEAD_SIZE), lambda i: (i, 0, 0))
    cache_spec = pl.BlockSpec((1, cache_len, width), lambda i: (i, 0, 0))
    return pl.pallas_call(
        attend_kernel,
        grid=(rows,),
        out_shape=(out, out),
        in_specs=[
            pl.BlockSpec(memory_space=pltpu.SMEM),
            spec,
            cache_spec,
            cache_spec,
            pl.BlockSpec((rows, width), lambda i: (0, 0)),
        ],
        out_specs=(spec, spec),
        compiler_params=pltpu.CompilerParams(vmem_limit_bytes=16 * 2**20),
        cost_estimate=pl.CostEstimate(
            flops=4 * rows * heads * cache_len * width,
            bytes_accessed=4 * rows * cache_len * width,
            transcendentals=rows * heads * cache_len,
        ),
        name="attend_cache",
    )(
        lengths,
        queries.reshape(rows, heads, HEAD_SIZE),
        stored_keys,
        stored_values,
        fresh_token_key.astype(jnp.float32),
    )


def fold_kernel(slots, place_ref, own_first_ref, up_ref, hid_own_ref, hid_other_ref, context_ref,
                own_weight_ref, *rest):
    blocks = rest[:slots]
    served, merged, fresh_ref, attended_ref, w_buf, m_buf, feat, in_sem, out_sem = rest[slots:]
    width = blocks[0].shape[1]
    half = hid_own_ref.shape[1]

    def place(slot):
        return pl.ds(pl.multiple_of(place_ref[slot] * width, width), width)

    def fetch(slot):
        return pltpu.make_async_copy(served.at[place(slot)], w_buf.at[slot], in_sem.at[slot])

    def store(slot):
        return pltpu.make_async_copy(m_buf.at[slot], merged.at[place(slot)], out_sem.at[slot])

    for slot in range(slots):
        fetch(slot).start()
    mine = own_first_ref[0]
    feat[mine] = hid_own_ref[...]
    feat[1 - mine] = hid_other_ref[...]
    up = up_ref[...]
    total = jnp.zeros(fresh_ref.shape, jnp.float32)
    for slot in range(slots):
        update = lax.dot_general(
            blocks[slot][...], up, (((0,), (0,)), ((), ())), preferred_element_type=jnp.float32
        )
        fetch(slot).wait()
        rows = (w_buf[slot].astype(jnp.float32) + ADAPTER_SCALE * update).astype(jnp.bfloat16)
        m_buf[slot] = rows
        store(slot).start()
        first = place_ref[slot] * width
        in_half = first // half
        features = feat[in_half, :, pl.ds(pl.multiple_of(first - in_half * half, width), width)]
        total = total + jnp.dot(features, rows, preferred_element_type=jnp.float32)
    fresh = total.astype(jnp.bfloat16)
    fresh_ref[...] = fresh
    value = fresh.astype(jnp.float32)
    heads = attended_ref.shape[1] // HEAD_SIZE
    group = heads // (fresh_ref.shape[1] // HEAD_SIZE)
    for h in range(heads):
        cols = slice(h * HEAD_SIZE, (h + 1) * HEAD_SIZE)
        at = (h // group) * HEAD_SIZE
        attended_ref[:, cols] = (
            context_ref[:, cols] + own_weight_ref[:, cols] * value[:, at : at + HEAD_SIZE]
        ).astype(jnp.bfloat16)
    for slot in range(slots):
        store(slot).wait()


def fold(place, own_first, up, hid_own, hid_other, context, own_weight, blocks, served):
    slots = len(blocks)
    rank, width = blocks[0].shape
    rows = hid_own.shape[0]
    depth, cols = served.shape
    vmem = pl.BlockSpec(memory_space=pltpu.VMEM)
    smem = pl.BlockSpec(memory_space=pltpu.SMEM)
    hbm = pl.BlockSpec(memory_space=pl.ANY)
    return pl.pallas_call(
        functools.partial(fold_kernel, slots),
        out_shape=(
            jax.ShapeDtypeStruct((depth, cols), jnp.bfloat16),
            jax.ShapeDtypeStruct((rows, cols), jnp.bfloat16),
            jax.ShapeDtypeStruct(context.shape, jnp.bfloat16),
        ),
        in_specs=[smem, smem] + [vmem] * (5 + slots) + [hbm],
        out_specs=(hbm, vmem, vmem),
        scratch_shapes=[
            pltpu.VMEM((slots, width, cols), jnp.bfloat16),
            pltpu.VMEM((slots, width, cols), jnp.bfloat16),
            pltpu.VMEM((2,) + hid_own.shape, jnp.bfloat16),
            pltpu.SemaphoreType.DMA((slots,)),
            pltpu.SemaphoreType.DMA((slots,)),
        ],
        compiler_params=pltpu.CompilerParams(vmem_limit_bytes=24 * 2**20),
        cost_estimate=pl.CostEstimate(
            flops=2 * depth * cols * (rank + rows),
            bytes_accessed=4 * depth * cols + 2 * rank * depth,
            transcendentals=0,
        ),
        name="fold_blocks",
    )(place, own_first, up, hid_own, hid_other, context, own_weight, *blocks, served)


def ring_member(spot, n):
    return jnp.where(spot < (n + 1) // 2, 2 * spot, 2 * (n - 1 - spot) + 1)


def body(
    hidden_in,
    queries,
    stored_keys,
    stored_values,
    fresh_token_key,
    lengths,
    served_value_weight,
    adapter_in,
    adapter_out,
    owner_rank,
):
    n = lax.axis_size("replica")
    replica = lax.axis_index("replica")
    core = lax.axis_index("tensor")
    swap = [(0, 1), (1, 0)]
    order = list(range(0, n, 2)) + list(range(n - 1 - n % 2, 0, -2))
    around = []
    for spot in range(n):
        here, there = order[spot], order[(spot + 1) % n]
        around.append((here * 2, there * 2))
        around.append((there * 2 + 1, here * 2 + 1))

    ring = [adapter_in]
    crossed = []
    for step in range(1, n // 2 + 1):
        ring.append(lax.ppermute(ring[-1], ("replica", "tensor"), around))
        if 2 * step < n:
            crossed.append(lax.ppermute(ring[-1], "tensor", swap))
    hid_other = lax.ppermute(hidden_in, "tensor", swap)
    ups = [adapter_out]
    for step in range(1, n):
        ups.append(lax.ppermute(adapter_out, "replica", [(i, (i + step) % n) for i in range(n)]))

    context, own_weight = attend(queries, stored_keys, stored_values, fresh_token_key, lengths)
    context = context.reshape(queries.shape)
    own_weight = own_weight.reshape(queries.shape)

    up = jnp.concatenate(ups[::-1] + ups[::-1], axis=0)
    per = adapter_out.shape[0]
    up = lax.dynamic_slice_in_dim(up, (n - 1 - replica) * per, n * per, axis=0)

    spot = jnp.where(replica % 2 == 0, replica // 2, n - 1 - replica // 2)
    way = jnp.where(core == 0, -1, 1)
    shifts = list(range(n // 2 + 1)) + [-k for k in range(1, len(crossed) + 1)]
    source = ring_member((spot + way * jnp.array(shifts, jnp.int32) + n) % n, n)
    spots = jnp.arange(n, dtype=jnp.int32)[None, :]
    place = jnp.sum(jnp.where(owner_rank[None, :] == source[:, None], spots, 0), axis=1)

    merged, fresh_token_value, attended = fold(
        place.astype(jnp.int32), core.astype(jnp.int32).reshape(1), up, hidden_in, hid_other,
        context, own_weight, ring + crossed, served_value_weight,
    )
    return (merged, fresh_token_value, attended)


def solution(mesh):
    in_specs = (
        P(("groups", "replica"), "tensor"),
        P(("groups", "replica"), "tensor"),
        P(("groups", "replica"), None, "tensor"),
        P(("groups", "replica"), None, "tensor"),
        P(("groups", "replica"), "tensor"),
        P(("groups", "replica")),
        P(None, "tensor"),
        P("groups", "replica"),
        P(("groups", "replica"), "tensor"),
        P("groups"),
    )
    out_specs = (
        P("groups", "tensor"),
        P(("groups", "replica"), "tensor"),
        P(("groups", "replica"), "tensor"),
    )
    return jax.shard_map(body, mesh=mesh, in_specs=in_specs, out_specs=out_specs, check_vma=False)
```

```python
import jax
import jax.numpy as jnp
from jax import lax
from jax.experimental import pallas as pl
from jax.experimental.pallas import tpu as pltpu
from jax.sharding import PartitionSpec as P

HEAD_SIZE = 128
ADAPTER_SCALE = 2.0


def attend_kernel(lengths_ref, q_ref, k_ref, v_ref, own_k_ref, context_ref, own_weight_ref):
    row = pl.program_id(0)
    length = lengths_ref[row]
    q = q_ref[0]
    heads = q.shape[0]
    local_heads = k_ref.shape[2] // HEAD_SIZE
    group = heads // local_heads
    cache_len = k_ref.shape[1]
    scaling = 1.0 / HEAD_SIZE**0.5
    head_of = lax.broadcasted_iota(jnp.int32, (heads, HEAD_SIZE), 0) // group
    q32 = q.astype(jnp.float32)
    spread = jnp.concatenate(
        [jnp.where(head_of == h, q32, 0.0) for h in range(local_heads)], axis=1
    )
    scores = (
        lax.dot_general(
            spread.astype(jnp.bfloat16), k_ref[0], (((1,), (1,)), ((), ())),
            preferred_element_type=jnp.float32,
        )
        * scaling
    )
    own_key = own_k_ref[pl.ds(row, 1), :]
    own = jnp.sum(spread * own_key, axis=1, keepdims=True) * scaling
    valid = lax.broadcasted_iota(jnp.int32, (heads, cache_len), 1) < length
    masked = jnp.where(valid, scores, -1e30)
    largest = jnp.maximum(jnp.max(masked, axis=1, keepdims=True), own)
    cached_exp = jnp.where(valid, jnp.exp(masked - largest), 0.0)
    own_exp = jnp.exp(own - largest)
    normaliser = jnp.sum(cached_exp, axis=1, keepdims=True) + own_exp
    weights = (cached_exp / normaliser).astype(jnp.bfloat16)
    weight_own = (own_exp / normaliser).astype(jnp.bfloat16).astype(jnp.float32)
    wide = jnp.dot(weights, v_ref[0], preferred_element_type=jnp.float32)
    context = wide[:, :HEAD_SIZE]
    for h in range(1, local_heads):
        context = jnp.where(
            head_of == h, wide[:, h * HEAD_SIZE : (h + 1) * HEAD_SIZE], context
        )
    context_ref[0] = context
    own_weight_ref[0] = jnp.broadcast_to(weight_own, (heads, HEAD_SIZE))


def attend(queries, stored_keys, stored_values, fresh_token_key, lengths):
    rows, cache_len, width = stored_keys.shape
    heads = queries.shape[1] // HEAD_SIZE
    out = jax.ShapeDtypeStruct((rows, heads, HEAD_SIZE), jnp.float32)
    spec = pl.BlockSpec((1, heads, HEAD_SIZE), lambda i: (i, 0, 0))
    cache_spec = pl.BlockSpec((1, cache_len, width), lambda i: (i, 0, 0))
    stored_keys, stored_values = (
        pltpu.with_memory_space_constraint(x, pltpu.HBM) for x in (stored_keys, stored_values)
    )
    return pl.pallas_call(
        attend_kernel,
        grid=(rows,),
        out_shape=(out, out),
        in_specs=[
            pl.BlockSpec(memory_space=pltpu.SMEM),
            spec,
            cache_spec,
            cache_spec,
            pl.BlockSpec((rows, width), lambda i: (0, 0)),
        ],
        out_specs=(spec, spec),
        compiler_params=pltpu.CompilerParams(vmem_limit_bytes=16 * 2**20),
        cost_estimate=pl.CostEstimate(
            flops=4 * rows * heads * cache_len * width,
            bytes_accessed=4 * rows * cache_len * width,
            transcendentals=rows * heads * cache_len,
        ),
        name="attend_cache",
    )(
        lengths,
        queries.reshape(rows, heads, HEAD_SIZE),
        stored_keys,
        stored_values,
        fresh_token_key.astype(jnp.float32),
    )


def fold_kernel(place_ref, core_ref, up_ref, hid_own_ref, hid_other_ref, context_ref,
                own_weight_ref, mine_ref, theirs_ref, served, merged, fresh_ref, attended_ref,
                m_buf, feat, out_sem):
    slots, _, width = mine_ref.shape
    rank = up_ref.shape[0]
    part = rank // 2
    half = hid_own_ref.shape[1]

    def place(slot):
        return pl.ds(pl.multiple_of(place_ref[slot] * width, width), width)

    def store(slot):
        return pltpu.make_async_copy(m_buf.at[slot], merged.at[place(slot)], out_sem.at[slot])

    core = core_ref[0]
    feat[core] = hid_own_ref[...]
    feat[1 - core] = hid_other_ref[...]
    up = up_ref[...].astype(jnp.float32) * ADAPTER_SCALE
    low, high = up[:part], up[part:]
    up = jnp.where(core == 0, up, jnp.concatenate([high, low], axis=0)).astype(jnp.bfloat16)
    total = jnp.zeros(fresh_ref.shape, jnp.float32)
    for slot in range(slots):
        block = jnp.concatenate([mine_ref[slot, :part], theirs_ref[slot, :part]], axis=0)
        update = lax.dot_general(
            block, up, (((0,), (0,)), ((), ())), preferred_element_type=jnp.float32
        )
        rows = (served[place(slot), :].astype(jnp.float32) + update).astype(jnp.bfloat16)
        m_buf[slot] = rows
        store(slot).start()
        first = place_ref[slot] * width
        in_half = first // half
        features = feat[in_half, :, pl.ds(pl.multiple_of(first - in_half * half, width), width)]
        total = total + jnp.dot(features, rows, preferred_element_type=jnp.float32)
    fresh = total.astype(jnp.bfloat16)
    fresh_ref[...] = fresh
    value = fresh.astype(jnp.float32)
    heads = attended_ref.shape[1] // HEAD_SIZE
    group = heads // (fresh_ref.shape[1] // HEAD_SIZE)
    for h in range(heads):
        cols = slice(h * HEAD_SIZE, (h + 1) * HEAD_SIZE)
        at = (h // group) * HEAD_SIZE
        attended_ref[:, cols] = (
            context_ref[:, cols] + own_weight_ref[:, cols] * value[:, at : at + HEAD_SIZE]
        ).astype(jnp.bfloat16)
    for slot in range(slots):
        store(slot).wait()


def fold(place, core, up, hid_own, hid_other, context, own_weight, mine, theirs, served):
    slots, _, width = mine.shape
    rank = up.shape[0]
    rows = hid_own.shape[0]
    depth, cols = served.shape
    vmem = pl.BlockSpec(memory_space=pltpu.VMEM)
    smem = pl.BlockSpec(memory_space=pltpu.SMEM)
    hbm = pl.BlockSpec(memory_space=pltpu.HBM)
    return pl.pallas_call(
        fold_kernel,
        out_shape=(
            jax.ShapeDtypeStruct((depth, cols), jnp.bfloat16),
            jax.ShapeDtypeStruct((rows, cols), jnp.bfloat16),
            jax.ShapeDtypeStruct(context.shape, jnp.bfloat16),
        ),
        in_specs=[smem, smem] + [vmem] * 8,
        out_specs=(hbm, vmem, vmem),
        scratch_shapes=[
            pltpu.VMEM((slots, width, cols), jnp.bfloat16),
            pltpu.VMEM((2,) + hid_own.shape, jnp.bfloat16),
            pltpu.SemaphoreType.DMA((slots,)),
        ],
        compiler_params=pltpu.CompilerParams(vmem_limit_bytes=24 * 2**20),
        cost_estimate=pl.CostEstimate(
            flops=2 * depth * cols * (rank + rows),
            bytes_accessed=4 * depth * cols + 2 * rank * depth,
            transcendentals=0,
        ),
        name="fold_blocks",
    )(place, core, up, hid_own, hid_other, context, own_weight, mine, theirs, served)


def body(
    hidden_in,
    queries,
    stored_keys,
    stored_values,
    fresh_token_key,
    lengths,
    served_value_weight,
    adapter_in,
    adapter_out,
    owner_rank,
):
    n = lax.axis_size("replica")
    core = lax.axis_index("tensor")
    swap = [(0, 1), (1, 0)]
    rank, width = adapter_in.shape
    part = rank // 2
    up_rows = adapter_out.size // width
    spare = -(part + up_rows) % 8

    load = jnp.concatenate(
        [
            lax.dynamic_slice_in_dim(adapter_in, core * part, part, axis=0),
            adapter_out.reshape(up_rows, width),
            jnp.zeros((spare, width), adapter_in.dtype),
        ],
        axis=0,
    )
    load = jnp.broadcast_to(load[None], (n,) + load.shape)
    mine = lax.all_to_all(load, "replica", split_axis=0, concat_axis=0)
    hid_other = lax.ppermute(hidden_in, "tensor", swap)
    theirs = lax.ppermute(mine, "tensor", swap)

    context, own_weight = attend(queries, stored_keys, stored_values, fresh_token_key, lengths)
    context = context.reshape(queries.shape)
    own_weight = own_weight.reshape(queries.shape)

    up = mine[:, part : part + up_rows].reshape(rank, adapter_out.shape[1])
    spots = jnp.arange(n, dtype=jnp.int32)
    place = jnp.sum(
        jnp.where(owner_rank[None, :] == spots[:, None], spots[None, :], 0), axis=1
    ).astype(jnp.int32)

    merged, fresh_token_value, attended = fold(
        place, core.astype(jnp.int32).reshape(1), up, hidden_in, hid_other,
        context, own_weight, mine, theirs, served_value_weight,
    )
    return (merged, fresh_token_value, attended)


def solution(mesh):
    in_specs = (
        P(("groups", "replica"), "tensor"),
        P(("groups", "replica"), "tensor"),
        P(("groups", "replica"), None, "tensor"),
        P(("groups", "replica"), None, "tensor"),
        P(("groups", "replica"), "tensor"),
        P(("groups", "replica")),
        P(None, "tensor"),
        P("groups", "replica"),
        P(("groups", "replica"), "tensor"),
        P("groups"),
    )
    out_specs = (
        P("groups", "tensor"),
        P(("groups", "replica"), "tensor"),
        P(("groups", "replica"), "tensor"),
    )
    return jax.shard_map(body, mesh=mesh, in_specs=in_specs, out_specs=out_specs, check_vma=False)
```

```python
import functools

import jax
import jax.numpy as jnp
from jax import lax
from jax.experimental import pallas as pl
from jax.experimental.pallas import tpu as pltpu
from jax.sharding import PartitionSpec as P

HEAD_SIZE = 128
ADAPTER_SCALE = 2.0


def attend_kernel(start, lengths_ref, q_ref, k_ref, v_ref, own_k_ref, after_ref, context_ref,
                  own_weight_ref):
    row = start + pl.program_id(0)
    length = lengths_ref[row]
    q = q_ref[0]
    heads = q.shape[0]
    local_heads = k_ref.shape[2] // HEAD_SIZE
    group = heads // local_heads
    cache_len = k_ref.shape[1]
    scaling = 1.0 / HEAD_SIZE**0.5
    head_of = lax.broadcasted_iota(jnp.int32, (heads, HEAD_SIZE), 0) // group
    q32 = q.astype(jnp.float32)
    spread = jnp.concatenate(
        [jnp.where(head_of == h, q32, 0.0) for h in range(local_heads)], axis=1
    )
    scores = (
        lax.dot_general(
            spread.astype(jnp.bfloat16), k_ref[0], (((1,), (1,)), ((), ())),
            preferred_element_type=jnp.float32,
        )
        * scaling
    )
    own_key = own_k_ref[pl.ds(row, 1), :]
    own = jnp.sum(spread * own_key, axis=1, keepdims=True) * scaling
    valid = lax.broadcasted_iota(jnp.int32, (heads, cache_len), 1) < length
    masked = jnp.where(valid, scores, -1e30)
    largest = jnp.maximum(jnp.max(masked, axis=1, keepdims=True), own)
    cached_exp = jnp.where(valid, jnp.exp(masked - largest), 0.0)
    own_exp = jnp.exp(own - largest)
    normaliser = jnp.sum(cached_exp, axis=1, keepdims=True) + own_exp
    weights = (cached_exp / normaliser).astype(jnp.bfloat16)
    weight_own = (own_exp / normaliser).astype(jnp.bfloat16).astype(jnp.float32)
    wide = jnp.dot(weights, v_ref[0], preferred_element_type=jnp.float32)
    context = wide[:, :HEAD_SIZE]
    for h in range(1, local_heads):
        context = jnp.where(
            head_of == h, wide[:, h * HEAD_SIZE : (h + 1) * HEAD_SIZE], context
        )
    context_ref[0] = context
    own_weight_ref[0] = jnp.broadcast_to(weight_own, (heads, HEAD_SIZE))


def attend(start, count, queries, stored_keys, stored_values, own_key, lengths, after):
    rows, cache_len, width = stored_keys.shape
    heads = queries.shape[1]
    out = jax.ShapeDtypeStruct((count, heads, HEAD_SIZE), jnp.float32)
    spec = pl.BlockSpec((1, heads, HEAD_SIZE), lambda i: (i, 0, 0))
    cache_spec = pl.BlockSpec((1, cache_len, width), lambda i: (start + i, 0, 0))
    return pl.pallas_call(
        functools.partial(attend_kernel, start),
        grid=(count,),
        out_shape=(out, out),
        in_specs=[
            pl.BlockSpec(memory_space=pltpu.SMEM),
            pl.BlockSpec((1, heads, HEAD_SIZE), lambda i: (start + i, 0, 0)),
            cache_spec,
            cache_spec,
            pl.BlockSpec((rows, width), lambda i: (0, 0)),
            pl.BlockSpec(memory_space=pl.ANY),
        ],
        out_specs=(spec, spec),
        compiler_params=pltpu.CompilerParams(vmem_limit_bytes=16 * 2**20),
        cost_estimate=pl.CostEstimate(
            flops=4 * count * heads * cache_len * width,
            bytes_accessed=4 * count * cache_len * width,
            transcendentals=count * heads * cache_len,
        ),
        name="attend_cache",
    )(lengths, queries, stored_keys, stored_values, own_key, after)


def fold_kernel(slots, first, prefetch, last, place_ref, core_ref, up_ref, hid_own_ref, hid_other_ref, *rest):
    rest = list(rest)
    served = rest.pop(0)
    blocks = [rest.pop(0) for _ in slots]
    if not first:
        rest.pop(0)
        total = rest.pop(0)[...]
    if last:
        ahead, context_ref, own_weight_ref = rest[:3]
        merged, fresh_ref, attended_ref = rest[3:6]
        rest = rest[6:]
    else:
        merged, total_ref = rest[:2]
        rest = rest[2:]
        if prefetch:
            ahead = rest.pop(0)
    w_buf, m_buf, feat, in_sem, out_sem = rest
    width = blocks[0].shape[1]
    half = hid_own_ref.shape[1]
    final = place_ref.shape[0] - 1

    def rows_of(slot):
        return pl.ds(pl.multiple_of(place_ref[slot] * width, width), width)

    def fetch(i, slot, into):
        return pltpu.make_async_copy(served.at[rows_of(slot)], into, in_sem.at[i])

    def store(i):
        return pltpu.make_async_copy(m_buf.at[i], merged.at[rows_of(slots[i])], out_sem.at[i])

    if not last:
        for i, slot in enumerate(slots):
            fetch(i, slot, w_buf.at[i]).start()
        if prefetch:
            fetch(len(slots), final, ahead).start()
    core = core_ref[0]
    feat[core] = hid_own_ref[...]
    feat[1 - core] = hid_other_ref[...]
    up = (up_ref[...].astype(jnp.float32) * ADAPTER_SCALE).astype(jnp.bfloat16)
    if first:
        total = jnp.zeros(total_ref.shape, jnp.float32)
    for i, slot in enumerate(slots):
        update = lax.dot_general(
            blocks[i][...], up, (((0,), (0,)), ((), ())), preferred_element_type=jnp.float32
        )
        if last:
            rows = ahead[...]
        else:
            fetch(i, slot, w_buf.at[i]).wait()
            rows = w_buf[i]
        rows = (rows.astype(jnp.float32) + update).astype(jnp.bfloat16)
        m_buf[i] = rows
        store(i).start()
        top = place_ref[slot] * width
        in_half = top // half
        features = feat[in_half, :, pl.ds(pl.multiple_of(top - in_half * half, width), width)]
        total = total + jnp.dot(features, rows, preferred_element_type=jnp.float32)
    if last:
        fresh = total.astype(jnp.bfloat16)
        fresh_ref[...] = fresh
        value = fresh.astype(jnp.float32)
        heads = attended_ref.shape[1] // HEAD_SIZE
        group = heads // (fresh_ref.shape[1] // HEAD_SIZE)
        for h in range(heads):
            cols = slice(h * HEAD_SIZE, (h + 1) * HEAD_SIZE)
            at = (h // group) * HEAD_SIZE
            attended_ref[:, cols] = (
                context_ref[:, cols] + own_weight_ref[:, cols] * value[:, at : at + HEAD_SIZE]
            ).astype(jnp.bfloat16)
    else:
        total_ref[...] = total
        if prefetch:
            fetch(len(slots), final, ahead).wait()
    for i in range(len(slots)):
        store(i).wait()


def fold(slots, place, core, up, hid_own, hid_other, served, blocks, prefetch=False, state=(),
         finish=()):
    first, last = not state, bool(finish)
    count = len(slots)
    rank, width = blocks[0].shape
    rows = hid_own.shape[0]
    depth, cols = served.shape
    vmem = pl.BlockSpec(memory_space=pltpu.VMEM)
    smem = pl.BlockSpec(memory_space=pltpu.SMEM)
    hbm = pl.BlockSpec(memory_space=pltpu.HBM)
    in_specs = [smem, smem, vmem, vmem, vmem, hbm] + [vmem] * count
    operands = [place, core, up, hid_own, hid_other, served, *blocks]
    aliases = {}
    if not first:
        aliases = {len(operands): 0}
        in_specs += [hbm, vmem]
        operands += state
    in_specs += [vmem] * len(finish)
    operands += finish
    out_shape = [jax.ShapeDtypeStruct((depth, cols), jnp.bfloat16)]
    if last:
        out_shape += [
            jax.ShapeDtypeStruct((rows, cols), jnp.bfloat16),
            jax.ShapeDtypeStruct(finish[1].shape, jnp.bfloat16),
        ]
    else:
        out_shape += [jax.ShapeDtypeStruct((rows, cols), jnp.float32)]
        if prefetch:
            out_shape += [jax.ShapeDtypeStruct((width, cols), jnp.bfloat16)]
    return pl.pallas_call(
        functools.partial(fold_kernel, slots, first, prefetch, last),
        out_shape=out_shape,
        in_specs=in_specs,
        out_specs=[hbm] + [vmem] * (len(out_shape) - 1),
        input_output_aliases=aliases,
        scratch_shapes=[
            pltpu.VMEM((1 if last else count, width, cols), jnp.bfloat16),
            pltpu.VMEM((count, width, cols), jnp.bfloat16),
            pltpu.VMEM((2,) + hid_own.shape, jnp.bfloat16),
            pltpu.SemaphoreType.DMA((count + 1,)),
            pltpu.SemaphoreType.DMA((count,)),
        ],
        compiler_params=pltpu.CompilerParams(vmem_limit_bytes=24 * 2**20),
        cost_estimate=pl.CostEstimate(
            flops=2 * count * width * cols * (rank + rows),
            bytes_accessed=4 * count * width * cols,
            transcendentals=0,
        ),
        name="fold_blocks",
    )(*operands)


def ring_member(spot, n):
    return jnp.where(spot < (n + 1) // 2, 2 * spot, 2 * (n - 1 - spot) + 1)


def body(
    hidden_in,
    queries,
    stored_keys,
    stored_values,
    fresh_token_key,
    lengths,
    served_value_weight,
    adapter_in,
    adapter_out,
    owner_rank,
):
    n = lax.axis_size("replica")
    replica = lax.axis_index("replica")
    core = lax.axis_index("tensor")
    swap = [(0, 1), (1, 0)]
    order = list(range(0, n, 2)) + list(range(n - 1 - n % 2, 0, -2))
    around = []
    for spot in range(n):
        here, there = order[spot], order[(spot + 1) % n]
        around.append((here * 2, there * 2))
        around.append((there * 2 + 1, here * 2 + 1))

    rows = queries.shape[0]
    split = rows // 2
    cache = [
        pltpu.with_memory_space_constraint(x, pltpu.HBM) for x in (stored_keys, stored_values)
    ]
    given = (queries.reshape(rows, -1, HEAD_SIZE), *cache, fresh_token_key.astype(jnp.float32), lengths)
    parts = []

    steps = n // 2
    shifts, cuts = [0], []
    for step in range(1, steps + 1):
        shifts += [step, -step] if 2 * step < n else [step]
        cuts.append(len(shifts))
    spot = jnp.where(replica % 2 == 0, replica // 2, n - 1 - replica // 2)
    way = jnp.where(core == 0, -1, 1)
    source = ring_member((spot + way * jnp.array(shifts, jnp.int32) + n) % n, n)
    spots = jnp.arange(n, dtype=jnp.int32)[None, :]
    place = jnp.sum(jnp.where(owner_rank[None, :] == source[:, None], spots, 0), axis=1)

    served = pltpu.with_memory_space_constraint(served_value_weight, pltpu.HBM)
    blocks, state, done = [adapter_in], [], 0
    passed = adapter_in
    for step in range(1, steps + 1):
        passed = lax.ppermute(passed, ("replica", "tensor"), around)
        if step == 1:
            hid_other = lax.ppermute(hidden_in, "tensor", swap)
            up = lax.all_to_all(
                jnp.broadcast_to(adapter_out[None], (n,) + adapter_out.shape),
                "replica", split_axis=0, concat_axis=0,
            ).reshape(n * adapter_out.shape[0], adapter_out.shape[1])
            common = (
                place.astype(jnp.int32), core.astype(jnp.int32).reshape(1), up, hidden_in,
                hid_other, served,
            )
            parts.append(attend(0, split, *given, up))
            beside = parts[0]
        elif step == 2:
            parts.append(attend(split, rows - split, *given, blocks[1]))
            beside = parts[1]
        else:
            upto = n - 1 if step == steps else cuts[step - 3]
            state = fold(
                range(done, upto), *common, blocks[done:upto], prefetch=step == steps, state=state
            )
            beside, done = state, upto
        if step < steps:
            passed, beside = lax.optimization_barrier((passed, beside))
            if step <= 2:
                parts[-1] = beside
            else:
                state = beside
        blocks.append(passed)
        if 2 * step < n:
            blocks.append(lax.ppermute(passed, "tensor", swap))
    context, own_weight = (
        jnp.concatenate(pair, axis=0).reshape(queries.shape) for pair in zip(*parts)
    )
    merged, total, ahead = state
    merged, fresh_token_value, attended = fold(
        range(done, n), *common, blocks[done:], state=[merged, total],
        finish=[ahead, context, own_weight],
    )
    return (merged, fresh_token_value, attended)


def solution(mesh):
    in_specs = (
        P(("groups", "replica"), "tensor"),
        P(("groups", "replica"), "tensor"),
        P(("groups", "replica"), None, "tensor"),
        P(("groups", "replica"), None, "tensor"),
        P(("groups", "replica"), "tensor"),
        P(("groups", "replica")),
        P(None, "tensor"),
        P("groups", "replica"),
        P(("groups", "replica"), "tensor"),
        P("groups"),
    )
    out_specs = (
        P("groups", "tensor"),
        P(("groups", "replica"), "tensor"),
        P(("groups", "replica"), "tensor"),
    )
    return jax.shard_map(body, mesh=mesh, in_specs=in_specs, out_specs=out_specs, check_vma=False)
```

```python
import functools

import jax
import jax.numpy as jnp
from jax import lax
from jax.experimental import pallas as pl
from jax.experimental.pallas import tpu as pltpu
from jax.sharding import PartitionSpec as P

HEAD_SIZE = 128
ADAPTER_SCALE = 2.0

SMEM = pl.BlockSpec(memory_space=pltpu.SMEM)
VMEM = pl.BlockSpec(memory_space=pltpu.VMEM)
HBM = pl.BlockSpec(memory_space=pltpu.HBM)


def in_hbm(*arrays):
    return [pltpu.with_memory_space_constraint(x, pltpu.HBM) for x in arrays]


def attend_kernel(rows, lengths_hbm, q_ref, own_k_ref, k_hbm, v_hbm, *rest):
    context_ref, own_weight_ref, lengths, k_buf, v_buf, length_sem, k_sem, v_sem = rest[-8:]

    def copies(i, row):
        return (
            pltpu.make_async_copy(k_hbm.at[row], k_buf.at[i], k_sem.at[i]),
            pltpu.make_async_copy(v_hbm.at[row], v_buf.at[i], v_sem.at[i]),
        )

    get_lengths = pltpu.make_async_copy(lengths_hbm, lengths, length_sem)
    get_lengths.start()
    for i, row in enumerate(rows):
        for copy in copies(i, row):
            copy.start()
    queries = q_ref[...].astype(jnp.float32)
    own_keys = own_k_ref[...].astype(jnp.float32)
    heads = queries.shape[1] // HEAD_SIZE
    cache_len, width = k_buf.shape[1:]
    local_heads = width // HEAD_SIZE
    group = heads // local_heads
    scaling = 1.0 / HEAD_SIZE**0.5
    head_of = lax.broadcasted_iota(jnp.int32, (heads, HEAD_SIZE), 0) // group
    position = lax.broadcasted_iota(jnp.int32, (heads, cache_len), 1)
    get_lengths.wait()
    for i, row in enumerate(rows):
        q = jnp.concatenate(
            [
                queries[row : row + 1, h * HEAD_SIZE : (h + 1) * HEAD_SIZE]
                for h in range(heads)
            ],
            axis=0,
        )
        spread = jnp.concatenate(
            [jnp.where(head_of == h, q, 0.0) for h in range(local_heads)], axis=1
        )
        own = jnp.sum(spread * own_keys[row : row + 1], axis=1, keepdims=True) * scaling
        get_keys, get_values = copies(i, row)
        get_keys.wait()
        scores = (
            lax.dot_general(
                spread.astype(jnp.bfloat16), k_buf[i], (((1,), (1,)), ((), ())),
                preferred_element_type=jnp.float32,
            )
            * scaling
        )
        valid = position < lengths[row]
        masked = jnp.where(valid, scores, -1e30)
        largest = jnp.maximum(jnp.max(masked, axis=1, keepdims=True), own)
        cached_exp = jnp.where(valid, jnp.exp(masked - largest), 0.0)
        own_exp = jnp.exp(own - largest)
        normaliser = jnp.sum(cached_exp, axis=1, keepdims=True) + own_exp
        weights = (cached_exp / normaliser).astype(jnp.bfloat16)
        weight_own = (own_exp / normaliser).astype(jnp.bfloat16).astype(jnp.float32)
        get_values.wait()
        wide = jnp.dot(weights, v_buf[i], preferred_element_type=jnp.float32)
        context = wide[:, :HEAD_SIZE]
        for h in range(1, local_heads):
            context = jnp.where(
                head_of == h, wide[:, h * HEAD_SIZE : (h + 1) * HEAD_SIZE], context
            )
        context_ref[i] = context
        own_weight_ref[i] = jnp.broadcast_to(weight_own, (heads, HEAD_SIZE))


def attend(rows, lengths, queries, own_key, stored_keys, stored_values, after):
    cache_len, width = stored_keys.shape[1:]
    heads = queries.shape[1] // HEAD_SIZE
    count = len(rows)
    out = jax.ShapeDtypeStruct((count, heads, HEAD_SIZE), jnp.float32)
    return pl.pallas_call(
        functools.partial(attend_kernel, rows),
        out_shape=(out, out),
        in_specs=[HBM, VMEM, VMEM, HBM, HBM] + [pl.BlockSpec(memory_space=pl.ANY)] * len(after),
        out_specs=(VMEM, VMEM),
        scratch_shapes=[
            pltpu.SMEM(lengths.shape, jnp.int32),
            pltpu.VMEM((count, cache_len, width), jnp.bfloat16),
            pltpu.VMEM((count, cache_len, width), jnp.bfloat16),
            pltpu.SemaphoreType.DMA,
            pltpu.SemaphoreType.DMA((count,)),
            pltpu.SemaphoreType.DMA((count,)),
        ],
        compiler_params=pltpu.CompilerParams(vmem_limit_bytes=16 * 2**20),
        cost_estimate=pl.CostEstimate(
            flops=4 * count * heads * cache_len * width,
            bytes_accessed=4 * count * cache_len * width,
            transcendentals=count * heads * cache_len,
        ),
        name="attend_cache",
    )(lengths, queries, own_key, stored_keys, stored_values, *after)


def fold_kernel(slots, first, prefetch, last, place_hbm, up_ref, features_ref, served, *rest):
    rest = list(rest)
    count, ahead_count = len(slots), len(prefetch)
    blocks = [rest.pop(0) for _ in slots]
    if not first:
        rest.pop(0)
        total = rest.pop(0)[...]
    if last:
        ahead, context_ref, own_weight_ref = rest[:3]
        merged, fresh_hbm, attended_hbm = rest[3:6]
        place, place_sem, m_buf, out_sem, fresh_ref, attended_ref, small_sem = rest[6:]
    else:
        merged, total_ref = rest[:2]
        rest = rest[2:]
        if prefetch:
            ahead = rest.pop(0)
        place, place_sem, m_buf, out_sem, w_buf, in_sem = rest
    width = blocks[0].shape[1]

    def rows_of(slot):
        return pl.ds(pl.multiple_of(place[slot] * width, width), width)

    def fetch(i, slot, into):
        return pltpu.make_async_copy(served.at[rows_of(slot)], into, in_sem.at[i])

    def store(i):
        return pltpu.make_async_copy(m_buf.at[i], merged.at[rows_of(slots[i])], out_sem.at[i])

    get_place = pltpu.make_async_copy(place_hbm, place, place_sem)
    get_place.start()
    up = (up_ref[...].astype(jnp.float32) * ADAPTER_SCALE).astype(jnp.bfloat16)
    if not last:
        get_place.wait()
        for i, slot in enumerate(slots):
            fetch(i, slot, w_buf.at[i]).start()
        for i, slot in enumerate(prefetch):
            fetch(count + i, slot, ahead.at[i]).start()
    if first:
        total = jnp.zeros(total_ref.shape, jnp.float32)
    for i, slot in enumerate(slots):
        update = lax.dot_general(
            blocks[i][...], up, (((0,), (0,)), ((), ())), preferred_element_type=jnp.float32
        )
        if last:
            rows = ahead[i]
        else:
            fetch(i, slot, w_buf.at[i]).wait()
            rows = w_buf[i]
        rows = (rows.astype(jnp.float32) + update).astype(jnp.bfloat16)
        m_buf[i] = rows
        if last and i == 0:
            get_place.wait()
        store(i).start()
        total = total + jnp.dot(
            features_ref[:, rows_of(slot)], rows, preferred_element_type=jnp.float32
        )
    if last:
        fresh = total.astype(jnp.bfloat16)
        fresh_ref[...] = fresh
        put_fresh = pltpu.make_async_copy(fresh_ref, fresh_hbm, small_sem.at[0])
        put_fresh.start()
        value = fresh.astype(jnp.float32)
        heads = attended_ref.shape[1] // HEAD_SIZE
        group = heads // (fresh_ref.shape[1] // HEAD_SIZE)
        for h in range(heads):
            cols = slice(h * HEAD_SIZE, (h + 1) * HEAD_SIZE)
            at = (h // group) * HEAD_SIZE
            attended_ref[:, cols] = (
                context_ref[:, cols] + own_weight_ref[:, cols] * value[:, at : at + HEAD_SIZE]
            ).astype(jnp.bfloat16)
        put_attended = pltpu.make_async_copy(attended_ref, attended_hbm, small_sem.at[1])
        put_attended.start()
        put_fresh.wait()
        put_attended.wait()
    else:
        total_ref[...] = total
        for i, slot in enumerate(prefetch):
            fetch(count + i, slot, ahead.at[i]).wait()
    for i in range(count):
        store(i).wait()


def fold(slots, place, up, features, served, blocks, prefetch=(), state=(), finish=()):
    first, last = not state, bool(finish)
    count = len(slots)
    rank, width = blocks[0].shape
    rows = features.shape[0]
    depth, cols = served.shape
    in_specs = [HBM, VMEM, VMEM, HBM] + [VMEM] * count
    operands = [place, up, features, served, *blocks]
    aliases = {}
    if not first:
        aliases = {len(operands): 0}
        in_specs += [HBM, VMEM]
        operands += state
    in_specs += [VMEM] * len(finish)
    operands += finish
    out_shape = [jax.ShapeDtypeStruct((depth, cols), jnp.bfloat16)]
    out_specs = [HBM]
    scratch = [
        pltpu.SMEM(place.shape, jnp.int32),
        pltpu.SemaphoreType.DMA,
        pltpu.VMEM((count, width, cols), jnp.bfloat16),
        pltpu.SemaphoreType.DMA((count,)),
    ]
    if last:
        smalls = [(rows, cols), finish[1].shape]
        out_shape += [jax.ShapeDtypeStruct(shape, jnp.bfloat16) for shape in smalls]
        out_specs += [HBM, HBM]
        scratch += [pltpu.VMEM(shape, jnp.bfloat16) for shape in smalls]
        scratch += [pltpu.SemaphoreType.DMA((2,))]
    else:
        out_shape += [jax.ShapeDtypeStruct((rows, cols), jnp.float32)]
        out_specs += [VMEM]
        if prefetch:
            out_shape += [jax.ShapeDtypeStruct((len(prefetch), width, cols), jnp.bfloat16)]
            out_specs += [VMEM]
        scratch += [
            pltpu.VMEM((count, width, cols), jnp.bfloat16),
            pltpu.SemaphoreType.DMA((count + len(prefetch),)),
        ]
    return pl.pallas_call(
        functools.partial(fold_kernel, slots, first, prefetch, last),
        out_shape=out_shape,
        in_specs=in_specs,
        out_specs=out_specs,
        input_output_aliases=aliases,
        scratch_shapes=scratch,
        compiler_params=pltpu.CompilerParams(vmem_limit_bytes=24 * 2**20),
        cost_estimate=pl.CostEstimate(
            flops=2 * count * width * cols * (rank + rows),
            bytes_accessed=4 * count * width * cols,
            transcendentals=0,
        ),
        name="fold_blocks",
    )(*operands)


def ring_member(spot, n):
    return jnp.where(spot < (n + 1) // 2, 2 * spot, 2 * (n - 1 - spot) + 1)


def body(
    hidden_in,
    queries,
    stored_keys,
    stored_values,
    fresh_token_key,
    lengths,
    served_value_weight,
    adapter_in,
    adapter_out,
    owner_rank,
):
    n = lax.axis_size("replica")
    replica = lax.axis_index("replica")
    core = lax.axis_index("tensor")
    swap = [(0, 1), (1, 0)]
    order = list(range(0, n, 2)) + list(range(n - 1 - n % 2, 0, -2))
    around = []
    for spot in range(n):
        here, there = order[spot], order[(spot + 1) % n]
        around.append((here * 2, there * 2))
        around.append((there * 2 + 1, here * 2 + 1))
    steps = n // 2
    rows = queries.shape[0]
    split = rows // 2
    given = (*in_hbm(lengths), queries, fresh_token_key, *in_hbm(stored_keys, stored_values))

    shifts, cuts = [0], []
    for step in range(1, steps + 1):
        shifts += [step, -step] if 2 * step < n else [step]
        cuts.append(len(shifts))
    spot = jnp.where(replica % 2 == 0, replica // 2, n - 1 - replica // 2)
    way = jnp.where(core == 0, -1, 1)
    source = ring_member((spot + way * jnp.array(shifts, jnp.int32) + n) % n, n)
    spots = jnp.arange(n, dtype=jnp.int32)[None, :]
    place = jnp.sum(jnp.where(owner_rank[None, :] == source[:, None], spots, 0), axis=1)
    place = place.astype(jnp.int32)

    def doubled(have):
        size = have.shape[0] // adapter_out.shape[0]
        more = have[: min(size, n - size) * adapter_out.shape[0]]
        back = [(i, (i - size) % n) for i in range(n)]
        return lax.ppermute(more, "replica", back)

    (served,) = in_hbm(served_value_weight)
    blocks, state, done = [adapter_in], [], 0
    parts = []
    passed = adapter_in
    up = adapter_out
    for step in range(1, steps + 1):
        passed = lax.ppermute(passed, ("replica", "tensor"), around)
        if step == 1:
            more = doubled(up)
        if step <= 2:
            part = range(split) if step == 1 else range(split, rows)
            beside = attend(part, *given, blocks[1:2])
            passed, beside, more = lax.optimization_barrier((passed, beside, more))
            parts.append(beside)
            up = jnp.concatenate([up, more], axis=0)
            more = doubled(up)
        if step == 1:
            hid_other, parts[0] = lax.optimization_barrier((hidden_in, parts[0]))
            hid_other = lax.ppermute(hid_other, "tensor", swap)
        if step == 2:
            up = jnp.concatenate([up, more], axis=0)
            while up.shape[0] < n * adapter_out.shape[0]:
                up = jnp.concatenate([up, doubled(up)], axis=0)
            up = jnp.roll(up, replica * adapter_out.shape[0], axis=0)
            features = jnp.concatenate([hidden_in, hid_other], axis=1)
            features = jnp.where(
                core == 0, features, jnp.concatenate([hid_other, hidden_in], axis=1)
            )
            common = (place, up, features, served)
        if step > 2:
            upto = n - 1 if step == steps else cuts[step - 3]
            prefetch = range(upto, n) if step == steps else ()
            state = fold(range(done, upto), *common, blocks[done:upto], prefetch, state)
            done = upto
            if step < steps:
                passed, state = lax.optimization_barrier((passed, state))
        blocks.append(passed)
        if 2 * step < n:
            blocks.append(lax.ppermute(passed, "tensor", swap))
    context, own_weight = (
        jnp.concatenate(pair, axis=0).reshape(queries.shape) for pair in zip(*parts)
    )
    merged, total, ahead = state
    merged, fresh_token_value, attended = fold(
        range(done, n), *common, blocks[done:], state=[merged, total],
        finish=[ahead, context, own_weight],
    )
    return (merged, fresh_token_value, attended)


def solution(mesh):
    in_specs = (
        P(("groups", "replica"), "tensor"),
        P(("groups", "replica"), "tensor"),
        P(("groups", "replica"), None, "tensor"),
        P(("groups", "replica"), None, "tensor"),
        P(("groups", "replica"), "tensor"),
        P(("groups", "replica")),
        P(None, "tensor"),
        P("groups", "replica"),
        P(("groups", "replica"), "tensor"),
        P("groups"),
    )
    out_specs = (
        P("groups", "tensor"),
        P(("groups", "replica"), "tensor"),
        P(("groups", "replica"), "tensor"),
    )
    return jax.shard_map(body, mesh=mesh, in_specs=in_specs, out_specs=out_specs, check_vma=False)
```

```python
import functools

import jax
import jax.numpy as jnp
from jax import lax
from jax.experimental import pallas as pl
from jax.experimental.pallas import tpu as pltpu
from jax.sharding import PartitionSpec as P

HEAD_SIZE = 128
ADAPTER_SCALE = 2.0

SMEM = pl.BlockSpec(memory_space=pltpu.SMEM)
VMEM = pl.BlockSpec(memory_space=pltpu.VMEM)
HBM = pl.BlockSpec(memory_space=pltpu.HBM)


def in_hbm(*arrays):
    return [pltpu.with_memory_space_constraint(x, pltpu.HBM) for x in arrays]


def attend_kernel(rows, lengths_hbm, q_ref, own_k_ref, k_hbm, v_hbm, served_hbm, context_ref,
                  own_weight_ref, served_ref, lengths, k_buf, v_buf, length_sem, k_sem, v_sem,
                  served_sem):
    def copies(i, row):
        return (
            pltpu.make_async_copy(k_hbm.at[row], k_buf.at[i], k_sem.at[i]),
            pltpu.make_async_copy(v_hbm.at[row], v_buf.at[i], v_sem.at[i]),
        )

    get_lengths = pltpu.make_async_copy(lengths_hbm, lengths, length_sem)
    get_lengths.start()
    for i, row in enumerate(rows):
        for copy in copies(i, row):
            copy.start()
    get_served = pltpu.make_async_copy(served_hbm, served_ref, served_sem)
    get_served.start()
    queries = q_ref[...].astype(jnp.float32)
    own_keys = own_k_ref[...].astype(jnp.float32)
    heads = queries.shape[1] // HEAD_SIZE
    cache_len, width = k_buf.shape[1:]
    local_heads = width // HEAD_SIZE
    group = heads // local_heads
    scaling = 1.0 / HEAD_SIZE**0.5
    head_of = lax.broadcasted_iota(jnp.int32, (heads, HEAD_SIZE), 0) // group
    position = lax.broadcasted_iota(jnp.int32, (heads, cache_len), 1)
    get_lengths.wait()
    for i, row in enumerate(rows):
        q = jnp.concatenate(
            [
                queries[row : row + 1, h * HEAD_SIZE : (h + 1) * HEAD_SIZE]
                for h in range(heads)
            ],
            axis=0,
        )
        spread = jnp.concatenate(
            [jnp.where(head_of == h, q, 0.0) for h in range(local_heads)], axis=1
        )
        own = jnp.sum(spread * own_keys[row : row + 1], axis=1, keepdims=True) * scaling
        get_keys, get_values = copies(i, row)
        get_keys.wait()
        scores = (
            lax.dot_general(
                spread.astype(jnp.bfloat16), k_buf[i], (((1,), (1,)), ((), ())),
                preferred_element_type=jnp.float32,
            )
            * scaling
        )
        valid = position < lengths[row]
        masked = jnp.where(valid, scores, -1e30)
        largest = jnp.maximum(jnp.max(masked, axis=1, keepdims=True), own)
        cached_exp = jnp.where(valid, jnp.exp(masked - largest), 0.0)
        own_exp = jnp.exp(own - largest)
        normaliser = jnp.sum(cached_exp, axis=1, keepdims=True) + own_exp
        weights = (cached_exp / normaliser).astype(jnp.bfloat16)
        weight_own = (own_exp / normaliser).astype(jnp.bfloat16).astype(jnp.float32)
        get_values.wait()
        wide = jnp.dot(weights, v_buf[i], preferred_element_type=jnp.float32)
        context = wide[:, :HEAD_SIZE]
        for h in range(1, local_heads):
            context = jnp.where(
                head_of == h, wide[:, h * HEAD_SIZE : (h + 1) * HEAD_SIZE], context
            )
        context_ref[i] = context
        own_weight_ref[i] = jnp.broadcast_to(weight_own, (heads, HEAD_SIZE))
    get_served.wait()


def attend(lengths, queries, own_key, stored_keys, stored_values, served):
    count, cache_len, width = stored_keys.shape
    heads = queries.shape[1] // HEAD_SIZE
    out = jax.ShapeDtypeStruct((count, heads, HEAD_SIZE), jnp.float32)
    return pl.pallas_call(
        functools.partial(attend_kernel, range(count)),
        out_shape=(out, out, jax.ShapeDtypeStruct(served.shape, served.dtype)),
        in_specs=[HBM, VMEM, VMEM, HBM, HBM, HBM],
        out_specs=(VMEM, VMEM, VMEM),
        scratch_shapes=[
            pltpu.SMEM(lengths.shape, jnp.int32),
            pltpu.VMEM((count, cache_len, width), jnp.bfloat16),
            pltpu.VMEM((count, cache_len, width), jnp.bfloat16),
            pltpu.SemaphoreType.DMA,
            pltpu.SemaphoreType.DMA((count,)),
            pltpu.SemaphoreType.DMA((count,)),
            pltpu.SemaphoreType.DMA,
        ],
        compiler_params=pltpu.CompilerParams(vmem_limit_bytes=16 * 2**20),
        cost_estimate=pl.CostEstimate(
            flops=4 * count * heads * cache_len * width,
            bytes_accessed=4 * count * cache_len * width + 4 * served.size,
            transcendentals=count * heads * cache_len,
        ),
        name="attend_cache",
    )(lengths, queries, own_key, stored_keys, stored_values, served)


def fold_kernel(groups, count, last, start_hbm, up_ref, features_ref, served_ref, *rest):
    rest = list(rest)
    arrays = [rest.pop(0) for _ in groups]
    if last:
        rest.pop(0)
        total_ref, context_ref, own_weight_ref = rest[:3]
        merged, fresh_hbm, attended_hbm = rest[3:6]
        start, start_sem, m_buf, out_sem, fresh_ref, attended_ref, small_sem = rest[6:]
        total = total_ref[...]
    else:
        merged, total_ref, start, start_sem, m_buf, out_sem = rest
        total = jnp.zeros(total_ref.shape, jnp.float32)
    rank = up_ref.shape[0]
    width = arrays[0].shape[2]

    get_start = pltpu.make_async_copy(start_hbm, start, start_sem)
    get_start.start()
    up = (up_ref[...].astype(jnp.float32) * ADAPTER_SCALE).astype(jnp.bfloat16)
    stores = []
    for array, (entry, slab, size) in zip(arrays, groups):
        for i in range(size):
            update = lax.dot_general(
                array[slab + i, :rank], up, (((0,), (0,)), ((), ())),
                preferred_element_type=jnp.float32,
            )
            if not stores:
                get_start.wait()
            rows = pl.ds(pl.multiple_of(start[entry + i], width), width)
            fold = (served_ref[rows, :].astype(jnp.float32) + update).astype(jnp.bfloat16)
            at = len(stores)
            m_buf[at] = fold
            stores.append(pltpu.make_async_copy(m_buf.at[at], merged.at[rows], out_sem.at[at]))
            stores[-1].start()
            total = total + jnp.dot(
                features_ref[:, rows], fold, preferred_element_type=jnp.float32
            )
    if last:
        fresh = total.astype(jnp.bfloat16)
        fresh_ref[...] = fresh
        put_fresh = pltpu.make_async_copy(fresh_ref, fresh_hbm, small_sem.at[0])
        put_fresh.start()
        value = fresh.astype(jnp.float32)
        heads = attended_ref.shape[1] // HEAD_SIZE
        group = heads // (fresh_ref.shape[1] // HEAD_SIZE)
        for h in range(heads):
            cols = slice(h * HEAD_SIZE, (h + 1) * HEAD_SIZE)
            at = (h // group) * HEAD_SIZE
            attended_ref[:, cols] = (
                context_ref[:, cols] + own_weight_ref[:, cols] * value[:, at : at + HEAD_SIZE]
            ).astype(jnp.bfloat16)
        put_attended = pltpu.make_async_copy(attended_ref, attended_hbm, small_sem.at[1])
        put_attended.start()
        put_fresh.wait()
        put_attended.wait()
    else:
        total_ref[...] = total
    for store in stores:
        store.wait()


def fold(groups, start, up, features, served, arrays, state=(), finish=()):
    count = sum(size for _, _, size in groups)
    last = bool(finish)
    rank, cols = up.shape
    width = arrays[0].shape[2]
    rows, depth = features.shape
    in_specs = [HBM, VMEM, VMEM, VMEM] + [VMEM] * len(arrays)
    operands = [start, up, features, served, *arrays]
    aliases = {}
    out_shape = [jax.ShapeDtypeStruct((depth, cols), jnp.bfloat16)]
    out_specs = [HBM]
    scratch = [
        pltpu.SMEM(start.shape, jnp.int32),
        pltpu.SemaphoreType.DMA,
        pltpu.VMEM((count, width, cols), jnp.bfloat16),
        pltpu.SemaphoreType.DMA((count,)),
    ]
    if last:
        aliases = {len(operands): 0}
        in_specs += [HBM, VMEM] + [VMEM] * len(finish)
        operands += [*state, *finish]
        smalls = [(rows, cols), finish[0].shape]
        out_shape += [jax.ShapeDtypeStruct(shape, jnp.bfloat16) for shape in smalls]
        out_specs += [HBM, HBM]
        scratch += [pltpu.VMEM(shape, jnp.bfloat16) for shape in smalls]
        scratch += [pltpu.SemaphoreType.DMA((2,))]
    else:
        out_shape += [jax.ShapeDtypeStruct((rows, cols), jnp.float32)]
        out_specs += [VMEM]
    return pl.pallas_call(
        functools.partial(fold_kernel, groups, count, last),
        out_shape=out_shape,
        in_specs=in_specs,
        out_specs=out_specs,
        input_output_aliases=aliases,
        scratch_shapes=scratch,
        compiler_params=pltpu.CompilerParams(vmem_limit_bytes=24 * 2**20),
        cost_estimate=pl.CostEstimate(
            flops=2 * count * width * cols * (rank + rows),
            bytes_accessed=4 * count * width * cols,
            transcendentals=0,
        ),
        name="fold_blocks",
    )(*operands)


def body(
    hidden_in,
    queries,
    stored_keys,
    stored_values,
    fresh_token_key,
    lengths,
    served_value_weight,
    adapter_in,
    adapter_out,
    owner_rank,
):
    n = lax.axis_size("replica")
    replica = lax.axis_index("replica")
    core = lax.axis_index("tensor")
    swap = [(0, 1), (1, 0)]
    rank, full = adapter_in.shape
    width = full // 2
    per, cols = adapter_out.shape

    bits = [n >> i for i in range(1, n.bit_length())]
    ways = [bits, bits[:-2] + bits[:-3:-1]]

    def exchange(x, step):
        pairs = [(2 * i + c, 2 * (i ^ ways[c][step]) + c) for i in range(n) for c in range(2)]
        return lax.ppermute(x, ("replica", "tensor"), pairs)

    slab = jnp.arange(n, dtype=jnp.int32)
    sources = []
    for way in ways:
        source = replica
        for step, bit in enumerate(way):
            source = source ^ (((slab >> step) & 1) * bit)
        sources.append(source)
    mine = jnp.where(core == 0, sources[0], sources[1])
    theirs = jnp.where(core == 0, sources[1], sources[0])

    source = jnp.concatenate([mine, theirs])
    place = jnp.sum(jnp.where(owner_rank[None, :] == source[:, None], slab[None, :], 0), axis=1)
    half = jnp.concatenate([jnp.full((n,), core), jnp.full((n,), 1 - core)])
    start = (place * full + half * width).astype(jnp.int32)

    up_rows = -(-per * cols // width)
    spare = -up_rows % 8
    slabs = jnp.concatenate(
        [
            lax.dynamic_slice_in_dim(adapter_in, core * width, width, axis=1),
            adapter_out.reshape(up_rows, width),
            jnp.zeros((spare, width), adapter_in.dtype),
        ],
        axis=0,
    )[None]
    *early, final = range(len(bits))
    for step in early:
        came = exchange(slabs, step)
        if step == early[0]:
            context, own_weight, served = attend(
                *in_hbm(lengths), queries, fresh_token_key,
                *in_hbm(stored_keys, stored_values, served_value_weight),
            )
            came, hidden, context, own_weight, served = lax.optimization_barrier(
                (came, hidden_in, context, own_weight, served)
            )
            hid_other = lax.ppermute(hidden, "tensor", swap)
        slabs = jnp.concatenate([slabs, came], axis=0)
    last = exchange(slabs, final)
    crossed = lax.ppermute(slabs, "tensor", swap)
    last_crossed = lax.ppermute(last, "tensor", swap)

    features = jnp.concatenate([hidden_in, hid_other], axis=1)
    features = jnp.where(core == 0, features, jnp.concatenate([hid_other, hidden_in], axis=1))

    ups = jnp.concatenate([slabs[:, rank : rank + up_rows], last[:, rank : rank + up_rows]], axis=0)
    ups = ups.reshape(n, per, cols)
    pick = (slab[:, None] == mine[None, :]).astype(jnp.bfloat16)
    up = jnp.einsum("ij,jkc->ikc", pick, ups, preferred_element_type=jnp.float32)
    up = up.astype(jnp.bfloat16).reshape(rank, cols)

    early_count = slabs.shape[0]
    late_count = n - early_count
    state = fold(
        [(0, 0, early_count), (n, 0, early_count), (early_count, 0, late_count)],
        start, up, features, served, [slabs, crossed, last],
    )
    context, own_weight = (x.reshape(queries.shape) for x in (context, own_weight))
    merged, fresh_token_value, attended = fold(
        [(n + early_count, 0, late_count)], start, up, features, served, [last_crossed],
        state=state, finish=[context, own_weight],
    )
    return (merged, fresh_token_value, attended)


def solution(mesh):
    in_specs = (
        P(("groups", "replica"), "tensor"),
        P(("groups", "replica"), "tensor"),
        P(("groups", "replica"), None, "tensor"),
        P(("groups", "replica"), None, "tensor"),
        P(("groups", "replica"), "tensor"),
        P(("groups", "replica")),
        P(None, "tensor"),
        P("groups", "replica"),
        P(("groups", "replica"), "tensor"),
        P("groups"),
    )
    out_specs = (
        P("groups", "tensor"),
        P(("groups", "replica"), "tensor"),
        P(("groups", "replica"), "tensor"),
    )
    return jax.shard_map(body, mesh=mesh, in_specs=in_specs, out_specs=out_specs, check_vma=False)
```

```python
import functools

import jax
import jax.numpy as jnp
from jax import lax
from jax.experimental import pallas as pl
from jax.experimental.pallas import tpu as pltpu
from jax.sharding import PartitionSpec as P

HEAD_SIZE = 128
ADAPTER_SCALE = 2.0

SMEM = pl.BlockSpec(memory_space=pltpu.SMEM)
VMEM = pl.BlockSpec(memory_space=pltpu.VMEM)
HBM = pl.BlockSpec(memory_space=pltpu.HBM)


def in_hbm(*arrays):
    return [pltpu.with_memory_space_constraint(x, pltpu.HBM) for x in arrays]


def attend_kernel(rows, lengths_hbm, q_hbm, own_k_hbm, k_hbm, v_hbm, *rest):
    context_ref, own_weight_ref, lengths, q_ref, own_k_ref, k_buf, v_buf, small_sem, k_sem, v_sem = (
        rest[-10:]
    )
    smalls = [
        pltpu.make_async_copy(source, into, small_sem.at[i])
        for i, (source, into) in enumerate(
            [(lengths_hbm, lengths), (q_hbm, q_ref), (own_k_hbm, own_k_ref)]
        )
    ]
    for copy in smalls:
        copy.start()

    def copies(i, row):
        return (
            pltpu.make_async_copy(k_hbm.at[row], k_buf.at[i], k_sem.at[i]),
            pltpu.make_async_copy(v_hbm.at[row], v_buf.at[i], v_sem.at[i]),
        )

    for i, row in enumerate(rows):
        for copy in copies(i, row):
            copy.start()
    for copy in smalls:
        copy.wait()
    queries = q_ref[...].astype(jnp.float32)
    own_keys = own_k_ref[...].astype(jnp.float32)
    heads = queries.shape[1] // HEAD_SIZE
    cache_len, width = k_buf.shape[1:]
    local_heads = width // HEAD_SIZE
    group = heads // local_heads
    scaling = 1.0 / HEAD_SIZE**0.5
    head_of = lax.broadcasted_iota(jnp.int32, (heads, HEAD_SIZE), 0) // group
    position = lax.broadcasted_iota(jnp.int32, (heads, cache_len), 1)
    for i, row in enumerate(rows):
        q = jnp.concatenate(
            [
                queries[row : row + 1, h * HEAD_SIZE : (h + 1) * HEAD_SIZE]
                for h in range(heads)
            ],
            axis=0,
        )
        spread = jnp.concatenate(
            [jnp.where(head_of == h, q, 0.0) for h in range(local_heads)], axis=1
        )
        own = jnp.sum(spread * own_keys[row : row + 1], axis=1, keepdims=True) * scaling
        get_keys, get_values = copies(i, row)
        get_keys.wait()
        scores = (
            lax.dot_general(
                spread.astype(jnp.bfloat16), k_buf[i], (((1,), (1,)), ((), ())),
                preferred_element_type=jnp.float32,
            )
            * scaling
        )
        valid = position < lengths[row]
        masked = jnp.where(valid, scores, -1e30)
        largest = jnp.maximum(jnp.max(masked, axis=1, keepdims=True), own)
        cached_exp = jnp.where(valid, jnp.exp(masked - largest), 0.0)
        own_exp = jnp.exp(own - largest)
        normaliser = jnp.sum(cached_exp, axis=1, keepdims=True) + own_exp
        weights = (cached_exp / normaliser).astype(jnp.bfloat16)
        weight_own = (own_exp / normaliser).astype(jnp.bfloat16).astype(jnp.float32)
        get_values.wait()
        wide = jnp.dot(weights, v_buf[i], preferred_element_type=jnp.float32)
        context = wide[:, :HEAD_SIZE]
        for h in range(1, local_heads):
            context = jnp.where(
                head_of == h, wide[:, h * HEAD_SIZE : (h + 1) * HEAD_SIZE], context
            )
        context_ref[i] = context
        own_weight_ref[i] = jnp.broadcast_to(weight_own, (heads, HEAD_SIZE))


def attend(rows, lengths, queries, own_key, stored_keys, stored_values, *after):
    cache_len, width = stored_keys.shape[1:]
    heads = queries.shape[1] // HEAD_SIZE
    count = len(rows)
    out = jax.ShapeDtypeStruct((count, heads, HEAD_SIZE), jnp.float32)
    return pl.pallas_call(
        functools.partial(attend_kernel, rows),
        out_shape=(out, out),
        in_specs=[HBM] * 5 + [pl.BlockSpec(memory_space=pl.ANY)] * len(after),
        out_specs=(VMEM, VMEM),
        scratch_shapes=[
            pltpu.SMEM(lengths.shape, jnp.int32),
            pltpu.VMEM(queries.shape, jnp.bfloat16),
            pltpu.VMEM(own_key.shape, jnp.bfloat16),
            pltpu.VMEM((count, cache_len, width), jnp.bfloat16),
            pltpu.VMEM((count, cache_len, width), jnp.bfloat16),
            pltpu.SemaphoreType.DMA((3,)),
            pltpu.SemaphoreType.DMA((count,)),
            pltpu.SemaphoreType.DMA((count,)),
        ],
        compiler_params=pltpu.CompilerParams(vmem_limit_bytes=16 * 2**20),
        cost_estimate=pl.CostEstimate(
            flops=4 * count * heads * cache_len * width,
            bytes_accessed=4 * count * cache_len * width,
            transcendentals=count * heads * cache_len,
        ),
        name="attend_cache",
    )(lengths, queries, own_key, stored_keys, stored_values, *after)


def fold_kernel(sizes, entry, ahead_from, stage, start_hbm, up_ref, features_ref, *rest):
    rest = list(rest)
    first, last = stage == 0, stage == 2
    served = rest.pop(0)
    arrays = [rest.pop(0) for _ in sizes]
    if not first:
        rest.pop(0)
        total = rest.pop(0)[...]
    if last:
        context_ref, own_weight_ref = rest[:2]
        merged, fresh_hbm, attended_hbm = rest[2:5]
        start, start_sem, m_buf, out_sem, fresh_ref, attended_ref, small_sem = rest[5:]
    elif first:
        merged, total_ref, ahead_ref, start, start_sem, m_buf, out_sem, w_buf, in_sem = rest
        total = jnp.zeros(total_ref.shape, jnp.float32)
    else:
        merged, total_ref, start, start_sem, m_buf, out_sem = rest
    width = arrays[0].shape[2]
    count = sum(sizes)

    def rows_of(i):
        return pl.ds(pl.multiple_of(start[entry + i], width), width)

    def fetch(i):
        into = w_buf.at[i] if i < count else ahead_ref.at[i - count]
        return pltpu.make_async_copy(served.at[rows_of(i)], into, in_sem.at[i])

    def store(i):
        return pltpu.make_async_copy(m_buf.at[i], merged.at[rows_of(i)], out_sem.at[i])

    get_start = pltpu.make_async_copy(start_hbm, start, start_sem)
    get_start.start()
    up = (up_ref[...].astype(jnp.float32) * ADAPTER_SCALE).astype(jnp.bfloat16)
    if first:
        get_start.wait()
        for i in range(start.shape[0]):
            fetch(i).start()
    slabs = [array.at[k] for array, size in zip(arrays, sizes) for k in range(size)]
    for i, slab in enumerate(slabs):
        update = lax.dot_general(
            slab[...], up, (((0,), (0,)), ((), ())), preferred_element_type=jnp.float32
        )
        if first:
            fetch(i).wait()
            rows = w_buf[i]
        else:
            rows = served[ahead_from + i]
        fold = (rows.astype(jnp.float32) + update).astype(jnp.bfloat16)
        m_buf[i] = fold
        if i == 0 and not first:
            get_start.wait()
        store(i).start()
        total = total + jnp.dot(
            features_ref[:, rows_of(i)], fold, preferred_element_type=jnp.float32
        )
    if last:
        fresh = total.astype(jnp.bfloat16)
        fresh_ref[...] = fresh
        put_fresh = pltpu.make_async_copy(fresh_ref, fresh_hbm, small_sem.at[0])
        put_fresh.start()
        value = fresh.astype(jnp.float32)
        heads = attended_ref.shape[1] // HEAD_SIZE
        group = heads // (fresh_ref.shape[1] // HEAD_SIZE)
        for h in range(heads):
            cols = slice(h * HEAD_SIZE, (h + 1) * HEAD_SIZE)
            at = (h // group) * HEAD_SIZE
            attended_ref[:, cols] = (
                context_ref[:, cols] + own_weight_ref[:, cols] * value[:, at : at + HEAD_SIZE]
            ).astype(jnp.bfloat16)
        put_attended = pltpu.make_async_copy(attended_ref, attended_hbm, small_sem.at[1])
        put_attended.start()
        put_fresh.wait()
        put_attended.wait()
    else:
        total_ref[...] = total
    if first:
        for i in range(count, start.shape[0]):
            fetch(i).wait()
    for i in range(count):
        store(i).wait()


def fold(stage, entry, start, up, features, served, arrays, ahead_from=0, state=(), finish=()):
    first, last = stage == 0, stage == 2
    sizes = [array.shape[0] for array in arrays]
    count = sum(sizes)
    ahead = start.shape[0] - count
    rank, cols = up.shape
    width = arrays[0].shape[2]
    rows, depth = features.shape
    in_specs = [HBM, VMEM, VMEM, HBM if first else VMEM] + [VMEM] * len(arrays)
    operands = [start, up, features, served, *arrays]
    aliases = {}
    out_shape = [jax.ShapeDtypeStruct((depth, cols), jnp.bfloat16)]
    out_specs = [HBM]
    scratch = [
        pltpu.SMEM(start.shape, jnp.int32),
        pltpu.SemaphoreType.DMA,
        pltpu.VMEM((count, width, cols), jnp.bfloat16),
        pltpu.SemaphoreType.DMA((count,)),
    ]
    if not first:
        aliases = {len(operands): 0}
        in_specs += [HBM, VMEM] + [VMEM] * len(finish)
        operands += [*state, *finish]
    if last:
        smalls = [(rows, cols), finish[0].shape]
        out_shape += [jax.ShapeDtypeStruct(shape, jnp.bfloat16) for shape in smalls]
        out_specs += [HBM, HBM]
        scratch += [pltpu.VMEM(shape, jnp.bfloat16) for shape in smalls]
        scratch += [pltpu.SemaphoreType.DMA((2,))]
    else:
        out_shape += [jax.ShapeDtypeStruct((rows, cols), jnp.float32)]
        out_specs += [VMEM]
    if first:
        out_shape += [jax.ShapeDtypeStruct((ahead, width, cols), jnp.bfloat16)]
        out_specs += [VMEM]
        scratch += [
            pltpu.VMEM((count, width, cols), jnp.bfloat16),
            pltpu.SemaphoreType.DMA((count + ahead,)),
        ]
    return pl.pallas_call(
        functools.partial(fold_kernel, sizes, entry, ahead_from, stage),
        out_shape=out_shape,
        in_specs=in_specs,
        out_specs=out_specs,
        input_output_aliases=aliases,
        scratch_shapes=scratch,
        compiler_params=pltpu.CompilerParams(vmem_limit_bytes=24 * 2**20),
        cost_estimate=pl.CostEstimate(
            flops=2 * count * width * cols * (rank + rows),
            bytes_accessed=4 * count * width * cols,
            transcendentals=0,
        ),
        name="fold_blocks",
    )(*operands)


def body(
    hidden_in,
    queries,
    stored_keys,
    stored_values,
    fresh_token_key,
    lengths,
    served_value_weight,
    adapter_in,
    adapter_out,
    owner_rank,
):
    n = lax.axis_size("replica")
    replica = lax.axis_index("replica")
    core = lax.axis_index("tensor")
    swap = [(0, 1), (1, 0)]
    full = adapter_in.shape[1]
    width = full // 2
    rows = queries.shape[0]

    bits = [n >> i for i in range(1, n.bit_length())]
    ways = [bits, bits[:-2] + bits[:-3:-1]]

    def exchange(x, step):
        pairs = [(2 * i + c, 2 * (i ^ ways[c][step]) + c) for i in range(n) for c in range(2)]
        return lax.ppermute(x, ("replica", "tensor"), pairs)

    def grown(up, bit):
        came = lax.ppermute(up, "replica", [(i, i ^ bit) for i in range(n)])
        above, below = jnp.concatenate([up, came], axis=0), jnp.concatenate([came, up], axis=0)
        return jnp.where((replica & bit) == 0, above, below)

    given = (
        *in_hbm(lengths, queries, fresh_token_key, stored_keys, stored_values),
    )
    slabs = lax.dynamic_slice_in_dim(adapter_in, core * width, width, axis=1)[None]
    up, hid_other = adapter_out, hidden_in
    *early, final = range(len(bits))
    parts = []
    split = rows // 2
    for step in early:
        came = exchange(slabs, step)
        if step == 0:
            grown_up = grown(up, 1)
            parts.append(attend(range(split), *given))
            up, parts[0], hid_other, owner_rank = lax.optimization_barrier(
                (grown_up, parts[0], hid_other, owner_rank)
            )
            grown_up = grown(up, 2)
            hid_other = lax.ppermute(hid_other, "tensor", swap)
            came, up = lax.optimization_barrier((came, grown_up))
        elif step == 1:
            grown_up = grown(up, 4)
            parts.append(attend(range(split, rows), *given, slabs, up))
            came, up, parts[1] = lax.optimization_barrier((came, grown_up, parts[1]))
        slabs = jnp.concatenate([slabs, came], axis=0)
    for step in range(3, len(bits)):
        up = grown(up, 1 << step)
    last = exchange(slabs, final)
    crossed = lax.ppermute(slabs, "tensor", swap)

    features = jnp.concatenate([hidden_in, hid_other], axis=1)
    features = jnp.where(core == 0, features, jnp.concatenate([hid_other, hidden_in], axis=1))

    slab = jnp.arange(n, dtype=jnp.int32)
    sources = []
    for way in ways:
        source = replica
        for step, bit in enumerate(way):
            source = source ^ (((slab >> step) & 1) * bit)
        sources.append(source)
    mine = jnp.where(core == 0, sources[0], sources[1])
    theirs = jnp.where(core == 0, sources[1], sources[0])
    count = slabs.shape[0]
    source = jnp.concatenate([mine[:count], theirs[:count], mine[count:], theirs[count:]])
    half = jnp.where((jnp.arange(2 * n) // count) % 2 == 0, core, 1 - core)
    place = jnp.sum(jnp.where(owner_rank[None, :] == source[:, None], slab[None, :], 0), axis=1)
    start = (place * full + half * width).astype(jnp.int32)

    merged, total, ahead = fold(
        0, 0, start, up, features, *in_hbm(served_value_weight), [slabs, crossed]
    )
    last, total = lax.optimization_barrier((last, total))
    last_crossed = lax.ppermute(last, "tensor", swap)
    merged, total = fold(
        1, 2 * count, start, up, features, ahead, [last], state=[merged, total]
    )
    context, own_weight = (
        jnp.concatenate(pair, axis=0).reshape(queries.shape) for pair in zip(*parts)
    )
    merged, fresh_token_value, attended = fold(
        2, 3 * count, start, up, features, ahead, [last_crossed], ahead_from=count,
        state=[merged, total], finish=[context, own_weight],
    )
    return (merged, fresh_token_value, attended)


def solution(mesh):
    in_specs = (
        P(("groups", "replica"), "tensor"),
        P(("groups", "replica"), "tensor"),
        P(("groups", "replica"), None, "tensor"),
        P(("groups", "replica"), None, "tensor"),
        P(("groups", "replica"), "tensor"),
        P(("groups", "replica")),
        P(None, "tensor"),
        P("groups", "replica"),
        P(("groups", "replica"), "tensor"),
        P("groups"),
    )
    out_specs = (
        P("groups", "tensor"),
        P(("groups", "replica"), "tensor"),
        P(("groups", "replica"), "tensor"),
    )
    return jax.shard_map(body, mesh=mesh, in_specs=in_specs, out_specs=out_specs, check_vma=False)
```

```python
import functools

import jax
import jax.numpy as jnp
from jax import lax
from jax.experimental import pallas as pl
from jax.experimental.pallas import tpu as pltpu
from jax.sharding import PartitionSpec as P

HEAD_SIZE = 128
ADAPTER_SCALE = 2.0

SMEM = pl.BlockSpec(memory_space=pltpu.SMEM)
VMEM = pl.BlockSpec(memory_space=pltpu.VMEM)
HBM = pl.BlockSpec(memory_space=pltpu.HBM)


def in_hbm(*arrays):
    return [pltpu.with_memory_space_constraint(x, pltpu.HBM) for x in arrays]


def attend_kernel(rows, fetch, lengths_hbm, q_hbm, own_k_hbm, k_hbm, v_hbm, *rest):
    rest = list(rest)
    if fetch:
        served_hbm, served_ref, served_sem = rest.pop(0), rest.pop(-10), rest.pop(-1)
    context_ref, own_weight_ref, lengths, q_ref, own_k_ref, k_buf, v_buf, small_sem, k_sem, v_sem = (
        rest[-10:]
    )
    smalls = [
        pltpu.make_async_copy(source, into, small_sem.at[i])
        for i, (source, into) in enumerate(
            [(lengths_hbm, lengths), (q_hbm, q_ref), (own_k_hbm, own_k_ref)]
        )
    ]
    for copy in smalls:
        copy.start()

    def copies(i, row):
        return (
            pltpu.make_async_copy(k_hbm.at[row], k_buf.at[i], k_sem.at[i]),
            pltpu.make_async_copy(v_hbm.at[row], v_buf.at[i], v_sem.at[i]),
        )

    for i, row in enumerate(rows):
        for copy in copies(i, row):
            copy.start()
    if fetch:
        get_served = pltpu.make_async_copy(served_hbm, served_ref, served_sem)
        get_served.start()
    for copy in smalls:
        copy.wait()
    queries = q_ref[...].astype(jnp.float32)
    own_keys = own_k_ref[...].astype(jnp.float32)
    heads = queries.shape[1] // HEAD_SIZE
    cache_len, width = k_buf.shape[1:]
    local_heads = width // HEAD_SIZE
    group = heads // local_heads
    scaling = 1.0 / HEAD_SIZE**0.5
    head_of = lax.broadcasted_iota(jnp.int32, (heads, HEAD_SIZE), 0) // group
    position = lax.broadcasted_iota(jnp.int32, (heads, cache_len), 1)
    for i, row in enumerate(rows):
        q = jnp.concatenate(
            [
                queries[row : row + 1, h * HEAD_SIZE : (h + 1) * HEAD_SIZE]
                for h in range(heads)
            ],
            axis=0,
        )
        spread = jnp.concatenate(
            [jnp.where(head_of == h, q, 0.0) for h in range(local_heads)], axis=1
        )
        own = jnp.sum(spread * own_keys[row : row + 1], axis=1, keepdims=True) * scaling
        get_keys, get_values = copies(i, row)
        get_keys.wait()
        scores = (
            lax.dot_general(
                spread.astype(jnp.bfloat16), k_buf[i], (((1,), (1,)), ((), ())),
                preferred_element_type=jnp.float32,
            )
            * scaling
        )
        valid = position < lengths[row]
        masked = jnp.where(valid, scores, -1e30)
        largest = jnp.maximum(jnp.max(masked, axis=1, keepdims=True), own)
        cached_exp = jnp.where(valid, jnp.exp(masked - largest), 0.0)
        own_exp = jnp.exp(own - largest)
        normaliser = jnp.sum(cached_exp, axis=1, keepdims=True) + own_exp
        weights = (cached_exp / normaliser).astype(jnp.bfloat16)
        weight_own = (own_exp / normaliser).astype(jnp.bfloat16).astype(jnp.float32)
        get_values.wait()
        wide = jnp.dot(weights, v_buf[i], preferred_element_type=jnp.float32)
        context = wide[:, :HEAD_SIZE]
        for h in range(1, local_heads):
            context = jnp.where(
                head_of == h, wide[:, h * HEAD_SIZE : (h + 1) * HEAD_SIZE], context
            )
        context_ref[i] = context
        own_weight_ref[i] = jnp.broadcast_to(weight_own, (heads, HEAD_SIZE))
    if fetch:
        get_served.wait()


def attend(rows, given, served=None, after=()):
    lengths, queries, own_key, stored_keys, stored_values = given
    fetch = served is not None
    cache_len, width = stored_keys.shape[1:]
    heads = queries.shape[1] // HEAD_SIZE
    count = len(rows)
    out_shape = [jax.ShapeDtypeStruct((count, heads, HEAD_SIZE), jnp.float32)] * 2
    if fetch:
        out_shape += [jax.ShapeDtypeStruct(served.shape, served.dtype)]
    return pl.pallas_call(
        functools.partial(attend_kernel, rows, fetch),
        out_shape=out_shape,
        in_specs=[HBM] * (5 + fetch) + [pl.BlockSpec(memory_space=pl.ANY)] * len(after),
        out_specs=[VMEM] * len(out_shape),
        scratch_shapes=[
            pltpu.SMEM(lengths.shape, jnp.int32),
            pltpu.VMEM(queries.shape, jnp.bfloat16),
            pltpu.VMEM(own_key.shape, jnp.bfloat16),
            pltpu.VMEM((count, cache_len, width), jnp.bfloat16),
            pltpu.VMEM((count, cache_len, width), jnp.bfloat16),
            pltpu.SemaphoreType.DMA((3,)),
            pltpu.SemaphoreType.DMA((count,)),
            pltpu.SemaphoreType.DMA((count,)),
        ]
        + [pltpu.SemaphoreType.DMA] * fetch,
        compiler_params=pltpu.CompilerParams(vmem_limit_bytes=12 * 2**20),
        cost_estimate=pl.CostEstimate(
            flops=4 * count * heads * cache_len * width,
            bytes_accessed=4 * count * cache_len * width,
            transcendentals=count * heads * cache_len,
        ),
        name="attend_cache",
    )(*given, *([served] if fetch else []), *after)


def fold_kernel(sizes, entry, stage, start_hbm, up_ref, features_ref, served_ref, *rest):
    rest = list(rest)
    first, last = stage == 0, stage == 2
    arrays = [rest.pop(0) for _ in sizes]
    if not first:
        rest.pop(0)
        total = rest.pop(0)[...]
    if last:
        context_ref, own_weight_ref = rest[:2]
        merged, fresh_hbm, attended_hbm = rest[2:5]
        start, start_sem, m_buf, out_sem, fresh_ref, attended_ref, small_sem = rest[5:]
    else:
        merged, total_ref, start, start_sem, m_buf, out_sem = rest
    if first:
        total = jnp.zeros(total_ref.shape, jnp.float32)
    width = arrays[0].shape[2]
    count = sum(sizes)

    def rows_of(i):
        return pl.ds(pl.multiple_of(start[entry + i], width), width)

    def store(i):
        return pltpu.make_async_copy(m_buf.at[i], merged.at[rows_of(i)], out_sem.at[i])

    get_start = pltpu.make_async_copy(start_hbm, start, start_sem)
    get_start.start()
    up = (up_ref[...].astype(jnp.float32) * ADAPTER_SCALE).astype(jnp.bfloat16)
    slabs = [array.at[k] for array, size in zip(arrays, sizes) for k in range(size)]
    for i, slab in enumerate(slabs):
        update = lax.dot_general(
            slab[...], up, (((0,), (0,)), ((), ())), preferred_element_type=jnp.float32
        )
        if i == 0:
            get_start.wait()
        fold = (served_ref[rows_of(i), :].astype(jnp.float32) + update).astype(jnp.bfloat16)
        m_buf[i] = fold
        store(i).start()
        total = total + jnp.dot(
            features_ref[:, rows_of(i)], fold, preferred_element_type=jnp.float32
        )
    if last:
        fresh = total.astype(jnp.bfloat16)
        fresh_ref[...] = fresh
        put_fresh = pltpu.make_async_copy(fresh_ref, fresh_hbm, small_sem.at[0])
        put_fresh.start()
        value = fresh.astype(jnp.float32)
        heads = attended_ref.shape[1] // HEAD_SIZE
        group = heads // (fresh_ref.shape[1] // HEAD_SIZE)
        for h in range(heads):
            cols = slice(h * HEAD_SIZE, (h + 1) * HEAD_SIZE)
            at = (h // group) * HEAD_SIZE
            attended_ref[:, cols] = (
                context_ref[:, cols] + own_weight_ref[:, cols] * value[:, at : at + HEAD_SIZE]
            ).astype(jnp.bfloat16)
        put_attended = pltpu.make_async_copy(attended_ref, attended_hbm, small_sem.at[1])
        put_attended.start()
        put_fresh.wait()
        put_attended.wait()
    else:
        total_ref[...] = total
    for i in range(count):
        store(i).wait()


def fold(stage, entry, start, up, features, served, arrays, state=(), finish=()):
    first, last = stage == 0, stage == 2
    sizes = [array.shape[0] for array in arrays]
    count = sum(sizes)
    rank, cols = up.shape
    width = arrays[0].shape[2]
    rows, depth = features.shape
    in_specs = [HBM, VMEM, VMEM, VMEM] + [VMEM] * len(arrays)
    operands = [start, up, features, served, *arrays]
    aliases = {}
    out_shape = [jax.ShapeDtypeStruct((depth, cols), jnp.bfloat16)]
    out_specs = [HBM]
    scratch = [
        pltpu.SMEM(start.shape, jnp.int32),
        pltpu.SemaphoreType.DMA,
        pltpu.VMEM((count, width, cols), jnp.bfloat16),
        pltpu.SemaphoreType.DMA((count,)),
    ]
    if not first:
        aliases = {len(operands): 0}
        in_specs += [HBM, VMEM] + [VMEM] * len(finish)
        operands += [*state, *finish]
    if last:
        smalls = [(rows, cols), finish[0].shape]
        out_shape += [jax.ShapeDtypeStruct(shape, jnp.bfloat16) for shape in smalls]
        out_specs += [HBM, HBM]
        scratch += [pltpu.VMEM(shape, jnp.bfloat16) for shape in smalls]
        scratch += [pltpu.SemaphoreType.DMA((2,))]
    else:
        out_shape += [jax.ShapeDtypeStruct((rows, cols), jnp.float32)]
        out_specs += [VMEM]
    return pl.pallas_call(
        functools.partial(fold_kernel, sizes, entry, stage),
        out_shape=out_shape,
        in_specs=in_specs,
        out_specs=out_specs,
        input_output_aliases=aliases,
        scratch_shapes=scratch,
        compiler_params=pltpu.CompilerParams(vmem_limit_bytes=12 * 2**20),
        cost_estimate=pl.CostEstimate(
            flops=2 * count * width * cols * (rank + rows),
            bytes_accessed=4 * count * width * cols,
            transcendentals=0,
        ),
        name="fold_blocks",
    )(*operands)


def body(
    hidden_in,
    queries,
    stored_keys,
    stored_values,
    fresh_token_key,
    lengths,
    served_value_weight,
    adapter_in,
    adapter_out,
    owner_rank,
):
    n = lax.axis_size("replica")
    replica = lax.axis_index("replica")
    core = lax.axis_index("tensor")
    swap = [(0, 1), (1, 0)]
    full = adapter_in.shape[1]
    width = full // 2
    rows = queries.shape[0]

    bits = [n >> i for i in range(1, n.bit_length())]
    ways = [bits, bits[:-2] + bits[:-3:-1]]

    def exchange(x, step):
        pairs = [(2 * i + c, 2 * (i ^ ways[c][step]) + c) for i in range(n) for c in range(2)]
        return lax.ppermute(x, ("replica", "tensor"), pairs)

    def grown(up, bit):
        came = lax.ppermute(up, "replica", [(i, i ^ bit) for i in range(n)])
        above, below = jnp.concatenate([up, came], axis=0), jnp.concatenate([came, up], axis=0)
        return jnp.where((replica & bit) == 0, above, below)

    given = (
        *in_hbm(lengths, queries, fresh_token_key, stored_keys, stored_values),
    )
    slabs = lax.dynamic_slice_in_dim(adapter_in, core * width, width, axis=1)[None]
    up, hid_other = adapter_out, hidden_in
    *early, final = range(len(bits))
    parts = []
    split = rows // 2
    for step in early:
        came = exchange(slabs, step)
        if step == 0:
            grown_up = grown(up, 1)
            parts.append(attend(range(split), given))
            up, parts[0], hid_other, owner_rank = lax.optimization_barrier(
                (grown_up, parts[0], hid_other, owner_rank)
            )
            grown_up = grown(up, 2)
            hid_other = lax.ppermute(hid_other, "tensor", swap)
        elif step == 1:
            *part, served = attend(
                range(split, rows), given, *in_hbm(served_value_weight), [slabs]
            )
            up, part = lax.optimization_barrier((grown_up, part))
            up = grown(up, 4)
            came, part = lax.optimization_barrier((came, part))
            parts.append(part)
        slabs = jnp.concatenate([slabs, came], axis=0)
    for step in range(3, len(bits)):
        up = grown(up, 1 << step)
    last = exchange(slabs, final)
    crossed = lax.ppermute(slabs, "tensor", swap)

    features = jnp.concatenate([hidden_in, hid_other], axis=1)
    features = jnp.where(core == 0, features, jnp.concatenate([hid_other, hidden_in], axis=1))

    slab = jnp.arange(n, dtype=jnp.int32)
    sources = []
    for way in ways:
        source = replica
        for step, bit in enumerate(way):
            source = source ^ (((slab >> step) & 1) * bit)
        sources.append(source)
    mine = jnp.where(core == 0, sources[0], sources[1])
    theirs = jnp.where(core == 0, sources[1], sources[0])
    count = slabs.shape[0]
    source = jnp.concatenate([mine[:count], theirs[:count], mine[count:], theirs[count:]])
    half = jnp.where((jnp.arange(2 * n) // count) % 2 == 0, core, 1 - core)
    place = jnp.sum(jnp.where(owner_rank[None, :] == source[:, None], slab[None, :], 0), axis=1)
    start = (place * full + half * width).astype(jnp.int32)

    merged, total = fold(
        0, 0, start, up, features, served, [slabs, crossed]
    )
    last, total = lax.optimization_barrier((last, total))
    last_crossed = lax.ppermute(last, "tensor", swap)
    merged, total = fold(
        1, 2 * count, start, up, features, served, [last], state=[merged, total]
    )
    context, own_weight = (
        jnp.concatenate(pair, axis=0).reshape(queries.shape) for pair in zip(*parts)
    )
    merged, fresh_token_value, attended = fold(
        2, 3 * count, start, up, features, served, [last_crossed], state=[merged, total],
        finish=[context, own_weight],
    )
    return (merged, fresh_token_value, attended)


def solution(mesh):
    in_specs = (
        P(("groups", "replica"), "tensor"),
        P(("groups", "replica"), "tensor"),
        P(("groups", "replica"), None, "tensor"),
        P(("groups", "replica"), None, "tensor"),
        P(("groups", "replica"), "tensor"),
        P(("groups", "replica")),
        P(None, "tensor"),
        P("groups", "replica"),
        P(("groups", "replica"), "tensor"),
        P("groups"),
    )
    out_specs = (
        P("groups", "tensor"),
        P(("groups", "replica"), "tensor"),
        P(("groups", "replica"), "tensor"),
    )
    return jax.shard_map(body, mesh=mesh, in_specs=in_specs, out_specs=out_specs, check_vma=False)
```

```python
import functools

import jax
import jax.numpy as jnp
from jax import lax
from jax.experimental import pallas as pl
from jax.experimental.pallas import tpu as pltpu
from jax.sharding import PartitionSpec as P

HEAD_SIZE = 128
ADAPTER_SCALE = 2.0

SMEM = pl.BlockSpec(memory_space=pltpu.SMEM)
VMEM = pl.BlockSpec(memory_space=pltpu.VMEM)
HBM = pl.BlockSpec(memory_space=pltpu.HBM)


def in_hbm(*arrays):
    return [pltpu.with_memory_space_constraint(x, pltpu.HBM) for x in arrays]


def attend_kernel(lengths_hbm, q_hbm, own_k_hbm, k_hbm, v_hbm, *rest):
    context_ref, own_weight_ref, lengths, q_ref, own_k_ref, k_buf, v_buf, small_sem, k_sem, v_sem = (
        rest[-10:]
    )
    smalls = [
        pltpu.make_async_copy(source, into, small_sem.at[i])
        for i, (source, into) in enumerate(
            [(lengths_hbm, lengths), (q_hbm, q_ref), (own_k_hbm, own_k_ref)]
        )
    ]
    for copy in smalls:
        copy.start()

    def copies(row):
        return (
            pltpu.make_async_copy(k_hbm.at[row], k_buf.at[row], k_sem.at[row]),
            pltpu.make_async_copy(v_hbm.at[row], v_buf.at[row], v_sem.at[row]),
        )

    for row in range(k_buf.shape[0]):
        for copy in copies(row):
            copy.start()
    for copy in smalls:
        copy.wait()
    queries = q_ref[...].astype(jnp.float32)
    own_keys = own_k_ref[...].astype(jnp.float32)
    heads = queries.shape[1] // HEAD_SIZE
    cache_len, width = k_buf.shape[1:]
    local_heads = width // HEAD_SIZE
    group = heads // local_heads
    scaling = 1.0 / HEAD_SIZE**0.5
    head_of = lax.broadcasted_iota(jnp.int32, (heads, HEAD_SIZE), 0) // group
    position = lax.broadcasted_iota(jnp.int32, (heads, cache_len), 1)
    for row in range(k_buf.shape[0]):
        q = jnp.concatenate(
            [
                queries[row : row + 1, h * HEAD_SIZE : (h + 1) * HEAD_SIZE]
                for h in range(heads)
            ],
            axis=0,
        )
        spread = jnp.concatenate(
            [jnp.where(head_of == h, q, 0.0) for h in range(local_heads)], axis=1
        )
        own = jnp.sum(spread * own_keys[row : row + 1], axis=1, keepdims=True) * scaling
        get_keys, get_values = copies(row)
        get_keys.wait()
        scores = (
            lax.dot_general(
                spread.astype(jnp.bfloat16), k_buf[row], (((1,), (1,)), ((), ())),
                preferred_element_type=jnp.float32,
            )
            * scaling
        )
        valid = position < lengths[row]
        masked = jnp.where(valid, scores, -1e30)
        largest = jnp.maximum(jnp.max(masked, axis=1, keepdims=True), own)
        cached_exp = jnp.where(valid, jnp.exp(masked - largest), 0.0)
        own_exp = jnp.exp(own - largest)
        normaliser = jnp.sum(cached_exp, axis=1, keepdims=True) + own_exp
        weights = (cached_exp / normaliser).astype(jnp.bfloat16)
        weight_own = (own_exp / normaliser).astype(jnp.bfloat16).astype(jnp.float32)
        get_values.wait()
        wide = jnp.dot(weights, v_buf[row], preferred_element_type=jnp.float32)
        context = wide[:, :HEAD_SIZE]
        for h in range(1, local_heads):
            context = jnp.where(
                head_of == h, wide[:, h * HEAD_SIZE : (h + 1) * HEAD_SIZE], context
            )
        context_ref[row] = context
        own_weight_ref[row] = jnp.broadcast_to(weight_own, (heads, HEAD_SIZE))


def attend(lengths, queries, own_key, stored_keys, stored_values, after):
    count, cache_len, width = stored_keys.shape
    heads = queries.shape[1] // HEAD_SIZE
    out = jax.ShapeDtypeStruct((count, heads, HEAD_SIZE), jnp.float32)
    return pl.pallas_call(
        attend_kernel,
        out_shape=(out, out),
        in_specs=[HBM] * 5 + [pl.BlockSpec(memory_space=pl.ANY)],
        out_specs=(VMEM, VMEM),
        scratch_shapes=[
            pltpu.SMEM(lengths.shape, jnp.int32),
            pltpu.VMEM(queries.shape, jnp.bfloat16),
            pltpu.VMEM(own_key.shape, jnp.bfloat16),
            pltpu.VMEM((count, cache_len, width), jnp.bfloat16),
            pltpu.VMEM((count, cache_len, width), jnp.bfloat16),
            pltpu.SemaphoreType.DMA((3,)),
            pltpu.SemaphoreType.DMA((count,)),
            pltpu.SemaphoreType.DMA((count,)),
        ],
        compiler_params=pltpu.CompilerParams(vmem_limit_bytes=12 * 2**20),
        cost_estimate=pl.CostEstimate(
            flops=4 * count * heads * cache_len * width,
            bytes_accessed=4 * count * cache_len * width,
            transcendentals=count * heads * cache_len,
        ),
        name="attend_cache",
    )(lengths, queries, own_key, stored_keys, stored_values, after)


def fetch_kernel(pieces, source, after, into, sem):
    del after
    size = source.shape[0] // pieces
    copies = [
        pltpu.make_async_copy(
            source.at[pl.ds(i * size, size)], into.at[pl.ds(i * size, size)], sem.at[i]
        )
        for i in range(pieces)
    ]
    for copy in copies:
        copy.start()
    for copy in copies:
        copy.wait()


def fetch(served, after):
    pieces = 8
    return pl.pallas_call(
        functools.partial(fetch_kernel, pieces),
        out_shape=jax.ShapeDtypeStruct(served.shape, served.dtype),
        in_specs=[HBM, pl.BlockSpec(memory_space=pl.ANY)],
        out_specs=VMEM,
        scratch_shapes=[pltpu.SemaphoreType.DMA((pieces,))],
        compiler_params=pltpu.CompilerParams(vmem_limit_bytes=12 * 2**20),
        cost_estimate=pl.CostEstimate(flops=1, bytes_accessed=1, transcendentals=0),
        name="fetch_served",
    )(served, after)


def fold_kernel(sizes, entry, stage, start_hbm, up_ref, features_ref, served_ref, *rest):
    rest = list(rest)
    first, last = stage == 0, stage == 2
    arrays = [rest.pop(0) for _ in sizes]
    if not first:
        rest.pop(0)
        total = rest.pop(0)[...]
    if last:
        context_ref, own_weight_ref = rest[:2]
        merged, fresh_hbm, attended_hbm = rest[2:5]
        start, start_sem, m_buf, out_sem, fresh_ref, attended_ref, small_sem = rest[5:]
    else:
        merged, total_ref, start, start_sem, m_buf, out_sem = rest
    if first:
        total = jnp.zeros(total_ref.shape, jnp.float32)
    width = arrays[0].shape[2]
    count = sum(sizes)

    def rows_of(i):
        return pl.ds(pl.multiple_of(start[entry + i], width), width)

    def store(i):
        return pltpu.make_async_copy(m_buf.at[i], merged.at[rows_of(i)], out_sem.at[i])

    get_start = pltpu.make_async_copy(start_hbm, start, start_sem)
    get_start.start()
    up = (up_ref[...].astype(jnp.float32) * ADAPTER_SCALE).astype(jnp.bfloat16)
    slabs = [array.at[k] for array, size in zip(arrays, sizes) for k in range(size)]
    for i, slab in enumerate(slabs):
        update = lax.dot_general(
            slab[...], up, (((0,), (0,)), ((), ())), preferred_element_type=jnp.float32
        )
        if i == 0:
            get_start.wait()
        fold = (served_ref[rows_of(i), :].astype(jnp.float32) + update).astype(jnp.bfloat16)
        m_buf[i] = fold
        store(i).start()
        total = total + jnp.dot(
            features_ref[:, rows_of(i)], fold, preferred_element_type=jnp.float32
        )
    if last:
        fresh = total.astype(jnp.bfloat16)
        fresh_ref[...] = fresh
        put_fresh = pltpu.make_async_copy(fresh_ref, fresh_hbm, small_sem.at[0])
        put_fresh.start()
        value = fresh.astype(jnp.float32)
        heads = attended_ref.shape[1] // HEAD_SIZE
        group = heads // (fresh_ref.shape[1] // HEAD_SIZE)
        for h in range(heads):
            cols = slice(h * HEAD_SIZE, (h + 1) * HEAD_SIZE)
            at = (h // group) * HEAD_SIZE
            attended_ref[:, cols] = (
                context_ref[:, cols] + own_weight_ref[:, cols] * value[:, at : at + HEAD_SIZE]
            ).astype(jnp.bfloat16)
        put_attended = pltpu.make_async_copy(attended_ref, attended_hbm, small_sem.at[1])
        put_attended.start()
        put_fresh.wait()
        put_attended.wait()
    else:
        total_ref[...] = total
    for i in range(count):
        store(i).wait()


def fold(stage, entry, start, up, features, served, arrays, state=(), finish=()):
    first, last = stage == 0, stage == 2
    sizes = [array.shape[0] for array in arrays]
    count = sum(sizes)
    rank, cols = up.shape
    width = arrays[0].shape[2]
    rows, depth = features.shape
    in_specs = [HBM, VMEM, VMEM, VMEM] + [VMEM] * len(arrays)
    operands = [start, up, features, served, *arrays]
    aliases = {}
    out_shape = [jax.ShapeDtypeStruct((depth, cols), jnp.bfloat16)]
    out_specs = [HBM]
    scratch = [
        pltpu.SMEM(start.shape, jnp.int32),
        pltpu.SemaphoreType.DMA,
        pltpu.VMEM((count, width, cols), jnp.bfloat16),
        pltpu.SemaphoreType.DMA((count,)),
    ]
    if not first:
        aliases = {len(operands): 0}
        in_specs += [HBM, VMEM] + [VMEM] * len(finish)
        operands += [*state, *finish]
    if last:
        smalls = [(rows, cols), finish[0].shape]
        out_shape += [jax.ShapeDtypeStruct(shape, jnp.bfloat16) for shape in smalls]
        out_specs += [HBM, HBM]
        scratch += [pltpu.VMEM(shape, jnp.bfloat16) for shape in smalls]
        scratch += [pltpu.SemaphoreType.DMA((2,))]
    else:
        out_shape += [jax.ShapeDtypeStruct((rows, cols), jnp.float32)]
        out_specs += [VMEM]
    return pl.pallas_call(
        functools.partial(fold_kernel, sizes, entry, stage),
        out_shape=out_shape,
        in_specs=in_specs,
        out_specs=out_specs,
        input_output_aliases=aliases,
        scratch_shapes=scratch,
        compiler_params=pltpu.CompilerParams(vmem_limit_bytes=12 * 2**20),
        cost_estimate=pl.CostEstimate(
            flops=2 * count * width * cols * (rank + rows),
            bytes_accessed=4 * count * width * cols,
            transcendentals=0,
        ),
        name="fold_blocks",
    )(*operands)


def body(
    hidden_in,
    queries,
    stored_keys,
    stored_values,
    fresh_token_key,
    lengths,
    served_value_weight,
    adapter_in,
    adapter_out,
    owner_rank,
):
    n = lax.axis_size("replica")
    replica = lax.axis_index("replica")
    core = lax.axis_index("tensor")
    swap = [(0, 1), (1, 0)]
    full = adapter_in.shape[1]
    width = full // 2

    bits = [n >> i for i in range(1, n.bit_length())]
    ways = [bits, bits[:-2] + bits[:-3:-1]]

    def exchange(x, step):
        pairs = [(2 * i + c, 2 * (i ^ ways[c][step]) + c) for i in range(n) for c in range(2)]
        return lax.ppermute(x, ("replica", "tensor"), pairs)

    def grown(up, bit):
        came = lax.ppermute(up, "replica", [(i, i ^ bit) for i in range(n)])
        above, below = jnp.concatenate([up, came], axis=0), jnp.concatenate([came, up], axis=0)
        return jnp.where((replica & bit) == 0, above, below)

    given = (
        *in_hbm(lengths, queries, fresh_token_key, stored_keys, stored_values),
    )
    hid_other = lax.ppermute(hidden_in, "tensor", swap)
    near = [adapter_out] + [
        lax.ppermute(adapter_out, "replica", [(i, i ^ b) for i in range(n)]) for b in (1, 2, 3)
    ]
    odd = (replica & 1) == 1
    pairs = [
        jnp.where(odd, jnp.concatenate([b, a], axis=0), jnp.concatenate([a, b], axis=0))
        for a, b in (near[:2], near[2:])
    ]
    up = jnp.where(
        (replica & 2) == 0, jnp.concatenate(pairs, axis=0), jnp.concatenate(pairs[::-1], axis=0)
    )
    slabs = lax.dynamic_slice_in_dim(adapter_in, core * width, width, axis=1)[None]
    *early, final = range(len(bits))
    for step in early:
        came = exchange(slabs, step)
        if step == 0:
            attention = attend(*given, slabs)
            came, attention, owner_rank = lax.optimization_barrier((came, attention, owner_rank))
        elif step == 1:
            served = fetch(*in_hbm(served_value_weight), slabs)
            up, served = lax.optimization_barrier((up, served))
            up = grown(up, 4)
            came, served = lax.optimization_barrier((came, served))
        slabs = jnp.concatenate([slabs, came], axis=0)
    for step in range(3, len(bits)):
        up = grown(up, 1 << step)
    last = exchange(slabs, final)

    features = jnp.concatenate([hidden_in, hid_other], axis=1)
    features = jnp.where(core == 0, features, jnp.concatenate([hid_other, hidden_in], axis=1))
    crossed, features = lax.optimization_barrier((slabs, features))
    crossed = lax.ppermute(crossed, "tensor", swap)

    slab = jnp.arange(n, dtype=jnp.int32)
    sources = []
    for way in ways:
        source = replica
        for step, bit in enumerate(way):
            source = source ^ (((slab >> step) & 1) * bit)
        sources.append(source)
    mine = jnp.where(core == 0, sources[0], sources[1])
    theirs = jnp.where(core == 0, sources[1], sources[0])
    count = slabs.shape[0]
    source = jnp.concatenate([mine[:count], theirs[:count], mine[count:], theirs[count:]])
    half = jnp.where((jnp.arange(2 * n) // count) % 2 == 0, core, 1 - core)
    place = jnp.sum(jnp.where(owner_rank[None, :] == source[:, None], slab[None, :], 0), axis=1)
    start = (place * full + half * width).astype(jnp.int32)

    merged, total = fold(
        0, 0, start, up, features, served, [slabs, crossed]
    )
    last, total = lax.optimization_barrier((last, total))
    last_crossed = lax.ppermute(last, "tensor", swap)
    merged, total = fold(
        1, 2 * count, start, up, features, served, [last], state=[merged, total]
    )
    context, own_weight = (x.reshape(queries.shape) for x in attention)
    merged, fresh_token_value, attended = fold(
        2, 3 * count, start, up, features, served, [last_crossed], state=[merged, total],
        finish=[context, own_weight],
    )
    return (merged, fresh_token_value, attended)


def solution(mesh):
    in_specs = (
        P(("groups", "replica"), "tensor"),
        P(("groups", "replica"), "tensor"),
        P(("groups", "replica"), None, "tensor"),
        P(("groups", "replica"), None, "tensor"),
        P(("groups", "replica"), "tensor"),
        P(("groups", "replica")),
        P(None, "tensor"),
        P("groups", "replica"),
        P(("groups", "replica"), "tensor"),
        P("groups"),
    )
    out_specs = (
        P("groups", "tensor"),
        P(("groups", "replica"), "tensor"),
        P(("groups", "replica"), "tensor"),
    )
    return jax.shard_map(body, mesh=mesh, in_specs=in_specs, out_specs=out_specs, check_vma=False)
```

```python
import functools

import jax
import jax.numpy as jnp
from jax import lax
from jax.experimental import pallas as pl
from jax.experimental.pallas import tpu as pltpu
from jax.sharding import PartitionSpec as P

HEAD_SIZE = 128
ADAPTER_SCALE = 2.0

SMEM = pl.BlockSpec(memory_space=pltpu.SMEM)
VMEM = pl.BlockSpec(memory_space=pltpu.VMEM)
HBM = pl.BlockSpec(memory_space=pltpu.HBM)


def in_hbm(*arrays):
    return [pltpu.with_memory_space_constraint(x, pltpu.HBM) for x in arrays]


def attend_kernel(rows, fetch, lengths_hbm, q_hbm, own_k_hbm, k_hbm, v_hbm, *rest):
    rest = list(rest)
    if fetch:
        served_hbm, served_ref, served_sem = rest.pop(0), rest.pop(-10), rest.pop(-1)
    context_ref, own_weight_ref, lengths, q_ref, own_k_ref, k_buf, v_buf, small_sem, k_sem, v_sem = (
        rest[-10:]
    )
    smalls = [
        pltpu.make_async_copy(source, into, small_sem.at[i])
        for i, (source, into) in enumerate(
            [(lengths_hbm, lengths), (q_hbm, q_ref), (own_k_hbm, own_k_ref)]
        )
    ]
    for copy in smalls:
        copy.start()

    def copies(i, row):
        return (
            pltpu.make_async_copy(k_hbm.at[row], k_buf.at[i], k_sem.at[i]),
            pltpu.make_async_copy(v_hbm.at[row], v_buf.at[i], v_sem.at[i]),
        )

    for i, row in enumerate(rows):
        for copy in copies(i, row):
            copy.start()
    if fetch:
        get_served = pltpu.make_async_copy(served_hbm, served_ref, served_sem)
        get_served.start()
    for copy in smalls:
        copy.wait()
    queries = q_ref[...].astype(jnp.float32)
    own_keys = own_k_ref[...].astype(jnp.float32)
    heads = queries.shape[1] // HEAD_SIZE
    cache_len, width = k_buf.shape[1:]
    local_heads = width // HEAD_SIZE
    group = heads // local_heads
    scaling = 1.0 / HEAD_SIZE**0.5
    head_of = lax.broadcasted_iota(jnp.int32, (heads, HEAD_SIZE), 0) // group
    position = lax.broadcasted_iota(jnp.int32, (heads, cache_len), 1)
    for i, row in enumerate(rows):
        q = jnp.concatenate(
            [
                queries[row : row + 1, h * HEAD_SIZE : (h + 1) * HEAD_SIZE]
                for h in range(heads)
            ],
            axis=0,
        )
        spread = jnp.concatenate(
            [jnp.where(head_of == h, q, 0.0) for h in range(local_heads)], axis=1
        )
        own = jnp.sum(spread * own_keys[row : row + 1], axis=1, keepdims=True) * scaling
        get_keys, get_values = copies(i, row)
        get_keys.wait()
        scores = (
            lax.dot_general(
                spread.astype(jnp.bfloat16), k_buf[i], (((1,), (1,)), ((), ())),
                preferred_element_type=jnp.float32,
            )
            * scaling
        )
        valid = position < lengths[row]
        masked = jnp.where(valid, scores, -1e30)
        largest = jnp.maximum(jnp.max(masked, axis=1, keepdims=True), own)
        cached_exp = jnp.where(valid, jnp.exp(masked - largest), 0.0)
        own_exp = jnp.exp(own - largest)
        normaliser = jnp.sum(cached_exp, axis=1, keepdims=True) + own_exp
        weights = (cached_exp / normaliser).astype(jnp.bfloat16)
        weight_own = (own_exp / normaliser).astype(jnp.bfloat16).astype(jnp.float32)
        get_values.wait()
        wide = jnp.dot(weights, v_buf[i], preferred_element_type=jnp.float32)
        context = wide[:, :HEAD_SIZE]
        for h in range(1, local_heads):
            context = jnp.where(
                head_of == h, wide[:, h * HEAD_SIZE : (h + 1) * HEAD_SIZE], context
            )
        context_ref[i] = context
        own_weight_ref[i] = jnp.broadcast_to(weight_own, (heads, HEAD_SIZE))
    if fetch:
        get_served.wait()


def attend(rows, given, served=None, after=()):
    lengths, queries, own_key, stored_keys, stored_values = given
    fetch = served is not None
    cache_len, width = stored_keys.shape[1:]
    heads = queries.shape[1] // HEAD_SIZE
    count = len(rows)
    out_shape = [jax.ShapeDtypeStruct((count, heads, HEAD_SIZE), jnp.float32)] * 2
    if fetch:
        out_shape += [jax.ShapeDtypeStruct(served.shape, served.dtype)]
    return pl.pallas_call(
        functools.partial(attend_kernel, rows, fetch),
        out_shape=out_shape,
        in_specs=[HBM] * (5 + fetch) + [pl.BlockSpec(memory_space=pl.ANY)] * len(after),
        out_specs=[VMEM] * len(out_shape),
        scratch_shapes=[
            pltpu.SMEM(lengths.shape, jnp.int32),
            pltpu.VMEM(queries.shape, jnp.bfloat16),
            pltpu.VMEM(own_key.shape, jnp.bfloat16),
            pltpu.VMEM((count, cache_len, width), jnp.bfloat16),
            pltpu.VMEM((count, cache_len, width), jnp.bfloat16),
            pltpu.SemaphoreType.DMA((3,)),
            pltpu.SemaphoreType.DMA((count,)),
            pltpu.SemaphoreType.DMA((count,)),
        ]
        + [pltpu.SemaphoreType.DMA] * fetch,
        compiler_params=pltpu.CompilerParams(vmem_limit_bytes=12 * 2**20),
        cost_estimate=pl.CostEstimate(
            flops=4 * count * heads * cache_len * width,
            bytes_accessed=4 * count * cache_len * width,
            transcendentals=count * heads * cache_len,
        ),
        name="attend_cache",
    )(*given, *([served] if fetch else []), *after)


class Merge:
    def __init__(self, start_hbm, start, start_sem, merged, out_sem, width):
        self.start, self.merged, self.out_sem, self.width = start, merged, out_sem, width
        self.get_start = pltpu.make_async_copy(start_hbm, start, start_sem)
        self.get_start.start()

    def rows_of(self, entry):
        return pl.ds(pl.multiple_of(self.start[entry], self.width), self.width)

    def store(self, source, entry, at):
        return pltpu.make_async_copy(source, self.merged.at[self.rows_of(entry)], self.out_sem.at[at])

    def rows(self, slab, up, served_ref, features_ref, entry, total):
        update = lax.dot_general(
            slab[: up.shape[0]], up, (((0,), (0,)), ((), ())), preferred_element_type=jnp.float32
        )
        if self.get_start is not None:
            self.get_start.wait()
            self.get_start = None
        rows = self.rows_of(entry)
        fold = (served_ref[rows, :].astype(jnp.float32) + update).astype(jnp.bfloat16)
        part = jnp.dot(features_ref[:, rows], fold, preferred_element_type=jnp.float32)
        return fold, total + part


def merge_kernel(per, left, start_hbm, pick_ref, features_ref, served_ref, slabs_ref, crossed_ref,
                 last_ref, merged, total_ref, up_ref, left_ref, start, start_sem, m_buf, out_sem):
    width = slabs_ref.shape[2]
    rank, cols = up_ref.shape
    merge = Merge(start_hbm, start, start_sem, merged, out_sem, width)
    ups = []
    for ref in (slabs_ref, last_ref):
        for k in range(ref.shape[0]):
            below = ref[k, rank:].astype(jnp.float32)
            if cols <= width:
                ups.append(below[:per, :cols])
            else:
                ups.append(
                    jnp.concatenate(
                        [below[i * per : (i + 1) * per] for i in range(cols // width)], axis=1
                    )
                )
    ups = jnp.concatenate(ups, axis=0).astype(jnp.bfloat16)
    up = jnp.dot(pick_ref[...], ups, preferred_element_type=jnp.float32).astype(jnp.bfloat16)
    up_ref[...] = up
    total = jnp.zeros(total_ref.shape, jnp.float32)
    slabs = [ref.at[k] for ref in (slabs_ref, crossed_ref, last_ref) for k in range(ref.shape[0])]
    keep = len(slabs) - left
    for i, slab in enumerate(slabs):
        fold, total = merge.rows(slab, up, served_ref, features_ref, i, total)
        if i < keep:
            m_buf[i] = fold
            merge.store(m_buf.at[i], i, i).start()
        else:
            left_ref[i - keep] = fold
    total_ref[...] = total
    for i in range(keep):
        merge.store(m_buf.at[i], i, i).wait()


def final_kernel(start_hbm, up_ref, features_ref, served_ref, left_ref, last_ref, merged_in,
                 total_ref, context_ref, own_weight_ref, merged, fresh_hbm, attended_hbm, start,
                 start_sem, m_buf, out_sem, fresh_ref, attended_ref, small_sem):
    del merged_in
    count, _, width = last_ref.shape
    left = left_ref.shape[0]
    merge = Merge(start_hbm, start, start_sem, merged, out_sem, width)
    first = start.shape[0] - count
    total = total_ref[...]
    stores = []
    for i in range(count):
        fold, total = merge.rows(
            last_ref.at[i], up_ref[...], served_ref, features_ref, first + i, total
        )
        if i == 0:
            stores += [
                merge.store(left_ref.at[k], first - left + k, count + k) for k in range(left)
            ]
            for store in stores:
                store.start()
        m_buf[i] = fold
        stores.append(merge.store(m_buf.at[i], first + i, i))
        stores[-1].start()
    fresh = total.astype(jnp.bfloat16)
    fresh_ref[...] = fresh
    put_fresh = pltpu.make_async_copy(fresh_ref, fresh_hbm, small_sem.at[0])
    put_fresh.start()
    value = fresh.astype(jnp.float32)
    heads = attended_ref.shape[1] // HEAD_SIZE
    group = heads // (fresh_ref.shape[1] // HEAD_SIZE)
    for h in range(heads):
        cols = slice(h * HEAD_SIZE, (h + 1) * HEAD_SIZE)
        at = (h // group) * HEAD_SIZE
        attended_ref[:, cols] = (
            context_ref[:, cols] + own_weight_ref[:, cols] * value[:, at : at + HEAD_SIZE]
        ).astype(jnp.bfloat16)
    put_attended = pltpu.make_async_copy(attended_ref, attended_hbm, small_sem.at[1])
    put_attended.start()
    for store in stores:
        store.wait()
    put_fresh.wait()
    put_attended.wait()


def merge(per, start, pick, features, served, slabs, crossed, last):
    left = 3
    count = slabs.shape[0] + crossed.shape[0] + last.shape[0]
    width = slabs.shape[2]
    rank = pick.shape[0]
    depth, cols = served.shape
    return pl.pallas_call(
        functools.partial(merge_kernel, per, left),
        out_shape=(
            jax.ShapeDtypeStruct((depth, cols), jnp.bfloat16),
            jax.ShapeDtypeStruct((features.shape[0], cols), jnp.float32),
            jax.ShapeDtypeStruct((rank, cols), jnp.bfloat16),
            jax.ShapeDtypeStruct((left, width, cols), jnp.bfloat16),
        ),
        in_specs=[HBM] + [VMEM] * 6,
        out_specs=(HBM, VMEM, VMEM, VMEM),
        scratch_shapes=[
            pltpu.SMEM(start.shape, jnp.int32),
            pltpu.SemaphoreType.DMA,
            pltpu.VMEM((count - left, width, cols), jnp.bfloat16),
            pltpu.SemaphoreType.DMA((count - left,)),
        ],
        compiler_params=pltpu.CompilerParams(vmem_limit_bytes=12 * 2**20),
        cost_estimate=pl.CostEstimate(
            flops=2 * count * width * cols * rank,
            bytes_accessed=4 * count * width * cols,
            transcendentals=0,
        ),
        name="merge_blocks",
    )(start, pick, features, served, slabs, crossed, last)


def finish(start, up, features, served, left, last, merged, total, context, own_weight):
    count, _, width = last.shape
    depth, cols = served.shape
    smalls = [total.shape, context.shape]
    return pl.pallas_call(
        final_kernel,
        out_shape=[
            jax.ShapeDtypeStruct(shape, jnp.bfloat16) for shape in [(depth, cols), *smalls]
        ],
        in_specs=[HBM] + [VMEM] * 5 + [HBM] + [VMEM] * 3,
        out_specs=[HBM] * 3,
        input_output_aliases={6: 0},
        scratch_shapes=[
            pltpu.SMEM(start.shape, jnp.int32),
            pltpu.SemaphoreType.DMA,
            pltpu.VMEM((count, width, cols), jnp.bfloat16),
            pltpu.SemaphoreType.DMA((count + left.shape[0],)),
        ]
        + [pltpu.VMEM(shape, jnp.bfloat16) for shape in smalls]
        + [pltpu.SemaphoreType.DMA((2,))],
        compiler_params=pltpu.CompilerParams(vmem_limit_bytes=12 * 2**20),
        cost_estimate=pl.CostEstimate(
            flops=2 * count * width * cols * up.shape[0],
            bytes_accessed=4 * count * width * cols,
            transcendentals=0,
        ),
        name="finish_rows",
    )(start, up, features, served, left, last, merged, total, context, own_weight)


def body(
    hidden_in,
    queries,
    stored_keys,
    stored_values,
    fresh_token_key,
    lengths,
    served_value_weight,
    adapter_in,
    adapter_out,
    owner_rank,
):
    n = lax.axis_size("replica")
    replica = lax.axis_index("replica")
    core = lax.axis_index("tensor")
    swap = [(0, 1), (1, 0)]
    full = adapter_in.shape[1]
    width = full // 2
    rows = queries.shape[0]
    per, cols = adapter_out.shape
    rank = n * per

    bits = [n >> i for i in range(1, n.bit_length())]
    ways = [bits, bits[:-2] + bits[:-3:-1]]

    def exchange(x, step):
        pairs = [(2 * i + c, 2 * (i ^ ways[c][step]) + c) for i in range(n) for c in range(2)]
        return lax.ppermute(x, ("replica", "tensor"), pairs)

    if cols <= width:
        below = jnp.pad(adapter_out, ((0, -per % 8), (0, width - cols)))
    else:
        below = jnp.concatenate(jnp.split(adapter_out, cols // width, axis=1), axis=0)
        below = jnp.pad(below, ((0, -below.shape[0] % 8), (0, 0)))
    slabs = jnp.concatenate(
        [lax.dynamic_slice_in_dim(adapter_in, core * width, width, axis=1), below], axis=0
    )[None]

    given = in_hbm(lengths, queries, fresh_token_key, stored_keys, stored_values)
    *early, final = range(len(bits))
    parts = []
    split = rows // 2
    for step in early:
        came = exchange(slabs, step)
        if step == 0:
            parts.append(attend(range(split), given, after=[slabs]))
            parts[0], hid_other, owner_rank = lax.optimization_barrier(
                (parts[0], hidden_in, owner_rank)
            )
            hid_other = lax.ppermute(hid_other, "tensor", swap)
            came, parts[0] = lax.optimization_barrier((came, parts[0]))
        elif step == 1:
            *part, served = attend(
                range(split, rows), given, *in_hbm(served_value_weight), [slabs]
            )
            came, part = lax.optimization_barrier((came, part))
            parts.append(part)
        slabs = jnp.concatenate([slabs, came], axis=0)
    last = exchange(slabs, final)

    features = jnp.concatenate([hidden_in, hid_other], axis=1)
    features = jnp.where(core == 0, features, jnp.concatenate([hid_other, hidden_in], axis=1))
    crossed, features = lax.optimization_barrier((slabs, features))
    crossed = lax.ppermute(crossed, "tensor", swap)

    slab = jnp.arange(n, dtype=jnp.int32)
    sources = []
    for way in ways:
        source = replica
        for step, bit in enumerate(way):
            source = source ^ (((slab >> step) & 1) * bit)
        sources.append(source)
    mine = jnp.where(core == 0, sources[0], sources[1])
    theirs = jnp.where(core == 0, sources[1], sources[0])
    count = slabs.shape[0]
    source = jnp.concatenate([mine[:count], theirs[:count], mine[count:], theirs[count:]])
    half = jnp.where((jnp.arange(2 * n) // count) % 2 == 0, core, 1 - core)
    place = jnp.sum(jnp.where(owner_rank[None, :] == source[:, None], slab[None, :], 0), axis=1)
    start = (place * full + half * width).astype(jnp.int32)

    row = jnp.arange(rank, dtype=jnp.int32)
    row_source = replica
    for step in range(len(bits)):
        bit = jnp.where(core == 0, ways[0][step], ways[1][step])
        row_source = row_source ^ (((row // per >> step) & 1) * bit)
    pick = jnp.where(
        row[:, None] == (row_source * per + row % per)[None, :], ADAPTER_SCALE, 0.0
    ).astype(jnp.bfloat16)

    context, own_weight = (
        jnp.concatenate(pair, axis=0).reshape(queries.shape) for pair in zip(*parts)
    )
    last, start, pick, context, own_weight = lax.optimization_barrier(
        (last, start, pick, context, own_weight)
    )
    last_crossed = lax.ppermute(last, "tensor", swap)
    merged, total, up, left = merge(per, start, pick, features, served, slabs, crossed, last)
    return tuple(
        finish(
            start, up, features, served, left, last_crossed, merged, total, context, own_weight
        )
    )


def solution(mesh):
    in_specs = (
        P(("groups", "replica"), "tensor"),
        P(("groups", "replica"), "tensor"),
        P(("groups", "replica"), None, "tensor"),
        P(("groups", "replica"), None, "tensor"),
        P(("groups", "replica"), "tensor"),
        P(("groups", "replica")),
        P(None, "tensor"),
        P("groups", "replica"),
        P(("groups", "replica"), "tensor"),
        P("groups"),
    )
    out_specs = (
        P("groups", "tensor"),
        P(("groups", "replica"), "tensor"),
        P(("groups", "replica"), "tensor"),
    )
    return jax.shard_map(body, mesh=mesh, in_specs=in_specs, out_specs=out_specs, check_vma=False)
```

```python
import functools

import jax
import jax.numpy as jnp
from jax import lax
from jax.experimental import pallas as pl
from jax.experimental.pallas import tpu as pltpu
from jax.sharding import PartitionSpec as P

HEAD_SIZE = 128
ADAPTER_SCALE = 2.0

SMEM = pl.BlockSpec(memory_space=pltpu.SMEM)
VMEM = pl.BlockSpec(memory_space=pltpu.VMEM)
HBM = pl.BlockSpec(memory_space=pltpu.HBM)


def in_hbm(*arrays):
    return [pltpu.with_memory_space_constraint(x, pltpu.HBM) for x in arrays]


def attend_kernel(rows, fetch, lengths_hbm, q_hbm, own_k_hbm, k_hbm, v_hbm, *rest):
    rest = list(rest)
    if fetch:
        served_hbm, served_ref, served_sem = rest.pop(0), rest.pop(-10), rest.pop(-1)
    context_ref, own_weight_ref, lengths, q_ref, own_k_ref, k_buf, v_buf, small_sem, k_sem, v_sem = (
        rest[-10:]
    )
    smalls = [
        pltpu.make_async_copy(source, into, small_sem.at[i])
        for i, (source, into) in enumerate(
            [(lengths_hbm, lengths), (q_hbm, q_ref), (own_k_hbm, own_k_ref)]
        )
    ]
    for copy in smalls:
        copy.start()

    def copies(i, row):
        return (
            pltpu.make_async_copy(k_hbm.at[row], k_buf.at[i], k_sem.at[i]),
            pltpu.make_async_copy(v_hbm.at[row], v_buf.at[i], v_sem.at[i]),
        )

    for i, row in enumerate(rows):
        for copy in copies(i, row):
            copy.start()
    if fetch:
        get_served = pltpu.make_async_copy(served_hbm, served_ref, served_sem)
        get_served.start()
    for copy in smalls:
        copy.wait()
    queries = q_ref[...].astype(jnp.float32)
    own_keys = own_k_ref[...].astype(jnp.float32)
    heads = queries.shape[1] // HEAD_SIZE
    cache_len, width = k_buf.shape[1:]
    local_heads = width // HEAD_SIZE
    group = heads // local_heads
    scaling = 1.0 / HEAD_SIZE**0.5
    head_of = lax.broadcasted_iota(jnp.int32, (heads, HEAD_SIZE), 0) // group
    position = lax.broadcasted_iota(jnp.int32, (heads, cache_len), 1)
    for i, row in enumerate(rows):
        q = jnp.concatenate(
            [
                queries[row : row + 1, h * HEAD_SIZE : (h + 1) * HEAD_SIZE]
                for h in range(heads)
            ],
            axis=0,
        )
        spread = jnp.concatenate(
            [jnp.where(head_of == h, q, 0.0) for h in range(local_heads)], axis=1
        )
        own = jnp.sum(spread * own_keys[row : row + 1], axis=1, keepdims=True) * scaling
        get_keys, get_values = copies(i, row)
        get_keys.wait()
        scores = (
            lax.dot_general(
                spread.astype(jnp.bfloat16), k_buf[i], (((1,), (1,)), ((), ())),
                preferred_element_type=jnp.float32,
            )
            * scaling
        )
        valid = position < lengths[row]
        masked = jnp.where(valid, scores, -1e30)
        largest = jnp.maximum(jnp.max(masked, axis=1, keepdims=True), own)
        cached_exp = jnp.where(valid, jnp.exp(masked - largest), 0.0)
        own_exp = jnp.exp(own - largest)
        normaliser = jnp.sum(cached_exp, axis=1, keepdims=True) + own_exp
        weights = (cached_exp / normaliser).astype(jnp.bfloat16)
        weight_own = (own_exp / normaliser).astype(jnp.bfloat16).astype(jnp.float32)
        get_values.wait()
        wide = jnp.dot(weights, v_buf[i], preferred_element_type=jnp.float32)
        context = wide[:, :HEAD_SIZE]
        for h in range(1, local_heads):
            context = jnp.where(
                head_of == h, wide[:, h * HEAD_SIZE : (h + 1) * HEAD_SIZE], context
            )
        context_ref[i] = context
        own_weight_ref[i] = jnp.broadcast_to(weight_own, (heads, HEAD_SIZE))
    if fetch:
        get_served.wait()


def attend(rows, given, served=None, after=()):
    lengths, queries, own_key, stored_keys, stored_values = given
    fetch = served is not None
    cache_len, width = stored_keys.shape[1:]
    heads = queries.shape[1] // HEAD_SIZE
    count = len(rows)
    out_shape = [jax.ShapeDtypeStruct((count, heads, HEAD_SIZE), jnp.float32)] * 2
    if fetch:
        out_shape += [jax.ShapeDtypeStruct(served.shape, served.dtype)]
    return pl.pallas_call(
        functools.partial(attend_kernel, rows, fetch),
        out_shape=out_shape,
        in_specs=[HBM] * (5 + fetch) + [pl.BlockSpec(memory_space=pl.ANY)] * len(after),
        out_specs=[VMEM] * len(out_shape),
        scratch_shapes=[
            pltpu.SMEM(lengths.shape, jnp.int32),
            pltpu.VMEM(queries.shape, jnp.bfloat16),
            pltpu.VMEM(own_key.shape, jnp.bfloat16),
            pltpu.VMEM((count, cache_len, width), jnp.bfloat16),
            pltpu.VMEM((count, cache_len, width), jnp.bfloat16),
            pltpu.SemaphoreType.DMA((3,)),
            pltpu.SemaphoreType.DMA((count,)),
            pltpu.SemaphoreType.DMA((count,)),
        ]
        + [pltpu.SemaphoreType.DMA] * fetch,
        compiler_params=pltpu.CompilerParams(vmem_limit_bytes=12 * 2**20),
        cost_estimate=pl.CostEstimate(
            flops=4 * count * heads * cache_len * width,
            bytes_accessed=4 * count * cache_len * width,
            transcendentals=count * heads * cache_len,
        ),
        name="attend_cache",
    )(*given, *([served] if fetch else []), *after)


def pack_kernel(per, block_hbm, up_hbm, slab_ref, half_ref, up_ref, sem):
    rank, width = half_ref.shape
    cols = up_ref.shape[1]
    first = pl.multiple_of(lax.axis_index("tensor") * width, width)
    copies = [
        pltpu.make_async_copy(block_hbm.at[:, pl.ds(first, width)], half_ref, sem.at[0]),
        pltpu.make_async_copy(up_hbm, up_ref, sem.at[1]),
    ]
    for copy in copies:
        copy.start()
    for copy in copies:
        copy.wait()
    slab_ref[0, :rank] = half_ref[...]
    up = up_ref[...].astype(jnp.float32)
    if cols <= width:
        below = jnp.concatenate([up, jnp.zeros((per, width - cols), jnp.float32)], axis=1)
    else:
        below = jnp.concatenate(
            [up[:, i * width : (i + 1) * width] for i in range(cols // width)], axis=0
        )
    spare = slab_ref.shape[1] - rank - below.shape[0]
    if spare:
        below = jnp.concatenate([below, jnp.zeros((spare, width), jnp.float32)], axis=0)
    slab_ref[0, rank:] = below.astype(jnp.bfloat16)


def pack(block, up):
    rank, full = block.shape
    per, cols = up.shape
    width = full // 2
    below = -(-per * max(cols // width, 1) // 8) * 8
    return pl.pallas_call(
        functools.partial(pack_kernel, per),
        out_shape=jax.ShapeDtypeStruct((1, rank + below, width), block.dtype),
        in_specs=[HBM, HBM],
        out_specs=VMEM,
        scratch_shapes=[
            pltpu.VMEM((rank, width), block.dtype),
            pltpu.VMEM(up.shape, up.dtype),
            pltpu.SemaphoreType.DMA((2,)),
        ],
        name="pack_slab",
    )(*in_hbm(block, up))


class Merge:
    def __init__(self, start_ref, merged, out_sem, width):
        self.start, self.merged, self.out_sem, self.width = start_ref[...], merged, out_sem, width
        self.entry = lax.broadcasted_iota(jnp.int32, self.start.shape, 1)

    def rows_of(self, entry):
        first = jnp.sum(jnp.where(self.entry == entry, self.start, 0))
        return pl.ds(pl.multiple_of(first, self.width), self.width)

    def store(self, source, rows, at):
        return pltpu.make_async_copy(source, self.merged.at[rows], self.out_sem.at[at])

    def rows(self, slab, up, served_ref, features_ref, rows, total):
        update = lax.dot_general(
            slab[: up.shape[0]], up, (((0,), (0,)), ((), ())), preferred_element_type=jnp.float32
        )
        fold = (served_ref[rows, :].astype(jnp.float32) + update).astype(jnp.bfloat16)
        part = jnp.dot(features_ref[:, rows], fold, preferred_element_type=jnp.float32)
        return fold, total + part


def merge_kernel(per, left, start_ref, pick_ref, features_ref, served_ref, slabs_ref, crossed_ref,
                 last_ref, merged, total_ref, up_ref, left_ref, m_buf, out_sem):
    width = slabs_ref.shape[2]
    rank, cols = up_ref.shape
    merge = Merge(start_ref, merged, out_sem, width)
    ups = []
    for ref in (slabs_ref, last_ref):
        for k in range(ref.shape[0]):
            below = ref[k, rank:].astype(jnp.float32)
            if cols <= width:
                ups.append(below[:per, :cols])
            else:
                ups.append(
                    jnp.concatenate(
                        [below[i * per : (i + 1) * per] for i in range(cols // width)], axis=1
                    )
                )
    ups = jnp.concatenate(ups, axis=0).astype(jnp.bfloat16)
    up = jnp.dot(pick_ref[...], ups, preferred_element_type=jnp.float32).astype(jnp.bfloat16)
    up_ref[...] = up
    total = jnp.zeros(total_ref.shape, jnp.float32)
    slabs = [ref.at[k] for ref in (slabs_ref, crossed_ref, last_ref) for k in range(ref.shape[0])]
    keep = len(slabs) - left
    stores = []
    for i, slab in enumerate(slabs):
        rows = merge.rows_of(i)
        fold, total = merge.rows(slab, up, served_ref, features_ref, rows, total)
        if i < keep:
            m_buf[i] = fold
            stores.append(merge.store(m_buf.at[i], rows, i))
            stores[-1].start()
        else:
            left_ref[i - keep] = fold
    total_ref[...] = total
    for store in stores:
        store.wait()


def final_kernel(start_ref, up_ref, features_ref, served_ref, left_ref, last_ref, merged_in,
                 total_ref, context_ref, own_weight_ref, merged, fresh_hbm, attended_hbm, m_buf,
                 out_sem, fresh_ref, attended_ref, small_sem):
    del merged_in
    count, _, width = last_ref.shape
    left = left_ref.shape[0]
    merge = Merge(start_ref, merged, out_sem, width)
    first = start_ref.shape[1] - count
    total = total_ref[...]
    stores = [
        merge.store(left_ref.at[k], merge.rows_of(first - left + k), count + k)
        for k in range(left)
    ]
    for store in stores:
        store.start()
    for i in range(count):
        rows = merge.rows_of(first + i)
        fold, total = merge.rows(last_ref.at[i], up_ref[...], served_ref, features_ref, rows, total)
        m_buf[i] = fold
        stores.append(merge.store(m_buf.at[i], rows, i))
        stores[-1].start()
    fresh = total.astype(jnp.bfloat16)
    fresh_ref[...] = fresh
    put_fresh = pltpu.make_async_copy(fresh_ref, fresh_hbm, small_sem.at[0])
    put_fresh.start()
    value = fresh.astype(jnp.float32)
    heads = attended_ref.shape[1] // HEAD_SIZE
    group = heads // (fresh_ref.shape[1] // HEAD_SIZE)
    for h in range(heads):
        cols = slice(h * HEAD_SIZE, (h + 1) * HEAD_SIZE)
        at = (h // group) * HEAD_SIZE
        attended_ref[:, cols] = (
            context_ref[:, cols] + own_weight_ref[:, cols] * value[:, at : at + HEAD_SIZE]
        ).astype(jnp.bfloat16)
    put_attended = pltpu.make_async_copy(attended_ref, attended_hbm, small_sem.at[1])
    put_attended.start()
    for store in stores:
        store.wait()
    put_fresh.wait()
    put_attended.wait()


def merge(per, start, pick, features, served, slabs, crossed, last):
    left = 3
    count = slabs.shape[0] + crossed.shape[0] + last.shape[0]
    width = slabs.shape[2]
    rank = pick.shape[0]
    depth, cols = served.shape
    return pl.pallas_call(
        functools.partial(merge_kernel, per, left),
        out_shape=(
            jax.ShapeDtypeStruct((depth, cols), jnp.bfloat16),
            jax.ShapeDtypeStruct((features.shape[0], cols), jnp.float32),
            jax.ShapeDtypeStruct((rank, cols), jnp.bfloat16),
            jax.ShapeDtypeStruct((left, width, cols), jnp.bfloat16),
        ),
        in_specs=[VMEM] * 7,
        out_specs=(HBM, VMEM, VMEM, VMEM),
        scratch_shapes=[
            pltpu.VMEM((count - left, width, cols), jnp.bfloat16),
            pltpu.SemaphoreType.DMA((count - left,)),
        ],
        compiler_params=pltpu.CompilerParams(vmem_limit_bytes=12 * 2**20),
        cost_estimate=pl.CostEstimate(
            flops=2 * count * width * cols * rank,
            bytes_accessed=4 * count * width * cols,
            transcendentals=0,
        ),
        name="merge_blocks",
    )(start, pick, features, served, slabs, crossed, last)


def finish(start, up, features, served, left, last, merged, total, context, own_weight):
    count, _, width = last.shape
    depth, cols = served.shape
    smalls = [total.shape, context.shape]
    return pl.pallas_call(
        final_kernel,
        out_shape=[
            jax.ShapeDtypeStruct(shape, jnp.bfloat16) for shape in [(depth, cols), *smalls]
        ],
        in_specs=[VMEM] * 6 + [HBM] + [VMEM] * 3,
        out_specs=[HBM] * 3,
        input_output_aliases={6: 0},
        scratch_shapes=[
            pltpu.VMEM((count, width, cols), jnp.bfloat16),
            pltpu.SemaphoreType.DMA((count + left.shape[0],)),
        ]
        + [pltpu.VMEM(shape, jnp.bfloat16) for shape in smalls]
        + [pltpu.SemaphoreType.DMA((2,))],
        compiler_params=pltpu.CompilerParams(vmem_limit_bytes=12 * 2**20),
        cost_estimate=pl.CostEstimate(
            flops=2 * count * width * cols * up.shape[0],
            bytes_accessed=4 * count * width * cols,
            transcendentals=0,
        ),
        name="finish_rows",
    )(start, up, features, served, left, last, merged, total, context, own_weight)


def body(
    hidden_in,
    queries,
    stored_keys,
    stored_values,
    fresh_token_key,
    lengths,
    served_value_weight,
    adapter_in,
    adapter_out,
    owner_rank,
):
    n = lax.axis_size("replica")
    replica = lax.axis_index("replica")
    core = lax.axis_index("tensor")
    swap = [(0, 1), (1, 0)]
    full = adapter_in.shape[1]
    width = full // 2
    rows = queries.shape[0]
    per, cols = adapter_out.shape
    rank = n * per

    bits = [n >> i for i in range(1, n.bit_length())]
    ways = [bits, bits[-1:] + bits[:-1]]

    def exchange(x, step):
        pairs = [(2 * i + c, 2 * (i ^ ways[c][step]) + c) for i in range(n) for c in range(2)]
        return lax.ppermute(x, ("replica", "tensor"), pairs)

    slabs = pack(adapter_in, adapter_out)

    given = in_hbm(lengths, queries, fresh_token_key, stored_keys, stored_values)
    *early, final = range(len(bits))
    parts = []
    split = rows // 2
    for step in early:
        came = exchange(slabs, step)
        if step == 0:
            parts.append(attend(range(split), given, after=[slabs]))
            parts[0], hid_other, owner_rank = lax.optimization_barrier(
                (parts[0], hidden_in, owner_rank)
            )
            hid_other = lax.ppermute(hid_other, "tensor", swap)
            came, parts[0] = lax.optimization_barrier((came, parts[0]))
        elif step == 1:
            *part, served = attend(
                range(split, rows), given, *in_hbm(served_value_weight), [slabs]
            )
            came, part = lax.optimization_barrier((came, part))
            parts.append(part)
        slabs = jnp.concatenate([slabs, came], axis=0)
    last = exchange(slabs, final)

    features = jnp.concatenate([hidden_in, hid_other], axis=1)
    features = jnp.where(core == 0, features, jnp.concatenate([hid_other, hidden_in], axis=1))
    crossed, features = lax.optimization_barrier((slabs, features))
    crossed = lax.ppermute(crossed, "tensor", swap)

    slab = jnp.arange(n, dtype=jnp.int32)
    sources = []
    for way in ways:
        source = replica
        for step, bit in enumerate(way):
            source = source ^ (((slab >> step) & 1) * bit)
        sources.append(source)
    mine = jnp.where(core == 0, sources[0], sources[1])
    theirs = jnp.where(core == 0, sources[1], sources[0])
    count = slabs.shape[0]
    source = jnp.concatenate([mine[:count], theirs[:count], mine[count:], theirs[count:]])
    half = jnp.where((jnp.arange(2 * n) // count) % 2 == 0, core, 1 - core)
    place = jnp.sum(jnp.where(owner_rank[None, :] == source[:, None], slab[None, :], 0), axis=1)
    start = (place * full + half * width).astype(jnp.int32)[None]

    row = jnp.arange(rank, dtype=jnp.int32)
    row_source = replica
    for step in range(len(bits)):
        bit = jnp.where(core == 0, ways[0][step], ways[1][step])
        row_source = row_source ^ (((row // per >> step) & 1) * bit)
    pick = jnp.where(
        row[:, None] == (row_source * per + row % per)[None, :], ADAPTER_SCALE, 0.0
    ).astype(jnp.bfloat16)

    context, own_weight = (
        jnp.concatenate(pair, axis=0).reshape(queries.shape) for pair in zip(*parts)
    )
    last, start, pick, context, own_weight = lax.optimization_barrier(
        (last, start, pick, context, own_weight)
    )
    last_crossed = lax.ppermute(last, "tensor", swap)
    merged, total, up, left = merge(per, start, pick, features, served, slabs, crossed, last)
    return tuple(
        finish(
            start, up, features, served, left, last_crossed, merged, total, context, own_weight
        )
    )


def solution(mesh):
    in_specs = (
        P(("groups", "replica"), "tensor"),
        P(("groups", "replica"), "tensor"),
        P(("groups", "replica"), None, "tensor"),
        P(("groups", "replica"), None, "tensor"),
        P(("groups", "replica"), "tensor"),
        P(("groups", "replica")),
        P(None, "tensor"),
        P("groups", "replica"),
        P(("groups", "replica"), "tensor"),
        P("groups"),
    )
    out_specs = (
        P("groups", "tensor"),
        P(("groups", "replica"), "tensor"),
        P(("groups", "replica"), "tensor"),
    )
    return jax.shard_map(body, mesh=mesh, in_specs=in_specs, out_specs=out_specs, check_vma=False)
```

```python
import functools

import jax
import jax.numpy as jnp
from jax import lax
from jax.experimental import pallas as pl
from jax.experimental.pallas import tpu as pltpu
from jax.sharding import PartitionSpec as P

HEAD_SIZE = 128
ADAPTER_SCALE = 2.0
PANEL = 128

SMEM = pl.BlockSpec(memory_space=pltpu.SMEM)
VMEM = pl.BlockSpec(memory_space=pltpu.VMEM)
HBM = pl.BlockSpec(memory_space=pltpu.HBM)


def in_hbm(*arrays):
    return [pltpu.with_memory_space_constraint(x, pltpu.HBM) for x in arrays]


def attend_kernel(rows, fetch, lengths_hbm, q_hbm, own_k_hbm, k_hbm, v_hbm, *rest):
    rest = list(rest)
    if fetch:
        served_hbm, served_ref, served_sem = rest.pop(0), rest.pop(-10), rest.pop(-1)
    context_ref, own_weight_ref, lengths, q_ref, own_k_ref, k_buf, v_buf, small_sem, k_sem, v_sem = (
        rest[-10:]
    )
    smalls = [
        pltpu.make_async_copy(source, into, small_sem.at[i])
        for i, (source, into) in enumerate(
            [(lengths_hbm, lengths), (q_hbm, q_ref), (own_k_hbm, own_k_ref)]
        )
    ]
    for copy in smalls:
        copy.start()

    def copies(i, row):
        return (
            pltpu.make_async_copy(k_hbm.at[row], k_buf.at[i], k_sem.at[i]),
            pltpu.make_async_copy(v_hbm.at[row], v_buf.at[i], v_sem.at[i]),
        )

    for i, row in enumerate(rows):
        for copy in copies(i, row):
            copy.start()
    if fetch:
        get_served = pltpu.make_async_copy(served_hbm, served_ref, served_sem)
        get_served.start()
    for copy in smalls:
        copy.wait()
    queries = q_ref[...].astype(jnp.float32)
    own_keys = own_k_ref[...].astype(jnp.float32)
    heads = queries.shape[1] // HEAD_SIZE
    cache_len, width = k_buf.shape[1:]
    local_heads = width // HEAD_SIZE
    group = heads // local_heads
    scaling = 1.0 / HEAD_SIZE**0.5
    head_of = lax.broadcasted_iota(jnp.int32, (heads, HEAD_SIZE), 0) // group
    position = lax.broadcasted_iota(jnp.int32, (heads, cache_len), 1)
    for i, row in enumerate(rows):
        q = jnp.concatenate(
            [
                queries[row : row + 1, h * HEAD_SIZE : (h + 1) * HEAD_SIZE]
                for h in range(heads)
            ],
            axis=0,
        )
        spread = jnp.concatenate(
            [jnp.where(head_of == h, q, 0.0) for h in range(local_heads)], axis=1
        )
        own = jnp.sum(spread * own_keys[row : row + 1], axis=1, keepdims=True) * scaling
        get_keys, get_values = copies(i, row)
        get_keys.wait()
        scores = (
            lax.dot_general(
                spread.astype(jnp.bfloat16), k_buf[i], (((1,), (1,)), ((), ())),
                preferred_element_type=jnp.float32,
            )
            * scaling
        )
        valid = position < lengths[row]
        masked = jnp.where(valid, scores, -1e30)
        largest = jnp.maximum(jnp.max(masked, axis=1, keepdims=True), own)
        cached_exp = jnp.where(valid, jnp.exp(masked - largest), 0.0)
        own_exp = jnp.exp(own - largest)
        normaliser = jnp.sum(cached_exp, axis=1, keepdims=True) + own_exp
        weights = (cached_exp / normaliser).astype(jnp.bfloat16)
        weight_own = (own_exp / normaliser).astype(jnp.bfloat16).astype(jnp.float32)
        get_values.wait()
        wide = jnp.dot(weights, v_buf[i], preferred_element_type=jnp.float32)
        context = wide[:, :HEAD_SIZE]
        for h in range(1, local_heads):
            context = jnp.where(
                head_of == h, wide[:, h * HEAD_SIZE : (h + 1) * HEAD_SIZE], context
            )
        context_ref[i] = context
        own_weight_ref[i] = jnp.broadcast_to(weight_own, (heads, HEAD_SIZE))
    if fetch:
        get_served.wait()


def attend(rows, given, served=None, after=()):
    lengths, queries, own_key, stored_keys, stored_values = given
    fetch = served is not None
    cache_len, width = stored_keys.shape[1:]
    heads = queries.shape[1] // HEAD_SIZE
    count = len(rows)
    out_shape = [jax.ShapeDtypeStruct((count, heads, HEAD_SIZE), jnp.float32)] * 2
    if fetch:
        out_shape += [jax.ShapeDtypeStruct(served.shape, served.dtype)]
    return pl.pallas_call(
        functools.partial(attend_kernel, rows, fetch),
        out_shape=out_shape,
        in_specs=[HBM] * (5 + fetch) + [pl.BlockSpec(memory_space=pl.ANY)] * len(after),
        out_specs=[VMEM] * len(out_shape),
        scratch_shapes=[
            pltpu.SMEM(lengths.shape, jnp.int32),
            pltpu.VMEM(queries.shape, jnp.bfloat16),
            pltpu.VMEM(own_key.shape, jnp.bfloat16),
            pltpu.VMEM((count, cache_len, width), jnp.bfloat16),
            pltpu.VMEM((count, cache_len, width), jnp.bfloat16),
            pltpu.SemaphoreType.DMA((3,)),
            pltpu.SemaphoreType.DMA((count,)),
            pltpu.SemaphoreType.DMA((count,)),
        ]
        + [pltpu.SemaphoreType.DMA] * fetch,
        compiler_params=pltpu.CompilerParams(vmem_limit_bytes=12 * 2**20),
        cost_estimate=pl.CostEstimate(
            flops=4 * count * heads * cache_len * width,
            bytes_accessed=4 * count * cache_len * width,
            transcendentals=count * heads * cache_len,
        ),
        name="attend_cache",
    )(*given, *([served] if fetch else []), *after)


class Merge:
    def __init__(self, start_ref, merged, out_sem, width):
        self.start, self.merged, self.out_sem, self.width = start_ref[...], merged, out_sem, width
        self.entry = lax.broadcasted_iota(jnp.int32, self.start.shape, 1)

    def rows_of(self, entry):
        first = jnp.sum(jnp.where(self.entry == entry, self.start, 0))
        return pl.ds(pl.multiple_of(first, self.width), self.width)

    def store(self, source, rows, at):
        return pltpu.make_async_copy(source, self.merged.at[rows], self.out_sem.at[at])

    def rows(self, slab, up, served_ref, features_ref, rows, total):
        rank = up.shape[0]
        block = jnp.concatenate(
            [slab[i * rank : (i + 1) * rank] for i in range(self.width // PANEL)], axis=1
        )
        update = lax.dot_general(
            block, up, (((0,), (0,)), ((), ())), preferred_element_type=jnp.float32
        )
        fold = (served_ref[rows, :].astype(jnp.float32) + update).astype(jnp.bfloat16)
        part = jnp.dot(features_ref[:, rows], fold, preferred_element_type=jnp.float32)
        return fold, total + part


def merge_kernel(per, left, start_ref, pick_ref, features_ref, served_ref, slabs_ref, crossed_ref,
                 last_ref, merged, total_ref, up_ref, left_ref, m_buf, out_sem):
    width = m_buf.shape[1]
    rank, cols = up_ref.shape
    merge = Merge(start_ref, merged, out_sem, width)
    ups = []
    for ref in (slabs_ref, last_ref):
        for k in range(ref.shape[0]):
            below = ref[k, rank * (width // PANEL) :].astype(jnp.float32)
            ups.append(
                jnp.concatenate(
                    [below[i * per : (i + 1) * per] for i in range(cols // PANEL)], axis=1
                )
            )
    ups = jnp.concatenate(ups, axis=0).astype(jnp.bfloat16)
    up = jnp.dot(pick_ref[...], ups, preferred_element_type=jnp.float32).astype(jnp.bfloat16)
    up_ref[...] = up
    total = jnp.zeros(total_ref.shape, jnp.float32)
    slabs = [ref.at[k] for ref in (slabs_ref, crossed_ref, last_ref) for k in range(ref.shape[0])]
    keep = len(slabs) - left
    stores = []
    for i, slab in enumerate(slabs):
        rows = merge.rows_of(i)
        fold, total = merge.rows(slab, up, served_ref, features_ref, rows, total)
        if i < keep:
            m_buf[i] = fold
            stores.append(merge.store(m_buf.at[i], rows, i))
            stores[-1].start()
        else:
            left_ref[i - keep] = fold
    total_ref[...] = total
    for store in stores:
        store.wait()


def final_kernel(start_ref, up_ref, features_ref, served_ref, left_ref, last_ref, merged_in,
                 total_ref, context_ref, own_weight_ref, merged, fresh_hbm, attended_hbm, m_buf,
                 out_sem, fresh_ref, attended_ref, small_sem):
    del merged_in
    count, width = last_ref.shape[0], m_buf.shape[1]
    left = left_ref.shape[0]
    merge = Merge(start_ref, merged, out_sem, width)
    first = start_ref.shape[1] - count
    total = total_ref[...]
    stores = [
        merge.store(left_ref.at[k], merge.rows_of(first - left + k), count + k)
        for k in range(left)
    ]
    for store in stores:
        store.start()
    for i in range(count):
        rows = merge.rows_of(first + i)
        fold, total = merge.rows(last_ref.at[i], up_ref[...], served_ref, features_ref, rows, total)
        m_buf[i] = fold
        stores.append(merge.store(m_buf.at[i], rows, i))
        stores[-1].start()
    fresh = total.astype(jnp.bfloat16)
    fresh_ref[...] = fresh
    put_fresh = pltpu.make_async_copy(fresh_ref, fresh_hbm, small_sem.at[0])
    put_fresh.start()
    value = fresh.astype(jnp.float32)
    heads = attended_ref.shape[1] // HEAD_SIZE
    group = heads // (fresh_ref.shape[1] // HEAD_SIZE)
    for h in range(heads):
        cols = slice(h * HEAD_SIZE, (h + 1) * HEAD_SIZE)
        at = (h // group) * HEAD_SIZE
        attended_ref[:, cols] = (
            context_ref[:, cols] + own_weight_ref[:, cols] * value[:, at : at + HEAD_SIZE]
        ).astype(jnp.bfloat16)
    put_attended = pltpu.make_async_copy(attended_ref, attended_hbm, small_sem.at[1])
    put_attended.start()
    for store in stores:
        store.wait()
    put_fresh.wait()
    put_attended.wait()


def merge(per, start, pick, features, served, slabs, crossed, last):
    left = 3
    count = slabs.shape[0] + crossed.shape[0] + last.shape[0]
    rank = pick.shape[0]
    depth, cols = served.shape
    width = depth // start.shape[1]
    return pl.pallas_call(
        functools.partial(merge_kernel, per, left),
        out_shape=(
            jax.ShapeDtypeStruct((depth, cols), jnp.bfloat16),
            jax.ShapeDtypeStruct((features.shape[0], cols), jnp.float32),
            jax.ShapeDtypeStruct((rank, cols), jnp.bfloat16),
            jax.ShapeDtypeStruct((left, width, cols), jnp.bfloat16),
        ),
        in_specs=[VMEM] * 7,
        out_specs=(HBM, VMEM, VMEM, VMEM),
        scratch_shapes=[
            pltpu.VMEM((count - left, width, cols), jnp.bfloat16),
            pltpu.SemaphoreType.DMA((count - left,)),
        ],
        compiler_params=pltpu.CompilerParams(vmem_limit_bytes=12 * 2**20),
        cost_estimate=pl.CostEstimate(
            flops=2 * count * width * cols * rank,
            bytes_accessed=4 * count * width * cols,
            transcendentals=0,
        ),
        name="merge_blocks",
    )(start, pick, features, served, slabs, crossed, last)


def finish(start, up, features, served, left, last, merged, total, context, own_weight):
    count = last.shape[0]
    depth, cols = served.shape
    width = depth // start.shape[1]
    smalls = [total.shape, context.shape]
    return pl.pallas_call(
        final_kernel,
        out_shape=[
            jax.ShapeDtypeStruct(shape, jnp.bfloat16) for shape in [(depth, cols), *smalls]
        ],
        in_specs=[VMEM] * 6 + [HBM] + [VMEM] * 3,
        out_specs=[HBM] * 3,
        input_output_aliases={6: 0},
        scratch_shapes=[
            pltpu.VMEM((count, width, cols), jnp.bfloat16),
            pltpu.SemaphoreType.DMA((count + left.shape[0],)),
        ]
        + [pltpu.VMEM(shape, jnp.bfloat16) for shape in smalls]
        + [pltpu.SemaphoreType.DMA((2,))],
        compiler_params=pltpu.CompilerParams(vmem_limit_bytes=12 * 2**20),
        cost_estimate=pl.CostEstimate(
            flops=2 * count * width * cols * up.shape[0],
            bytes_accessed=4 * count * width * cols,
            transcendentals=0,
        ),
        name="finish_rows",
    )(start, up, features, served, left, last, merged, total, context, own_weight)


def panels(x):
    return [x[:, i : i + PANEL] for i in range(0, x.shape[1], PANEL)]


def body(
    hidden_in,
    queries,
    stored_keys,
    stored_values,
    fresh_token_key,
    lengths,
    served_value_weight,
    adapter_in,
    adapter_out,
    owner_rank,
):
    n = lax.axis_size("replica")
    replica = lax.axis_index("replica")
    core = lax.axis_index("tensor")
    swap = [(0, 1), (1, 0)]
    full = adapter_in.shape[1]
    width = full // 2
    rows = queries.shape[0]
    per, cols = adapter_out.shape
    rank = n * per

    bits = [n >> i for i in range(1, n.bit_length())]
    ways = [bits, bits[:-2] + bits[:-3:-1]]

    def exchange(x, step):
        pairs = [(2 * i + c, 2 * (i ^ ways[c][step]) + c) for i in range(n) for c in range(2)]
        return lax.ppermute(x, ("replica", "tensor"), pairs)

    below = jnp.concatenate(panels(adapter_out), axis=0)
    below = jnp.pad(below, ((0, -below.shape[0] % 8), (0, 0)))
    block = lax.dynamic_slice_in_dim(adapter_in, core * width, width, axis=1)
    block, below = lax.optimization_barrier((block, below))
    slabs = jnp.concatenate([*panels(block), below], axis=0)[None]

    given = in_hbm(lengths, queries, fresh_token_key, stored_keys, stored_values)
    *early, final = range(len(bits))
    parts = []
    split = rows // 2
    for step in early:
        came = exchange(slabs, step)
        if step == 0:
            parts.append(attend(range(split), given, after=[slabs]))
            parts[0], hid_other, owner_rank = lax.optimization_barrier(
                (parts[0], hidden_in, owner_rank)
            )
            hid_other = lax.ppermute(hid_other, "tensor", swap)
            came, parts[0] = lax.optimization_barrier((came, parts[0]))
        elif step == 1:
            *part, served = attend(
                range(split, rows), given, *in_hbm(served_value_weight), [slabs]
            )
            came, part = lax.optimization_barrier((came, part))
            parts.append(part)
        slabs = jnp.concatenate([slabs, came], axis=0)
    last = exchange(slabs, final)

    features = jnp.concatenate([hidden_in, hid_other], axis=1)
    features = jnp.where(core == 0, features, jnp.concatenate([hid_other, hidden_in], axis=1))
    crossed, features = lax.optimization_barrier((slabs, features))
    crossed = lax.ppermute(crossed, "tensor", swap)

    slab = jnp.arange(n, dtype=jnp.int32)
    sources = []
    for way in ways:
        source = replica
        for step, bit in enumerate(way):
            source = source ^ (((slab >> step) & 1) * bit)
        sources.append(source)
    mine = jnp.where(core == 0, sources[0], sources[1])
    theirs = jnp.where(core == 0, sources[1], sources[0])
    count = slabs.shape[0]
    source = jnp.concatenate([mine[:count], theirs[:count], mine[count:], theirs[count:]])
    half = jnp.where((jnp.arange(2 * n) // count) % 2 == 0, core, 1 - core)
    place = jnp.sum(jnp.where(owner_rank[None, :] == source[:, None], slab[None, :], 0), axis=1)
    start = (place * full + half * width).astype(jnp.int32)[None]

    row = jnp.arange(rank, dtype=jnp.int32)
    row_source = replica
    for step in range(len(bits)):
        bit = jnp.where(core == 0, ways[0][step], ways[1][step])
        row_source = row_source ^ (((row // per >> step) & 1) * bit)
    pick = jnp.where(
        row[:, None] == (row_source * per + row % per)[None, :], ADAPTER_SCALE, 0.0
    ).astype(jnp.bfloat16)

    context, own_weight = (
        jnp.concatenate(pair, axis=0).reshape(queries.shape) for pair in zip(*parts)
    )
    last, start, pick, context, own_weight = lax.optimization_barrier(
        (last, start, pick, context, own_weight)
    )
    last_crossed = lax.ppermute(last, "tensor", swap)
    merged, total, up, left = merge(per, start, pick, features, served, slabs, crossed, last)
    return tuple(
        finish(
            start, up, features, served, left, last_crossed, merged, total, context, own_weight
        )
    )


def solution(mesh):
    in_specs = (
        P(("groups", "replica"), "tensor"),
        P(("groups", "replica"), "tensor"),
        P(("groups", "replica"), None, "tensor"),
        P(("groups", "replica"), None, "tensor"),
        P(("groups", "replica"), "tensor"),
        P(("groups", "replica")),
        P(None, "tensor"),
        P("groups", "replica"),
        P(("groups", "replica"), "tensor"),
        P("groups"),
    )
    out_specs = (
        P("groups", "tensor"),
        P(("groups", "replica"), "tensor"),
        P(("groups", "replica"), "tensor"),
    )
    return jax.shard_map(body, mesh=mesh, in_specs=in_specs, out_specs=out_specs, check_vma=False)
```

```python
import functools

import jax
import jax.numpy as jnp
from jax import lax
from jax.experimental import pallas as pl
from jax.experimental.pallas import tpu as pltpu
from jax.sharding import PartitionSpec as P

HEAD_SIZE = 128
ADAPTER_SCALE = 2.0
PANEL = 128

SMEM = pl.BlockSpec(memory_space=pltpu.SMEM)
VMEM = pl.BlockSpec(memory_space=pltpu.VMEM)
HBM = pl.BlockSpec(memory_space=pltpu.HBM)


def in_hbm(*arrays):
    return [pltpu.with_memory_space_constraint(x, pltpu.HBM) for x in arrays]


def attend_kernel(rows, fetch, lengths_hbm, q_hbm, own_k_hbm, k_hbm, v_hbm, *rest):
    rest = list(rest)
    if fetch:
        served_hbm, served_ref, served_sem = rest.pop(0), rest.pop(-10), rest.pop(-1)
    context_ref, own_weight_ref, lengths, q_ref, own_k_ref, k_buf, v_buf, small_sem, k_sem, v_sem = (
        rest[-10:]
    )
    smalls = [
        pltpu.make_async_copy(source, into, small_sem.at[i])
        for i, (source, into) in enumerate(
            [(lengths_hbm, lengths), (q_hbm, q_ref), (own_k_hbm, own_k_ref)]
        )
    ]
    for copy in smalls:
        copy.start()

    def copies(i, row):
        return (
            pltpu.make_async_copy(k_hbm.at[row], k_buf.at[i], k_sem.at[i]),
            pltpu.make_async_copy(v_hbm.at[row], v_buf.at[i], v_sem.at[i]),
        )

    for i, row in enumerate(rows):
        for copy in copies(i, row):
            copy.start()
    if fetch:
        get_served = pltpu.make_async_copy(served_hbm, served_ref, served_sem)
        get_served.start()
    for copy in smalls:
        copy.wait()
    queries = q_ref[...].astype(jnp.float32)
    own_keys = own_k_ref[...].astype(jnp.float32)
    heads = queries.shape[1] // HEAD_SIZE
    cache_len, width = k_buf.shape[1:]
    local_heads = width // HEAD_SIZE
    group = heads // local_heads
    scaling = 1.0 / HEAD_SIZE**0.5
    head_of = lax.broadcasted_iota(jnp.int32, (heads, HEAD_SIZE), 0) // group
    position = lax.broadcasted_iota(jnp.int32, (heads, cache_len), 1)
    for i, row in enumerate(rows):
        q = jnp.concatenate(
            [
                queries[row : row + 1, h * HEAD_SIZE : (h + 1) * HEAD_SIZE]
                for h in range(heads)
            ],
            axis=0,
        )
        spread = jnp.concatenate(
            [jnp.where(head_of == h, q, 0.0) for h in range(local_heads)], axis=1
        )
        own = jnp.sum(spread * own_keys[row : row + 1], axis=1, keepdims=True) * scaling
        get_keys, get_values = copies(i, row)
        get_keys.wait()
        scores = (
            lax.dot_general(
                spread.astype(jnp.bfloat16), k_buf[i], (((1,), (1,)), ((), ())),
                preferred_element_type=jnp.float32,
            )
            * scaling
        )
        valid = position < lengths[row]
        masked = jnp.where(valid, scores, -1e30)
        largest = jnp.maximum(jnp.max(masked, axis=1, keepdims=True), own)
        cached_exp = jnp.where(valid, jnp.exp(masked - largest), 0.0)
        own_exp = jnp.exp(own - largest)
        normaliser = jnp.sum(cached_exp, axis=1, keepdims=True) + own_exp
        weights = (cached_exp / normaliser).astype(jnp.bfloat16)
        weight_own = (own_exp / normaliser).astype(jnp.bfloat16).astype(jnp.float32)
        get_values.wait()
        wide = jnp.dot(weights, v_buf[i], preferred_element_type=jnp.float32)
        context = wide[:, :HEAD_SIZE]
        for h in range(1, local_heads):
            context = jnp.where(
                head_of == h, wide[:, h * HEAD_SIZE : (h + 1) * HEAD_SIZE], context
            )
        context_ref[i] = context
        own_weight_ref[i] = jnp.broadcast_to(weight_own, (heads, HEAD_SIZE))
    if fetch:
        get_served.wait()


def attend(rows, given, served=None, after=()):
    lengths, queries, own_key, stored_keys, stored_values = given
    fetch = served is not None
    cache_len, width = stored_keys.shape[1:]
    heads = queries.shape[1] // HEAD_SIZE
    count = len(rows)
    out_shape = [jax.ShapeDtypeStruct((count, heads, HEAD_SIZE), jnp.float32)] * 2
    if fetch:
        out_shape += [jax.ShapeDtypeStruct(served.shape, served.dtype)]
    return pl.pallas_call(
        functools.partial(attend_kernel, rows, fetch),
        out_shape=out_shape,
        in_specs=[HBM] * (5 + fetch) + [pl.BlockSpec(memory_space=pl.ANY)] * len(after),
        out_specs=[VMEM] * len(out_shape),
        scratch_shapes=[
            pltpu.SMEM(lengths.shape, jnp.int32),
            pltpu.VMEM(queries.shape, jnp.bfloat16),
            pltpu.VMEM(own_key.shape, jnp.bfloat16),
            pltpu.VMEM((count, cache_len, width), jnp.bfloat16),
            pltpu.VMEM((count, cache_len, width), jnp.bfloat16),
            pltpu.SemaphoreType.DMA((3,)),
            pltpu.SemaphoreType.DMA((count,)),
            pltpu.SemaphoreType.DMA((count,)),
        ]
        + [pltpu.SemaphoreType.DMA] * fetch,
        compiler_params=pltpu.CompilerParams(vmem_limit_bytes=12 * 2**20),
        cost_estimate=pl.CostEstimate(
            flops=4 * count * heads * cache_len * width,
            bytes_accessed=4 * count * cache_len * width,
            transcendentals=count * heads * cache_len,
        ),
        name="attend_cache",
    )(*given, *([served] if fetch else []), *after)


class Merge:
    def __init__(self, start_ref, merged, out_sem, width):
        self.start, self.merged, self.out_sem, self.width = start_ref[...], merged, out_sem, width
        self.entry = lax.broadcasted_iota(jnp.int32, self.start.shape, 1)

    def rows_of(self, entry):
        first = jnp.sum(jnp.where(self.entry == entry, self.start, 0))
        return pl.ds(pl.multiple_of(first, self.width), self.width)

    def store(self, source, rows, at):
        return pltpu.make_async_copy(source, self.merged.at[rows], self.out_sem.at[at])

    def rows(self, slab, up, served_ref, features_ref, rows, total):
        rank = up.shape[0]
        block = jnp.concatenate(
            [slab[i * rank : (i + 1) * rank] for i in range(self.width // PANEL)], axis=1
        )
        update = lax.dot_general(
            block, up, (((0,), (0,)), ((), ())), preferred_element_type=jnp.float32
        )
        fold = (served_ref[rows, :].astype(jnp.float32) + update).astype(jnp.bfloat16)
        part = jnp.dot(features_ref[:, rows], fold, preferred_element_type=jnp.float32)
        return fold, total + part


def merge_kernel(per, left, start_ref, pick_ref, features_ref, served_ref, slabs_ref, crossed_ref,
                 last_ref, merged, total_ref, up_ref, left_ref, m_buf, out_sem):
    width = m_buf.shape[1]
    rank, cols = up_ref.shape
    merge = Merge(start_ref, merged, out_sem, width)
    ups = []
    for ref in (slabs_ref, last_ref):
        for k in range(ref.shape[0]):
            below = ref[k, rank * (width // PANEL) :].astype(jnp.float32)
            ups.append(
                jnp.concatenate(
                    [below[i * per : (i + 1) * per] for i in range(cols // PANEL)], axis=1
                )
            )
    ups = jnp.concatenate(ups, axis=0).astype(jnp.bfloat16)
    up = jnp.dot(pick_ref[...], ups, preferred_element_type=jnp.float32).astype(jnp.bfloat16)
    up_ref[...] = up
    total = jnp.zeros(total_ref.shape, jnp.float32)
    slabs = [ref.at[k] for ref in (slabs_ref, crossed_ref, last_ref) for k in range(ref.shape[0])]
    keep = len(slabs) - left
    stores = []
    for i, slab in enumerate(slabs):
        rows = merge.rows_of(i)
        fold, total = merge.rows(slab, up, served_ref, features_ref, rows, total)
        if i < keep:
            m_buf[i] = fold
            stores.append(merge.store(m_buf.at[i], rows, i))
            stores[-1].start()
        else:
            left_ref[i - keep] = fold
    total_ref[...] = total
    for store in stores:
        store.wait()


def final_kernel(start_ref, up_ref, features_ref, served_ref, left_ref, last_ref, merged_in,
                 total_ref, context_ref, own_weight_ref, merged, fresh_hbm, attended_hbm, m_buf,
                 out_sem, fresh_ref, attended_ref, small_sem):
    del merged_in
    count, width = last_ref.shape[0], m_buf.shape[1]
    left = left_ref.shape[0]
    merge = Merge(start_ref, merged, out_sem, width)
    first = start_ref.shape[1] - count
    total = total_ref[...]
    stores = [
        merge.store(left_ref.at[k], merge.rows_of(first - left + k), count + k)
        for k in range(left)
    ]
    for store in stores:
        store.start()
    for i in range(count):
        rows = merge.rows_of(first + i)
        fold, total = merge.rows(last_ref.at[i], up_ref[...], served_ref, features_ref, rows, total)
        m_buf[i] = fold
        stores.append(merge.store(m_buf.at[i], rows, i))
        stores[-1].start()
    fresh = total.astype(jnp.bfloat16)
    fresh_ref[...] = fresh
    put_fresh = pltpu.make_async_copy(fresh_ref, fresh_hbm, small_sem.at[0])
    put_fresh.start()
    value = fresh.astype(jnp.float32)
    heads = attended_ref.shape[1] // HEAD_SIZE
    group = heads // (fresh_ref.shape[1] // HEAD_SIZE)
    for h in range(heads):
        cols = slice(h * HEAD_SIZE, (h + 1) * HEAD_SIZE)
        at = (h // group) * HEAD_SIZE
        attended_ref[:, cols] = (
            context_ref[:, cols] + own_weight_ref[:, cols] * value[:, at : at + HEAD_SIZE]
        ).astype(jnp.bfloat16)
    put_attended = pltpu.make_async_copy(attended_ref, attended_hbm, small_sem.at[1])
    put_attended.start()
    for store in stores:
        store.wait()
    put_fresh.wait()
    put_attended.wait()


def merge(per, start, pick, features, served, slabs, crossed, last):
    left = 3
    count = slabs.shape[0] + crossed.shape[0] + last.shape[0]
    rank = pick.shape[0]
    depth, cols = served.shape
    width = depth // start.shape[1]
    return pl.pallas_call(
        functools.partial(merge_kernel, per, left),
        out_shape=(
            jax.ShapeDtypeStruct((depth, cols), jnp.bfloat16),
            jax.ShapeDtypeStruct((features.shape[0], cols), jnp.float32),
            jax.ShapeDtypeStruct((rank, cols), jnp.bfloat16),
            jax.ShapeDtypeStruct((left, width, cols), jnp.bfloat16),
        ),
        in_specs=[VMEM] * 7,
        out_specs=(HBM, VMEM, VMEM, VMEM),
        scratch_shapes=[
            pltpu.VMEM((count - left, width, cols), jnp.bfloat16),
            pltpu.SemaphoreType.DMA((count - left,)),
        ],
        compiler_params=pltpu.CompilerParams(vmem_limit_bytes=12 * 2**20),
        cost_estimate=pl.CostEstimate(
            flops=2 * count * width * cols * rank,
            bytes_accessed=4 * count * width * cols,
            transcendentals=0,
        ),
        name="merge_blocks",
    )(start, pick, features, served, slabs, crossed, last)


def finish(start, up, features, served, left, last, merged, total, context, own_weight):
    count = last.shape[0]
    depth, cols = served.shape
    width = depth // start.shape[1]
    smalls = [total.shape, context.shape]
    return pl.pallas_call(
        final_kernel,
        out_shape=[
            jax.ShapeDtypeStruct(shape, jnp.bfloat16) for shape in [(depth, cols), *smalls]
        ],
        in_specs=[VMEM] * 6 + [HBM] + [VMEM] * 3,
        out_specs=[HBM] * 3,
        input_output_aliases={6: 0},
        scratch_shapes=[
            pltpu.VMEM((count, width, cols), jnp.bfloat16),
            pltpu.SemaphoreType.DMA((count + left.shape[0],)),
        ]
        + [pltpu.VMEM(shape, jnp.bfloat16) for shape in smalls]
        + [pltpu.SemaphoreType.DMA((2,))],
        compiler_params=pltpu.CompilerParams(vmem_limit_bytes=12 * 2**20),
        cost_estimate=pl.CostEstimate(
            flops=2 * count * width * cols * up.shape[0],
            bytes_accessed=4 * count * width * cols,
            transcendentals=0,
        ),
        name="finish_rows",
    )(start, up, features, served, left, last, merged, total, context, own_weight)


def panels(x):
    return [x[:, i : i + PANEL] for i in range(0, x.shape[1], PANEL)]


def body(
    hidden_in,
    queries,
    stored_keys,
    stored_values,
    fresh_token_key,
    lengths,
    served_value_weight,
    adapter_in,
    adapter_out,
    owner_rank,
):
    n = lax.axis_size("replica")
    replica = lax.axis_index("replica")
    core = lax.axis_index("tensor")
    swap = [(0, 1), (1, 0)]
    full = adapter_in.shape[1]
    width = full // 2
    rows = queries.shape[0]
    per, cols = adapter_out.shape
    rank = n * per

    bits = [n >> i for i in range(1, n.bit_length())]
    ways = [bits, bits[:-2] + bits[:-3:-1]]

    def exchange(x, step):
        pairs = [(2 * i + c, 2 * (i ^ ways[c][step]) + c) for i in range(n) for c in range(2)]
        return lax.ppermute(x, ("replica", "tensor"), pairs)

    below = jnp.concatenate(panels(adapter_out), axis=0)
    below = jnp.pad(below, ((0, -below.shape[0] % 8), (0, 0)))
    block = lax.dynamic_slice_in_dim(adapter_in, core * width, width, axis=1)
    block, below = lax.optimization_barrier((block, below))
    slabs = jnp.concatenate([*panels(block), below], axis=0)[None]

    given = in_hbm(lengths, queries, fresh_token_key, stored_keys, stored_values)
    *early, final = range(len(bits))
    parts, images = [], []
    split = rows // 2
    came = slabs
    for step in early:
        piece, came = came, exchange(slabs, step)
        if step == 0:
            parts.append(attend(range(split), given, after=[slabs]))
            parts[0], hid_other, owner_rank, piece = lax.optimization_barrier(
                (parts[0], hidden_in, owner_rank, piece)
            )
            hid_other = lax.ppermute(hid_other, "tensor", swap)
            came, parts[0] = lax.optimization_barrier((came, parts[0]))
        elif step == 1:
            *part, served = attend(
                range(split, rows), given, *in_hbm(served_value_weight), [slabs]
            )
            part, piece = lax.optimization_barrier((part, piece))
            came, part = lax.optimization_barrier((came, part))
            parts.append(part)
        images.append(exchange(piece, final))
        slabs = jnp.concatenate([slabs, came], axis=0)
    last = exchange(came, final)
    slabs = jnp.concatenate([slabs, *images], axis=0)

    features = jnp.concatenate([hidden_in, hid_other], axis=1)
    features = jnp.where(core == 0, features, jnp.concatenate([hid_other, hidden_in], axis=1))
    crossed, features = lax.optimization_barrier((slabs, features))
    crossed = lax.ppermute(crossed, "tensor", swap)

    slab = jnp.arange(n, dtype=jnp.int32)
    sources = []
    for way in ways:
        source = replica
        for step, bit in enumerate(way):
            source = source ^ (((slab >> step) & 1) * bit)
        sources.append(source)
    mine = jnp.where(core == 0, sources[0], sources[1])
    theirs = jnp.where(core == 0, sources[1], sources[0])
    count = slabs.shape[0]
    source = jnp.concatenate([mine[:count], theirs[:count], mine[count:], theirs[count:]])
    half = jnp.concatenate(
        [jnp.full((size,), c) for size in (count, n - count) for c in (core, 1 - core)]
    )
    place = jnp.sum(jnp.where(owner_rank[None, :] == source[:, None], slab[None, :], 0), axis=1)
    start = (place * full + half * width).astype(jnp.int32)[None]

    row = jnp.arange(rank, dtype=jnp.int32)
    row_source = replica
    for step in range(len(bits)):
        bit = jnp.where(core == 0, ways[0][step], ways[1][step])
        row_source = row_source ^ (((row // per >> step) & 1) * bit)
    pick = jnp.where(
        row[:, None] == (row_source * per + row % per)[None, :], ADAPTER_SCALE, 0.0
    ).astype(jnp.bfloat16)

    context, own_weight = (
        jnp.concatenate(pair, axis=0).reshape(queries.shape) for pair in zip(*parts)
    )
    last, start, pick, context, own_weight = lax.optimization_barrier(
        (last, start, pick, context, own_weight)
    )
    last_crossed = lax.ppermute(last, "tensor", swap)
    merged, total, up, left = merge(per, start, pick, features, served, slabs, crossed, last)
    return tuple(
        finish(
            start, up, features, served, left, last_crossed, merged, total, context, own_weight
        )
    )


def solution(mesh):
    in_specs = (
        P(("groups", "replica"), "tensor"),
        P(("groups", "replica"), "tensor"),
        P(("groups", "replica"), None, "tensor"),
        P(("groups", "replica"), None, "tensor"),
        P(("groups", "replica"), "tensor"),
        P(("groups", "replica")),
        P(None, "tensor"),
        P("groups", "replica"),
        P(("groups", "replica"), "tensor"),
        P("groups"),
    )
    out_specs = (
        P("groups", "tensor"),
        P(("groups", "replica"), "tensor"),
        P(("groups", "replica"), "tensor"),
    )
    return jax.shard_map(body, mesh=mesh, in_specs=in_specs, out_specs=out_specs, check_vma=False)
```

```python
import functools

import jax
import jax.numpy as jnp
from jax import lax
from jax.experimental import pallas as pl
from jax.experimental.pallas import tpu as pltpu
from jax.sharding import PartitionSpec as P

HEAD_SIZE = 128
ADAPTER_SCALE = 2.0
PANEL = 128

SMEM = pl.BlockSpec(memory_space=pltpu.SMEM)
VMEM = pl.BlockSpec(memory_space=pltpu.VMEM)
HBM = pl.BlockSpec(memory_space=pltpu.HBM)


def in_hbm(*arrays):
    return [pltpu.with_memory_space_constraint(x, pltpu.HBM) for x in arrays]


def attend_kernel(rows, fetch, lengths_hbm, q_hbm, own_k_hbm, k_hbm, v_hbm, *rest):
    rest = list(rest)
    if fetch:
        served_hbm, served_ref, served_sem = rest.pop(0), rest.pop(-10), rest.pop(-1)
    context_ref, own_weight_ref, lengths, q_ref, own_k_ref, k_buf, v_buf, small_sem, k_sem, v_sem = (
        rest[-10:]
    )
    smalls = [
        pltpu.make_async_copy(source, into, small_sem.at[i])
        for i, (source, into) in enumerate(
            [(lengths_hbm, lengths), (q_hbm, q_ref), (own_k_hbm, own_k_ref)]
        )
    ]
    for copy in smalls:
        copy.start()

    def copies(i, row):
        return (
            pltpu.make_async_copy(k_hbm.at[row], k_buf.at[i], k_sem.at[i]),
            pltpu.make_async_copy(v_hbm.at[row], v_buf.at[i], v_sem.at[i]),
        )

    for i, row in enumerate(rows):
        for copy in copies(i, row):
            copy.start()
    if fetch:
        get_served = pltpu.make_async_copy(served_hbm, served_ref, served_sem)
        get_served.start()
    for copy in smalls:
        copy.wait()
    queries = q_ref[...].astype(jnp.float32)
    own_keys = own_k_ref[...].astype(jnp.float32)
    heads = queries.shape[1] // HEAD_SIZE
    cache_len, width = k_buf.shape[1:]
    local_heads = width // HEAD_SIZE
    group = heads // local_heads
    scaling = 1.0 / HEAD_SIZE**0.5
    head_of = lax.broadcasted_iota(jnp.int32, (heads, HEAD_SIZE), 0) // group
    position = lax.broadcasted_iota(jnp.int32, (heads, cache_len), 1)
    for i, row in enumerate(rows):
        q = jnp.concatenate(
            [
                queries[row : row + 1, h * HEAD_SIZE : (h + 1) * HEAD_SIZE]
                for h in range(heads)
            ],
            axis=0,
        )
        spread = jnp.concatenate(
            [jnp.where(head_of == h, q, 0.0) for h in range(local_heads)], axis=1
        )
        own = jnp.sum(spread * own_keys[row : row + 1], axis=1, keepdims=True) * scaling
        get_keys, get_values = copies(i, row)
        get_keys.wait()
        scores = (
            lax.dot_general(
                spread.astype(jnp.bfloat16), k_buf[i], (((1,), (1,)), ((), ())),
                preferred_element_type=jnp.float32,
            )
            * scaling
        )
        valid = position < lengths[row]
        masked = jnp.where(valid, scores, -1e30)
        largest = jnp.maximum(jnp.max(masked, axis=1, keepdims=True), own)
        cached_exp = jnp.where(valid, jnp.exp(masked - largest), 0.0)
        own_exp = jnp.exp(own - largest)
        normaliser = jnp.sum(cached_exp, axis=1, keepdims=True) + own_exp
        weights = (cached_exp / normaliser).astype(jnp.bfloat16)
        weight_own = (own_exp / normaliser).astype(jnp.bfloat16).astype(jnp.float32)
        get_values.wait()
        wide = jnp.dot(weights, v_buf[i], preferred_element_type=jnp.float32)
        context = wide[:, :HEAD_SIZE]
        for h in range(1, local_heads):
            context = jnp.where(
                head_of == h, wide[:, h * HEAD_SIZE : (h + 1) * HEAD_SIZE], context
            )
        context_ref[i] = context
        own_weight_ref[i] = jnp.broadcast_to(weight_own, (heads, HEAD_SIZE))
    if fetch:
        get_served.wait()


def attend(rows, given, served=None, after=()):
    lengths, queries, own_key, stored_keys, stored_values = given
    fetch = served is not None
    cache_len, width = stored_keys.shape[1:]
    heads = queries.shape[1] // HEAD_SIZE
    count = len(rows)
    out_shape = [jax.ShapeDtypeStruct((count, heads, HEAD_SIZE), jnp.float32)] * 2
    if fetch:
        out_shape += [jax.ShapeDtypeStruct(served.shape, served.dtype)]
    return pl.pallas_call(
        functools.partial(attend_kernel, rows, fetch),
        out_shape=out_shape,
        in_specs=[HBM] * (5 + fetch) + [pl.BlockSpec(memory_space=pl.ANY)] * len(after),
        out_specs=[VMEM] * len(out_shape),
        scratch_shapes=[
            pltpu.SMEM(lengths.shape, jnp.int32),
            pltpu.VMEM(queries.shape, jnp.bfloat16),
            pltpu.VMEM(own_key.shape, jnp.bfloat16),
            pltpu.VMEM((count, cache_len, width), jnp.bfloat16),
            pltpu.VMEM((count, cache_len, width), jnp.bfloat16),
            pltpu.SemaphoreType.DMA((3,)),
            pltpu.SemaphoreType.DMA((count,)),
            pltpu.SemaphoreType.DMA((count,)),
        ]
        + [pltpu.SemaphoreType.DMA] * fetch,
        compiler_params=pltpu.CompilerParams(vmem_limit_bytes=12 * 2**20),
        cost_estimate=pl.CostEstimate(
            flops=4 * count * heads * cache_len * width,
            bytes_accessed=4 * count * cache_len * width,
            transcendentals=count * heads * cache_len,
        ),
        name="attend_cache",
    )(*given, *([served] if fetch else []), *after)


def gate_kernel(x_ref, after, out_ref):
    del after
    out_ref[...] = x_ref[...]


def gate(x, after):
    return pl.pallas_call(
        gate_kernel,
        out_shape=jax.ShapeDtypeStruct(x.shape, x.dtype),
        in_specs=[VMEM, pl.BlockSpec(memory_space=pl.ANY)],
        out_specs=VMEM,
        name="gate_rows",
    )(x, after)


class Merge:
    def __init__(self, start_ref, merged, out_sem, width):
        self.start, self.merged, self.out_sem, self.width = start_ref[...], merged, out_sem, width
        self.entry = lax.broadcasted_iota(jnp.int32, self.start.shape, 1)

    def rows_of(self, entry):
        first = jnp.sum(jnp.where(self.entry == entry, self.start, 0))
        return pl.ds(pl.multiple_of(first, self.width), self.width)

    def store(self, source, rows, at):
        return pltpu.make_async_copy(source, self.merged.at[rows], self.out_sem.at[at])

    def rows(self, slab, up, served_ref, features_ref, rows, total):
        rank = up.shape[0]
        block = jnp.concatenate(
            [slab[i * rank : (i + 1) * rank] for i in range(self.width // PANEL)], axis=1
        )
        update = lax.dot_general(
            block, up, (((0,), (0,)), ((), ())), preferred_element_type=jnp.float32
        )
        fold = (served_ref[rows, :].astype(jnp.float32) + update).astype(jnp.bfloat16)
        part = jnp.dot(features_ref[:, rows], fold, preferred_element_type=jnp.float32)
        return fold, total + part


def merge_kernel(per, left, start_ref, pick_ref, features_ref, served_ref, slabs_ref, crossed_ref,
                 last_ref, merged, total_ref, up_ref, left_ref, m_buf, out_sem):
    width = m_buf.shape[1]
    rank, cols = up_ref.shape
    merge = Merge(start_ref, merged, out_sem, width)
    ups = []
    for ref in (slabs_ref, last_ref):
        for k in range(ref.shape[0]):
            below = ref[k, rank * (width // PANEL) :].astype(jnp.float32)
            ups.append(
                jnp.concatenate(
                    [below[i * per : (i + 1) * per] for i in range(cols // PANEL)], axis=1
                )
            )
    ups = jnp.concatenate(ups, axis=0).astype(jnp.bfloat16)
    up = jnp.dot(pick_ref[...], ups, preferred_element_type=jnp.float32).astype(jnp.bfloat16)
    up_ref[...] = up
    total = jnp.zeros(total_ref.shape, jnp.float32)
    refs = (slabs_ref, last_ref, crossed_ref)
    slabs = [ref.at[k] for ref in refs for k in range(ref.shape[0])]
    keep = len(slabs) - left
    stores = []
    for i, slab in enumerate(slabs):
        rows = merge.rows_of(i)
        fold, total = merge.rows(slab, up, served_ref, features_ref, rows, total)
        if i < keep:
            m_buf[i] = fold
            stores.append(merge.store(m_buf.at[i], rows, i))
            stores[-1].start()
        else:
            left_ref[i - keep] = fold
    total_ref[...] = total
    for store in stores:
        store.wait()


def final_kernel(start_ref, up_ref, features_ref, served_ref, left_ref, last_ref, merged_in,
                 total_ref, context_ref, own_weight_ref, merged, fresh_hbm, attended_hbm, m_buf,
                 out_sem, fresh_ref, attended_ref, small_sem):
    del merged_in
    count, width = last_ref.shape[0], m_buf.shape[1]
    left = left_ref.shape[0]
    merge = Merge(start_ref, merged, out_sem, width)
    first = start_ref.shape[1] - count
    total = total_ref[...]
    stores = [
        merge.store(left_ref.at[k], merge.rows_of(first - left + k), count + k)
        for k in range(left)
    ]
    for store in stores:
        store.start()
    for i in range(count):
        rows = merge.rows_of(first + i)
        fold, total = merge.rows(last_ref.at[i], up_ref[...], served_ref, features_ref, rows, total)
        m_buf[i] = fold
        stores.append(merge.store(m_buf.at[i], rows, i))
        stores[-1].start()
    fresh = total.astype(jnp.bfloat16)
    fresh_ref[...] = fresh
    put_fresh = pltpu.make_async_copy(fresh_ref, fresh_hbm, small_sem.at[0])
    put_fresh.start()
    value = fresh.astype(jnp.float32)
    heads = attended_ref.shape[1] // HEAD_SIZE
    group = heads // (fresh_ref.shape[1] // HEAD_SIZE)
    for h in range(heads):
        cols = slice(h * HEAD_SIZE, (h + 1) * HEAD_SIZE)
        at = (h // group) * HEAD_SIZE
        attended_ref[:, cols] = (
            context_ref[:, cols] + own_weight_ref[:, cols] * value[:, at : at + HEAD_SIZE]
        ).astype(jnp.bfloat16)
    put_attended = pltpu.make_async_copy(attended_ref, attended_hbm, small_sem.at[1])
    put_attended.start()
    for store in stores:
        store.wait()
    put_fresh.wait()
    put_attended.wait()


def merge(per, start, pick, features, served, slabs, crossed, last):
    left = 3
    count = slabs.shape[0] + crossed.shape[0] + last.shape[0]
    rank = pick.shape[0]
    depth, cols = served.shape
    width = depth // start.shape[1]
    return pl.pallas_call(
        functools.partial(merge_kernel, per, left),
        out_shape=(
            jax.ShapeDtypeStruct((depth, cols), jnp.bfloat16),
            jax.ShapeDtypeStruct((features.shape[0], cols), jnp.float32),
            jax.ShapeDtypeStruct((rank, cols), jnp.bfloat16),
            jax.ShapeDtypeStruct((left, width, cols), jnp.bfloat16),
        ),
        in_specs=[VMEM] * 7,
        out_specs=(HBM, VMEM, VMEM, VMEM),
        scratch_shapes=[
            pltpu.VMEM((count - left, width, cols), jnp.bfloat16),
            pltpu.SemaphoreType.DMA((count - left,)),
        ],
        compiler_params=pltpu.CompilerParams(vmem_limit_bytes=12 * 2**20),
        cost_estimate=pl.CostEstimate(
            flops=2 * count * width * cols * rank,
            bytes_accessed=4 * count * width * cols,
            transcendentals=0,
        ),
        name="merge_blocks",
    )(start, pick, features, served, slabs, crossed, last)


def finish(start, up, features, served, left, last, merged, total, context, own_weight):
    count = last.shape[0]
    depth, cols = served.shape
    width = depth // start.shape[1]
    smalls = [total.shape, context.shape]
    return pl.pallas_call(
        final_kernel,
        out_shape=[
            jax.ShapeDtypeStruct(shape, jnp.bfloat16) for shape in [(depth, cols), *smalls]
        ],
        in_specs=[VMEM] * 6 + [HBM] + [VMEM] * 3,
        out_specs=[HBM] * 3,
        input_output_aliases={6: 0},
        scratch_shapes=[
            pltpu.VMEM((count, width, cols), jnp.bfloat16),
            pltpu.SemaphoreType.DMA((count + left.shape[0],)),
        ]
        + [pltpu.VMEM(shape, jnp.bfloat16) for shape in smalls]
        + [pltpu.SemaphoreType.DMA((2,))],
        compiler_params=pltpu.CompilerParams(vmem_limit_bytes=12 * 2**20),
        cost_estimate=pl.CostEstimate(
            flops=2 * count * width * cols * up.shape[0],
            bytes_accessed=4 * count * width * cols,
            transcendentals=0,
        ),
        name="finish_rows",
    )(start, up, features, served, left, last, merged, total, context, own_weight)


def panels(x):
    return [x[:, i : i + PANEL] for i in range(0, x.shape[1], PANEL)]


def body(
    hidden_in,
    queries,
    stored_keys,
    stored_values,
    fresh_token_key,
    lengths,
    served_value_weight,
    adapter_in,
    adapter_out,
    owner_rank,
):
    n = lax.axis_size("replica")
    replica = lax.axis_index("replica")
    core = lax.axis_index("tensor")
    swap = [(0, 1), (1, 0)]
    full = adapter_in.shape[1]
    width = full // 2
    rows = queries.shape[0]
    per, cols = adapter_out.shape
    rank = n * per

    bits = [n >> i for i in range(1, n.bit_length())]
    ways = [bits, bits[:-2] + bits[:-3:-1]]

    def exchange(x, step):
        pairs = [(2 * i + c, 2 * (i ^ ways[c][step]) + c) for i in range(n) for c in range(2)]
        return lax.ppermute(x, ("replica", "tensor"), pairs)

    below = jnp.concatenate(panels(adapter_out), axis=0)
    below = jnp.pad(below, ((0, -below.shape[0] % 8), (0, 0)))
    block = lax.dynamic_slice_in_dim(adapter_in, core * width, width, axis=1)
    block, below = lax.optimization_barrier((block, below))
    slabs = jnp.concatenate([*panels(block), below], axis=0)[None]

    given = in_hbm(lengths, queries, fresh_token_key, stored_keys, stored_values)
    *early, first, second, third = range(len(bits))
    for step in early:
        slabs = jnp.concatenate([slabs, exchange(slabs, step)], axis=0)

    split = rows - rows // 4
    came = exchange(slabs, first)
    ahead = exchange(slabs, second)
    parts = [attend(range(split), given, after=[slabs])]
    parts[0], hid_other = lax.optimization_barrier((parts[0], hidden_in))
    hid_other = lax.ppermute(hid_other, "tensor", swap)
    came, ahead, parts[0] = lax.optimization_barrier((came, ahead, parts[0]))
    slabs = jnp.concatenate([slabs, came, ahead], axis=0)
    came = exchange(came, second)
    images = exchange(slabs, third)
    *part, served = attend(range(split, rows), given, *in_hbm(served_value_weight), [slabs])
    came, part, owner_rank = lax.optimization_barrier((came, part, owner_rank))
    parts.append(part)
    last = exchange(came, third)
    slabs = jnp.concatenate([slabs, came], axis=0)
    features = jnp.concatenate([hidden_in, hid_other], axis=1)
    features = jnp.where(core == 0, features, jnp.concatenate([hid_other, hidden_in], axis=1))

    slab = jnp.arange(n, dtype=jnp.int32)
    sources = []
    for way in ways:
        source = replica
        for step, bit in enumerate(way):
            source = source ^ (((slab >> step) & 1) * bit)
        sources.append(source)
    mine = jnp.where(core == 0, sources[0], sources[1])
    theirs = jnp.where(core == 0, sources[1], sources[0])
    source = jnp.concatenate([mine, theirs])
    half = jnp.concatenate([jnp.full((n,), core), jnp.full((n,), 1 - core)])
    place = jnp.sum(jnp.where(owner_rank[None, :] == source[:, None], slab[None, :], 0), axis=1)
    start = (place * full + half * width).astype(jnp.int32)[None]

    row = jnp.arange(rank, dtype=jnp.int32)
    row_source = replica
    for step in range(len(bits)):
        bit = jnp.where(core == 0, ways[0][step], ways[1][step])
        row_source = row_source ^ (((row // per >> step) & 1) * bit)
    pick = jnp.where(
        row[:, None] == (row_source * per + row % per)[None, :], ADAPTER_SCALE, 0.0
    ).astype(jnp.bfloat16)

    context, own_weight = (
        jnp.concatenate(pair, axis=0).reshape(queries.shape) for pair in zip(*parts)
    )
    crossed, start, features = lax.optimization_barrier((slabs, start, features))
    crossed = lax.ppermute(crossed, "tensor", swap)
    start = gate(start, images)
    last, start, pick, context, own_weight, features, crossed = lax.optimization_barrier(
        (last, start, pick, context, own_weight, features, crossed)
    )
    last = jnp.concatenate([images, last], axis=0)
    last_crossed = lax.ppermute(last, "tensor", swap)
    merged, total, up, left = merge(per, start, pick, features, served, slabs, crossed, last)
    return tuple(
        finish(
            start, up, features, served, left, last_crossed, merged, total, context, own_weight
        )
    )


def solution(mesh):
    in_specs = (
        P(("groups", "replica"), "tensor"),
        P(("groups", "replica"), "tensor"),
        P(("groups", "replica"), None, "tensor"),
        P(("groups", "replica"), None, "tensor"),
        P(("groups", "replica"), "tensor"),
        P(("groups", "replica")),
        P(None, "tensor"),
        P("groups", "replica"),
        P(("groups", "replica"), "tensor"),
        P("groups"),
    )
    out_specs = (
        P("groups", "tensor"),
        P(("groups", "replica"), "tensor"),
        P(("groups", "replica"), "tensor"),
    )
    return jax.shard_map(body, mesh=mesh, in_specs=in_specs, out_specs=out_specs, check_vma=False)
```

```python
import functools

import jax
import jax.numpy as jnp
from jax import lax
from jax.experimental import pallas as pl
from jax.experimental.pallas import tpu as pltpu
from jax.sharding import PartitionSpec as P

HEAD_SIZE = 128
ADAPTER_SCALE = 2.0
PANEL = 128

SMEM = pl.BlockSpec(memory_space=pltpu.SMEM)
VMEM = pl.BlockSpec(memory_space=pltpu.VMEM)
HBM = pl.BlockSpec(memory_space=pltpu.HBM)


def in_hbm(*arrays):
    return [pltpu.with_memory_space_constraint(x, pltpu.HBM) for x in arrays]


def attend_kernel(rows, fetch, lengths_hbm, q_hbm, own_k_hbm, k_hbm, v_hbm, *rest):
    rest = list(rest)
    if fetch:
        served_hbm, served_ref, served_sem = rest.pop(0), rest.pop(-10), rest.pop(-1)
    context_ref, own_weight_ref, lengths, q_ref, own_k_ref, k_buf, v_buf, small_sem, k_sem, v_sem = (
        rest[-10:]
    )
    smalls = [
        pltpu.make_async_copy(source, into, small_sem.at[i])
        for i, (source, into) in enumerate(
            [(lengths_hbm, lengths), (q_hbm, q_ref), (own_k_hbm, own_k_ref)]
        )
    ]
    for copy in smalls:
        copy.start()

    def copies(i, row):
        return (
            pltpu.make_async_copy(k_hbm.at[row], k_buf.at[i], k_sem.at[i]),
            pltpu.make_async_copy(v_hbm.at[row], v_buf.at[i], v_sem.at[i]),
        )

    for i, row in enumerate(rows):
        for copy in copies(i, row):
            copy.start()
    if fetch:
        get_served = pltpu.make_async_copy(served_hbm, served_ref, served_sem)
        get_served.start()
    for copy in smalls:
        copy.wait()
    queries = q_ref[...].astype(jnp.float32)
    own_keys = own_k_ref[...].astype(jnp.float32)
    heads = queries.shape[1] // HEAD_SIZE
    cache_len, width = k_buf.shape[1:]
    local_heads = width // HEAD_SIZE
    group = heads // local_heads
    scaling = 1.0 / HEAD_SIZE**0.5
    head_of = lax.broadcasted_iota(jnp.int32, (heads, HEAD_SIZE), 0) // group
    position = lax.broadcasted_iota(jnp.int32, (heads, cache_len), 1)
    for i, row in enumerate(rows):
        q = jnp.concatenate(
            [
                queries[row : row + 1, h * HEAD_SIZE : (h + 1) * HEAD_SIZE]
                for h in range(heads)
            ],
            axis=0,
        )
        spread = jnp.concatenate(
            [jnp.where(head_of == h, q, 0.0) for h in range(local_heads)], axis=1
        )
        own = jnp.sum(spread * own_keys[row : row + 1], axis=1, keepdims=True) * scaling
        get_keys, get_values = copies(i, row)
        get_keys.wait()
        scores = (
            lax.dot_general(
                spread.astype(jnp.bfloat16), k_buf[i], (((1,), (1,)), ((), ())),
                preferred_element_type=jnp.float32,
            )
            * scaling
        )
        valid = position < lengths[row]
        masked = jnp.where(valid, scores, -1e30)
        largest = jnp.maximum(jnp.max(masked, axis=1, keepdims=True), own)
        cached_exp = jnp.where(valid, jnp.exp(masked - largest), 0.0)
        own_exp = jnp.exp(own - largest)
        normaliser = jnp.sum(cached_exp, axis=1, keepdims=True) + own_exp
        weights = (cached_exp / normaliser).astype(jnp.bfloat16)
        weight_own = (own_exp / normaliser).astype(jnp.bfloat16).astype(jnp.float32)
        get_values.wait()
        wide = jnp.dot(weights, v_buf[i], preferred_element_type=jnp.float32)
        context = wide[:, :HEAD_SIZE]
        for h in range(1, local_heads):
            context = jnp.where(
                head_of == h, wide[:, h * HEAD_SIZE : (h + 1) * HEAD_SIZE], context
            )
        context_ref[i] = context
        own_weight_ref[i] = jnp.broadcast_to(weight_own, (heads, HEAD_SIZE))
    if fetch:
        get_served.wait()


def attend(rows, given, served=None, after=()):
    lengths, queries, own_key, stored_keys, stored_values = given
    fetch = served is not None
    cache_len, width = stored_keys.shape[1:]
    heads = queries.shape[1] // HEAD_SIZE
    count = len(rows)
    out_shape = [jax.ShapeDtypeStruct((count, heads, HEAD_SIZE), jnp.float32)] * 2
    if fetch:
        out_shape += [jax.ShapeDtypeStruct(served.shape, served.dtype)]
    return pl.pallas_call(
        functools.partial(attend_kernel, rows, fetch),
        out_shape=out_shape,
        in_specs=[HBM] * (5 + fetch) + [pl.BlockSpec(memory_space=pl.ANY)] * len(after),
        out_specs=[VMEM] * len(out_shape),
        scratch_shapes=[
            pltpu.SMEM(lengths.shape, jnp.int32),
            pltpu.VMEM(queries.shape, jnp.bfloat16),
            pltpu.VMEM(own_key.shape, jnp.bfloat16),
            pltpu.VMEM((count, cache_len, width), jnp.bfloat16),
            pltpu.VMEM((count, cache_len, width), jnp.bfloat16),
            pltpu.SemaphoreType.DMA((3,)),
            pltpu.SemaphoreType.DMA((count,)),
            pltpu.SemaphoreType.DMA((count,)),
        ]
        + [pltpu.SemaphoreType.DMA] * fetch,
        compiler_params=pltpu.CompilerParams(vmem_limit_bytes=12 * 2**20),
        cost_estimate=pl.CostEstimate(
            flops=4 * count * heads * cache_len * width,
            bytes_accessed=4 * count * cache_len * width,
            transcendentals=count * heads * cache_len,
        ),
        name="attend_cache",
    )(*given, *([served] if fetch else []), *after)


def gate_kernel(x_ref, after, out_ref):
    del after
    out_ref[...] = x_ref[...]


def gate(x, after):
    return pl.pallas_call(
        gate_kernel,
        out_shape=jax.ShapeDtypeStruct(x.shape, x.dtype),
        in_specs=[VMEM, pl.BlockSpec(memory_space=pl.ANY)],
        out_specs=VMEM,
        compiler_params=pltpu.CompilerParams(vmem_limit_bytes=2**20),
        name="gate_rows",
    )(x, after)


class Merge:
    def __init__(self, start_ref, merged, out_sem, width):
        self.start, self.merged, self.out_sem, self.width = start_ref[...], merged, out_sem, width
        self.entry = lax.broadcasted_iota(jnp.int32, self.start.shape, 1)

    def rows_of(self, entry):
        first = jnp.sum(jnp.where(self.entry == entry, self.start, 0))
        return pl.ds(pl.multiple_of(first, self.width), self.width)

    def store(self, source, rows, at):
        return pltpu.make_async_copy(source, self.merged.at[rows], self.out_sem.at[at])

    def rows(self, slab, up, served_ref, features_ref, rows, total):
        rank = up.shape[0]
        block = jnp.concatenate(
            [slab[i * rank : (i + 1) * rank] for i in range(self.width // PANEL)], axis=1
        )
        update = lax.dot_general(
            block, up, (((0,), (0,)), ((), ())), preferred_element_type=jnp.float32
        )
        fold = (served_ref[rows, :].astype(jnp.float32) + update).astype(jnp.bfloat16)
        part = jnp.dot(features_ref[:, rows], fold, preferred_element_type=jnp.float32)
        return fold, total + part


def merge_kernel(per, left, start_ref, pick_ref, features_ref, served_ref, slabs_ref, crossed_ref,
                 last_ref, merged, total_ref, up_ref, left_ref, m_buf, out_sem):
    width = m_buf.shape[1]
    rank, cols = up_ref.shape
    merge = Merge(start_ref, merged, out_sem, width)
    ups = []
    for ref in (slabs_ref, last_ref):
        for k in range(ref.shape[0]):
            below = ref[k, rank * (width // PANEL) :].astype(jnp.float32)
            ups.append(
                jnp.concatenate(
                    [below[i * per : (i + 1) * per] for i in range(cols // PANEL)], axis=1
                )
            )
    ups = jnp.concatenate(ups, axis=0).astype(jnp.bfloat16)
    up = jnp.dot(pick_ref[...], ups, preferred_element_type=jnp.float32).astype(jnp.bfloat16)
    up_ref[...] = up
    total = jnp.zeros(total_ref.shape, jnp.float32)
    refs = (slabs_ref, last_ref, crossed_ref)
    slabs = [ref.at[k] for ref in refs for k in range(ref.shape[0])]
    keep = len(slabs) - left
    stores = []
    for i, slab in enumerate(slabs):
        rows = merge.rows_of(i)
        fold, total = merge.rows(slab, up, served_ref, features_ref, rows, total)
        if i < keep:
            m_buf[i] = fold
            stores.append(merge.store(m_buf.at[i], rows, i))
            stores[-1].start()
        else:
            left_ref[i - keep] = fold
    total_ref[...] = total
    for store in stores:
        store.wait()


def final_kernel(start_ref, up_ref, features_ref, served_ref, left_ref, last_ref, merged_in,
                 total_ref, context_ref, own_weight_ref, merged, fresh_hbm, attended_hbm, m_buf,
                 out_sem, fresh_ref, attended_ref, small_sem):
    del merged_in
    count, width = last_ref.shape[0], m_buf.shape[1]
    left = left_ref.shape[0]
    merge = Merge(start_ref, merged, out_sem, width)
    first = start_ref.shape[1] - count
    total = total_ref[...]
    stores = [
        merge.store(left_ref.at[k], merge.rows_of(first - left + k), count + k)
        for k in range(left)
    ]
    for store in stores:
        store.start()
    for i in range(count):
        rows = merge.rows_of(first + i)
        fold, total = merge.rows(last_ref.at[i], up_ref[...], served_ref, features_ref, rows, total)
        m_buf[i] = fold
        stores.append(merge.store(m_buf.at[i], rows, i))
        stores[-1].start()
    fresh = total.astype(jnp.bfloat16)
    fresh_ref[...] = fresh
    put_fresh = pltpu.make_async_copy(fresh_ref, fresh_hbm, small_sem.at[0])
    put_fresh.start()
    value = fresh.astype(jnp.float32)
    heads = attended_ref.shape[1] // HEAD_SIZE
    group = heads // (fresh_ref.shape[1] // HEAD_SIZE)
    for h in range(heads):
        cols = slice(h * HEAD_SIZE, (h + 1) * HEAD_SIZE)
        at = (h // group) * HEAD_SIZE
        attended_ref[:, cols] = (
            context_ref[:, cols] + own_weight_ref[:, cols] * value[:, at : at + HEAD_SIZE]
        ).astype(jnp.bfloat16)
    put_attended = pltpu.make_async_copy(attended_ref, attended_hbm, small_sem.at[1])
    put_attended.start()
    for store in stores:
        store.wait()
    put_fresh.wait()
    put_attended.wait()


def merge(per, start, pick, features, served, slabs, crossed, last):
    left = 3
    count = slabs.shape[0] + crossed.shape[0] + last.shape[0]
    rank = pick.shape[0]
    depth, cols = served.shape
    width = depth // start.shape[1]
    return pl.pallas_call(
        functools.partial(merge_kernel, per, left),
        out_shape=(
            jax.ShapeDtypeStruct((depth, cols), jnp.bfloat16),
            jax.ShapeDtypeStruct((features.shape[0], cols), jnp.float32),
            jax.ShapeDtypeStruct((rank, cols), jnp.bfloat16),
            jax.ShapeDtypeStruct((left, width, cols), jnp.bfloat16),
        ),
        in_specs=[VMEM] * 7,
        out_specs=(HBM, VMEM, VMEM, VMEM),
        scratch_shapes=[
            pltpu.VMEM((count - left, width, cols), jnp.bfloat16),
            pltpu.SemaphoreType.DMA((count - left,)),
        ],
        compiler_params=pltpu.CompilerParams(vmem_limit_bytes=12 * 2**20),
        cost_estimate=pl.CostEstimate(
            flops=2 * count * width * cols * rank,
            bytes_accessed=4 * count * width * cols,
            transcendentals=0,
        ),
        name="merge_blocks",
    )(start, pick, features, served, slabs, crossed, last)


def finish(start, up, features, served, left, last, merged, total, context, own_weight):
    count = last.shape[0]
    depth, cols = served.shape
    width = depth // start.shape[1]
    smalls = [total.shape, context.shape]
    return pl.pallas_call(
        final_kernel,
        out_shape=[
            jax.ShapeDtypeStruct(shape, jnp.bfloat16) for shape in [(depth, cols), *smalls]
        ],
        in_specs=[VMEM] * 6 + [HBM] + [VMEM] * 3,
        out_specs=[HBM] * 3,
        input_output_aliases={6: 0},
        scratch_shapes=[
            pltpu.VMEM((count, width, cols), jnp.bfloat16),
            pltpu.SemaphoreType.DMA((count + left.shape[0],)),
        ]
        + [pltpu.VMEM(shape, jnp.bfloat16) for shape in smalls]
        + [pltpu.SemaphoreType.DMA((2,))],
        compiler_params=pltpu.CompilerParams(vmem_limit_bytes=12 * 2**20),
        cost_estimate=pl.CostEstimate(
            flops=2 * count * width * cols * up.shape[0],
            bytes_accessed=4 * count * width * cols,
            transcendentals=0,
        ),
        name="finish_rows",
    )(start, up, features, served, left, last, merged, total, context, own_weight)


def panels(x):
    return [x[:, i : i + PANEL] for i in range(0, x.shape[1], PANEL)]


def body(
    hidden_in,
    queries,
    stored_keys,
    stored_values,
    fresh_token_key,
    lengths,
    served_value_weight,
    adapter_in,
    adapter_out,
    owner_rank,
):
    n = lax.axis_size("replica")
    replica = lax.axis_index("replica")
    core = lax.axis_index("tensor")
    swap = [(0, 1), (1, 0)]
    full = adapter_in.shape[1]
    width = full // 2
    rows = queries.shape[0]
    per, cols = adapter_out.shape
    rank = n * per

    bits = [n >> i for i in range(1, n.bit_length())]
    ways = [bits, bits[:-2] + bits[:-3:-1]]

    def exchange(x, step):
        pairs = [(2 * i + c, 2 * (i ^ ways[c][step]) + c) for i in range(n) for c in range(2)]
        return lax.ppermute(x, ("replica", "tensor"), pairs)

    below = jnp.concatenate(panels(adapter_out), axis=0)
    below = jnp.pad(below, ((0, -below.shape[0] % 8), (0, 0)))
    block = lax.dynamic_slice_in_dim(adapter_in, core * width, width, axis=1)
    block, below = lax.optimization_barrier((block, below))
    slabs = jnp.concatenate([*panels(block), below], axis=0)[None]

    given = in_hbm(lengths, queries, fresh_token_key, stored_keys, stored_values)
    *early, first, second, third = range(len(bits))
    for step in early:
        slabs = jnp.concatenate([slabs, exchange(slabs, step)], axis=0)

    split = rows - rows // 4
    came = exchange(slabs, first)
    ahead = exchange(slabs, second)
    parts = [attend(range(split), given, after=[slabs])]
    parts[0], hid_other = lax.optimization_barrier((parts[0], hidden_in))
    hid_other = lax.ppermute(hid_other, "tensor", swap)
    came, ahead, parts[0] = lax.optimization_barrier((came, ahead, parts[0]))
    slabs = jnp.concatenate([slabs, came, ahead], axis=0)
    came = exchange(came, second)
    images = exchange(slabs, third)
    *part, served = attend(range(split, rows), given, *in_hbm(served_value_weight), [slabs])
    came, part, owner_rank = lax.optimization_barrier((came, part, owner_rank))
    parts.append(part)
    last = exchange(came, third)
    slabs = jnp.concatenate([slabs, came], axis=0)
    features = jnp.concatenate([hidden_in, hid_other], axis=1)
    features = jnp.where(core == 0, features, jnp.concatenate([hid_other, hidden_in], axis=1))

    slab = jnp.arange(n, dtype=jnp.int32)
    sources = []
    for way in ways:
        source = replica
        for step, bit in enumerate(way):
            source = source ^ (((slab >> step) & 1) * bit)
        sources.append(source)
    mine = jnp.where(core == 0, sources[0], sources[1])
    theirs = jnp.where(core == 0, sources[1], sources[0])
    source = jnp.concatenate([mine, theirs])
    half = jnp.concatenate([jnp.full((n,), core), jnp.full((n,), 1 - core)])
    place = jnp.sum(jnp.where(owner_rank[None, :] == source[:, None], slab[None, :], 0), axis=1)
    start = (place * full + half * width).astype(jnp.int32)[None]

    row = jnp.arange(rank, dtype=jnp.int32)
    row_source = replica
    for step in range(len(bits)):
        bit = jnp.where(core == 0, ways[0][step], ways[1][step])
        row_source = row_source ^ (((row // per >> step) & 1) * bit)
    pick = jnp.where(
        row[:, None] == (row_source * per + row % per)[None, :], ADAPTER_SCALE, 0.0
    ).astype(jnp.bfloat16)

    context, own_weight = (
        jnp.concatenate(pair, axis=0).reshape(queries.shape) for pair in zip(*parts)
    )
    crossed, start, features = lax.optimization_barrier((slabs, start, features))
    crossed = lax.ppermute(crossed, "tensor", swap)
    start = gate(start, images)
    last, start, pick, context, own_weight, features, crossed = lax.optimization_barrier(
        (last, start, pick, context, own_weight, features, crossed)
    )
    last = jnp.concatenate([images, last], axis=0)
    last_crossed = lax.ppermute(last, "tensor", swap)
    merged, total, up, left = merge(per, start, pick, features, served, slabs, crossed, last)
    return tuple(
        finish(
            start, up, features, served, left, last_crossed, merged, total, context, own_weight
        )
    )


def solution(mesh):
    in_specs = (
        P(("groups", "replica"), "tensor"),
        P(("groups", "replica"), "tensor"),
        P(("groups", "replica"), None, "tensor"),
        P(("groups", "replica"), None, "tensor"),
        P(("groups", "replica"), "tensor"),
        P(("groups", "replica")),
        P(None, "tensor"),
        P("groups", "replica"),
        P(("groups", "replica"), "tensor"),
        P("groups"),
    )
    out_specs = (
        P("groups", "tensor"),
        P(("groups", "replica"), "tensor"),
        P(("groups", "replica"), "tensor"),
    )
    return jax.shard_map(body, mesh=mesh, in_specs=in_specs, out_specs=out_specs, check_vma=False)
```

```python
import functools

import jax
import jax.numpy as jnp
from jax import lax
from jax.experimental import pallas as pl
from jax.experimental.pallas import tpu as pltpu
from jax.sharding import PartitionSpec as P

HEAD_SIZE = 128
ADAPTER_SCALE = 2.0
PANEL = 128

SMEM = pl.BlockSpec(memory_space=pltpu.SMEM)
VMEM = pl.BlockSpec(memory_space=pltpu.VMEM)
HBM = pl.BlockSpec(memory_space=pltpu.HBM)


def in_hbm(*arrays):
    return [pltpu.with_memory_space_constraint(x, pltpu.HBM) for x in arrays]


def attend_kernel(rows, fetch, lengths_hbm, q_hbm, own_k_hbm, k_hbm, v_hbm, *rest):
    rest = list(rest)
    if fetch:
        served_hbm, served_ref, served_sem = rest.pop(0), rest.pop(-10), rest.pop(-1)
    context_ref, own_weight_ref, lengths, q_ref, own_k_ref, k_buf, v_buf, small_sem, k_sem, v_sem = (
        rest[-10:]
    )
    smalls = [
        pltpu.make_async_copy(source, into, small_sem.at[i])
        for i, (source, into) in enumerate(
            [(lengths_hbm, lengths), (q_hbm, q_ref), (own_k_hbm, own_k_ref)]
        )
    ]
    for copy in smalls:
        copy.start()

    def copies(i, row):
        return (
            pltpu.make_async_copy(k_hbm.at[row], k_buf.at[i], k_sem.at[i]),
            pltpu.make_async_copy(v_hbm.at[row], v_buf.at[i], v_sem.at[i]),
        )

    for i, row in enumerate(rows):
        for copy in copies(i, row):
            copy.start()
    if fetch:
        get_served = pltpu.make_async_copy(served_hbm, served_ref, served_sem)
        get_served.start()
    for copy in smalls:
        copy.wait()
    queries = q_ref[...].astype(jnp.float32)
    own_keys = own_k_ref[...].astype(jnp.float32)
    heads = queries.shape[1] // HEAD_SIZE
    cache_len, width = k_buf.shape[1:]
    local_heads = width // HEAD_SIZE
    group = heads // local_heads
    scaling = 1.0 / HEAD_SIZE**0.5
    head_of = lax.broadcasted_iota(jnp.int32, (heads, HEAD_SIZE), 0) // group
    position = lax.broadcasted_iota(jnp.int32, (heads, cache_len), 1)
    for i, row in enumerate(rows):
        q = jnp.concatenate(
            [
                queries[row : row + 1, h * HEAD_SIZE : (h + 1) * HEAD_SIZE]
                for h in range(heads)
            ],
            axis=0,
        )
        spread = jnp.concatenate(
            [jnp.where(head_of == h, q, 0.0) for h in range(local_heads)], axis=1
        )
        own = jnp.sum(spread * own_keys[row : row + 1], axis=1, keepdims=True) * scaling
        get_keys, get_values = copies(i, row)
        get_keys.wait()
        scores = (
            lax.dot_general(
                spread.astype(jnp.bfloat16), k_buf[i], (((1,), (1,)), ((), ())),
                preferred_element_type=jnp.float32,
            )
            * scaling
        )
        valid = position < lengths[row]
        masked = jnp.where(valid, scores, -1e30)
        largest = jnp.maximum(jnp.max(masked, axis=1, keepdims=True), own)
        cached_exp = jnp.where(valid, jnp.exp(masked - largest), 0.0)
        own_exp = jnp.exp(own - largest)
        normaliser = jnp.sum(cached_exp, axis=1, keepdims=True) + own_exp
        weights = (cached_exp / normaliser).astype(jnp.bfloat16)
        weight_own = (own_exp / normaliser).astype(jnp.bfloat16).astype(jnp.float32)
        get_values.wait()
        wide = jnp.dot(weights, v_buf[i], preferred_element_type=jnp.float32)
        context = wide[:, :HEAD_SIZE]
        for h in range(1, local_heads):
            context = jnp.where(
                head_of == h, wide[:, h * HEAD_SIZE : (h + 1) * HEAD_SIZE], context
            )
        context_ref[i] = context
        own_weight_ref[i] = jnp.broadcast_to(weight_own, (heads, HEAD_SIZE))
    if fetch:
        get_served.wait()


def attend(rows, given, served=None, after=()):
    lengths, queries, own_key, stored_keys, stored_values = given
    fetch = served is not None
    cache_len, width = stored_keys.shape[1:]
    heads = queries.shape[1] // HEAD_SIZE
    count = len(rows)
    out_shape = [jax.ShapeDtypeStruct((count, heads, HEAD_SIZE), jnp.float32)] * 2
    if fetch:
        out_shape += [jax.ShapeDtypeStruct(served.shape, served.dtype)]
    return pl.pallas_call(
        functools.partial(attend_kernel, rows, fetch),
        out_shape=out_shape,
        in_specs=[HBM] * (5 + fetch) + [pl.BlockSpec(memory_space=pl.ANY)] * len(after),
        out_specs=[VMEM] * len(out_shape),
        scratch_shapes=[
            pltpu.SMEM(lengths.shape, jnp.int32),
            pltpu.VMEM(queries.shape, jnp.bfloat16),
            pltpu.VMEM(own_key.shape, jnp.bfloat16),
            pltpu.VMEM((count, cache_len, width), jnp.bfloat16),
            pltpu.VMEM((count, cache_len, width), jnp.bfloat16),
            pltpu.SemaphoreType.DMA((3,)),
            pltpu.SemaphoreType.DMA((count,)),
            pltpu.SemaphoreType.DMA((count,)),
        ]
        + [pltpu.SemaphoreType.DMA] * fetch,
        compiler_params=pltpu.CompilerParams(vmem_limit_bytes=12 * 2**20),
        cost_estimate=pl.CostEstimate(
            flops=4 * count * heads * cache_len * width,
            bytes_accessed=4 * count * cache_len * width,
            transcendentals=count * heads * cache_len,
        ),
        name="attend_cache",
    )(*given, *([served] if fetch else []), *after)


class Merge:
    def __init__(self, start_ref, merged, out_sem, width):
        self.start, self.merged, self.out_sem, self.width = start_ref[...], merged, out_sem, width
        self.entry = lax.broadcasted_iota(jnp.int32, self.start.shape, 1)

    def rows_of(self, entry):
        first = jnp.sum(jnp.where(self.entry == entry, self.start, 0))
        return pl.ds(pl.multiple_of(first, self.width), self.width)

    def store(self, source, rows, at):
        return pltpu.make_async_copy(source, self.merged.at[rows], self.out_sem.at[at])

    def rows(self, slab, up, served_ref, features_ref, rows, total):
        rank = up.shape[0]
        block = jnp.concatenate(
            [slab[i * rank : (i + 1) * rank] for i in range(self.width // PANEL)], axis=1
        )
        update = lax.dot_general(
            block, up, (((0,), (0,)), ((), ())), preferred_element_type=jnp.float32
        )
        fold = (served_ref[rows, :].astype(jnp.float32) + update).astype(jnp.bfloat16)
        part = jnp.dot(features_ref[:, rows], fold, preferred_element_type=jnp.float32)
        return fold, total + part


def merge_kernel(per, left, start_ref, pick_ref, features_ref, served_ref, slabs_ref, crossed_ref,
                 last_ref, merged, total_ref, up_ref, left_ref, m_buf, out_sem):
    width = m_buf.shape[1]
    rank, cols = up_ref.shape
    merge = Merge(start_ref, merged, out_sem, width)
    ups = []
    for ref in (slabs_ref, last_ref):
        for k in range(ref.shape[0]):
            below = ref[k, rank * (width // PANEL) :].astype(jnp.float32)
            ups.append(
                jnp.concatenate(
                    [below[i * per : (i + 1) * per] for i in range(cols // PANEL)], axis=1
                )
            )
    ups = jnp.concatenate(ups, axis=0).astype(jnp.bfloat16)
    up = jnp.dot(pick_ref[...], ups, preferred_element_type=jnp.float32).astype(jnp.bfloat16)
    up_ref[...] = up
    total = jnp.zeros(total_ref.shape, jnp.float32)
    refs = (slabs_ref, last_ref, crossed_ref)
    slabs = [ref.at[k] for ref in refs for k in range(ref.shape[0])]
    keep = len(slabs) - left
    stores = []
    for i, slab in enumerate(slabs):
        rows = merge.rows_of(i)
        fold, total = merge.rows(slab, up, served_ref, features_ref, rows, total)
        if i < keep:
            m_buf[i] = fold
            stores.append(merge.store(m_buf.at[i], rows, i))
            stores[-1].start()
        else:
            left_ref[i - keep] = fold
    total_ref[...] = total
    for store in stores:
        store.wait()


def final_kernel(start_ref, up_ref, features_ref, served_ref, left_ref, last_ref, merged_in,
                 total_ref, context_ref, own_weight_ref, merged, fresh_hbm, attended_hbm, m_buf,
                 out_sem, fresh_ref, attended_ref, small_sem):
    del merged_in
    count, width = last_ref.shape[0], m_buf.shape[1]
    left = left_ref.shape[0]
    merge = Merge(start_ref, merged, out_sem, width)
    first = start_ref.shape[1] - count
    total = total_ref[...]
    stores = [
        merge.store(left_ref.at[k], merge.rows_of(first - left + k), count + k)
        for k in range(left)
    ]
    for store in stores:
        store.start()
    for i in range(count):
        rows = merge.rows_of(first + i)
        fold, total = merge.rows(last_ref.at[i], up_ref[...], served_ref, features_ref, rows, total)
        m_buf[i] = fold
        stores.append(merge.store(m_buf.at[i], rows, i))
        stores[-1].start()
    fresh = total.astype(jnp.bfloat16)
    fresh_ref[...] = fresh
    put_fresh = pltpu.make_async_copy(fresh_ref, fresh_hbm, small_sem.at[0])
    put_fresh.start()
    value = fresh.astype(jnp.float32)
    heads = attended_ref.shape[1] // HEAD_SIZE
    group = heads // (fresh_ref.shape[1] // HEAD_SIZE)
    for h in range(heads):
        cols = slice(h * HEAD_SIZE, (h + 1) * HEAD_SIZE)
        at = (h // group) * HEAD_SIZE
        attended_ref[:, cols] = (
            context_ref[:, cols] + own_weight_ref[:, cols] * value[:, at : at + HEAD_SIZE]
        ).astype(jnp.bfloat16)
    put_attended = pltpu.make_async_copy(attended_ref, attended_hbm, small_sem.at[1])
    put_attended.start()
    for store in stores:
        store.wait()
    put_fresh.wait()
    put_attended.wait()


def merge(per, start, pick, features, served, slabs, crossed, last):
    left = 3
    count = slabs.shape[0] + crossed.shape[0] + last.shape[0]
    rank = pick.shape[0]
    depth, cols = served.shape
    width = depth // start.shape[1]
    return pl.pallas_call(
        functools.partial(merge_kernel, per, left),
        out_shape=(
            jax.ShapeDtypeStruct((depth, cols), jnp.bfloat16),
            jax.ShapeDtypeStruct((features.shape[0], cols), jnp.float32),
            jax.ShapeDtypeStruct((rank, cols), jnp.bfloat16),
            jax.ShapeDtypeStruct((left, width, cols), jnp.bfloat16),
        ),
        in_specs=[VMEM] * 7,
        out_specs=(HBM, VMEM, VMEM, VMEM),
        scratch_shapes=[
            pltpu.VMEM((count - left, width, cols), jnp.bfloat16),
            pltpu.SemaphoreType.DMA((count - left,)),
        ],
        compiler_params=pltpu.CompilerParams(vmem_limit_bytes=12 * 2**20),
        cost_estimate=pl.CostEstimate(
            flops=2 * count * width * cols * rank,
            bytes_accessed=4 * count * width * cols,
            transcendentals=0,
        ),
        name="merge_blocks",
    )(start, pick, features, served, slabs, crossed, last)


def finish(start, up, features, served, left, last, merged, total, context, own_weight):
    count = last.shape[0]
    depth, cols = served.shape
    width = depth // start.shape[1]
    smalls = [total.shape, context.shape]
    return pl.pallas_call(
        final_kernel,
        out_shape=[
            jax.ShapeDtypeStruct(shape, jnp.bfloat16) for shape in [(depth, cols), *smalls]
        ],
        in_specs=[VMEM] * 6 + [HBM] + [VMEM] * 3,
        out_specs=[HBM] * 3,
        input_output_aliases={6: 0},
        scratch_shapes=[
            pltpu.VMEM((count, width, cols), jnp.bfloat16),
            pltpu.SemaphoreType.DMA((count + left.shape[0],)),
        ]
        + [pltpu.VMEM(shape, jnp.bfloat16) for shape in smalls]
        + [pltpu.SemaphoreType.DMA((2,))],
        compiler_params=pltpu.CompilerParams(vmem_limit_bytes=12 * 2**20),
        cost_estimate=pl.CostEstimate(
            flops=2 * count * width * cols * up.shape[0],
            bytes_accessed=4 * count * width * cols,
            transcendentals=0,
        ),
        name="finish_rows",
    )(start, up, features, served, left, last, merged, total, context, own_weight)


def panels(x):
    return [x[:, i : i + PANEL] for i in range(0, x.shape[1], PANEL)]


def body(
    hidden_in,
    queries,
    stored_keys,
    stored_values,
    fresh_token_key,
    lengths,
    served_value_weight,
    adapter_in,
    adapter_out,
    owner_rank,
):
    n = lax.axis_size("replica")
    replica = lax.axis_index("replica")
    core = lax.axis_index("tensor")
    swap = [(0, 1), (1, 0)]
    full = adapter_in.shape[1]
    width = full // 2
    rows = queries.shape[0]
    per, cols = adapter_out.shape
    rank = n * per

    bits = [n >> i for i in range(1, n.bit_length())]
    ways = [bits, bits[:-2] + bits[:-3:-1]]

    def exchange(x, step):
        pairs = [(2 * i + c, 2 * (i ^ ways[c][step]) + c) for i in range(n) for c in range(2)]
        return lax.ppermute(x, ("replica", "tensor"), pairs)

    below = jnp.concatenate(panels(adapter_out), axis=0)
    below = jnp.pad(below, ((0, -below.shape[0] % 8), (0, 0)))
    block = lax.dynamic_slice_in_dim(adapter_in, core * width, width, axis=1)
    block, below = lax.optimization_barrier((block, below))
    slabs = jnp.concatenate([*panels(block), below], axis=0)[None]

    given = in_hbm(lengths, queries, fresh_token_key, stored_keys, stored_values)
    *early, first, second, third = range(len(bits))
    for step in early:
        slabs = jnp.concatenate([slabs, exchange(slabs, step)], axis=0)

    cuts = [0, rows // 2, rows - rows // 4, rows]
    first_rows, second_rows, third_rows = (range(*cut) for cut in zip(cuts, cuts[1:]))
    came = exchange(slabs, first)
    ahead = exchange(slabs, second)
    *part, served = attend(first_rows, given, *in_hbm(served_value_weight), [slabs])
    parts = [part]
    part, hid_other = lax.optimization_barrier((part, hidden_in))
    hid_other = lax.ppermute(hid_other, "tensor", swap)
    came, part = lax.optimization_barrier((came, part))
    slabs = jnp.concatenate([slabs, came, ahead], axis=0)
    came = exchange(came, second)
    images = exchange(slabs, third)
    parts.append(attend(second_rows, given, after=[slabs]))
    came, parts[1], hid_other, owner_rank = lax.optimization_barrier(
        (came, parts[1], hid_other, owner_rank)
    )
    last = exchange(came, third)
    slabs = jnp.concatenate([slabs, came], axis=0)
    parts.append(attend(third_rows, given, after=[images]))
    features = jnp.concatenate([hidden_in, hid_other], axis=1)
    features = jnp.where(core == 0, features, jnp.concatenate([hid_other, hidden_in], axis=1))

    slab = jnp.arange(n, dtype=jnp.int32)
    sources = []
    for way in ways:
        source = replica
        for step, bit in enumerate(way):
            source = source ^ (((slab >> step) & 1) * bit)
        sources.append(source)
    mine = jnp.where(core == 0, sources[0], sources[1])
    theirs = jnp.where(core == 0, sources[1], sources[0])
    source = jnp.concatenate([mine, theirs])
    half = jnp.concatenate([jnp.full((n,), core), jnp.full((n,), 1 - core)])
    place = jnp.sum(jnp.where(owner_rank[None, :] == source[:, None], slab[None, :], 0), axis=1)
    start = (place * full + half * width).astype(jnp.int32)[None]

    row = jnp.arange(rank, dtype=jnp.int32)
    row_source = replica
    for step in range(len(bits)):
        bit = jnp.where(core == 0, ways[0][step], ways[1][step])
        row_source = row_source ^ (((row // per >> step) & 1) * bit)
    pick = jnp.where(
        row[:, None] == (row_source * per + row % per)[None, :], ADAPTER_SCALE, 0.0
    ).astype(jnp.bfloat16)

    context, own_weight = (
        jnp.concatenate(pair, axis=0).reshape(queries.shape) for pair in zip(*parts)
    )
    crossed, start = lax.optimization_barrier((slabs, start))
    crossed = lax.ppermute(crossed, "tensor", swap)
    last, start, pick, context, own_weight, features, crossed = lax.optimization_barrier(
        (last, start, pick, context, own_weight, features, crossed)
    )
    last = jnp.concatenate([images, last], axis=0)
    last_crossed = lax.ppermute(last, "tensor", swap)
    merged, total, up, left = merge(per, start, pick, features, served, slabs, crossed, last)
    return tuple(
        finish(
            start, up, features, served, left, last_crossed, merged, total, context, own_weight
        )
    )


def solution(mesh):
    in_specs = (
        P(("groups", "replica"), "tensor"),
        P(("groups", "replica"), "tensor"),
        P(("groups", "replica"), None, "tensor"),
        P(("groups", "replica"), None, "tensor"),
        P(("groups", "replica"), "tensor"),
        P(("groups", "replica")),
        P(None, "tensor"),
        P("groups", "replica"),
        P(("groups", "replica"), "tensor"),
        P("groups"),
    )
    out_specs = (
        P("groups", "tensor"),
        P(("groups", "replica"), "tensor"),
        P(("groups", "replica"), "tensor"),
    )
    return jax.shard_map(body, mesh=mesh, in_specs=in_specs, out_specs=out_specs, check_vma=False)
```

```python
import functools

import jax
import jax.numpy as jnp
from jax import lax
from jax.experimental import pallas as pl
from jax.experimental.pallas import tpu as pltpu
from jax.sharding import PartitionSpec as P

HEAD_SIZE = 128
ADAPTER_SCALE = 2.0
PANEL = 128

SMEM = pl.BlockSpec(memory_space=pltpu.SMEM)
VMEM = pl.BlockSpec(memory_space=pltpu.VMEM)
HBM = pl.BlockSpec(memory_space=pltpu.HBM)


def in_hbm(*arrays):
    return [pltpu.with_memory_space_constraint(x, pltpu.HBM) for x in arrays]


def attend_kernel(rows, fetch, lengths_hbm, q_hbm, own_k_hbm, k_hbm, v_hbm, *rest):
    rest = list(rest)
    if fetch:
        served_hbm, served_ref, served_sem = rest.pop(0), rest.pop(-10), rest.pop(-1)
    context_ref, own_weight_ref, lengths, q_ref, own_k_ref, k_buf, v_buf, small_sem, k_sem, v_sem = (
        rest[-10:]
    )
    smalls = [
        pltpu.make_async_copy(source, into, small_sem.at[i])
        for i, (source, into) in enumerate(
            [(lengths_hbm, lengths), (q_hbm, q_ref), (own_k_hbm, own_k_ref)]
        )
    ]
    for copy in smalls:
        copy.start()

    def copies(i, row):
        return (
            pltpu.make_async_copy(k_hbm.at[row], k_buf.at[i], k_sem.at[i]),
            pltpu.make_async_copy(v_hbm.at[row], v_buf.at[i], v_sem.at[i]),
        )

    for i, row in enumerate(rows):
        for copy in copies(i, row):
            copy.start()
    if fetch:
        get_served = pltpu.make_async_copy(served_hbm, served_ref, served_sem)
        get_served.start()
    for copy in smalls:
        copy.wait()
    queries = q_ref[...].astype(jnp.float32)
    own_keys = own_k_ref[...].astype(jnp.float32)
    heads = queries.shape[1] // HEAD_SIZE
    cache_len, width = k_buf.shape[1:]
    local_heads = width // HEAD_SIZE
    group = heads // local_heads
    scaling = 1.0 / HEAD_SIZE**0.5
    head_of = lax.broadcasted_iota(jnp.int32, (heads, HEAD_SIZE), 0) // group
    position = lax.broadcasted_iota(jnp.int32, (heads, cache_len), 1)
    for i, row in enumerate(rows):
        q = jnp.concatenate(
            [
                queries[row : row + 1, h * HEAD_SIZE : (h + 1) * HEAD_SIZE]
                for h in range(heads)
            ],
            axis=0,
        )
        spread = jnp.concatenate(
            [jnp.where(head_of == h, q, 0.0) for h in range(local_heads)], axis=1
        )
        own = jnp.sum(spread * own_keys[row : row + 1], axis=1, keepdims=True) * scaling
        get_keys, get_values = copies(i, row)
        get_keys.wait()
        scores = (
            lax.dot_general(
                spread.astype(jnp.bfloat16), k_buf[i], (((1,), (1,)), ((), ())),
                preferred_element_type=jnp.float32,
            )
            * scaling
        )
        valid = position < lengths[row]
        masked = jnp.where(valid, scores, -1e30)
        largest = jnp.maximum(jnp.max(masked, axis=1, keepdims=True), own)
        cached_exp = jnp.where(valid, jnp.exp(masked - largest), 0.0)
        own_exp = jnp.exp(own - largest)
        normaliser = jnp.sum(cached_exp, axis=1, keepdims=True) + own_exp
        weights = (cached_exp / normaliser).astype(jnp.bfloat16)
        weight_own = (own_exp / normaliser).astype(jnp.bfloat16).astype(jnp.float32)
        get_values.wait()
        wide = jnp.dot(weights, v_buf[i], preferred_element_type=jnp.float32)
        context = wide[:, :HEAD_SIZE]
        for h in range(1, local_heads):
            context = jnp.where(
                head_of == h, wide[:, h * HEAD_SIZE : (h + 1) * HEAD_SIZE], context
            )
        context_ref[i] = context
        own_weight_ref[i] = jnp.broadcast_to(weight_own, (heads, HEAD_SIZE))
    if fetch:
        get_served.wait()


def attend(rows, given, served=None, after=()):
    lengths, queries, own_key, stored_keys, stored_values = given
    fetch = served is not None
    cache_len, width = stored_keys.shape[1:]
    heads = queries.shape[1] // HEAD_SIZE
    count = len(rows)
    out_shape = [jax.ShapeDtypeStruct((count, heads, HEAD_SIZE), jnp.float32)] * 2
    if fetch:
        out_shape += [jax.ShapeDtypeStruct(served.shape, served.dtype)]
    return pl.pallas_call(
        functools.partial(attend_kernel, rows, fetch),
        out_shape=out_shape,
        in_specs=[HBM] * (5 + fetch) + [pl.BlockSpec(memory_space=pl.ANY)] * len(after),
        out_specs=[VMEM] * len(out_shape),
        scratch_shapes=[
            pltpu.SMEM(lengths.shape, jnp.int32),
            pltpu.VMEM(queries.shape, jnp.bfloat16),
            pltpu.VMEM(own_key.shape, jnp.bfloat16),
            pltpu.VMEM((count, cache_len, width), jnp.bfloat16),
            pltpu.VMEM((count, cache_len, width), jnp.bfloat16),
            pltpu.SemaphoreType.DMA((3,)),
            pltpu.SemaphoreType.DMA((count,)),
            pltpu.SemaphoreType.DMA((count,)),
        ]
        + [pltpu.SemaphoreType.DMA] * fetch,
        compiler_params=pltpu.CompilerParams(vmem_limit_bytes=12 * 2**20),
        cost_estimate=pl.CostEstimate(
            flops=4 * count * heads * cache_len * width,
            bytes_accessed=4 * count * cache_len * width,
            transcendentals=count * heads * cache_len,
        ),
        name="attend_cache",
    )(*given, *([served] if fetch else []), *after)


class Merge:
    def __init__(self, start_ref, merged, out_sem, width):
        self.start, self.merged, self.out_sem, self.width = start_ref[...], merged, out_sem, width
        self.entry = lax.broadcasted_iota(jnp.int32, self.start.shape, 1)

    def rows_of(self, entry):
        first = jnp.sum(jnp.where(self.entry == entry, self.start, 0))
        return pl.ds(pl.multiple_of(first, self.width), self.width)

    def store(self, source, rows, at):
        return pltpu.make_async_copy(source, self.merged.at[rows], self.out_sem.at[at])

    def rows(self, slab, up, served_ref, features_ref, rows, total):
        rank = up.shape[0]
        block = jnp.concatenate(
            [slab[i * rank : (i + 1) * rank] for i in range(self.width // PANEL)], axis=1
        )
        update = lax.dot_general(
            block, up, (((0,), (0,)), ((), ())), preferred_element_type=jnp.float32
        )
        fold = (served_ref[rows, :].astype(jnp.float32) + update).astype(jnp.bfloat16)
        part = jnp.dot(features_ref[:, rows], fold, preferred_element_type=jnp.float32)
        return fold, total + part


def merge_kernel(per, left, start_ref, pick_ref, features_ref, served_ref, slabs_ref, crossed_ref,
                 last_ref, merged, total_ref, up_ref, left_ref, m_buf, out_sem):
    width = m_buf.shape[1]
    rank, cols = up_ref.shape
    merge = Merge(start_ref, merged, out_sem, width)
    ups = []
    for ref in (slabs_ref, last_ref):
        for k in range(ref.shape[0]):
            below = ref[k, rank * (width // PANEL) :].astype(jnp.float32)
            ups.append(
                jnp.concatenate(
                    [below[i * per : (i + 1) * per] for i in range(cols // PANEL)], axis=1
                )
            )
    ups = jnp.concatenate(ups, axis=0).astype(jnp.bfloat16)
    up = jnp.dot(pick_ref[...], ups, preferred_element_type=jnp.float32).astype(jnp.bfloat16)
    up_ref[...] = up
    total = jnp.zeros(total_ref.shape, jnp.float32)
    refs = (slabs_ref, last_ref, crossed_ref)
    slabs = [ref.at[k] for ref in refs for k in range(ref.shape[0])]
    keep = len(slabs) - left
    stores = []
    for i, slab in enumerate(slabs):
        rows = merge.rows_of(i)
        fold, total = merge.rows(slab, up, served_ref, features_ref, rows, total)
        if i < keep:
            m_buf[i] = fold
            stores.append(merge.store(m_buf.at[i], rows, i))
            stores[-1].start()
        else:
            left_ref[i - keep] = fold
    total_ref[...] = total
    for store in stores:
        store.wait()


def final_kernel(start_ref, up_ref, features_ref, served_ref, left_ref, last_ref, merged_in,
                 total_ref, context_ref, own_weight_ref, merged, fresh_hbm, attended_hbm, m_buf,
                 out_sem, fresh_ref, attended_ref, small_sem):
    del merged_in
    count, width = last_ref.shape[0], m_buf.shape[1]
    left = left_ref.shape[0]
    merge = Merge(start_ref, merged, out_sem, width)
    first = start_ref.shape[1] - count
    total = total_ref[...]
    stores = [
        merge.store(left_ref.at[k], merge.rows_of(first - left + k), count + k)
        for k in range(left)
    ]
    for store in stores:
        store.start()
    for i in range(count):
        rows = merge.rows_of(first + i)
        fold, total = merge.rows(last_ref.at[i], up_ref[...], served_ref, features_ref, rows, total)
        m_buf[i] = fold
        stores.append(merge.store(m_buf.at[i], rows, i))
        stores[-1].start()
    fresh = total.astype(jnp.bfloat16)
    fresh_ref[...] = fresh
    put_fresh = pltpu.make_async_copy(fresh_ref, fresh_hbm, small_sem.at[0])
    put_fresh.start()
    value = fresh.astype(jnp.float32)
    heads = attended_ref.shape[1] // HEAD_SIZE
    group = heads // (fresh_ref.shape[1] // HEAD_SIZE)
    for h in range(heads):
        cols = slice(h * HEAD_SIZE, (h + 1) * HEAD_SIZE)
        at = (h // group) * HEAD_SIZE
        attended_ref[:, cols] = (
            context_ref[:, cols] + own_weight_ref[:, cols] * value[:, at : at + HEAD_SIZE]
        ).astype(jnp.bfloat16)
    put_attended = pltpu.make_async_copy(attended_ref, attended_hbm, small_sem.at[1])
    put_attended.start()
    for store in stores:
        store.wait()
    put_fresh.wait()
    put_attended.wait()


def merge(per, start, pick, features, served, slabs, crossed, last):
    left = 3
    count = slabs.shape[0] + crossed.shape[0] + last.shape[0]
    rank = pick.shape[0]
    depth, cols = served.shape
    width = depth // start.shape[1]
    return pl.pallas_call(
        functools.partial(merge_kernel, per, left),
        out_shape=(
            jax.ShapeDtypeStruct((depth, cols), jnp.bfloat16),
            jax.ShapeDtypeStruct((features.shape[0], cols), jnp.float32),
            jax.ShapeDtypeStruct((rank, cols), jnp.bfloat16),
            jax.ShapeDtypeStruct((left, width, cols), jnp.bfloat16),
        ),
        in_specs=[VMEM] * 7,
        out_specs=(HBM, VMEM, VMEM, VMEM),
        scratch_shapes=[
            pltpu.VMEM((count - left, width, cols), jnp.bfloat16),
            pltpu.SemaphoreType.DMA((count - left,)),
        ],
        compiler_params=pltpu.CompilerParams(vmem_limit_bytes=12 * 2**20),
        cost_estimate=pl.CostEstimate(
            flops=2 * count * width * cols * rank,
            bytes_accessed=4 * count * width * cols,
            transcendentals=0,
        ),
        name="merge_blocks",
    )(start, pick, features, served, slabs, crossed, last)


def finish(start, up, features, served, left, last, merged, total, context, own_weight):
    count = last.shape[0]
    depth, cols = served.shape
    width = depth // start.shape[1]
    smalls = [total.shape, context.shape]
    return pl.pallas_call(
        final_kernel,
        out_shape=[
            jax.ShapeDtypeStruct(shape, jnp.bfloat16) for shape in [(depth, cols), *smalls]
        ],
        in_specs=[VMEM] * 6 + [HBM] + [VMEM] * 3,
        out_specs=[HBM] * 3,
        input_output_aliases={6: 0},
        scratch_shapes=[
            pltpu.VMEM((count, width, cols), jnp.bfloat16),
            pltpu.SemaphoreType.DMA((count + left.shape[0],)),
        ]
        + [pltpu.VMEM(shape, jnp.bfloat16) for shape in smalls]
        + [pltpu.SemaphoreType.DMA((2,))],
        compiler_params=pltpu.CompilerParams(vmem_limit_bytes=12 * 2**20),
        cost_estimate=pl.CostEstimate(
            flops=2 * count * width * cols * up.shape[0],
            bytes_accessed=4 * count * width * cols,
            transcendentals=0,
        ),
        name="finish_rows",
    )(start, up, features, served, left, last, merged, total, context, own_weight)


def panels(x):
    return [x[:, i : i + PANEL] for i in range(0, x.shape[1], PANEL)]


def body(
    hidden_in,
    queries,
    stored_keys,
    stored_values,
    fresh_token_key,
    lengths,
    served_value_weight,
    adapter_in,
    adapter_out,
    owner_rank,
):
    n = lax.axis_size("replica")
    replica = lax.axis_index("replica")
    core = lax.axis_index("tensor")
    swap = [(0, 1), (1, 0)]
    full = adapter_in.shape[1]
    width = full // 2
    rows = queries.shape[0]
    per, cols = adapter_out.shape
    rank = n * per

    bits = [n >> i for i in range(1, n.bit_length())]
    ways = [bits, bits[:-2] + bits[:-3:-1]]

    def exchange(x, step):
        pairs = [(2 * i + c, 2 * (i ^ ways[c][step]) + c) for i in range(n) for c in range(2)]
        return lax.ppermute(x, ("replica", "tensor"), pairs)

    below = jnp.concatenate(panels(adapter_out), axis=0)
    below = jnp.pad(below, ((0, -below.shape[0] % 8), (0, 0)))
    block = lax.dynamic_slice_in_dim(adapter_in, core * width, width, axis=1)
    block, below = lax.optimization_barrier((block, below))
    slabs = jnp.concatenate([*panels(block), below], axis=0)[None]

    given = in_hbm(lengths, queries, fresh_token_key, stored_keys, stored_values)
    *early, first, second, third = range(len(bits))
    for step in early:
        slabs = jnp.concatenate([slabs, exchange(slabs, step)], axis=0)

    cuts = [0, rows // 2, rows - rows // 4, rows]
    first_rows, second_rows, third_rows = (range(*cut) for cut in zip(cuts, cuts[1:]))
    hid_other = lax.ppermute(hidden_in, "tensor", swap)
    came = exchange(slabs, first)
    part = attend(first_rows, given, after=[slabs])
    part, ahead = lax.optimization_barrier((part, slabs))
    ahead = exchange(ahead, second)
    came, part = lax.optimization_barrier((came, part))
    parts = [part]
    slabs = jnp.concatenate([slabs, came, ahead], axis=0)
    came = exchange(came, second)
    images = exchange(slabs, third)
    *part, served = attend(second_rows, given, *in_hbm(served_value_weight), [slabs])
    came, part, hid_other, owner_rank = lax.optimization_barrier(
        (came, part, hid_other, owner_rank)
    )
    parts.append(part)
    last = exchange(came, third)
    slabs = jnp.concatenate([slabs, came], axis=0)
    parts.append(attend(third_rows, given, after=[images]))
    features = jnp.concatenate([hidden_in, hid_other], axis=1)
    features = jnp.where(core == 0, features, jnp.concatenate([hid_other, hidden_in], axis=1))

    slab = jnp.arange(n, dtype=jnp.int32)
    sources = []
    for way in ways:
        source = replica
        for step, bit in enumerate(way):
            source = source ^ (((slab >> step) & 1) * bit)
        sources.append(source)
    mine = jnp.where(core == 0, sources[0], sources[1])
    theirs = jnp.where(core == 0, sources[1], sources[0])
    source = jnp.concatenate([mine, theirs])
    half = jnp.concatenate([jnp.full((n,), core), jnp.full((n,), 1 - core)])
    place = jnp.sum(jnp.where(owner_rank[None, :] == source[:, None], slab[None, :], 0), axis=1)
    start = (place * full + half * width).astype(jnp.int32)[None]

    row = jnp.arange(rank, dtype=jnp.int32)
    row_source = replica
    for step in range(len(bits)):
        bit = jnp.where(core == 0, ways[0][step], ways[1][step])
        row_source = row_source ^ (((row // per >> step) & 1) * bit)
    pick = jnp.where(
        row[:, None] == (row_source * per + row % per)[None, :], ADAPTER_SCALE, 0.0
    ).astype(jnp.bfloat16)

    context, own_weight = (
        jnp.concatenate(pair, axis=0).reshape(queries.shape) for pair in zip(*parts)
    )
    crossed, start = lax.optimization_barrier((slabs, start))
    crossed = lax.ppermute(crossed, "tensor", swap)
    last, start, pick, context, own_weight, features, crossed = lax.optimization_barrier(
        (last, start, pick, context, own_weight, features, crossed)
    )
    last = jnp.concatenate([images, last], axis=0)
    last_crossed = lax.ppermute(last, "tensor", swap)
    merged, total, up, left = merge(per, start, pick, features, served, slabs, crossed, last)
    return tuple(
        finish(
            start, up, features, served, left, last_crossed, merged, total, context, own_weight
        )
    )


def solution(mesh):
    in_specs = (
        P(("groups", "replica"), "tensor"),
        P(("groups", "replica"), "tensor"),
        P(("groups", "replica"), None, "tensor"),
        P(("groups", "replica"), None, "tensor"),
        P(("groups", "replica"), "tensor"),
        P(("groups", "replica")),
        P(None, "tensor"),
        P("groups", "replica"),
        P(("groups", "replica"), "tensor"),
        P("groups"),
    )
    out_specs = (
        P("groups", "tensor"),
        P(("groups", "replica"), "tensor"),
        P(("groups", "replica"), "tensor"),
    )
    return jax.shard_map(body, mesh=mesh, in_specs=in_specs, out_specs=out_specs, check_vma=False)
```

```python
import functools

import jax
import jax.numpy as jnp
from jax import lax
from jax.experimental import pallas as pl
from jax.experimental.pallas import tpu as pltpu
from jax.sharding import PartitionSpec as P

HEAD_SIZE = 128
ADAPTER_SCALE = 2.0
PANEL = 128

SMEM = pl.BlockSpec(memory_space=pltpu.SMEM)
VMEM = pl.BlockSpec(memory_space=pltpu.VMEM)
HBM = pl.BlockSpec(memory_space=pltpu.HBM)


def in_hbm(*arrays):
    return [pltpu.with_memory_space_constraint(x, pltpu.HBM) for x in arrays]


def attend_kernel(rows, fetch, lengths_hbm, q_hbm, own_k_hbm, k_hbm, v_hbm, *rest):
    rest = list(rest)
    if fetch:
        served_hbm, served_ref, served_sem = rest.pop(0), rest.pop(-10), rest.pop(-1)
    context_ref, own_weight_ref, lengths, q_ref, own_k_ref, k_buf, v_buf, small_sem, k_sem, v_sem = (
        rest[-10:]
    )
    smalls = [
        pltpu.make_async_copy(source, into, small_sem.at[i])
        for i, (source, into) in enumerate(
            [(lengths_hbm, lengths), (q_hbm, q_ref), (own_k_hbm, own_k_ref)]
        )
    ]
    for copy in smalls:
        copy.start()

    def copies(i, row):
        return (
            pltpu.make_async_copy(k_hbm.at[row], k_buf.at[i], k_sem.at[i]),
            pltpu.make_async_copy(v_hbm.at[row], v_buf.at[i], v_sem.at[i]),
        )

    for i, row in enumerate(rows):
        for copy in copies(i, row):
            copy.start()
    if fetch:
        get_served = pltpu.make_async_copy(served_hbm, served_ref, served_sem)
        get_served.start()
    for copy in smalls:
        copy.wait()
    queries = q_ref[...].astype(jnp.float32)
    own_keys = own_k_ref[...].astype(jnp.float32)
    heads = queries.shape[1] // HEAD_SIZE
    cache_len, width = k_buf.shape[1:]
    local_heads = width // HEAD_SIZE
    group = heads // local_heads
    scaling = 1.0 / HEAD_SIZE**0.5
    head_of = lax.broadcasted_iota(jnp.int32, (heads, HEAD_SIZE), 0) // group
    position = lax.broadcasted_iota(jnp.int32, (heads, cache_len), 1)
    for i, row in enumerate(rows):
        q = jnp.concatenate(
            [
                queries[row : row + 1, h * HEAD_SIZE : (h + 1) * HEAD_SIZE]
                for h in range(heads)
            ],
            axis=0,
        )
        spread = jnp.concatenate(
            [jnp.where(head_of == h, q, 0.0) for h in range(local_heads)], axis=1
        )
        own = jnp.sum(spread * own_keys[row : row + 1], axis=1, keepdims=True) * scaling
        get_keys, get_values = copies(i, row)
        get_keys.wait()
        scores = (
            lax.dot_general(
                spread.astype(jnp.bfloat16), k_buf[i], (((1,), (1,)), ((), ())),
                preferred_element_type=jnp.float32,
            )
            * scaling
        )
        valid = position < lengths[row]
        masked = jnp.where(valid, scores, -1e30)
        largest = jnp.maximum(jnp.max(masked, axis=1, keepdims=True), own)
        cached_exp = jnp.where(valid, jnp.exp(masked - largest), 0.0)
        own_exp = jnp.exp(own - largest)
        normaliser = jnp.sum(cached_exp, axis=1, keepdims=True) + own_exp
        weights = (cached_exp / normaliser).astype(jnp.bfloat16)
        weight_own = (own_exp / normaliser).astype(jnp.bfloat16).astype(jnp.float32)
        get_values.wait()
        wide = jnp.dot(weights, v_buf[i], preferred_element_type=jnp.float32)
        context = wide[:, :HEAD_SIZE]
        for h in range(1, local_heads):
            context = jnp.where(
                head_of == h, wide[:, h * HEAD_SIZE : (h + 1) * HEAD_SIZE], context
            )
        context_ref[i] = context
        own_weight_ref[i] = jnp.broadcast_to(weight_own, (heads, HEAD_SIZE))
    if fetch:
        get_served.wait()


def attend(rows, given, served=None, after=()):
    lengths, queries, own_key, stored_keys, stored_values = given
    fetch = served is not None
    cache_len, width = stored_keys.shape[1:]
    heads = queries.shape[1] // HEAD_SIZE
    count = len(rows)
    out_shape = [jax.ShapeDtypeStruct((count, heads, HEAD_SIZE), jnp.float32)] * 2
    if fetch:
        out_shape += [jax.ShapeDtypeStruct(served.shape, served.dtype)]
    return pl.pallas_call(
        functools.partial(attend_kernel, rows, fetch),
        out_shape=out_shape,
        in_specs=[HBM] * (5 + fetch) + [pl.BlockSpec(memory_space=pl.ANY)] * len(after),
        out_specs=[VMEM] * len(out_shape),
        scratch_shapes=[
            pltpu.SMEM(lengths.shape, jnp.int32),
            pltpu.VMEM(queries.shape, jnp.bfloat16),
            pltpu.VMEM(own_key.shape, jnp.bfloat16),
            pltpu.VMEM((count, cache_len, width), jnp.bfloat16),
            pltpu.VMEM((count, cache_len, width), jnp.bfloat16),
            pltpu.SemaphoreType.DMA((3,)),
            pltpu.SemaphoreType.DMA((count,)),
            pltpu.SemaphoreType.DMA((count,)),
        ]
        + [pltpu.SemaphoreType.DMA] * fetch,
        compiler_params=pltpu.CompilerParams(vmem_limit_bytes=12 * 2**20),
        cost_estimate=pl.CostEstimate(
            flops=4 * count * heads * cache_len * width,
            bytes_accessed=4 * count * cache_len * width,
            transcendentals=count * heads * cache_len,
        ),
        name="attend_cache",
    )(*given, *([served] if fetch else []), *after)


class Merge:
    def __init__(self, start_ref, merged, out_sem, width):
        self.start, self.merged, self.out_sem, self.width = start_ref[...], merged, out_sem, width
        self.entry = lax.broadcasted_iota(jnp.int32, self.start.shape, 1)

    def rows_of(self, entry):
        first = jnp.sum(jnp.where(self.entry == entry, self.start, 0))
        return pl.ds(pl.multiple_of(first, self.width), self.width)

    def store(self, source, rows, at):
        return pltpu.make_async_copy(source, self.merged.at[rows], self.out_sem.at[at])

    def rows(self, slab, up, served_ref, features_ref, rows, total):
        rank = up.shape[0]
        block = jnp.concatenate(
            [slab[i * rank : (i + 1) * rank] for i in range(self.width // PANEL)], axis=1
        )
        update = lax.dot_general(
            block, up, (((0,), (0,)), ((), ())), preferred_element_type=jnp.float32
        )
        fold = (served_ref[rows, :].astype(jnp.float32) + update).astype(jnp.bfloat16)
        part = jnp.dot(features_ref[:, rows], fold, preferred_element_type=jnp.float32)
        return fold, total + part


def merge_kernel(per, left, start_ref, pick_ref, features_ref, served_ref, slabs_ref, crossed_ref,
                 last_ref, merged, total_ref, up_ref, left_ref, m_buf, out_sem):
    width = m_buf.shape[1]
    rank, cols = up_ref.shape
    merge = Merge(start_ref, merged, out_sem, width)
    ups = []
    for ref in (slabs_ref, last_ref):
        for k in range(ref.shape[0]):
            below = ref[k, rank * (width // PANEL) :].astype(jnp.float32)
            ups.append(
                jnp.concatenate(
                    [below[i * per : (i + 1) * per] for i in range(cols // PANEL)], axis=1
                )
            )
    ups = jnp.concatenate(ups, axis=0).astype(jnp.bfloat16)
    up = jnp.dot(pick_ref[...], ups, preferred_element_type=jnp.float32).astype(jnp.bfloat16)
    up_ref[...] = up
    total = jnp.zeros(total_ref.shape, jnp.float32)
    refs = (slabs_ref, last_ref, crossed_ref)
    slabs = [ref.at[k] for ref in refs for k in range(ref.shape[0])]
    keep = len(slabs) - left
    stores = []
    for i, slab in enumerate(slabs):
        rows = merge.rows_of(i)
        fold, total = merge.rows(slab, up, served_ref, features_ref, rows, total)
        if i < keep:
            m_buf[i] = fold
            stores.append(merge.store(m_buf.at[i], rows, i))
            stores[-1].start()
        else:
            left_ref[i - keep] = fold
    total_ref[...] = total
    for store in stores:
        store.wait()


def final_kernel(start_ref, up_ref, features_ref, served_ref, left_ref, last_ref, merged_in,
                 total_ref, context_ref, own_weight_ref, merged, fresh_hbm, attended_hbm, m_buf,
                 out_sem, fresh_ref, attended_ref, small_sem):
    del merged_in
    count, width = last_ref.shape[0], m_buf.shape[1]
    left = left_ref.shape[0]
    merge = Merge(start_ref, merged, out_sem, width)
    first = start_ref.shape[1] - count
    total = total_ref[...]
    stores = [
        merge.store(left_ref.at[k], merge.rows_of(first - left + k), count + k)
        for k in range(left)
    ]
    for store in stores:
        store.start()
    for i in range(count):
        rows = merge.rows_of(first + i)
        fold, total = merge.rows(last_ref.at[i], up_ref[...], served_ref, features_ref, rows, total)
        m_buf[i] = fold
        stores.append(merge.store(m_buf.at[i], rows, i))
        stores[-1].start()
    fresh = total.astype(jnp.bfloat16)
    fresh_ref[...] = fresh
    put_fresh = pltpu.make_async_copy(fresh_ref, fresh_hbm, small_sem.at[0])
    put_fresh.start()
    value = fresh.astype(jnp.float32)
    heads = attended_ref.shape[1] // HEAD_SIZE
    group = heads // (fresh_ref.shape[1] // HEAD_SIZE)
    for h in range(heads):
        cols = slice(h * HEAD_SIZE, (h + 1) * HEAD_SIZE)
        at = (h // group) * HEAD_SIZE
        attended_ref[:, cols] = (
            context_ref[:, cols] + own_weight_ref[:, cols] * value[:, at : at + HEAD_SIZE]
        ).astype(jnp.bfloat16)
    put_attended = pltpu.make_async_copy(attended_ref, attended_hbm, small_sem.at[1])
    put_attended.start()
    for store in stores:
        store.wait()
    put_fresh.wait()
    put_attended.wait()


def merge(per, start, pick, features, served, slabs, crossed, last):
    left = 3
    count = slabs.shape[0] + crossed.shape[0] + last.shape[0]
    rank = pick.shape[0]
    depth, cols = served.shape
    width = depth // start.shape[1]
    return pl.pallas_call(
        functools.partial(merge_kernel, per, left),
        out_shape=(
            jax.ShapeDtypeStruct((depth, cols), jnp.bfloat16),
            jax.ShapeDtypeStruct((features.shape[0], cols), jnp.float32),
            jax.ShapeDtypeStruct((rank, cols), jnp.bfloat16),
            jax.ShapeDtypeStruct((left, width, cols), jnp.bfloat16),
        ),
        in_specs=[VMEM] * 7,
        out_specs=(HBM, VMEM, VMEM, VMEM),
        scratch_shapes=[
            pltpu.VMEM((count - left, width, cols), jnp.bfloat16),
            pltpu.SemaphoreType.DMA((count - left,)),
        ],
        compiler_params=pltpu.CompilerParams(vmem_limit_bytes=12 * 2**20),
        cost_estimate=pl.CostEstimate(
            flops=2 * count * width * cols * rank,
            bytes_accessed=4 * count * width * cols,
            transcendentals=0,
        ),
        name="merge_blocks",
    )(start, pick, features, served, slabs, crossed, last)


def finish(start, up, features, served, left, last, merged, total, context, own_weight):
    count = last.shape[0]
    depth, cols = served.shape
    width = depth // start.shape[1]
    smalls = [total.shape, context.shape]
    return pl.pallas_call(
        final_kernel,
        out_shape=[
            jax.ShapeDtypeStruct(shape, jnp.bfloat16) for shape in [(depth, cols), *smalls]
        ],
        in_specs=[VMEM] * 6 + [HBM] + [VMEM] * 3,
        out_specs=[HBM] * 3,
        input_output_aliases={6: 0},
        scratch_shapes=[
            pltpu.VMEM((count, width, cols), jnp.bfloat16),
            pltpu.SemaphoreType.DMA((count + left.shape[0],)),
        ]
        + [pltpu.VMEM(shape, jnp.bfloat16) for shape in smalls]
        + [pltpu.SemaphoreType.DMA((2,))],
        compiler_params=pltpu.CompilerParams(vmem_limit_bytes=12 * 2**20),
        cost_estimate=pl.CostEstimate(
            flops=2 * count * width * cols * up.shape[0],
            bytes_accessed=4 * count * width * cols,
            transcendentals=0,
        ),
        name="finish_rows",
    )(start, up, features, served, left, last, merged, total, context, own_weight)


def panels(x):
    return [x[:, i : i + PANEL] for i in range(0, x.shape[1], PANEL)]


def body(
    hidden_in,
    queries,
    stored_keys,
    stored_values,
    fresh_token_key,
    lengths,
    served_value_weight,
    adapter_in,
    adapter_out,
    owner_rank,
):
    n = lax.axis_size("replica")
    replica = lax.axis_index("replica")
    core = lax.axis_index("tensor")
    swap = [(0, 1), (1, 0)]
    full = adapter_in.shape[1]
    width = full // 2
    rows = queries.shape[0]
    per, cols = adapter_out.shape
    rank = n * per

    bits = [n >> i for i in range(1, n.bit_length())]
    ways = [bits, bits[:-2] + bits[:-3:-1]]

    def exchange(x, step):
        pairs = [(2 * i + c, 2 * (i ^ ways[c][step]) + c) for i in range(n) for c in range(2)]
        return lax.ppermute(x, ("replica", "tensor"), pairs)

    below = jnp.concatenate(panels(adapter_out), axis=0)
    below = jnp.pad(below, ((0, -below.shape[0] % 8), (0, 0)))
    block = lax.dynamic_slice_in_dim(adapter_in, core * width, width, axis=1)
    block, below = lax.optimization_barrier((block, below))
    slabs = jnp.concatenate([*panels(block), below], axis=0)[None]

    given = in_hbm(lengths, queries, fresh_token_key, stored_keys, stored_values)
    *early, first, second, third = range(len(bits))
    for step in early:
        slabs = jnp.concatenate([slabs, exchange(slabs, step)], axis=0)

    cuts = [0, rows // 2, rows - rows // 4, rows]
    first_rows, second_rows, third_rows = (range(*cut) for cut in zip(cuts, cuts[1:]))
    hid_other = lax.ppermute(hidden_in, "tensor", swap)
    came = exchange(slabs, first)
    part = attend(first_rows, given, after=[slabs])
    came, part = lax.optimization_barrier((came, part))
    parts = [part]
    slabs = jnp.concatenate([slabs, came], axis=0)
    came = exchange(slabs, second)
    images = exchange(slabs, third)
    *part, served = attend(second_rows, given, *in_hbm(served_value_weight), [slabs])
    came, part, hid_other, owner_rank = lax.optimization_barrier(
        (came, part, hid_other, owner_rank)
    )
    parts.append(part)
    last = exchange(came, third)
    slabs = jnp.concatenate([slabs, came, images], axis=0)
    parts.append(attend(third_rows, given, after=[images]))
    features = jnp.concatenate([hidden_in, hid_other], axis=1)
    features = jnp.where(core == 0, features, jnp.concatenate([hid_other, hidden_in], axis=1))

    slab = jnp.arange(n, dtype=jnp.int32)
    sources = []
    for way in ways:
        source = replica
        for step, bit in enumerate(way):
            source = source ^ (((slab >> step) & 1) * bit)
        sources.append(source)
    mine = jnp.where(core == 0, sources[0], sources[1])
    theirs = jnp.where(core == 0, sources[1], sources[0])
    source = jnp.concatenate([mine, theirs])
    half = jnp.concatenate([jnp.full((n,), core), jnp.full((n,), 1 - core)])
    place = jnp.sum(jnp.where(owner_rank[None, :] == source[:, None], slab[None, :], 0), axis=1)
    start = (place * full + half * width).astype(jnp.int32)[None]

    row = jnp.arange(rank, dtype=jnp.int32)
    row_source = replica
    for step in range(len(bits)):
        bit = jnp.where(core == 0, ways[0][step], ways[1][step])
        row_source = row_source ^ (((row // per >> step) & 1) * bit)
    pick = jnp.where(
        row[:, None] == (row_source * per + row % per)[None, :], ADAPTER_SCALE, 0.0
    ).astype(jnp.bfloat16)

    context, own_weight = (
        jnp.concatenate(pair, axis=0).reshape(queries.shape) for pair in zip(*parts)
    )
    crossed, start = lax.optimization_barrier((slabs, start))
    crossed = lax.ppermute(crossed, "tensor", swap)
    last, start, pick, context, own_weight, features, crossed = lax.optimization_barrier(
        (last, start, pick, context, own_weight, features, crossed)
    )
    last_crossed = lax.ppermute(last, "tensor", swap)
    merged, total, up, left = merge(per, start, pick, features, served, slabs, crossed, last)
    return tuple(
        finish(
            start, up, features, served, left, last_crossed, merged, total, context, own_weight
        )
    )


def solution(mesh):
    in_specs = (
        P(("groups", "replica"), "tensor"),
        P(("groups", "replica"), "tensor"),
        P(("groups", "replica"), None, "tensor"),
        P(("groups", "replica"), None, "tensor"),
        P(("groups", "replica"), "tensor"),
        P(("groups", "replica")),
        P(None, "tensor"),
        P("groups", "replica"),
        P(("groups", "replica"), "tensor"),
        P("groups"),
    )
    out_specs = (
        P("groups", "tensor"),
        P(("groups", "replica"), "tensor"),
        P(("groups", "replica"), "tensor"),
    )
    return jax.shard_map(body, mesh=mesh, in_specs=in_specs, out_specs=out_specs, check_vma=False)
```

```python
import functools

import jax
import jax.numpy as jnp
from jax import lax
from jax.experimental import pallas as pl
from jax.experimental.pallas import tpu as pltpu
from jax.sharding import PartitionSpec as P

HEAD_SIZE = 128
ADAPTER_SCALE = 2.0
PANEL = 128

SMEM = pl.BlockSpec(memory_space=pltpu.SMEM)
VMEM = pl.BlockSpec(memory_space=pltpu.VMEM)
HBM = pl.BlockSpec(memory_space=pltpu.HBM)


def in_hbm(*arrays):
    return [pltpu.with_memory_space_constraint(x, pltpu.HBM) for x in arrays]


def attend_kernel(rows, fetch, lengths_hbm, q_hbm, own_k_hbm, k_hbm, v_hbm, *rest):
    rest = list(rest)
    if fetch:
        served_hbm, served_ref, served_sem = rest.pop(0), rest.pop(-10), rest.pop(-1)
    context_ref, own_weight_ref, lengths, q_ref, own_k_ref, k_buf, v_buf, small_sem, k_sem, v_sem = (
        rest[-10:]
    )
    smalls = [
        pltpu.make_async_copy(source, into, small_sem.at[i])
        for i, (source, into) in enumerate(
            [(lengths_hbm, lengths), (q_hbm, q_ref), (own_k_hbm, own_k_ref)]
        )
    ]
    for copy in smalls:
        copy.start()

    def copies(i, row):
        return (
            pltpu.make_async_copy(k_hbm.at[row], k_buf.at[i], k_sem.at[i]),
            pltpu.make_async_copy(v_hbm.at[row], v_buf.at[i], v_sem.at[i]),
        )

    for i, row in enumerate(rows):
        for copy in copies(i, row):
            copy.start()
    if fetch:
        get_served = pltpu.make_async_copy(served_hbm, served_ref, served_sem)
        get_served.start()
    for copy in smalls:
        copy.wait()
    queries = q_ref[...].astype(jnp.float32)
    own_keys = own_k_ref[...].astype(jnp.float32)
    heads = queries.shape[1] // HEAD_SIZE
    cache_len, width = k_buf.shape[1:]
    local_heads = width // HEAD_SIZE
    group = heads // local_heads
    scaling = 1.0 / HEAD_SIZE**0.5
    head_of = lax.broadcasted_iota(jnp.int32, (heads, HEAD_SIZE), 0) // group
    position = lax.broadcasted_iota(jnp.int32, (heads, cache_len), 1)
    for i, row in enumerate(rows):
        q = jnp.concatenate(
            [
                queries[row : row + 1, h * HEAD_SIZE : (h + 1) * HEAD_SIZE]
                for h in range(heads)
            ],
            axis=0,
        )
        spread = jnp.concatenate(
            [jnp.where(head_of == h, q, 0.0) for h in range(local_heads)], axis=1
        )
        own = jnp.sum(spread * own_keys[row : row + 1], axis=1, keepdims=True) * scaling
        get_keys, get_values = copies(i, row)
        get_keys.wait()
        scores = (
            lax.dot_general(
                spread.astype(jnp.bfloat16), k_buf[i], (((1,), (1,)), ((), ())),
                preferred_element_type=jnp.float32,
            )
            * scaling
        )
        valid = position < lengths[row]
        masked = jnp.where(valid, scores, -1e30)
        largest = jnp.maximum(jnp.max(masked, axis=1, keepdims=True), own)
        cached_exp = jnp.where(valid, jnp.exp(masked - largest), 0.0)
        own_exp = jnp.exp(own - largest)
        normaliser = jnp.sum(cached_exp, axis=1, keepdims=True) + own_exp
        weights = (cached_exp / normaliser).astype(jnp.bfloat16)
        weight_own = (own_exp / normaliser).astype(jnp.bfloat16).astype(jnp.float32)
        get_values.wait()
        wide = jnp.dot(weights, v_buf[i], preferred_element_type=jnp.float32)
        context = wide[:, :HEAD_SIZE]
        for h in range(1, local_heads):
            context = jnp.where(
                head_of == h, wide[:, h * HEAD_SIZE : (h + 1) * HEAD_SIZE], context
            )
        context_ref[i] = context
        own_weight_ref[i] = jnp.broadcast_to(weight_own, (heads, HEAD_SIZE))
    if fetch:
        get_served.wait()


def attend(rows, given, served=None, after=()):
    lengths, queries, own_key, stored_keys, stored_values = given
    fetch = served is not None
    cache_len, width = stored_keys.shape[1:]
    heads = queries.shape[1] // HEAD_SIZE
    count = len(rows)
    out_shape = [jax.ShapeDtypeStruct((count, heads, HEAD_SIZE), jnp.float32)] * 2
    if fetch:
        out_shape += [jax.ShapeDtypeStruct(served.shape, served.dtype)]
    return pl.pallas_call(
        functools.partial(attend_kernel, rows, fetch),
        out_shape=out_shape,
        in_specs=[HBM] * (5 + fetch) + [pl.BlockSpec(memory_space=pl.ANY)] * len(after),
        out_specs=[VMEM] * len(out_shape),
        scratch_shapes=[
            pltpu.SMEM(lengths.shape, jnp.int32),
            pltpu.VMEM(queries.shape, jnp.bfloat16),
            pltpu.VMEM(own_key.shape, jnp.bfloat16),
            pltpu.VMEM((count, cache_len, width), jnp.bfloat16),
            pltpu.VMEM((count, cache_len, width), jnp.bfloat16),
            pltpu.SemaphoreType.DMA((3,)),
            pltpu.SemaphoreType.DMA((count,)),
            pltpu.SemaphoreType.DMA((count,)),
        ]
        + [pltpu.SemaphoreType.DMA] * fetch,
        compiler_params=pltpu.CompilerParams(vmem_limit_bytes=12 * 2**20),
        cost_estimate=pl.CostEstimate(
            flops=4 * count * heads * cache_len * width,
            bytes_accessed=4 * count * cache_len * width,
            transcendentals=count * heads * cache_len,
        ),
        name="attend_cache",
    )(*given, *([served] if fetch else []), *after)


class Merge:
    def __init__(self, start_ref, merged, out_sem, width):
        self.start, self.merged, self.out_sem, self.width = start_ref[...], merged, out_sem, width
        self.entry = lax.broadcasted_iota(jnp.int32, self.start.shape, 1)

    def rows_of(self, entry):
        first = jnp.sum(jnp.where(self.entry == entry, self.start, 0))
        return pl.ds(pl.multiple_of(first, self.width), self.width)

    def store(self, source, rows, at):
        return pltpu.make_async_copy(source, self.merged.at[rows], self.out_sem.at[at])

    def rows(self, slab, up, served_ref, features_ref, rows, total):
        rank = up.shape[0]
        block = jnp.concatenate(
            [slab[i * rank : (i + 1) * rank] for i in range(self.width // PANEL)], axis=1
        )
        update = lax.dot_general(
            block, up, (((0,), (0,)), ((), ())), preferred_element_type=jnp.float32
        )
        fold = (served_ref[rows, :].astype(jnp.float32) + update).astype(jnp.bfloat16)
        part = jnp.dot(features_ref[:, rows], fold, preferred_element_type=jnp.float32)
        return fold, total + part


def merge_kernel(per, left, start_ref, pick_ref, features_ref, served_ref, slabs_ref, crossed_ref,
                 last_ref, merged, total_ref, up_ref, left_ref, m_buf, out_sem):
    width = m_buf.shape[1]
    rank, cols = up_ref.shape
    merge = Merge(start_ref, merged, out_sem, width)
    ups = []
    for ref in (slabs_ref, last_ref):
        for k in range(ref.shape[0]):
            below = ref[k, rank * (width // PANEL) :].astype(jnp.float32)
            ups.append(
                jnp.concatenate(
                    [below[i * per : (i + 1) * per] for i in range(cols // PANEL)], axis=1
                )
            )
    ups = jnp.concatenate(ups, axis=0).astype(jnp.bfloat16)
    up = jnp.dot(pick_ref[...], ups, preferred_element_type=jnp.float32).astype(jnp.bfloat16)
    up_ref[...] = up
    total = jnp.zeros(total_ref.shape, jnp.float32)
    refs = (slabs_ref, last_ref, crossed_ref)
    slabs = [ref.at[k] for ref in refs for k in range(ref.shape[0])]
    keep = len(slabs) - left
    stores = []
    for i, slab in enumerate(slabs):
        rows = merge.rows_of(i)
        fold, total = merge.rows(slab, up, served_ref, features_ref, rows, total)
        if i < keep:
            m_buf[i] = fold
            stores.append(merge.store(m_buf.at[i], rows, i))
            stores[-1].start()
        else:
            left_ref[i - keep] = fold
    total_ref[...] = total
    for store in stores:
        store.wait()


def final_kernel(start_ref, up_ref, features_ref, served_ref, left_ref, last_ref, merged_in,
                 total_ref, context_ref, own_weight_ref, merged, fresh_hbm, attended_hbm, m_buf,
                 out_sem, fresh_ref, attended_ref, small_sem):
    del merged_in
    count, width = last_ref.shape[0], m_buf.shape[1]
    left = left_ref.shape[0]
    merge = Merge(start_ref, merged, out_sem, width)
    first = start_ref.shape[1] - count
    total = total_ref[...]
    stores = [
        merge.store(left_ref.at[k], merge.rows_of(first - left + k), count + k)
        for k in range(left)
    ]
    for store in stores:
        store.start()
    for i in range(count):
        rows = merge.rows_of(first + i)
        fold, total = merge.rows(last_ref.at[i], up_ref[...], served_ref, features_ref, rows, total)
        m_buf[i] = fold
        stores.append(merge.store(m_buf.at[i], rows, i))
        stores[-1].start()
    fresh = total.astype(jnp.bfloat16)
    fresh_ref[...] = fresh
    put_fresh = pltpu.make_async_copy(fresh_ref, fresh_hbm, small_sem.at[0])
    put_fresh.start()
    value = fresh.astype(jnp.float32)
    heads = attended_ref.shape[1] // HEAD_SIZE
    group = heads // (fresh_ref.shape[1] // HEAD_SIZE)
    for h in range(heads):
        cols = slice(h * HEAD_SIZE, (h + 1) * HEAD_SIZE)
        at = (h // group) * HEAD_SIZE
        attended_ref[:, cols] = (
            context_ref[:, cols] + own_weight_ref[:, cols] * value[:, at : at + HEAD_SIZE]
        ).astype(jnp.bfloat16)
    put_attended = pltpu.make_async_copy(attended_ref, attended_hbm, small_sem.at[1])
    put_attended.start()
    for store in stores:
        store.wait()
    put_fresh.wait()
    put_attended.wait()


def merge(per, start, pick, features, served, slabs, crossed, last):
    left = 3
    count = slabs.shape[0] + crossed.shape[0] + last.shape[0]
    rank = pick.shape[0]
    depth, cols = served.shape
    width = depth // start.shape[1]
    return pl.pallas_call(
        functools.partial(merge_kernel, per, left),
        out_shape=(
            jax.ShapeDtypeStruct((depth, cols), jnp.bfloat16),
            jax.ShapeDtypeStruct((features.shape[0], cols), jnp.float32),
            jax.ShapeDtypeStruct((rank, cols), jnp.bfloat16),
            jax.ShapeDtypeStruct((left, width, cols), jnp.bfloat16),
        ),
        in_specs=[VMEM] * 7,
        out_specs=(HBM, VMEM, VMEM, VMEM),
        scratch_shapes=[
            pltpu.VMEM((count - left, width, cols), jnp.bfloat16),
            pltpu.SemaphoreType.DMA((count - left,)),
        ],
        compiler_params=pltpu.CompilerParams(vmem_limit_bytes=12 * 2**20),
        cost_estimate=pl.CostEstimate(
            flops=2 * count * width * cols * rank,
            bytes_accessed=4 * count * width * cols,
            transcendentals=0,
        ),
        name="merge_blocks",
    )(start, pick, features, served, slabs, crossed, last)


def finish(start, up, features, served, left, last, merged, total, context, own_weight):
    count = last.shape[0]
    depth, cols = served.shape
    width = depth // start.shape[1]
    smalls = [total.shape, context.shape]
    return pl.pallas_call(
        final_kernel,
        out_shape=[
            jax.ShapeDtypeStruct(shape, jnp.bfloat16) for shape in [(depth, cols), *smalls]
        ],
        in_specs=[VMEM] * 6 + [HBM] + [VMEM] * 3,
        out_specs=[HBM] * 3,
        input_output_aliases={6: 0},
        scratch_shapes=[
            pltpu.VMEM((count, width, cols), jnp.bfloat16),
            pltpu.SemaphoreType.DMA((count + left.shape[0],)),
        ]
        + [pltpu.VMEM(shape, jnp.bfloat16) for shape in smalls]
        + [pltpu.SemaphoreType.DMA((2,))],
        compiler_params=pltpu.CompilerParams(vmem_limit_bytes=12 * 2**20),
        cost_estimate=pl.CostEstimate(
            flops=2 * count * width * cols * up.shape[0],
            bytes_accessed=4 * count * width * cols,
            transcendentals=0,
        ),
        name="finish_rows",
    )(start, up, features, served, left, last, merged, total, context, own_weight)


def panels(x):
    return [x[:, i : i + PANEL] for i in range(0, x.shape[1], PANEL)]


def body(
    hidden_in,
    queries,
    stored_keys,
    stored_values,
    fresh_token_key,
    lengths,
    served_value_weight,
    adapter_in,
    adapter_out,
    owner_rank,
):
    n = lax.axis_size("replica")
    replica = lax.axis_index("replica")
    core = lax.axis_index("tensor")
    swap = [(0, 1), (1, 0)]
    full = adapter_in.shape[1]
    width = full // 2
    rows = queries.shape[0]
    per, cols = adapter_out.shape
    rank = n * per

    bits = [n >> i for i in range(1, n.bit_length())]
    ways = [bits, bits[:-2] + bits[:-3:-1]]

    def exchange(x, *steps):
        pairs = [
            (2 * i + c, 2 * (i ^ sum(ways[c][step] for step in steps)) + c)
            for i in range(n)
            for c in range(2)
        ]
        return lax.ppermute(x, ("replica", "tensor"), pairs)

    below = jnp.concatenate(panels(adapter_out), axis=0)
    below = jnp.pad(below, ((0, -below.shape[0] % 8), (0, 0)))
    block = lax.dynamic_slice_in_dim(adapter_in, core * width, width, axis=1)
    block, below = lax.optimization_barrier((block, below))
    slabs = jnp.concatenate([*panels(block), below], axis=0)[None]

    given = in_hbm(lengths, queries, fresh_token_key, stored_keys, stored_values)
    *early, first, second, third = range(len(bits))
    for step in early:
        slabs = jnp.concatenate([slabs, exchange(slabs, step)], axis=0)

    split = rows - rows // 4
    hid_other = lax.ppermute(hidden_in, "tensor", swap)
    came = exchange(slabs, first)
    part = attend(range(split), given, after=[slabs])
    came, part = lax.optimization_barrier((came, part))
    parts = [part]
    slabs = jnp.concatenate([slabs, came], axis=0)
    last = [exchange(slabs, third), exchange(slabs, second, third)]
    came = exchange(slabs, second)
    *part, served = attend(range(split, rows), given, *in_hbm(served_value_weight), [slabs])
    came, part, hid_other, owner_rank = lax.optimization_barrier(
        (came, part, hid_other, owner_rank)
    )
    parts.append(part)
    slabs = jnp.concatenate([slabs, came], axis=0)
    features = jnp.concatenate([hidden_in, hid_other], axis=1)
    features = jnp.where(core == 0, features, jnp.concatenate([hid_other, hidden_in], axis=1))

    slab = jnp.arange(n, dtype=jnp.int32)
    sources = []
    for way in ways:
        source = replica
        for step, bit in enumerate(way):
            source = source ^ (((slab >> step) & 1) * bit)
        sources.append(source)
    mine = jnp.where(core == 0, sources[0], sources[1])
    theirs = jnp.where(core == 0, sources[1], sources[0])
    source = jnp.concatenate([mine, theirs])
    half = jnp.concatenate([jnp.full((n,), core), jnp.full((n,), 1 - core)])
    place = jnp.sum(jnp.where(owner_rank[None, :] == source[:, None], slab[None, :], 0), axis=1)
    start = (place * full + half * width).astype(jnp.int32)[None]

    row = jnp.arange(rank, dtype=jnp.int32)
    row_source = replica
    for step in range(len(bits)):
        bit = jnp.where(core == 0, ways[0][step], ways[1][step])
        row_source = row_source ^ (((row // per >> step) & 1) * bit)
    pick = jnp.where(
        row[:, None] == (row_source * per + row % per)[None, :], ADAPTER_SCALE, 0.0
    ).astype(jnp.bfloat16)

    context, own_weight = (
        jnp.concatenate(pair, axis=0).reshape(queries.shape) for pair in zip(*parts)
    )
    crossed, start = lax.optimization_barrier((slabs, start))
    crossed = lax.ppermute(crossed, "tensor", swap)
    last, start, pick, context, own_weight, features, crossed = lax.optimization_barrier(
        (last, start, pick, context, own_weight, features, crossed)
    )
    last = jnp.concatenate(last, axis=0)
    last_crossed = lax.ppermute(last, "tensor", swap)
    merged, total, up, left = merge(per, start, pick, features, served, slabs, crossed, last)
    return tuple(
        finish(
            start, up, features, served, left, last_crossed, merged, total, context, own_weight
        )
    )


def solution(mesh):
    in_specs = (
        P(("groups", "replica"), "tensor"),
        P(("groups", "replica"), "tensor"),
        P(("groups", "replica"), None, "tensor"),
        P(("groups", "replica"), None, "tensor"),
        P(("groups", "replica"), "tensor"),
        P(("groups", "replica")),
        P(None, "tensor"),
        P("groups", "replica"),
        P(("groups", "replica"), "tensor"),
        P("groups"),
    )
    out_specs = (
        P("groups", "tensor"),
        P(("groups", "replica"), "tensor"),
        P(("groups", "replica"), "tensor"),
    )
    return jax.shard_map(body, mesh=mesh, in_specs=in_specs, out_specs=out_specs, check_vma=False)
```

```python
import functools

import jax
import jax.numpy as jnp
from jax import lax
from jax.experimental import pallas as pl
from jax.experimental.pallas import tpu as pltpu
from jax.sharding import PartitionSpec as P

HEAD_SIZE = 128
ADAPTER_SCALE = 2.0
PANEL = 128

SMEM = pl.BlockSpec(memory_space=pltpu.SMEM)
VMEM = pl.BlockSpec(memory_space=pltpu.VMEM)
HBM = pl.BlockSpec(memory_space=pltpu.HBM)


def in_hbm(*arrays):
    return [pltpu.with_memory_space_constraint(x, pltpu.HBM) for x in arrays]


def attend_kernel(rows, lengths_hbm, q_hbm, own_k_hbm, k_hbm, v_hbm, *rest):
    context_ref, own_weight_ref, lengths, q_ref, own_k_ref, k_buf, v_buf, small_sem, k_sem, v_sem = (
        rest[-10:]
    )
    smalls = [
        pltpu.make_async_copy(source, into, small_sem.at[i])
        for i, (source, into) in enumerate(
            [(lengths_hbm, lengths), (q_hbm, q_ref), (own_k_hbm, own_k_ref)]
        )
    ]
    for copy in smalls:
        copy.start()

    def copies(i, row):
        return (
            pltpu.make_async_copy(k_hbm.at[row], k_buf.at[i], k_sem.at[i]),
            pltpu.make_async_copy(v_hbm.at[row], v_buf.at[i], v_sem.at[i]),
        )

    for i, row in enumerate(rows):
        for copy in copies(i, row):
            copy.start()
    for copy in smalls:
        copy.wait()
    queries = q_ref[...].astype(jnp.float32)
    own_keys = own_k_ref[...].astype(jnp.float32)
    heads = queries.shape[1] // HEAD_SIZE
    cache_len, width = k_buf.shape[1:]
    local_heads = width // HEAD_SIZE
    group = heads // local_heads
    scaling = 1.0 / HEAD_SIZE**0.5
    head_of = lax.broadcasted_iota(jnp.int32, (heads, HEAD_SIZE), 0) // group
    position = lax.broadcasted_iota(jnp.int32, (heads, cache_len), 1)
    for i, row in enumerate(rows):
        q = jnp.concatenate(
            [
                queries[row : row + 1, h * HEAD_SIZE : (h + 1) * HEAD_SIZE]
                for h in range(heads)
            ],
            axis=0,
        )
        spread = jnp.concatenate(
            [jnp.where(head_of == h, q, 0.0) for h in range(local_heads)], axis=1
        )
        own = jnp.sum(spread * own_keys[row : row + 1], axis=1, keepdims=True) * scaling
        get_keys, get_values = copies(i, row)
        get_keys.wait()
        scores = (
            lax.dot_general(
                spread.astype(jnp.bfloat16), k_buf[i], (((1,), (1,)), ((), ())),
                preferred_element_type=jnp.float32,
            )
            * scaling
        )
        valid = position < lengths[row]
        masked = jnp.where(valid, scores, -1e30)
        largest = jnp.maximum(jnp.max(masked, axis=1, keepdims=True), own)
        cached_exp = jnp.where(valid, jnp.exp(masked - largest), 0.0)
        own_exp = jnp.exp(own - largest)
        normaliser = jnp.sum(cached_exp, axis=1, keepdims=True) + own_exp
        weights = (cached_exp / normaliser).astype(jnp.bfloat16)
        weight_own = (own_exp / normaliser).astype(jnp.bfloat16).astype(jnp.float32)
        get_values.wait()
        wide = jnp.dot(weights, v_buf[i], preferred_element_type=jnp.float32)
        context = wide[:, :HEAD_SIZE]
        for h in range(1, local_heads):
            context = jnp.where(
                head_of == h, wide[:, h * HEAD_SIZE : (h + 1) * HEAD_SIZE], context
            )
        context_ref[i] = context
        own_weight_ref[i] = jnp.broadcast_to(weight_own, (heads, HEAD_SIZE))


def attend(rows, given, after):
    lengths, queries, own_key, stored_keys, stored_values = given
    cache_len, width = stored_keys.shape[1:]
    heads = queries.shape[1] // HEAD_SIZE
    count = len(rows)
    out_shape = [jax.ShapeDtypeStruct((count, heads, HEAD_SIZE), jnp.float32)] * 2
    return pl.pallas_call(
        functools.partial(attend_kernel, rows),
        out_shape=out_shape,
        in_specs=[HBM] * 5 + [pl.BlockSpec(memory_space=pl.ANY)] * len(after),
        out_specs=[VMEM] * len(out_shape),
        scratch_shapes=[
            pltpu.SMEM(lengths.shape, jnp.int32),
            pltpu.VMEM(queries.shape, jnp.bfloat16),
            pltpu.VMEM(own_key.shape, jnp.bfloat16),
            pltpu.VMEM((count, cache_len, width), jnp.bfloat16),
            pltpu.VMEM((count, cache_len, width), jnp.bfloat16),
            pltpu.SemaphoreType.DMA((3,)),
            pltpu.SemaphoreType.DMA((count,)),
            pltpu.SemaphoreType.DMA((count,)),
        ],
        compiler_params=pltpu.CompilerParams(vmem_limit_bytes=12 * 2**20),
        cost_estimate=pl.CostEstimate(
            flops=4 * count * heads * cache_len * width,
            bytes_accessed=4 * count * cache_len * width,
            transcendentals=count * heads * cache_len,
        ),
        name="attend_cache",
    )(*given, *after)


def fetch_kernel(pieces, source, after, into, sem):
    del after
    size = source.shape[0] // pieces
    copies = [
        pltpu.make_async_copy(
            source.at[pl.ds(i * size, size)], into.at[pl.ds(i * size, size)], sem.at[i]
        )
        for i in range(pieces)
    ]
    for copy in copies:
        copy.start()
    for copy in copies:
        copy.wait()


def fetch(served, after):
    pieces = 8
    return pl.pallas_call(
        functools.partial(fetch_kernel, pieces),
        out_shape=jax.ShapeDtypeStruct(served.shape, served.dtype),
        in_specs=[HBM, pl.BlockSpec(memory_space=pl.ANY)],
        out_specs=VMEM,
        scratch_shapes=[pltpu.SemaphoreType.DMA((pieces,))],
        compiler_params=pltpu.CompilerParams(vmem_limit_bytes=12 * 2**20),
        cost_estimate=pl.CostEstimate(
            flops=0, bytes_accessed=4 * served.size, transcendentals=0
        ),
        name="fetch_served",
    )(served, after)


class Merge:
    def __init__(self, start_ref, merged, out_sem, width):
        self.start, self.merged, self.out_sem, self.width = start_ref[...], merged, out_sem, width
        self.entry = lax.broadcasted_iota(jnp.int32, self.start.shape, 1)

    def rows_of(self, entry):
        first = jnp.sum(jnp.where(self.entry == entry, self.start, 0))
        return pl.ds(pl.multiple_of(first, self.width), self.width)

    def store(self, source, rows, at):
        return pltpu.make_async_copy(source, self.merged.at[rows], self.out_sem.at[at])

    def rows(self, slab, up, served_ref, features_ref, rows, total):
        rank = up.shape[0]
        block = jnp.concatenate(
            [slab[i * rank : (i + 1) * rank] for i in range(self.width // PANEL)], axis=1
        )
        update = lax.dot_general(
            block, up, (((0,), (0,)), ((), ())), preferred_element_type=jnp.float32
        )
        fold = (served_ref[rows, :].astype(jnp.float32) + update).astype(jnp.bfloat16)
        part = jnp.dot(features_ref[:, rows], fold, preferred_element_type=jnp.float32)
        return fold, total + part


def merge_kernel(per, left, start_ref, pick_ref, features_ref, served_ref, slabs_ref, crossed_ref,
                 last_ref, merged, total_ref, up_ref, left_ref, m_buf, out_sem):
    width = m_buf.shape[1]
    rank, cols = up_ref.shape
    merge = Merge(start_ref, merged, out_sem, width)
    ups = []
    for ref in (slabs_ref, last_ref):
        for k in range(ref.shape[0]):
            below = ref[k, rank * (width // PANEL) :].astype(jnp.float32)
            ups.append(
                jnp.concatenate(
                    [below[i * per : (i + 1) * per] for i in range(cols // PANEL)], axis=1
                )
            )
    ups = jnp.concatenate(ups, axis=0).astype(jnp.bfloat16)
    up = jnp.dot(pick_ref[...], ups, preferred_element_type=jnp.float32).astype(jnp.bfloat16)
    up_ref[...] = up
    total = jnp.zeros(total_ref.shape, jnp.float32)
    refs = (slabs_ref, last_ref, crossed_ref)
    slabs = [ref.at[k] for ref in refs for k in range(ref.shape[0])]
    keep = len(slabs) - left
    stores = []
    for i, slab in enumerate(slabs):
        rows = merge.rows_of(i)
        fold, total = merge.rows(slab, up, served_ref, features_ref, rows, total)
        if i < keep:
            m_buf[i] = fold
            stores.append(merge.store(m_buf.at[i], rows, i))
            stores[-1].start()
        else:
            left_ref[i - keep] = fold
    total_ref[...] = total
    for store in stores:
        store.wait()


def final_kernel(start_ref, up_ref, features_ref, served_ref, left_ref, last_ref, merged_in,
                 total_ref, context_ref, own_weight_ref, merged, fresh_hbm, attended_hbm, m_buf,
                 out_sem, fresh_ref, attended_ref, small_sem):
    del merged_in
    count, width = last_ref.shape[0], m_buf.shape[1]
    left = left_ref.shape[0]
    merge = Merge(start_ref, merged, out_sem, width)
    first = start_ref.shape[1] - count
    total = total_ref[...]
    stores = [
        merge.store(left_ref.at[k], merge.rows_of(first - left + k), count + k)
        for k in range(left)
    ]
    for store in stores:
        store.start()
    for i in range(count):
        rows = merge.rows_of(first + i)
        fold, total = merge.rows(last_ref.at[i], up_ref[...], served_ref, features_ref, rows, total)
        m_buf[i] = fold
        stores.append(merge.store(m_buf.at[i], rows, i))
        stores[-1].start()
    fresh = total.astype(jnp.bfloat16)
    fresh_ref[...] = fresh
    put_fresh = pltpu.make_async_copy(fresh_ref, fresh_hbm, small_sem.at[0])
    put_fresh.start()
    value = fresh.astype(jnp.float32)
    heads = attended_ref.shape[1] // HEAD_SIZE
    group = heads // (fresh_ref.shape[1] // HEAD_SIZE)
    for h in range(heads):
        cols = slice(h * HEAD_SIZE, (h + 1) * HEAD_SIZE)
        at = (h // group) * HEAD_SIZE
        attended_ref[:, cols] = (
            context_ref[:, cols] + own_weight_ref[:, cols] * value[:, at : at + HEAD_SIZE]
        ).astype(jnp.bfloat16)
    put_attended = pltpu.make_async_copy(attended_ref, attended_hbm, small_sem.at[1])
    put_attended.start()
    for store in stores:
        store.wait()
    put_fresh.wait()
    put_attended.wait()


def merge(per, start, pick, features, served, slabs, crossed, last):
    left = 3
    count = slabs.shape[0] + crossed.shape[0] + last.shape[0]
    rank = pick.shape[0]
    depth, cols = served.shape
    width = depth // start.shape[1]
    return pl.pallas_call(
        functools.partial(merge_kernel, per, left),
        out_shape=(
            jax.ShapeDtypeStruct((depth, cols), jnp.bfloat16),
            jax.ShapeDtypeStruct((features.shape[0], cols), jnp.float32),
            jax.ShapeDtypeStruct((rank, cols), jnp.bfloat16),
            jax.ShapeDtypeStruct((left, width, cols), jnp.bfloat16),
        ),
        in_specs=[VMEM] * 7,
        out_specs=(HBM, VMEM, VMEM, VMEM),
        scratch_shapes=[
            pltpu.VMEM((count - left, width, cols), jnp.bfloat16),
            pltpu.SemaphoreType.DMA((count - left,)),
        ],
        compiler_params=pltpu.CompilerParams(vmem_limit_bytes=12 * 2**20),
        cost_estimate=pl.CostEstimate(
            flops=2 * count * width * cols * rank,
            bytes_accessed=4 * count * width * cols,
            transcendentals=0,
        ),
        name="merge_blocks",
    )(start, pick, features, served, slabs, crossed, last)


def finish(start, up, features, served, left, last, merged, total, context, own_weight):
    count = last.shape[0]
    depth, cols = served.shape
    width = depth // start.shape[1]
    smalls = [total.shape, context.shape]
    return pl.pallas_call(
        final_kernel,
        out_shape=[
            jax.ShapeDtypeStruct(shape, jnp.bfloat16) for shape in [(depth, cols), *smalls]
        ],
        in_specs=[VMEM] * 6 + [HBM] + [VMEM] * 3,
        out_specs=[HBM] * 3,
        input_output_aliases={6: 0},
        scratch_shapes=[
            pltpu.VMEM((count, width, cols), jnp.bfloat16),
            pltpu.SemaphoreType.DMA((count + left.shape[0],)),
        ]
        + [pltpu.VMEM(shape, jnp.bfloat16) for shape in smalls]
        + [pltpu.SemaphoreType.DMA((2,))],
        compiler_params=pltpu.CompilerParams(vmem_limit_bytes=12 * 2**20),
        cost_estimate=pl.CostEstimate(
            flops=2 * count * width * cols * up.shape[0],
            bytes_accessed=4 * count * width * cols,
            transcendentals=0,
        ),
        name="finish_rows",
    )(start, up, features, served, left, last, merged, total, context, own_weight)


def panels(x):
    return [x[:, i : i + PANEL] for i in range(0, x.shape[1], PANEL)]


def body(
    hidden_in,
    queries,
    stored_keys,
    stored_values,
    fresh_token_key,
    lengths,
    served_value_weight,
    adapter_in,
    adapter_out,
    owner_rank,
):
    n = lax.axis_size("replica")
    replica = lax.axis_index("replica")
    core = lax.axis_index("tensor")
    swap = [(0, 1), (1, 0)]
    full = adapter_in.shape[1]
    width = full // 2
    rows = queries.shape[0]
    per, cols = adapter_out.shape
    rank = n * per

    bits = [n >> i for i in range(1, n.bit_length())]
    ways = [bits, bits[:-2] + bits[:-3:-1]]

    def exchange(x, *steps, cores=(0, 1)):
        pairs = [
            (2 * i + c, 2 * (i ^ sum(ways[c][step] for step in steps)) + c)
            for i in range(n)
            for c in cores
        ]
        return lax.ppermute(x, ("replica", "tensor"), pairs)

    below = jnp.concatenate(panels(adapter_out), axis=0)
    below = jnp.pad(below, ((0, -below.shape[0] % 8), (0, 0)))
    block = lax.dynamic_slice_in_dim(adapter_in, core * width, width, axis=1)
    block, below = lax.optimization_barrier((block, below))
    slabs = jnp.concatenate([*panels(block), below], axis=0)[None]

    given = in_hbm(lengths, queries, fresh_token_key, stored_keys, stored_values)
    *early, first, second, third = range(len(bits))
    for step in early:
        slabs = jnp.concatenate([slabs, exchange(slabs, step)], axis=0)

    split = rows - rows // 4
    hid_other = lax.ppermute(hidden_in, "tensor", swap)
    came = exchange(slabs, first)
    part = attend(range(split), given, [slabs])
    came, part = lax.optimization_barrier((came, part))
    parts = [part]
    slabs = jnp.concatenate([slabs, came], axis=0)
    images = exchange(slabs, third)
    straight = exchange(slabs, second, third, cores=(0,))
    came = exchange(slabs, second)
    part = attend(range(split, rows), given, [slabs])
    came, part, hid_other, owner_rank = lax.optimization_barrier(
        (came, part, hid_other, owner_rank)
    )
    parts.append(part)
    relayed = exchange(came, third, cores=(1,))
    served = fetch(*in_hbm(served_value_weight), came)
    straight, relayed, served = lax.optimization_barrier((straight, relayed, served))
    last = jnp.where(core == 0, straight, relayed)
    slabs = jnp.concatenate([slabs, came, images], axis=0)
    features = jnp.concatenate([hidden_in, hid_other], axis=1)
    features = jnp.where(core == 0, features, jnp.concatenate([hid_other, hidden_in], axis=1))

    slab = jnp.arange(n, dtype=jnp.int32)
    sources = []
    for way in ways:
        source = replica
        for step, bit in enumerate(way):
            source = source ^ (((slab >> step) & 1) * bit)
        sources.append(source)
    mine = jnp.where(core == 0, sources[0], sources[1])
    theirs = jnp.where(core == 0, sources[1], sources[0])
    source = jnp.concatenate([mine, theirs])
    half = jnp.concatenate([jnp.full((n,), core), jnp.full((n,), 1 - core)])
    place = jnp.sum(jnp.where(owner_rank[None, :] == source[:, None], slab[None, :], 0), axis=1)
    start = (place * full + half * width).astype(jnp.int32)[None]

    row = jnp.arange(rank, dtype=jnp.int32)
    row_source = replica
    for step in range(len(bits)):
        bit = jnp.where(core == 0, ways[0][step], ways[1][step])
        row_source = row_source ^ (((row // per >> step) & 1) * bit)
    pick = jnp.where(
        row[:, None] == (row_source * per + row % per)[None, :], ADAPTER_SCALE, 0.0
    ).astype(jnp.bfloat16)

    context, own_weight = (
        jnp.concatenate(pair, axis=0).reshape(queries.shape) for pair in zip(*parts)
    )
    crossed, start = lax.optimization_barrier((slabs, start))
    crossed = lax.ppermute(crossed, "tensor", swap)
    last, start, pick, context, own_weight, features, crossed = lax.optimization_barrier(
        (last, start, pick, context, own_weight, features, crossed)
    )
    last_crossed = lax.ppermute(last, "tensor", swap)
    merged, total, up, left = merge(per, start, pick, features, served, slabs, crossed, last)
    return tuple(
        finish(
            start, up, features, served, left, last_crossed, merged, total, context, own_weight
        )
    )


def solution(mesh):
    in_specs = (
        P(("groups", "replica"), "tensor"),
        P(("groups", "replica"), "tensor"),
        P(("groups", "replica"), None, "tensor"),
        P(("groups", "replica"), None, "tensor"),
        P(("groups", "replica"), "tensor"),
        P(("groups", "replica")),
        P(None, "tensor"),
        P("groups", "replica"),
        P(("groups", "replica"), "tensor"),
        P("groups"),
    )
    out_specs = (
        P("groups", "tensor"),
        P(("groups", "replica"), "tensor"),
        P(("groups", "replica"), "tensor"),
    )
    return jax.shard_map(body, mesh=mesh, in_specs=in_specs, out_specs=out_specs, check_vma=False)
```

```python
import functools

import jax
import jax.numpy as jnp
from jax import lax
from jax.experimental import pallas as pl
from jax.experimental.pallas import tpu as pltpu
from jax.sharding import PartitionSpec as P

HEAD_SIZE = 128
ADAPTER_SCALE = 2.0
PANEL = 128

SMEM = pl.BlockSpec(memory_space=pltpu.SMEM)
VMEM = pl.BlockSpec(memory_space=pltpu.VMEM)
HBM = pl.BlockSpec(memory_space=pltpu.HBM)


def in_hbm(*arrays):
    return [pltpu.with_memory_space_constraint(x, pltpu.HBM) for x in arrays]


def attend_kernel(rows, fetch, lengths_hbm, q_hbm, own_k_hbm, k_hbm, v_hbm, *rest):
    rest = list(rest)
    if fetch:
        served_hbm, served_ref, served_sem = rest.pop(0), rest.pop(-10), rest.pop(-1)
    context_ref, own_weight_ref, lengths, q_ref, own_k_ref, k_buf, v_buf, small_sem, k_sem, v_sem = (
        rest[-10:]
    )
    smalls = [
        pltpu.make_async_copy(source, into, small_sem.at[i])
        for i, (source, into) in enumerate(
            [(lengths_hbm, lengths), (q_hbm, q_ref), (own_k_hbm, own_k_ref)]
        )
    ]
    for copy in smalls:
        copy.start()

    def copies(i, row):
        return (
            pltpu.make_async_copy(k_hbm.at[row], k_buf.at[i], k_sem.at[i]),
            pltpu.make_async_copy(v_hbm.at[row], v_buf.at[i], v_sem.at[i]),
        )

    for i, row in enumerate(rows):
        for copy in copies(i, row):
            copy.start()
    if fetch:
        get_served = pltpu.make_async_copy(served_hbm, served_ref, served_sem)
        get_served.start()
    for copy in smalls:
        copy.wait()
    queries = q_ref[...].astype(jnp.float32)
    own_keys = own_k_ref[...].astype(jnp.float32)
    heads = queries.shape[1] // HEAD_SIZE
    cache_len, width = k_buf.shape[1:]
    local_heads = width // HEAD_SIZE
    group = heads // local_heads
    scaling = 1.0 / HEAD_SIZE**0.5
    head_of = lax.broadcasted_iota(jnp.int32, (heads, HEAD_SIZE), 0) // group
    position = lax.broadcasted_iota(jnp.int32, (heads, cache_len), 1)
    for i, row in enumerate(rows):
        q = jnp.concatenate(
            [
                queries[row : row + 1, h * HEAD_SIZE : (h + 1) * HEAD_SIZE]
                for h in range(heads)
            ],
            axis=0,
        )
        spread = jnp.concatenate(
            [jnp.where(head_of == h, q, 0.0) for h in range(local_heads)], axis=1
        )
        own = jnp.sum(spread * own_keys[row : row + 1], axis=1, keepdims=True) * scaling
        get_keys, get_values = copies(i, row)
        get_keys.wait()
        scores = (
            lax.dot_general(
                spread.astype(jnp.bfloat16), k_buf[i], (((1,), (1,)), ((), ())),
                preferred_element_type=jnp.float32,
            )
            * scaling
        )
        valid = position < lengths[row]
        masked = jnp.where(valid, scores, -1e30)
        largest = jnp.maximum(jnp.max(masked, axis=1, keepdims=True), own)
        cached_exp = jnp.where(valid, jnp.exp(masked - largest), 0.0)
        own_exp = jnp.exp(own - largest)
        normaliser = jnp.sum(cached_exp, axis=1, keepdims=True) + own_exp
        weights = (cached_exp / normaliser).astype(jnp.bfloat16)
        weight_own = (own_exp / normaliser).astype(jnp.bfloat16).astype(jnp.float32)
        get_values.wait()
        wide = jnp.dot(weights, v_buf[i], preferred_element_type=jnp.float32)
        context = wide[:, :HEAD_SIZE]
        for h in range(1, local_heads):
            context = jnp.where(
                head_of == h, wide[:, h * HEAD_SIZE : (h + 1) * HEAD_SIZE], context
            )
        context_ref[i] = context
        own_weight_ref[i] = jnp.broadcast_to(weight_own, (heads, HEAD_SIZE))
    if fetch:
        get_served.wait()


def attend(rows, given, served=None, after=()):
    lengths, queries, own_key, stored_keys, stored_values = given
    fetch = served is not None
    cache_len, width = stored_keys.shape[1:]
    heads = queries.shape[1] // HEAD_SIZE
    count = len(rows)
    out_shape = [jax.ShapeDtypeStruct((count, heads, HEAD_SIZE), jnp.float32)] * 2
    if fetch:
        out_shape += [jax.ShapeDtypeStruct(served.shape, served.dtype)]
    return pl.pallas_call(
        functools.partial(attend_kernel, rows, fetch),
        out_shape=out_shape,
        in_specs=[HBM] * (5 + fetch) + [pl.BlockSpec(memory_space=pl.ANY)] * len(after),
        out_specs=[VMEM] * len(out_shape),
        scratch_shapes=[
            pltpu.SMEM(lengths.shape, jnp.int32),
            pltpu.VMEM(queries.shape, jnp.bfloat16),
            pltpu.VMEM(own_key.shape, jnp.bfloat16),
            pltpu.VMEM((count, cache_len, width), jnp.bfloat16),
            pltpu.VMEM((count, cache_len, width), jnp.bfloat16),
            pltpu.SemaphoreType.DMA((3,)),
            pltpu.SemaphoreType.DMA((count,)),
            pltpu.SemaphoreType.DMA((count,)),
        ]
        + [pltpu.SemaphoreType.DMA] * fetch,
        compiler_params=pltpu.CompilerParams(vmem_limit_bytes=12 * 2**20),
        cost_estimate=pl.CostEstimate(
            flops=4 * count * heads * cache_len * width,
            bytes_accessed=4 * count * cache_len * width,
            transcendentals=count * heads * cache_len,
        ),
        name="attend_cache",
    )(*given, *([served] if fetch else []), *after)


class Merge:
    def __init__(self, start_ref, merged, out_sem, width):
        self.start, self.merged, self.out_sem, self.width = start_ref[...], merged, out_sem, width
        self.entry = lax.broadcasted_iota(jnp.int32, self.start.shape, 1)

    def rows_of(self, entry):
        first = jnp.sum(jnp.where(self.entry == entry, self.start, 0))
        return pl.ds(pl.multiple_of(first, self.width), self.width)

    def store(self, source, rows, at):
        return pltpu.make_async_copy(source, self.merged.at[rows], self.out_sem.at[at])

    def rows(self, slab, up, served_ref, features_ref, rows, total):
        rank = up.shape[0]
        block = jnp.concatenate(
            [slab[i * rank : (i + 1) * rank] for i in range(self.width // PANEL)], axis=1
        )
        update = lax.dot_general(
            block, up, (((0,), (0,)), ((), ())), preferred_element_type=jnp.float32
        )
        fold = (served_ref[rows, :].astype(jnp.float32) + update).astype(jnp.bfloat16)
        part = jnp.dot(features_ref[:, rows], fold, preferred_element_type=jnp.float32)
        return fold, total + part


def merge_kernel(per, left, start_ref, pick_ref, features_ref, served_ref, slabs_ref, crossed_ref,
                 last_ref, merged, total_ref, up_ref, left_ref, m_buf, out_sem):
    width = m_buf.shape[1]
    rank, cols = up_ref.shape
    merge = Merge(start_ref, merged, out_sem, width)
    ups = []
    for ref in (slabs_ref, last_ref):
        for k in range(ref.shape[0]):
            below = ref[k, rank * (width // PANEL) :].astype(jnp.float32)
            ups.append(
                jnp.concatenate(
                    [below[i * per : (i + 1) * per] for i in range(cols // PANEL)], axis=1
                )
            )
    ups = jnp.concatenate(ups, axis=0).astype(jnp.bfloat16)
    up = jnp.dot(pick_ref[...], ups, preferred_element_type=jnp.float32).astype(jnp.bfloat16)
    up_ref[...] = up
    total = jnp.zeros(total_ref.shape, jnp.float32)
    refs = (slabs_ref, last_ref, crossed_ref)
    slabs = [ref.at[k] for ref in refs for k in range(ref.shape[0])]
    keep = len(slabs) - left
    stores = []
    for i, slab in enumerate(slabs):
        rows = merge.rows_of(i)
        fold, total = merge.rows(slab, up, served_ref, features_ref, rows, total)
        if i < keep:
            m_buf[i] = fold
            stores.append(merge.store(m_buf.at[i], rows, i))
            stores[-1].start()
        else:
            left_ref[i - keep] = fold
    total_ref[...] = total
    for store in stores:
        store.wait()


def final_kernel(start_ref, up_ref, features_ref, served_ref, left_ref, last_ref, merged_in,
                 total_ref, context_ref, own_weight_ref, merged, fresh_hbm, attended_hbm, m_buf,
                 out_sem, fresh_ref, attended_ref, small_sem):
    del merged_in
    count, width = last_ref.shape[0], m_buf.shape[1]
    left = left_ref.shape[0]
    merge = Merge(start_ref, merged, out_sem, width)
    first = start_ref.shape[1] - count
    total = total_ref[...]
    stores = [
        merge.store(left_ref.at[k], merge.rows_of(first - left + k), count + k)
        for k in range(left)
    ]
    for store in stores:
        store.start()
    for i in range(count):
        rows = merge.rows_of(first + i)
        fold, total = merge.rows(last_ref.at[i], up_ref[...], served_ref, features_ref, rows, total)
        m_buf[i] = fold
        stores.append(merge.store(m_buf.at[i], rows, i))
        stores[-1].start()
    fresh = total.astype(jnp.bfloat16)
    fresh_ref[...] = fresh
    put_fresh = pltpu.make_async_copy(fresh_ref, fresh_hbm, small_sem.at[0])
    put_fresh.start()
    value = fresh.astype(jnp.float32)
    heads = attended_ref.shape[1] // HEAD_SIZE
    group = heads // (fresh_ref.shape[1] // HEAD_SIZE)
    for h in range(heads):
        cols = slice(h * HEAD_SIZE, (h + 1) * HEAD_SIZE)
        at = (h // group) * HEAD_SIZE
        attended_ref[:, cols] = (
            context_ref[:, cols] + own_weight_ref[:, cols] * value[:, at : at + HEAD_SIZE]
        ).astype(jnp.bfloat16)
    put_attended = pltpu.make_async_copy(attended_ref, attended_hbm, small_sem.at[1])
    put_attended.start()
    for store in stores:
        store.wait()
    put_fresh.wait()
    put_attended.wait()


def merge(per, start, pick, features, served, slabs, crossed, last):
    left = 3
    count = slabs.shape[0] + crossed.shape[0] + last.shape[0]
    rank = pick.shape[0]
    depth, cols = served.shape
    width = depth // start.shape[1]
    return pl.pallas_call(
        functools.partial(merge_kernel, per, left),
        out_shape=(
            jax.ShapeDtypeStruct((depth, cols), jnp.bfloat16),
            jax.ShapeDtypeStruct((features.shape[0], cols), jnp.float32),
            jax.ShapeDtypeStruct((rank, cols), jnp.bfloat16),
            jax.ShapeDtypeStruct((left, width, cols), jnp.bfloat16),
        ),
        in_specs=[VMEM] * 7,
        out_specs=(HBM, VMEM, VMEM, VMEM),
        scratch_shapes=[
            pltpu.VMEM((count - left, width, cols), jnp.bfloat16),
            pltpu.SemaphoreType.DMA((count - left,)),
        ],
        compiler_params=pltpu.CompilerParams(vmem_limit_bytes=12 * 2**20),
        cost_estimate=pl.CostEstimate(
            flops=2 * count * width * cols * rank,
            bytes_accessed=4 * count * width * cols,
            transcendentals=0,
        ),
        name="merge_blocks",
    )(start, pick, features, served, slabs, crossed, last)


def finish(start, up, features, served, left, last, merged, total, context, own_weight):
    count = last.shape[0]
    depth, cols = served.shape
    width = depth // start.shape[1]
    smalls = [total.shape, context.shape]
    return pl.pallas_call(
        final_kernel,
        out_shape=[
            jax.ShapeDtypeStruct(shape, jnp.bfloat16) for shape in [(depth, cols), *smalls]
        ],
        in_specs=[VMEM] * 6 + [HBM] + [VMEM] * 3,
        out_specs=[HBM] * 3,
        input_output_aliases={6: 0},
        scratch_shapes=[
            pltpu.VMEM((count, width, cols), jnp.bfloat16),
            pltpu.SemaphoreType.DMA((count + left.shape[0],)),
        ]
        + [pltpu.VMEM(shape, jnp.bfloat16) for shape in smalls]
        + [pltpu.SemaphoreType.DMA((2,))],
        compiler_params=pltpu.CompilerParams(vmem_limit_bytes=12 * 2**20),
        cost_estimate=pl.CostEstimate(
            flops=2 * count * width * cols * up.shape[0],
            bytes_accessed=4 * count * width * cols,
            transcendentals=0,
        ),
        name="finish_rows",
    )(start, up, features, served, left, last, merged, total, context, own_weight)


def panels(x):
    return [x[:, i : i + PANEL] for i in range(0, x.shape[1], PANEL)]


def body(
    hidden_in,
    queries,
    stored_keys,
    stored_values,
    fresh_token_key,
    lengths,
    served_value_weight,
    adapter_in,
    adapter_out,
    owner_rank,
):
    n = lax.axis_size("replica")
    replica = lax.axis_index("replica")
    core = lax.axis_index("tensor")
    swap = [(0, 1), (1, 0)]
    full = adapter_in.shape[1]
    width = full // 2
    rows = queries.shape[0]
    per, cols = adapter_out.shape
    rank = n * per

    bits = [n >> i for i in range(1, n.bit_length())]
    ways = [bits[:-2] + bits[:-3:-1], bits]

    def exchange(x, step):
        pairs = [(2 * i + c, 2 * (i ^ ways[c][step]) + c) for i in range(n) for c in range(2)]
        return lax.ppermute(x, ("replica", "tensor"), pairs)

    below = jnp.concatenate(panels(adapter_out), axis=0)
    below = jnp.pad(below, ((0, -below.shape[0] % 8), (0, 0)))
    block = lax.dynamic_slice_in_dim(adapter_in, core * width, width, axis=1)
    block, below = lax.optimization_barrier((block, below))
    slabs = jnp.concatenate([*panels(block), below], axis=0)[None]

    given = in_hbm(lengths, queries, fresh_token_key, stored_keys, stored_values)
    *early, first, second, third = range(len(bits))
    for step in early:
        slabs = jnp.concatenate([slabs, exchange(slabs, step)], axis=0)

    cuts = [0, rows // 2, rows - rows // 4, rows]
    first_rows, second_rows, third_rows = (range(*cut) for cut in zip(cuts, cuts[1:]))
    hid_other = lax.ppermute(hidden_in, "tensor", swap)
    came = exchange(slabs, first)
    part = attend(first_rows, given, after=[slabs])
    came, part = lax.optimization_barrier((came, part))
    parts = [part]
    slabs = jnp.concatenate([slabs, came], axis=0)
    came = exchange(slabs, second)
    images = exchange(slabs, third)
    *part, served = attend(second_rows, given, *in_hbm(served_value_weight), [slabs])
    came, part, hid_other, owner_rank = lax.optimization_barrier(
        (came, part, hid_other, owner_rank)
    )
    parts.append(part)
    last = exchange(came, third)
    slabs = jnp.concatenate([slabs, came, images], axis=0)
    parts.append(attend(third_rows, given, after=[images]))
    features = jnp.concatenate([hidden_in, hid_other], axis=1)
    features = jnp.where(core == 0, features, jnp.concatenate([hid_other, hidden_in], axis=1))

    slab = jnp.arange(n, dtype=jnp.int32)
    sources = []
    for way in ways:
        source = replica
        for step, bit in enumerate(way):
            source = source ^ (((slab >> step) & 1) * bit)
        sources.append(source)
    mine = jnp.where(core == 0, sources[0], sources[1])
    theirs = jnp.where(core == 0, sources[1], sources[0])
    source = jnp.concatenate([mine, theirs])
    half = jnp.concatenate([jnp.full((n,), core), jnp.full((n,), 1 - core)])
    place = jnp.sum(jnp.where(owner_rank[None, :] == source[:, None], slab[None, :], 0), axis=1)
    start = (place * full + half * width).astype(jnp.int32)[None]

    row = jnp.arange(rank, dtype=jnp.int32)
    row_source = replica
    for step in range(len(bits)):
        bit = jnp.where(core == 0, ways[0][step], ways[1][step])
        row_source = row_source ^ (((row // per >> step) & 1) * bit)
    pick = jnp.where(
        row[:, None] == (row_source * per + row % per)[None, :], ADAPTER_SCALE, 0.0
    ).astype(jnp.bfloat16)

    context, own_weight = (
        jnp.concatenate(pair, axis=0).reshape(queries.shape) for pair in zip(*parts)
    )
    crossed, start = lax.optimization_barrier((slabs, start))
    crossed = lax.ppermute(crossed, "tensor", swap)
    last, start, pick, context, own_weight, features, crossed = lax.optimization_barrier(
        (last, start, pick, context, own_weight, features, crossed)
    )
    last_crossed = lax.ppermute(last, "tensor", swap)
    merged, total, up, left = merge(per, start, pick, features, served, slabs, crossed, last)
    return tuple(
        finish(
            start, up, features, served, left, last_crossed, merged, total, context, own_weight
        )
    )


def solution(mesh):
    in_specs = (
        P(("groups", "replica"), "tensor"),
        P(("groups", "replica"), "tensor"),
        P(("groups", "replica"), None, "tensor"),
        P(("groups", "replica"), None, "tensor"),
        P(("groups", "replica"), "tensor"),
        P(("groups", "replica")),
        P(None, "tensor"),
        P("groups", "replica"),
        P(("groups", "replica"), "tensor"),
        P("groups"),
    )
    out_specs = (
        P("groups", "tensor"),
        P(("groups", "replica"), "tensor"),
        P(("groups", "replica"), "tensor"),
    )
    return jax.shard_map(body, mesh=mesh, in_specs=in_specs, out_specs=out_specs, check_vma=False)
```

```python
import functools

import jax
import jax.numpy as jnp
from jax import lax
from jax.experimental import pallas as pl
from jax.experimental.pallas import tpu as pltpu
from jax.sharding import PartitionSpec as P

HEAD_SIZE = 128
ADAPTER_SCALE = 2.0
PANEL = 128

SMEM = pl.BlockSpec(memory_space=pltpu.SMEM)
VMEM = pl.BlockSpec(memory_space=pltpu.VMEM)
HBM = pl.BlockSpec(memory_space=pltpu.HBM)


def in_hbm(*arrays):
    return [pltpu.with_memory_space_constraint(x, pltpu.HBM) for x in arrays]


def attend_kernel(rows, fetch, lengths_hbm, q_hbm, own_k_hbm, k_hbm, v_hbm, *rest):
    rest = list(rest)
    if fetch:
        served_hbm, served_ref, served_sem = rest.pop(0), rest.pop(-10), rest.pop(-1)
    context_ref, own_weight_ref, lengths, q_ref, own_k_ref, k_buf, v_buf, small_sem, k_sem, v_sem = (
        rest[-10:]
    )
    smalls = [
        pltpu.make_async_copy(source, into, small_sem.at[i])
        for i, (source, into) in enumerate(
            [(lengths_hbm, lengths), (q_hbm, q_ref), (own_k_hbm, own_k_ref)]
        )
    ]
    for copy in smalls:
        copy.start()

    def copies(i, row):
        return (
            pltpu.make_async_copy(k_hbm.at[row], k_buf.at[i], k_sem.at[i]),
            pltpu.make_async_copy(v_hbm.at[row], v_buf.at[i], v_sem.at[i]),
        )

    for i, row in enumerate(rows):
        for copy in copies(i, row):
            copy.start()
    if fetch:
        get_served = pltpu.make_async_copy(served_hbm, served_ref, served_sem)
        get_served.start()
    for copy in smalls:
        copy.wait()
    queries = q_ref[...].astype(jnp.float32)
    own_keys = own_k_ref[...].astype(jnp.float32)
    heads = queries.shape[1] // HEAD_SIZE
    cache_len, width = k_buf.shape[1:]
    local_heads = width // HEAD_SIZE
    group = heads // local_heads
    scaling = 1.0 / HEAD_SIZE**0.5
    head_of = lax.broadcasted_iota(jnp.int32, (heads, HEAD_SIZE), 0) // group
    position = lax.broadcasted_iota(jnp.int32, (heads, cache_len), 1)
    for i, row in enumerate(rows):
        q = jnp.concatenate(
            [
                queries[row : row + 1, h * HEAD_SIZE : (h + 1) * HEAD_SIZE]
                for h in range(heads)
            ],
            axis=0,
        )
        spread = jnp.concatenate(
            [jnp.where(head_of == h, q, 0.0) for h in range(local_heads)], axis=1
        )
        own = jnp.sum(spread * own_keys[row : row + 1], axis=1, keepdims=True) * scaling
        get_keys, get_values = copies(i, row)
        get_keys.wait()
        scores = (
            lax.dot_general(
                spread.astype(jnp.bfloat16), k_buf[i], (((1,), (1,)), ((), ())),
                preferred_element_type=jnp.float32,
            )
            * scaling
        )
        valid = position < lengths[row]
        masked = jnp.where(valid, scores, -1e30)
        largest = jnp.maximum(jnp.max(masked, axis=1, keepdims=True), own)
        cached_exp = jnp.where(valid, jnp.exp(masked - largest), 0.0)
        own_exp = jnp.exp(own - largest)
        normaliser = jnp.sum(cached_exp, axis=1, keepdims=True) + own_exp
        weights = (cached_exp / normaliser).astype(jnp.bfloat16)
        weight_own = (own_exp / normaliser).astype(jnp.bfloat16).astype(jnp.float32)
        get_values.wait()
        wide = jnp.dot(weights, v_buf[i], preferred_element_type=jnp.float32)
        context = wide[:, :HEAD_SIZE]
        for h in range(1, local_heads):
            context = jnp.where(
                head_of == h, wide[:, h * HEAD_SIZE : (h + 1) * HEAD_SIZE], context
            )
        context_ref[i] = context
        own_weight_ref[i] = jnp.broadcast_to(weight_own, (heads, HEAD_SIZE))
    if fetch:
        get_served.wait()


def attend(rows, given, served=None, after=()):
    lengths, queries, own_key, stored_keys, stored_values = given
    fetch = served is not None
    cache_len, width = stored_keys.shape[1:]
    heads = queries.shape[1] // HEAD_SIZE
    count = len(rows)
    out_shape = [jax.ShapeDtypeStruct((count, heads, HEAD_SIZE), jnp.float32)] * 2
    if fetch:
        out_shape += [jax.ShapeDtypeStruct(served.shape, served.dtype)]
    return pl.pallas_call(
        functools.partial(attend_kernel, rows, fetch),
        out_shape=out_shape,
        in_specs=[HBM] * (5 + fetch) + [pl.BlockSpec(memory_space=pl.ANY)] * len(after),
        out_specs=[VMEM] * len(out_shape),
        scratch_shapes=[
            pltpu.SMEM(lengths.shape, jnp.int32),
            pltpu.VMEM(queries.shape, jnp.bfloat16),
            pltpu.VMEM(own_key.shape, jnp.bfloat16),
            pltpu.VMEM((count, cache_len, width), jnp.bfloat16),
            pltpu.VMEM((count, cache_len, width), jnp.bfloat16),
            pltpu.SemaphoreType.DMA((3,)),
            pltpu.SemaphoreType.DMA((count,)),
            pltpu.SemaphoreType.DMA((count,)),
        ]
        + [pltpu.SemaphoreType.DMA] * fetch,
        compiler_params=pltpu.CompilerParams(vmem_limit_bytes=12 * 2**20),
        cost_estimate=pl.CostEstimate(
            flops=4 * count * heads * cache_len * width,
            bytes_accessed=4 * count * cache_len * width,
            transcendentals=count * heads * cache_len,
        ),
        name="attend_cache",
    )(*given, *([served] if fetch else []), *after)


class Merge:
    def __init__(self, start_ref, merged, out_sem, width):
        self.start, self.merged, self.out_sem, self.width = start_ref[...], merged, out_sem, width
        self.entry = lax.broadcasted_iota(jnp.int32, self.start.shape, 1)

    def rows_of(self, entry):
        first = jnp.sum(jnp.where(self.entry == entry, self.start, 0))
        return pl.ds(pl.multiple_of(first, self.width), self.width)

    def store(self, source, rows, at):
        return pltpu.make_async_copy(source, self.merged.at[rows], self.out_sem.at[at])

    def rows(self, slab, up, served_ref, features_ref, rows, total):
        rank = up.shape[0]
        block = jnp.concatenate(
            [slab[i * rank : (i + 1) * rank] for i in range(self.width // PANEL)], axis=1
        )
        update = lax.dot_general(
            block, up, (((0,), (0,)), ((), ())), preferred_element_type=jnp.float32
        )
        fold = (served_ref[rows, :].astype(jnp.float32) + update).astype(jnp.bfloat16)
        part = jnp.dot(features_ref[:, rows], fold, preferred_element_type=jnp.float32)
        return fold, total + part


def merge_kernel(per, left, start_ref, pick_ref, features_ref, served_ref, slabs_ref, crossed_ref,
                 last_ref, merged, total_ref, up_ref, left_ref, m_buf, out_sem):
    width = m_buf.shape[1]
    rank, cols = up_ref.shape
    merge = Merge(start_ref, merged, out_sem, width)
    ups = []
    for ref in (slabs_ref, last_ref):
        for k in range(ref.shape[0]):
            below = ref[k, rank * (width // PANEL) :].astype(jnp.float32)
            ups.append(
                jnp.concatenate(
                    [below[i * per : (i + 1) * per] for i in range(cols // PANEL)], axis=1
                )
            )
    ups = jnp.concatenate(ups, axis=0).astype(jnp.bfloat16)
    up = jnp.dot(pick_ref[...], ups, preferred_element_type=jnp.float32).astype(jnp.bfloat16)
    up_ref[...] = up
    total = jnp.zeros(total_ref.shape, jnp.float32)
    refs = (slabs_ref, last_ref, crossed_ref)
    slabs = [ref.at[k] for ref in refs for k in range(ref.shape[0])]
    keep = len(slabs) - left
    stores = []
    for i, slab in enumerate(slabs):
        rows = merge.rows_of(i)
        fold, total = merge.rows(slab, up, served_ref, features_ref, rows, total)
        if i < keep:
            m_buf[i] = fold
            stores.append(merge.store(m_buf.at[i], rows, i))
            stores[-1].start()
        else:
            left_ref[i - keep] = fold
    total_ref[...] = total
    for store in stores:
        store.wait()


def final_kernel(start_ref, up_ref, features_ref, served_ref, left_ref, last_ref, merged_in,
                 total_ref, context_ref, own_weight_ref, merged, fresh_hbm, attended_hbm, m_buf,
                 out_sem, fresh_ref, attended_ref, small_sem):
    del merged_in
    count, width = last_ref.shape[0], m_buf.shape[1]
    left = left_ref.shape[0]
    merge = Merge(start_ref, merged, out_sem, width)
    first = start_ref.shape[1] - count
    total = total_ref[...]
    stores = [
        merge.store(left_ref.at[k], merge.rows_of(first - left + k), count + k)
        for k in range(left)
    ]
    for store in stores:
        store.start()
    for i in range(count):
        rows = merge.rows_of(first + i)
        fold, total = merge.rows(last_ref.at[i], up_ref[...], served_ref, features_ref, rows, total)
        m_buf[i] = fold
        stores.append(merge.store(m_buf.at[i], rows, i))
        stores[-1].start()
    fresh = total.astype(jnp.bfloat16)
    fresh_ref[...] = fresh
    put_fresh = pltpu.make_async_copy(fresh_ref, fresh_hbm, small_sem.at[0])
    put_fresh.start()
    value = fresh.astype(jnp.float32)
    heads = attended_ref.shape[1] // HEAD_SIZE
    group = heads // (fresh_ref.shape[1] // HEAD_SIZE)
    for h in range(heads):
        cols = slice(h * HEAD_SIZE, (h + 1) * HEAD_SIZE)
        at = (h // group) * HEAD_SIZE
        attended_ref[:, cols] = (
            context_ref[:, cols] + own_weight_ref[:, cols] * value[:, at : at + HEAD_SIZE]
        ).astype(jnp.bfloat16)
    put_attended = pltpu.make_async_copy(attended_ref, attended_hbm, small_sem.at[1])
    put_attended.start()
    for store in stores:
        store.wait()
    put_fresh.wait()
    put_attended.wait()


def merge(per, start, pick, features, served, slabs, crossed, last):
    left = 3
    count = slabs.shape[0] + crossed.shape[0] + last.shape[0]
    rank = pick.shape[0]
    depth, cols = served.shape
    width = depth // start.shape[1]
    return pl.pallas_call(
        functools.partial(merge_kernel, per, left),
        out_shape=(
            jax.ShapeDtypeStruct((depth, cols), jnp.bfloat16),
            jax.ShapeDtypeStruct((features.shape[0], cols), jnp.float32),
            jax.ShapeDtypeStruct((rank, cols), jnp.bfloat16),
            jax.ShapeDtypeStruct((left, width, cols), jnp.bfloat16),
        ),
        in_specs=[VMEM] * 7,
        out_specs=(HBM, VMEM, VMEM, VMEM),
        scratch_shapes=[
            pltpu.VMEM((count - left, width, cols), jnp.bfloat16),
            pltpu.SemaphoreType.DMA((count - left,)),
        ],
        compiler_params=pltpu.CompilerParams(vmem_limit_bytes=12 * 2**20),
        cost_estimate=pl.CostEstimate(
            flops=2 * count * width * cols * rank,
            bytes_accessed=4 * count * width * cols,
            transcendentals=0,
        ),
        name="merge_blocks",
    )(start, pick, features, served, slabs, crossed, last)


def finish(start, up, features, served, left, last, merged, total, context, own_weight):
    count = last.shape[0]
    depth, cols = served.shape
    width = depth // start.shape[1]
    smalls = [total.shape, context.shape]
    return pl.pallas_call(
        final_kernel,
        out_shape=[
            jax.ShapeDtypeStruct(shape, jnp.bfloat16) for shape in [(depth, cols), *smalls]
        ],
        in_specs=[VMEM] * 6 + [HBM] + [VMEM] * 3,
        out_specs=[HBM] * 3,
        input_output_aliases={6: 0},
        scratch_shapes=[
            pltpu.VMEM((count, width, cols), jnp.bfloat16),
            pltpu.SemaphoreType.DMA((count + left.shape[0],)),
        ]
        + [pltpu.VMEM(shape, jnp.bfloat16) for shape in smalls]
        + [pltpu.SemaphoreType.DMA((2,))],
        compiler_params=pltpu.CompilerParams(vmem_limit_bytes=12 * 2**20),
        cost_estimate=pl.CostEstimate(
            flops=2 * count * width * cols * up.shape[0],
            bytes_accessed=4 * count * width * cols,
            transcendentals=0,
        ),
        name="finish_rows",
    )(start, up, features, served, left, last, merged, total, context, own_weight)


def panels(x):
    return [x[:, i : i + PANEL] for i in range(0, x.shape[1], PANEL)]


def body(
    hidden_in,
    queries,
    stored_keys,
    stored_values,
    fresh_token_key,
    lengths,
    served_value_weight,
    adapter_in,
    adapter_out,
    owner_rank,
):
    n = lax.axis_size("replica")
    replica = lax.axis_index("replica")
    core = lax.axis_index("tensor")
    swap = [(0, 1), (1, 0)]
    full = adapter_in.shape[1]
    width = full // 2
    rows = queries.shape[0]
    per, cols = adapter_out.shape
    rank = n * per

    bits = [n >> i for i in range(1, n.bit_length())]
    ways = [bits, bits[:-2] + bits[:-3:-1]]

    def exchange(x, *steps):
        pairs = [
            (2 * i + c, 2 * (i ^ sum(ways[c][step] for step in steps)) + c)
            for i in range(n)
            for c in range(2)
        ]
        return lax.ppermute(x, ("replica", "tensor"), pairs)

    below = jnp.concatenate(panels(adapter_out), axis=0)
    below = jnp.pad(below, ((0, -below.shape[0] % 8), (0, 0)))
    block = lax.dynamic_slice_in_dim(adapter_in, core * width, width, axis=1)
    block, below = lax.optimization_barrier((block, below))
    slabs = jnp.concatenate([*panels(block), below], axis=0)[None]

    given = in_hbm(lengths, queries, fresh_token_key, stored_keys, stored_values)
    *early, first, second, third = range(len(bits))
    for step in early:
        slabs = jnp.concatenate([slabs, exchange(slabs, step)], axis=0)

    split = rows // 2
    hid_other = lax.ppermute(hidden_in, "tensor", swap)
    came = exchange(slabs, first)
    part = attend(range(split), given, after=[slabs])
    came, part = lax.optimization_barrier((came, part))
    parts = [part]
    slabs = jnp.concatenate([slabs, came], axis=0)
    images = exchange(slabs, third)
    last = exchange(slabs, second, third)
    came = exchange(slabs, second)
    *part, served = attend(range(split, rows), given, *in_hbm(served_value_weight), [slabs])
    came, part, hid_other, owner_rank = lax.optimization_barrier(
        (came, part, hid_other, owner_rank)
    )
    parts.append(part)
    slabs = jnp.concatenate([slabs, came], axis=0)
    features = jnp.concatenate([hidden_in, hid_other], axis=1)
    features = jnp.where(core == 0, features, jnp.concatenate([hid_other, hidden_in], axis=1))

    slab = jnp.arange(n, dtype=jnp.int32)
    sources = []
    for way in ways:
        source = replica
        for step, bit in enumerate(way):
            source = source ^ (((slab >> step) & 1) * bit)
        sources.append(source)
    mine = jnp.where(core == 0, sources[0], sources[1])
    theirs = jnp.where(core == 0, sources[1], sources[0])
    source = jnp.concatenate([mine, theirs])
    half = jnp.concatenate([jnp.full((n,), core), jnp.full((n,), 1 - core)])
    place = jnp.sum(jnp.where(owner_rank[None, :] == source[:, None], slab[None, :], 0), axis=1)
    start = (place * full + half * width).astype(jnp.int32)[None]

    row = jnp.arange(rank, dtype=jnp.int32)
    row_source = replica
    for step in range(len(bits)):
        bit = jnp.where(core == 0, ways[0][step], ways[1][step])
        row_source = row_source ^ (((row // per >> step) & 1) * bit)
    pick = jnp.where(
        row[:, None] == (row_source * per + row % per)[None, :], ADAPTER_SCALE, 0.0
    ).astype(jnp.bfloat16)

    context, own_weight = (
        jnp.concatenate(pair, axis=0).reshape(queries.shape) for pair in zip(*parts)
    )
    crossed, start = lax.optimization_barrier((slabs, start))
    crossed = [lax.ppermute(x, "tensor", swap) for x in (crossed, images)]
    crossed = jnp.concatenate(crossed, axis=0)
    last, start, pick, context, own_weight, features, crossed = lax.optimization_barrier(
        (last, start, pick, context, own_weight, features, crossed)
    )
    last_crossed = lax.ppermute(last, "tensor", swap)
    last = jnp.concatenate([images, last], axis=0)
    merged, total, up, left = merge(per, start, pick, features, served, slabs, crossed, last)
    return tuple(
        finish(
            start, up, features, served, left, last_crossed, merged, total, context, own_weight
        )
    )


def solution(mesh):
    in_specs = (
        P(("groups", "replica"), "tensor"),
        P(("groups", "replica"), "tensor"),
        P(("groups", "replica"), None, "tensor"),
        P(("groups", "replica"), None, "tensor"),
        P(("groups", "replica"), "tensor"),
        P(("groups", "replica")),
        P(None, "tensor"),
        P("groups", "replica"),
        P(("groups", "replica"), "tensor"),
        P("groups"),
    )
    out_specs = (
        P("groups", "tensor"),
        P(("groups", "replica"), "tensor"),
        P(("groups", "replica"), "tensor"),
    )
    return jax.shard_map(body, mesh=mesh, in_specs=in_specs, out_specs=out_specs, check_vma=False)
```

```python
import functools

import jax
import jax.numpy as jnp
from jax import lax
from jax.experimental import pallas as pl
from jax.experimental.pallas import tpu as pltpu
from jax.sharding import PartitionSpec as P

HEAD_SIZE = 128
ADAPTER_SCALE = 2.0
PANEL = 128

SMEM = pl.BlockSpec(memory_space=pltpu.SMEM)
VMEM = pl.BlockSpec(memory_space=pltpu.VMEM)
HBM = pl.BlockSpec(memory_space=pltpu.HBM)


def in_hbm(*arrays):
    return [pltpu.with_memory_space_constraint(x, pltpu.HBM) for x in arrays]


def attend_kernel(rows, fetch, lengths_hbm, q_hbm, own_k_hbm, k_hbm, v_hbm, *rest):
    rest = list(rest)
    if fetch:
        served_hbm, served_ref, served_sem = rest.pop(0), rest.pop(-10), rest.pop(-1)
    context_ref, own_weight_ref, lengths, q_ref, own_k_ref, k_buf, v_buf, small_sem, k_sem, v_sem = (
        rest[-10:]
    )
    smalls = [
        pltpu.make_async_copy(source, into, small_sem.at[i])
        for i, (source, into) in enumerate(
            [(lengths_hbm, lengths), (q_hbm, q_ref), (own_k_hbm, own_k_ref)]
        )
    ]
    for copy in smalls:
        copy.start()

    def copies(i, row):
        return (
            pltpu.make_async_copy(k_hbm.at[row], k_buf.at[i], k_sem.at[i]),
            pltpu.make_async_copy(v_hbm.at[row], v_buf.at[i], v_sem.at[i]),
        )

    for i, row in enumerate(rows):
        for copy in copies(i, row):
            copy.start()
    if fetch:
        get_served = pltpu.make_async_copy(served_hbm, served_ref, served_sem)
        get_served.start()
    for copy in smalls:
        copy.wait()
    queries = q_ref[...].astype(jnp.float32)
    own_keys = own_k_ref[...].astype(jnp.float32)
    heads = queries.shape[1] // HEAD_SIZE
    cache_len, width = k_buf.shape[1:]
    local_heads = width // HEAD_SIZE
    group = heads // local_heads
    scaling = 1.0 / HEAD_SIZE**0.5
    head_of = lax.broadcasted_iota(jnp.int32, (heads, HEAD_SIZE), 0) // group
    position = lax.broadcasted_iota(jnp.int32, (heads, cache_len), 1)
    for i, row in enumerate(rows):
        q = jnp.concatenate(
            [
                queries[row : row + 1, h * HEAD_SIZE : (h + 1) * HEAD_SIZE]
                for h in range(heads)
            ],
            axis=0,
        )
        spread = jnp.concatenate(
            [jnp.where(head_of == h, q, 0.0) for h in range(local_heads)], axis=1
        )
        own = jnp.sum(spread * own_keys[row : row + 1], axis=1, keepdims=True) * scaling
        get_keys, get_values = copies(i, row)
        get_keys.wait()
        scores = (
            lax.dot_general(
                spread.astype(jnp.bfloat16), k_buf[i], (((1,), (1,)), ((), ())),
                preferred_element_type=jnp.float32,
            )
            * scaling
        )
        valid = position < lengths[row]
        masked = jnp.where(valid, scores, -1e30)
        largest = jnp.maximum(jnp.max(masked, axis=1, keepdims=True), own)
        cached_exp = jnp.where(valid, jnp.exp(masked - largest), 0.0)
        own_exp = jnp.exp(own - largest)
        normaliser = jnp.sum(cached_exp, axis=1, keepdims=True) + own_exp
        weights = (cached_exp / normaliser).astype(jnp.bfloat16)
        weight_own = (own_exp / normaliser).astype(jnp.bfloat16).astype(jnp.float32)
        get_values.wait()
        wide = jnp.dot(weights, v_buf[i], preferred_element_type=jnp.float32)
        context = wide[:, :HEAD_SIZE]
        for h in range(1, local_heads):
            context = jnp.where(
                head_of == h, wide[:, h * HEAD_SIZE : (h + 1) * HEAD_SIZE], context
            )
        context_ref[i] = context
        own_weight_ref[i] = jnp.broadcast_to(weight_own, (heads, HEAD_SIZE))
    if fetch:
        get_served.wait()


def attend(rows, given, served=None, after=()):
    lengths, queries, own_key, stored_keys, stored_values = given
    fetch = served is not None
    cache_len, width = stored_keys.shape[1:]
    heads = queries.shape[1] // HEAD_SIZE
    count = len(rows)
    out_shape = [jax.ShapeDtypeStruct((count, heads, HEAD_SIZE), jnp.float32)] * 2
    if fetch:
        out_shape += [jax.ShapeDtypeStruct(served.shape, served.dtype)]
    return pl.pallas_call(
        functools.partial(attend_kernel, rows, fetch),
        out_shape=out_shape,
        in_specs=[HBM] * (5 + fetch) + [pl.BlockSpec(memory_space=pl.ANY)] * len(after),
        out_specs=[VMEM] * len(out_shape),
        scratch_shapes=[
            pltpu.SMEM(lengths.shape, jnp.int32),
            pltpu.VMEM(queries.shape, jnp.bfloat16),
            pltpu.VMEM(own_key.shape, jnp.bfloat16),
            pltpu.VMEM((count, cache_len, width), jnp.bfloat16),
            pltpu.VMEM((count, cache_len, width), jnp.bfloat16),
            pltpu.SemaphoreType.DMA((3,)),
            pltpu.SemaphoreType.DMA((count,)),
            pltpu.SemaphoreType.DMA((count,)),
        ]
        + [pltpu.SemaphoreType.DMA] * fetch,
        compiler_params=pltpu.CompilerParams(vmem_limit_bytes=12 * 2**20),
        cost_estimate=pl.CostEstimate(
            flops=4 * count * heads * cache_len * width,
            bytes_accessed=4 * count * cache_len * width,
            transcendentals=count * heads * cache_len,
        ),
        name="attend_cache",
    )(*given, *([served] if fetch else []), *after)


class Merge:
    def __init__(self, start_ref, merged, out_sem, width):
        self.start, self.merged, self.out_sem, self.width = start_ref[...], merged, out_sem, width
        self.entry = lax.broadcasted_iota(jnp.int32, self.start.shape, 1)

    def rows_of(self, entry):
        first = jnp.sum(jnp.where(self.entry == entry, self.start, 0))
        return pl.ds(pl.multiple_of(first, self.width), self.width)

    def store(self, source, rows, at):
        return pltpu.make_async_copy(source, self.merged.at[rows], self.out_sem.at[at])

    def rows(self, slab, up, served_ref, features_ref, rows, total):
        rank = up.shape[0]
        block = jnp.concatenate(
            [slab[i * rank : (i + 1) * rank] for i in range(self.width // PANEL)], axis=1
        )
        update = lax.dot_general(
            block, up, (((0,), (0,)), ((), ())), preferred_element_type=jnp.float32
        )
        fold = (served_ref[rows, :].astype(jnp.float32) + update).astype(jnp.bfloat16)
        part = jnp.dot(features_ref[:, rows], fold, preferred_element_type=jnp.float32)
        return fold, total + part


def merge_kernel(per, left, start_ref, pick_ref, features_ref, served_ref, slabs_ref, crossed_ref,
                 last_ref, merged, total_ref, up_ref, left_ref, m_buf, out_sem):
    width = m_buf.shape[1]
    rank, cols = up_ref.shape
    merge = Merge(start_ref, merged, out_sem, width)
    ups = []
    for ref in (slabs_ref, last_ref):
        for k in range(ref.shape[0]):
            below = ref[k, rank * (width // PANEL) :].astype(jnp.float32)
            ups.append(
                jnp.concatenate(
                    [below[i * per : (i + 1) * per] for i in range(cols // PANEL)], axis=1
                )
            )
    ups = jnp.concatenate(ups, axis=0).astype(jnp.bfloat16)
    up = jnp.dot(pick_ref[...], ups, preferred_element_type=jnp.float32).astype(jnp.bfloat16)
    up_ref[...] = up
    total = jnp.zeros(total_ref.shape, jnp.float32)
    refs = (slabs_ref, last_ref, crossed_ref)
    slabs = [ref.at[k] for ref in refs for k in range(ref.shape[0])]
    keep = len(slabs) - left
    stores = []
    for i, slab in enumerate(slabs):
        rows = merge.rows_of(i)
        fold, total = merge.rows(slab, up, served_ref, features_ref, rows, total)
        if i < keep:
            m_buf[i] = fold
            stores.append(merge.store(m_buf.at[i], rows, i))
            stores[-1].start()
        else:
            left_ref[i - keep] = fold
    total_ref[...] = total
    for store in stores:
        store.wait()


def final_kernel(start_ref, up_ref, features_ref, served_ref, left_ref, last_ref, merged_in,
                 total_ref, context_ref, own_weight_ref, merged, fresh_hbm, attended_hbm, m_buf,
                 out_sem, fresh_ref, attended_ref, small_sem):
    del merged_in
    count, width = last_ref.shape[0], m_buf.shape[1]
    left = left_ref.shape[0]
    merge = Merge(start_ref, merged, out_sem, width)
    first = start_ref.shape[1] - count
    total = total_ref[...]
    stores = [
        merge.store(left_ref.at[k], merge.rows_of(first - left + k), count + k)
        for k in range(left)
    ]
    for store in stores:
        store.start()
    for i in range(count):
        rows = merge.rows_of(first + i)
        fold, total = merge.rows(last_ref.at[i], up_ref[...], served_ref, features_ref, rows, total)
        m_buf[i] = fold
        stores.append(merge.store(m_buf.at[i], rows, i))
        stores[-1].start()
    fresh = total.astype(jnp.bfloat16)
    fresh_ref[...] = fresh
    put_fresh = pltpu.make_async_copy(fresh_ref, fresh_hbm, small_sem.at[0])
    put_fresh.start()
    value = fresh.astype(jnp.float32)
    heads = attended_ref.shape[1] // HEAD_SIZE
    group = heads // (fresh_ref.shape[1] // HEAD_SIZE)
    for h in range(heads):
        cols = slice(h * HEAD_SIZE, (h + 1) * HEAD_SIZE)
        at = (h // group) * HEAD_SIZE
        attended_ref[:, cols] = (
            context_ref[:, cols] + own_weight_ref[:, cols] * value[:, at : at + HEAD_SIZE]
        ).astype(jnp.bfloat16)
    put_attended = pltpu.make_async_copy(attended_ref, attended_hbm, small_sem.at[1])
    put_attended.start()
    for store in stores:
        store.wait()
    put_fresh.wait()
    put_attended.wait()


def merge(per, start, pick, features, served, slabs, crossed, last):
    left = 3
    count = slabs.shape[0] + crossed.shape[0] + last.shape[0]
    rank = pick.shape[0]
    depth, cols = served.shape
    width = depth // start.shape[1]
    return pl.pallas_call(
        functools.partial(merge_kernel, per, left),
        out_shape=(
            jax.ShapeDtypeStruct((depth, cols), jnp.bfloat16),
            jax.ShapeDtypeStruct((features.shape[0], cols), jnp.float32),
            jax.ShapeDtypeStruct((rank, cols), jnp.bfloat16),
            jax.ShapeDtypeStruct((left, width, cols), jnp.bfloat16),
        ),
        in_specs=[VMEM] * 7,
        out_specs=(HBM, VMEM, VMEM, VMEM),
        scratch_shapes=[
            pltpu.VMEM((count - left, width, cols), jnp.bfloat16),
            pltpu.SemaphoreType.DMA((count - left,)),
        ],
        compiler_params=pltpu.CompilerParams(vmem_limit_bytes=12 * 2**20),
        cost_estimate=pl.CostEstimate(
            flops=2 * count * width * cols * rank,
            bytes_accessed=4 * count * width * cols,
            transcendentals=0,
        ),
        name="merge_blocks",
    )(start, pick, features, served, slabs, crossed, last)


def finish(start, up, features, served, left, last, merged, total, context, own_weight):
    count = last.shape[0]
    depth, cols = served.shape
    width = depth // start.shape[1]
    smalls = [total.shape, context.shape]
    return pl.pallas_call(
        final_kernel,
        out_shape=[
            jax.ShapeDtypeStruct(shape, jnp.bfloat16) for shape in [(depth, cols), *smalls]
        ],
        in_specs=[VMEM] * 6 + [HBM] + [VMEM] * 3,
        out_specs=[HBM] * 3,
        input_output_aliases={6: 0},
        scratch_shapes=[
            pltpu.VMEM((count, width, cols), jnp.bfloat16),
            pltpu.SemaphoreType.DMA((count + left.shape[0],)),
        ]
        + [pltpu.VMEM(shape, jnp.bfloat16) for shape in smalls]
        + [pltpu.SemaphoreType.DMA((2,))],
        compiler_params=pltpu.CompilerParams(vmem_limit_bytes=12 * 2**20),
        cost_estimate=pl.CostEstimate(
            flops=2 * count * width * cols * up.shape[0],
            bytes_accessed=4 * count * width * cols,
            transcendentals=0,
        ),
        name="finish_rows",
    )(start, up, features, served, left, last, merged, total, context, own_weight)


def panels(x):
    return [x[:, i : i + PANEL] for i in range(0, x.shape[1], PANEL)]


def body(
    hidden_in,
    queries,
    stored_keys,
    stored_values,
    fresh_token_key,
    lengths,
    served_value_weight,
    adapter_in,
    adapter_out,
    owner_rank,
):
    n = lax.axis_size("replica")
    replica = lax.axis_index("replica")
    core = lax.axis_index("tensor")
    swap = [(0, 1), (1, 0)]
    full = adapter_in.shape[1]
    width = full // 2
    rows = queries.shape[0]
    per, cols = adapter_out.shape
    rank = n * per

    bits = [n >> i for i in range(1, n.bit_length())]
    ways = [bits[:-2] + bits[:-3:-1], bits]

    def exchange(x, *steps):
        pairs = [
            (2 * i + c, 2 * (i ^ sum(ways[c][step] for step in steps)) + c)
            for i in range(n)
            for c in range(2)
        ]
        return lax.ppermute(x, ("replica", "tensor"), pairs)

    below = jnp.concatenate(panels(adapter_out), axis=0)
    below = jnp.pad(below, ((0, -below.shape[0] % 8), (0, 0)))
    block = lax.dynamic_slice_in_dim(adapter_in, core * width, width, axis=1)
    block, below = lax.optimization_barrier((block, below))
    slabs = jnp.concatenate([*panels(block), below], axis=0)[None]

    given = in_hbm(lengths, queries, fresh_token_key, stored_keys, stored_values)
    *early, first, second, third = range(len(bits))
    for step in early:
        slabs = jnp.concatenate([slabs, exchange(slabs, step)], axis=0)

    split = rows // 2
    hid_other = lax.ppermute(hidden_in, "tensor", swap)
    came = exchange(slabs, first)
    part = attend(range(split), given, after=[slabs])
    came, part = lax.optimization_barrier((came, part))
    parts = [part]
    slabs = jnp.concatenate([slabs, came], axis=0)
    images = exchange(slabs, third)
    last = exchange(slabs, second, third)
    came = exchange(slabs, second)
    *part, served = attend(range(split, rows), given, *in_hbm(served_value_weight), [slabs])
    came, part, hid_other, owner_rank = lax.optimization_barrier(
        (came, part, hid_other, owner_rank)
    )
    parts.append(part)
    slabs = jnp.concatenate([slabs, came], axis=0)
    features = jnp.concatenate([hidden_in, hid_other], axis=1)
    features = jnp.where(core == 0, features, jnp.concatenate([hid_other, hidden_in], axis=1))

    slab = jnp.arange(n, dtype=jnp.int32)
    sources = []
    for way in ways:
        source = replica
        for step, bit in enumerate(way):
            source = source ^ (((slab >> step) & 1) * bit)
        sources.append(source)
    mine = jnp.where(core == 0, sources[0], sources[1])
    theirs = jnp.where(core == 0, sources[1], sources[0])
    source = jnp.concatenate([mine, theirs])
    half = jnp.concatenate([jnp.full((n,), core), jnp.full((n,), 1 - core)])
    place = jnp.sum(jnp.where(owner_rank[None, :] == source[:, None], slab[None, :], 0), axis=1)
    start = (place * full + half * width).astype(jnp.int32)[None]

    row = jnp.arange(rank, dtype=jnp.int32)
    row_source = replica
    for step in range(len(bits)):
        bit = jnp.where(core == 0, ways[0][step], ways[1][step])
        row_source = row_source ^ (((row // per >> step) & 1) * bit)
    pick = jnp.where(
        row[:, None] == (row_source * per + row % per)[None, :], ADAPTER_SCALE, 0.0
    ).astype(jnp.bfloat16)

    context, own_weight = (
        jnp.concatenate(pair, axis=0).reshape(queries.shape) for pair in zip(*parts)
    )
    crossed, start = lax.optimization_barrier((slabs, start))
    crossed = [lax.ppermute(x, "tensor", swap) for x in (crossed, images)]
    crossed = jnp.concatenate(crossed, axis=0)
    last, start, pick, context, own_weight, features, crossed = lax.optimization_barrier(
        (last, start, pick, context, own_weight, features, crossed)
    )
    last_crossed = lax.ppermute(last, "tensor", swap)
    last = jnp.concatenate([images, last], axis=0)
    merged, total, up, left = merge(per, start, pick, features, served, slabs, crossed, last)
    return tuple(
        finish(
            start, up, features, served, left, last_crossed, merged, total, context, own_weight
        )
    )


def solution(mesh):
    in_specs = (
        P(("groups", "replica"), "tensor"),
        P(("groups", "replica"), "tensor"),
        P(("groups", "replica"), None, "tensor"),
        P(("groups", "replica"), None, "tensor"),
        P(("groups", "replica"), "tensor"),
        P(("groups", "replica")),
        P(None, "tensor"),
        P("groups", "replica"),
        P(("groups", "replica"), "tensor"),
        P("groups"),
    )
    out_specs = (
        P("groups", "tensor"),
        P(("groups", "replica"), "tensor"),
        P(("groups", "replica"), "tensor"),
    )
    return jax.shard_map(body, mesh=mesh, in_specs=in_specs, out_specs=out_specs, check_vma=False)
```

```python
import functools

import jax
import jax.numpy as jnp
from jax import lax
from jax.experimental import pallas as pl
from jax.experimental.pallas import tpu as pltpu
from jax.sharding import PartitionSpec as P

HEAD_SIZE = 128
ADAPTER_SCALE = 2.0
PANEL = 128

SMEM = pl.BlockSpec(memory_space=pltpu.SMEM)
VMEM = pl.BlockSpec(memory_space=pltpu.VMEM)
HBM = pl.BlockSpec(memory_space=pltpu.HBM)


def in_hbm(*arrays):
    return [pltpu.with_memory_space_constraint(x, pltpu.HBM) for x in arrays]


def attend_kernel(rows, fetch, lengths_hbm, q_hbm, own_k_hbm, k_hbm, v_hbm, *rest):
    rest = list(rest)
    if fetch:
        served_hbm, served_ref, served_sem = rest.pop(0), rest.pop(-10), rest.pop(-1)
    context_ref, own_weight_ref, lengths, q_ref, own_k_ref, k_buf, v_buf, small_sem, k_sem, v_sem = (
        rest[-10:]
    )
    smalls = [
        pltpu.make_async_copy(source, into, small_sem.at[i])
        for i, (source, into) in enumerate(
            [(lengths_hbm, lengths), (q_hbm, q_ref), (own_k_hbm, own_k_ref)]
        )
    ]
    for copy in smalls:
        copy.start()

    def copies(i, row):
        return (
            pltpu.make_async_copy(k_hbm.at[row], k_buf.at[i], k_sem.at[i]),
            pltpu.make_async_copy(v_hbm.at[row], v_buf.at[i], v_sem.at[i]),
        )

    for i, row in enumerate(rows):
        for copy in copies(i, row):
            copy.start()
    if fetch:
        get_served = pltpu.make_async_copy(served_hbm, served_ref, served_sem)
        get_served.start()
    for copy in smalls:
        copy.wait()
    queries = q_ref[...].astype(jnp.float32)
    own_keys = own_k_ref[...].astype(jnp.float32)
    heads = queries.shape[1] // HEAD_SIZE
    cache_len, width = k_buf.shape[1:]
    local_heads = width // HEAD_SIZE
    group = heads // local_heads
    scaling = 1.0 / HEAD_SIZE**0.5
    head_of = lax.broadcasted_iota(jnp.int32, (heads, HEAD_SIZE), 0) // group
    position = lax.broadcasted_iota(jnp.int32, (heads, cache_len), 1)
    for i, row in enumerate(rows):
        q = jnp.concatenate(
            [
                queries[row : row + 1, h * HEAD_SIZE : (h + 1) * HEAD_SIZE]
                for h in range(heads)
            ],
            axis=0,
        )
        spread = jnp.concatenate(
            [jnp.where(head_of == h, q, 0.0) for h in range(local_heads)], axis=1
        )
        own = jnp.sum(spread * own_keys[row : row + 1], axis=1, keepdims=True) * scaling
        get_keys, get_values = copies(i, row)
        get_keys.wait()
        scores = (
            lax.dot_general(
                spread.astype(jnp.bfloat16), k_buf[i], (((1,), (1,)), ((), ())),
                preferred_element_type=jnp.float32,
            )
            * scaling
        )
        valid = position < lengths[row]
        masked = jnp.where(valid, scores, -1e30)
        largest = jnp.maximum(jnp.max(masked, axis=1, keepdims=True), own)
        cached_exp = jnp.where(valid, jnp.exp(masked - largest), 0.0)
        own_exp = jnp.exp(own - largest)
        normaliser = jnp.sum(cached_exp, axis=1, keepdims=True) + own_exp
        weights = (cached_exp / normaliser).astype(jnp.bfloat16)
        weight_own = (own_exp / normaliser).astype(jnp.bfloat16).astype(jnp.float32)
        get_values.wait()
        wide = jnp.dot(weights, v_buf[i], preferred_element_type=jnp.float32)
        context = wide[:, :HEAD_SIZE]
        for h in range(1, local_heads):
            context = jnp.where(
                head_of == h, wide[:, h * HEAD_SIZE : (h + 1) * HEAD_SIZE], context
            )
        context_ref[i] = context
        own_weight_ref[i] = jnp.broadcast_to(weight_own, (heads, HEAD_SIZE))
    if fetch:
        get_served.wait()


def attend(rows, given, served=None, after=()):
    lengths, queries, own_key, stored_keys, stored_values = given
    fetch = served is not None
    cache_len, width = stored_keys.shape[1:]
    heads = queries.shape[1] // HEAD_SIZE
    count = len(rows)
    out_shape = [jax.ShapeDtypeStruct((count, heads, HEAD_SIZE), jnp.float32)] * 2
    if fetch:
        out_shape += [jax.ShapeDtypeStruct(served.shape, served.dtype)]
    return pl.pallas_call(
        functools.partial(attend_kernel, rows, fetch),
        out_shape=out_shape,
        in_specs=[HBM] * (5 + fetch) + [pl.BlockSpec(memory_space=pl.ANY)] * len(after),
        out_specs=[VMEM] * len(out_shape),
        scratch_shapes=[
            pltpu.SMEM(lengths.shape, jnp.int32),
            pltpu.VMEM(queries.shape, jnp.bfloat16),
            pltpu.VMEM(own_key.shape, jnp.bfloat16),
            pltpu.VMEM((count, cache_len, width), jnp.bfloat16),
            pltpu.VMEM((count, cache_len, width), jnp.bfloat16),
            pltpu.SemaphoreType.DMA((3,)),
            pltpu.SemaphoreType.DMA((count,)),
            pltpu.SemaphoreType.DMA((count,)),
        ]
        + [pltpu.SemaphoreType.DMA] * fetch,
        compiler_params=pltpu.CompilerParams(vmem_limit_bytes=12 * 2**20),
        cost_estimate=pl.CostEstimate(
            flops=4 * count * heads * cache_len * width,
            bytes_accessed=4 * count * cache_len * width,
            transcendentals=count * heads * cache_len,
        ),
        name="attend_cache",
    )(*given, *([served] if fetch else []), *after)


class Merge:
    def __init__(self, start_ref, merged, out_sem, width):
        self.start, self.merged, self.out_sem, self.width = start_ref[...], merged, out_sem, width
        self.entry = lax.broadcasted_iota(jnp.int32, self.start.shape, 1)

    def rows_of(self, entry):
        first = jnp.sum(jnp.where(self.entry == entry, self.start, 0))
        return pl.ds(pl.multiple_of(first, self.width), self.width)

    def store(self, source, rows, at):
        return pltpu.make_async_copy(source, self.merged.at[rows], self.out_sem.at[at])

    def rows(self, slab, up, served_ref, features_ref, rows, total):
        rank = up.shape[0]
        block = jnp.concatenate(
            [slab[i * rank : (i + 1) * rank] for i in range(self.width // PANEL)], axis=1
        )
        update = lax.dot_general(
            block, up, (((0,), (0,)), ((), ())), preferred_element_type=jnp.float32
        )
        fold = (served_ref[rows, :].astype(jnp.float32) + update).astype(jnp.bfloat16)
        part = jnp.dot(features_ref[:, rows], fold, preferred_element_type=jnp.float32)
        return fold, total + part


def merge_kernel(per, left, start_ref, pick_ref, features_ref, served_ref, slabs_ref, crossed_ref,
                 last_ref, merged, total_ref, up_ref, left_ref, m_buf, out_sem):
    width = m_buf.shape[1]
    rank, cols = up_ref.shape
    merge = Merge(start_ref, merged, out_sem, width)
    ups = []
    for ref in (slabs_ref, last_ref):
        for k in range(ref.shape[0]):
            below = ref[k, rank * (width // PANEL) :].astype(jnp.float32)
            ups.append(
                jnp.concatenate(
                    [below[i * per : (i + 1) * per] for i in range(cols // PANEL)], axis=1
                )
            )
    ups = jnp.concatenate(ups, axis=0).astype(jnp.bfloat16)
    up = jnp.dot(pick_ref[...], ups, preferred_element_type=jnp.float32).astype(jnp.bfloat16)
    up_ref[...] = up
    total = jnp.zeros(total_ref.shape, jnp.float32)
    refs = (slabs_ref, last_ref, crossed_ref)
    slabs = [ref.at[k] for ref in refs for k in range(ref.shape[0])]
    keep = len(slabs) - left
    stores = []
    for i, slab in enumerate(slabs):
        rows = merge.rows_of(i)
        fold, total = merge.rows(slab, up, served_ref, features_ref, rows, total)
        if i < keep:
            m_buf[i] = fold
            stores.append(merge.store(m_buf.at[i], rows, i))
            stores[-1].start()
        else:
            left_ref[i - keep] = fold
    total_ref[...] = total
    for store in stores:
        store.wait()


def final_kernel(start_ref, up_ref, features_ref, served_ref, left_ref, last_ref, merged_in,
                 total_ref, context_ref, own_weight_ref, merged, fresh_hbm, attended_hbm, m_buf,
                 out_sem, fresh_ref, attended_ref, small_sem):
    del merged_in
    count, width = last_ref.shape[0], m_buf.shape[1]
    left = left_ref.shape[0]
    merge = Merge(start_ref, merged, out_sem, width)
    first = start_ref.shape[1] - count
    total = total_ref[...]
    stores = [
        merge.store(left_ref.at[k], merge.rows_of(first - left + k), count + k)
        for k in range(left)
    ]
    for store in stores:
        store.start()
    for i in range(count):
        rows = merge.rows_of(first + i)
        fold, total = merge.rows(last_ref.at[i], up_ref[...], served_ref, features_ref, rows, total)
        m_buf[i] = fold
        stores.append(merge.store(m_buf.at[i], rows, i))
        stores[-1].start()
    fresh = total.astype(jnp.bfloat16)
    fresh_ref[...] = fresh
    put_fresh = pltpu.make_async_copy(fresh_ref, fresh_hbm, small_sem.at[0])
    put_fresh.start()
    value = fresh.astype(jnp.float32)
    heads = attended_ref.shape[1] // HEAD_SIZE
    group = heads // (fresh_ref.shape[1] // HEAD_SIZE)
    for h in range(heads):
        cols = slice(h * HEAD_SIZE, (h + 1) * HEAD_SIZE)
        at = (h // group) * HEAD_SIZE
        attended_ref[:, cols] = (
            context_ref[:, cols] + own_weight_ref[:, cols] * value[:, at : at + HEAD_SIZE]
        ).astype(jnp.bfloat16)
    put_attended = pltpu.make_async_copy(attended_ref, attended_hbm, small_sem.at[1])
    put_attended.start()
    for store in stores:
        store.wait()
    put_fresh.wait()
    put_attended.wait()


def merge(per, start, pick, features, served, slabs, crossed, last):
    left = 3
    count = slabs.shape[0] + crossed.shape[0] + last.shape[0]
    rank = pick.shape[0]
    depth, cols = served.shape
    width = depth // start.shape[1]
    return pl.pallas_call(
        functools.partial(merge_kernel, per, left),
        out_shape=(
            jax.ShapeDtypeStruct((depth, cols), jnp.bfloat16),
            jax.ShapeDtypeStruct((features.shape[0], cols), jnp.float32),
            jax.ShapeDtypeStruct((rank, cols), jnp.bfloat16),
            jax.ShapeDtypeStruct((left, width, cols), jnp.bfloat16),
        ),
        in_specs=[VMEM] * 7,
        out_specs=(HBM, VMEM, VMEM, VMEM),
        scratch_shapes=[
            pltpu.VMEM((count - left, width, cols), jnp.bfloat16),
            pltpu.SemaphoreType.DMA((count - left,)),
        ],
        compiler_params=pltpu.CompilerParams(vmem_limit_bytes=12 * 2**20),
        cost_estimate=pl.CostEstimate(
            flops=2 * count * width * cols * rank,
            bytes_accessed=4 * count * width * cols,
            transcendentals=0,
        ),
        name="merge_blocks",
    )(start, pick, features, served, slabs, crossed, last)


def finish(start, up, features, served, left, last, merged, total, context, own_weight):
    count = last.shape[0]
    depth, cols = served.shape
    width = depth // start.shape[1]
    smalls = [total.shape, context.shape]
    return pl.pallas_call(
        final_kernel,
        out_shape=[
            jax.ShapeDtypeStruct(shape, jnp.bfloat16) for shape in [(depth, cols), *smalls]
        ],
        in_specs=[VMEM] * 6 + [HBM] + [VMEM] * 3,
        out_specs=[HBM] * 3,
        input_output_aliases={6: 0},
        scratch_shapes=[
            pltpu.VMEM((count, width, cols), jnp.bfloat16),
            pltpu.SemaphoreType.DMA((count + left.shape[0],)),
        ]
        + [pltpu.VMEM(shape, jnp.bfloat16) for shape in smalls]
        + [pltpu.SemaphoreType.DMA((2,))],
        compiler_params=pltpu.CompilerParams(vmem_limit_bytes=12 * 2**20),
        cost_estimate=pl.CostEstimate(
            flops=2 * count * width * cols * up.shape[0],
            bytes_accessed=4 * count * width * cols,
            transcendentals=0,
        ),
        name="finish_rows",
    )(start, up, features, served, left, last, merged, total, context, own_weight)


def panels(x):
    return [x[:, i : i + PANEL] for i in range(0, x.shape[1], PANEL)]


def body(
    hidden_in,
    queries,
    stored_keys,
    stored_values,
    fresh_token_key,
    lengths,
    served_value_weight,
    adapter_in,
    adapter_out,
    owner_rank,
):
    n = lax.axis_size("replica")
    replica = lax.axis_index("replica")
    core = lax.axis_index("tensor")
    swap = [(0, 1), (1, 0)]
    full = adapter_in.shape[1]
    width = full // 2
    rows = queries.shape[0]
    per, cols = adapter_out.shape
    rank = n * per

    bits = [n >> i for i in range(1, n.bit_length())]
    ways = [bits, bits[:-2] + bits[:-3:-1]]

    def exchange(x, *steps):
        pairs = [
            (2 * i + c, 2 * (i ^ sum(ways[c][step] for step in steps)) + c)
            for i in range(n)
            for c in range(2)
        ]
        return lax.ppermute(x, ("replica", "tensor"), pairs)

    below = jnp.concatenate(panels(adapter_out), axis=0)
    below = jnp.pad(below, ((0, -below.shape[0] % 8), (0, 0)))
    block = lax.dynamic_slice_in_dim(adapter_in, core * width, width, axis=1)
    block, below = lax.optimization_barrier((block, below))
    slabs = jnp.concatenate([*panels(block), below], axis=0)[None]

    given = in_hbm(lengths, queries, fresh_token_key, stored_keys, stored_values)
    *early, first, second, third = range(len(bits))
    for step in early:
        slabs = jnp.concatenate([slabs, exchange(slabs, step)], axis=0)

    split = rows // 2
    hid_other = lax.ppermute(hidden_in, "tensor", swap)
    came = exchange(slabs, first)
    part = attend(range(split), given, after=[slabs])
    came, part = lax.optimization_barrier((came, part))
    parts = [part]
    slabs = jnp.concatenate([slabs, came], axis=0)
    last = exchange(slabs, second, third)
    images = exchange(slabs, third)
    came = exchange(slabs, second)
    *part, served = attend(range(split, rows), given, *in_hbm(served_value_weight), [slabs])
    came, part, hid_other, owner_rank = lax.optimization_barrier(
        (came, part, hid_other, owner_rank)
    )
    parts.append(part)
    slabs = jnp.concatenate([slabs, came], axis=0)
    features = jnp.concatenate([hidden_in, hid_other], axis=1)
    features = jnp.where(core == 0, features, jnp.concatenate([hid_other, hidden_in], axis=1))

    slab = jnp.arange(n, dtype=jnp.int32)
    sources = []
    for way in ways:
        source = replica
        for step, bit in enumerate(way):
            source = source ^ (((slab >> step) & 1) * bit)
        sources.append(source)
    mine = jnp.where(core == 0, sources[0], sources[1])
    theirs = jnp.where(core == 0, sources[1], sources[0])
    source = jnp.concatenate([mine, theirs])
    half = jnp.concatenate([jnp.full((n,), core), jnp.full((n,), 1 - core)])
    place = jnp.sum(jnp.where(owner_rank[None, :] == source[:, None], slab[None, :], 0), axis=1)
    start = (place * full + half * width).astype(jnp.int32)[None]

    row = jnp.arange(rank, dtype=jnp.int32)
    row_source = replica
    for step in range(len(bits)):
        bit = jnp.where(core == 0, ways[0][step], ways[1][step])
        row_source = row_source ^ (((row // per >> step) & 1) * bit)
    pick = jnp.where(
        row[:, None] == (row_source * per + row % per)[None, :], ADAPTER_SCALE, 0.0
    ).astype(jnp.bfloat16)

    context, own_weight = (
        jnp.concatenate(pair, axis=0).reshape(queries.shape) for pair in zip(*parts)
    )
    crossed, start = lax.optimization_barrier((slabs, start))
    crossed = lax.ppermute(crossed, "tensor", swap)
    last, start, pick, context, own_weight, features, crossed = lax.optimization_barrier(
        (last, start, pick, context, own_weight, features, crossed)
    )
    last = jnp.concatenate([images, last], axis=0)
    last_crossed = lax.ppermute(last, "tensor", swap)
    merged, total, up, left = merge(per, start, pick, features, served, slabs, crossed, last)
    return tuple(
        finish(
            start, up, features, served, left, last_crossed, merged, total, context, own_weight
        )
    )


def solution(mesh):
    in_specs = (
        P(("groups", "replica"), "tensor"),
        P(("groups", "replica"), "tensor"),
        P(("groups", "replica"), None, "tensor"),
        P(("groups", "replica"), None, "tensor"),
        P(("groups", "replica"), "tensor"),
        P(("groups", "replica")),
        P(None, "tensor"),
        P("groups", "replica"),
        P(("groups", "replica"), "tensor"),
        P("groups"),
    )
    out_specs = (
        P("groups", "tensor"),
        P(("groups", "replica"), "tensor"),
        P(("groups", "replica"), "tensor"),
    )
    return jax.shard_map(body, mesh=mesh, in_specs=in_specs, out_specs=out_specs, check_vma=False)
```

```python
import functools

import jax
import jax.numpy as jnp
from jax import lax
from jax.experimental import pallas as pl
from jax.experimental.pallas import tpu as pltpu
from jax.sharding import PartitionSpec as P

HEAD_SIZE = 128
ADAPTER_SCALE = 2.0
PANEL = 128

SMEM = pl.BlockSpec(memory_space=pltpu.SMEM)
VMEM = pl.BlockSpec(memory_space=pltpu.VMEM)
HBM = pl.BlockSpec(memory_space=pltpu.HBM)


def in_hbm(*arrays):
    return [pltpu.with_memory_space_constraint(x, pltpu.HBM) for x in arrays]


def attend_kernel(rows, fetch, lengths_hbm, q_hbm, own_k_hbm, k_hbm, v_hbm, *rest):
    rest = list(rest)
    if fetch:
        served_hbm, served_ref, served_sem = rest.pop(0), rest.pop(-10), rest.pop(-1)
    context_ref, own_weight_ref, lengths, q_ref, own_k_ref, k_buf, v_buf, small_sem, k_sem, v_sem = (
        rest[-10:]
    )
    smalls = [
        pltpu.make_async_copy(source, into, small_sem.at[i])
        for i, (source, into) in enumerate(
            [(lengths_hbm, lengths), (q_hbm, q_ref), (own_k_hbm, own_k_ref)]
        )
    ]
    for copy in smalls:
        copy.start()

    def copies(i, row):
        return (
            pltpu.make_async_copy(k_hbm.at[row], k_buf.at[i], k_sem.at[i]),
            pltpu.make_async_copy(v_hbm.at[row], v_buf.at[i], v_sem.at[i]),
        )

    for i, row in enumerate(rows):
        for copy in copies(i, row):
            copy.start()
    if fetch:
        get_served = pltpu.make_async_copy(served_hbm, served_ref, served_sem)
        get_served.start()
    for copy in smalls:
        copy.wait()
    queries = q_ref[...].astype(jnp.float32)
    own_keys = own_k_ref[...].astype(jnp.float32)
    heads = queries.shape[1] // HEAD_SIZE
    cache_len, width = k_buf.shape[1:]
    local_heads = width // HEAD_SIZE
    group = heads // local_heads
    scaling = 1.0 / HEAD_SIZE**0.5
    head_of = lax.broadcasted_iota(jnp.int32, (heads, HEAD_SIZE), 0) // group
    position = lax.broadcasted_iota(jnp.int32, (heads, cache_len), 1)
    for i, row in enumerate(rows):
        q = jnp.concatenate(
            [
                queries[row : row + 1, h * HEAD_SIZE : (h + 1) * HEAD_SIZE]
                for h in range(heads)
            ],
            axis=0,
        )
        spread = jnp.concatenate(
            [jnp.where(head_of == h, q, 0.0) for h in range(local_heads)], axis=1
        )
        own = jnp.sum(spread * own_keys[row : row + 1], axis=1, keepdims=True) * scaling
        get_keys, get_values = copies(i, row)
        get_keys.wait()
        scores = (
            lax.dot_general(
                spread.astype(jnp.bfloat16), k_buf[i], (((1,), (1,)), ((), ())),
                preferred_element_type=jnp.float32,
            )
            * scaling
        )
        valid = position < lengths[row]
        masked = jnp.where(valid, scores, -1e30)
        largest = jnp.maximum(jnp.max(masked, axis=1, keepdims=True), own)
        cached_exp = jnp.where(valid, jnp.exp(masked - largest), 0.0)
        own_exp = jnp.exp(own - largest)
        normaliser = jnp.sum(cached_exp, axis=1, keepdims=True) + own_exp
        weights = (cached_exp / normaliser).astype(jnp.bfloat16)
        weight_own = (own_exp / normaliser).astype(jnp.bfloat16).astype(jnp.float32)
        get_values.wait()
        wide = jnp.dot(weights, v_buf[i], preferred_element_type=jnp.float32)
        context = wide[:, :HEAD_SIZE]
        for h in range(1, local_heads):
            context = jnp.where(
                head_of == h, wide[:, h * HEAD_SIZE : (h + 1) * HEAD_SIZE], context
            )
        context_ref[i] = context
        own_weight_ref[i] = jnp.broadcast_to(weight_own, (heads, HEAD_SIZE))
    if fetch:
        get_served.wait()


def attend(rows, given, served=None, after=()):
    lengths, queries, own_key, stored_keys, stored_values = given
    fetch = served is not None
    cache_len, width = stored_keys.shape[1:]
    heads = queries.shape[1] // HEAD_SIZE
    count = len(rows)
    out_shape = [jax.ShapeDtypeStruct((count, heads, HEAD_SIZE), jnp.float32)] * 2
    if fetch:
        out_shape += [jax.ShapeDtypeStruct(served.shape, served.dtype)]
    return pl.pallas_call(
        functools.partial(attend_kernel, rows, fetch),
        out_shape=out_shape,
        in_specs=[HBM] * (5 + fetch) + [pl.BlockSpec(memory_space=pl.ANY)] * len(after),
        out_specs=[VMEM] * len(out_shape),
        scratch_shapes=[
            pltpu.SMEM(lengths.shape, jnp.int32),
            pltpu.VMEM(queries.shape, jnp.bfloat16),
            pltpu.VMEM(own_key.shape, jnp.bfloat16),
            pltpu.VMEM((count, cache_len, width), jnp.bfloat16),
            pltpu.VMEM((count, cache_len, width), jnp.bfloat16),
            pltpu.SemaphoreType.DMA((3,)),
            pltpu.SemaphoreType.DMA((count,)),
            pltpu.SemaphoreType.DMA((count,)),
        ]
        + [pltpu.SemaphoreType.DMA] * fetch,
        compiler_params=pltpu.CompilerParams(vmem_limit_bytes=12 * 2**20),
        cost_estimate=pl.CostEstimate(
            flops=4 * count * heads * cache_len * width,
            bytes_accessed=4 * count * cache_len * width,
            transcendentals=count * heads * cache_len,
        ),
        name="attend_cache",
    )(*given, *([served] if fetch else []), *after)


def base_kernel(features_ref, served_ref, after, base_ref):
    del after
    base_ref[...] = jnp.dot(
        features_ref[...], served_ref[...], preferred_element_type=jnp.float32
    )


def base_value(features, served, after):
    rows, depth = features.shape
    cols = served.shape[1]
    return pl.pallas_call(
        base_kernel,
        out_shape=jax.ShapeDtypeStruct((rows, cols), jnp.float32),
        in_specs=[VMEM, VMEM, pl.BlockSpec(memory_space=pl.ANY)],
        out_specs=VMEM,
        compiler_params=pltpu.CompilerParams(vmem_limit_bytes=12 * 2**20),
        cost_estimate=pl.CostEstimate(
            flops=2 * rows * depth * cols, bytes_accessed=0, transcendentals=0
        ),
        name="base_value",
    )(features, served, after)


class Merge:
    def __init__(self, start_ref, merged, out_sem, width):
        self.start, self.merged, self.out_sem, self.width = start_ref[...], merged, out_sem, width
        self.entry = lax.broadcasted_iota(jnp.int32, self.start.shape, 1)

    def rows_of(self, entry):
        first = jnp.sum(jnp.where(self.entry == entry, self.start, 0))
        return pl.ds(pl.multiple_of(first, self.width), self.width)

    def store(self, source, rows, at):
        return pltpu.make_async_copy(source, self.merged.at[rows], self.out_sem.at[at])

    def rows(self, slab, up, served_ref, features_ref, rows, total):
        rank = up.shape[0]
        block = jnp.concatenate(
            [slab[i * rank : (i + 1) * rank] for i in range(self.width // PANEL)], axis=1
        )
        update = lax.dot_general(
            block, up, (((0,), (0,)), ((), ())), preferred_element_type=jnp.float32
        )
        fold = (served_ref[rows, :].astype(jnp.float32) + update).astype(jnp.bfloat16)
        part = lax.dot_general(
            features_ref[:, rows], block, (((1,), (1,)), ((), ())),
            preferred_element_type=jnp.float32,
        )
        return fold, total + part


def merge_kernel(per, left, start_ref, pick_ref, features_ref, served_ref, slabs_ref, crossed_ref,
                 last_ref, merged, total_ref, up_ref, left_ref, m_buf, out_sem):
    width = m_buf.shape[1]
    rank, cols = up_ref.shape
    merge = Merge(start_ref, merged, out_sem, width)
    ups = []
    for ref in (slabs_ref, last_ref):
        for k in range(ref.shape[0]):
            below = ref[k, rank * (width // PANEL) :].astype(jnp.float32)
            ups.append(
                jnp.concatenate(
                    [below[i * per : (i + 1) * per] for i in range(cols // PANEL)], axis=1
                )
            )
    ups = jnp.concatenate(ups, axis=0).astype(jnp.bfloat16)
    up = jnp.dot(pick_ref[...], ups, preferred_element_type=jnp.float32).astype(jnp.bfloat16)
    up_ref[...] = up
    total = jnp.zeros(total_ref.shape, jnp.float32)
    refs = (slabs_ref, last_ref, crossed_ref)
    slabs = [ref.at[k] for ref in refs for k in range(ref.shape[0])]
    keep = len(slabs) - left
    stores = []
    for i, slab in enumerate(slabs):
        rows = merge.rows_of(i)
        fold, total = merge.rows(slab, up, served_ref, features_ref, rows, total)
        if i < keep:
            m_buf[i] = fold
            stores.append(merge.store(m_buf.at[i], rows, i))
            stores[-1].start()
        else:
            left_ref[i - keep] = fold
    total_ref[...] = total
    for store in stores:
        store.wait()


def final_kernel(start_ref, up_ref, features_ref, served_ref, left_ref, last_ref, merged_in,
                 total_ref, context_ref, own_weight_ref, base_ref, merged, fresh_hbm, attended_hbm, m_buf,
                 out_sem, fresh_ref, attended_ref, small_sem):
    del merged_in
    count, width = last_ref.shape[0], m_buf.shape[1]
    left = left_ref.shape[0]
    merge = Merge(start_ref, merged, out_sem, width)
    first = start_ref.shape[1] - count
    total = total_ref[...]
    stores = [
        merge.store(left_ref.at[k], merge.rows_of(first - left + k), count + k)
        for k in range(left)
    ]
    for store in stores:
        store.start()
    for i in range(count):
        rows = merge.rows_of(first + i)
        fold, total = merge.rows(last_ref.at[i], up_ref[...], served_ref, features_ref, rows, total)
        m_buf[i] = fold
        stores.append(merge.store(m_buf.at[i], rows, i))
        stores[-1].start()
    high = total.astype(jnp.bfloat16)
    low = (total - high.astype(jnp.float32)).astype(jnp.bfloat16)
    fresh = base_ref[...]
    for part in (low, high):
        fresh = fresh + jnp.dot(part, up_ref[...], preferred_element_type=jnp.float32)
    fresh = fresh.astype(jnp.bfloat16)
    fresh_ref[...] = fresh
    put_fresh = pltpu.make_async_copy(fresh_ref, fresh_hbm, small_sem.at[0])
    put_fresh.start()
    value = fresh.astype(jnp.float32)
    heads = attended_ref.shape[1] // HEAD_SIZE
    group = heads // (fresh_ref.shape[1] // HEAD_SIZE)
    for h in range(heads):
        cols = slice(h * HEAD_SIZE, (h + 1) * HEAD_SIZE)
        at = (h // group) * HEAD_SIZE
        attended_ref[:, cols] = (
            context_ref[:, cols] + own_weight_ref[:, cols] * value[:, at : at + HEAD_SIZE]
        ).astype(jnp.bfloat16)
    put_attended = pltpu.make_async_copy(attended_ref, attended_hbm, small_sem.at[1])
    put_attended.start()
    for store in stores:
        store.wait()
    put_fresh.wait()
    put_attended.wait()


def merge(per, start, pick, features, served, slabs, crossed, last):
    left = 3
    count = slabs.shape[0] + crossed.shape[0] + last.shape[0]
    rank = pick.shape[0]
    depth, cols = served.shape
    width = depth // start.shape[1]
    return pl.pallas_call(
        functools.partial(merge_kernel, per, left),
        out_shape=(
            jax.ShapeDtypeStruct((depth, cols), jnp.bfloat16),
            jax.ShapeDtypeStruct((features.shape[0], rank), jnp.float32),
            jax.ShapeDtypeStruct((rank, cols), jnp.bfloat16),
            jax.ShapeDtypeStruct((left, width, cols), jnp.bfloat16),
        ),
        in_specs=[VMEM] * 7,
        out_specs=(HBM, VMEM, VMEM, VMEM),
        scratch_shapes=[
            pltpu.VMEM((count - left, width, cols), jnp.bfloat16),
            pltpu.SemaphoreType.DMA((count - left,)),
        ],
        compiler_params=pltpu.CompilerParams(vmem_limit_bytes=12 * 2**20),
        cost_estimate=pl.CostEstimate(
            flops=2 * count * width * cols * rank,
            bytes_accessed=4 * count * width * cols,
            transcendentals=0,
        ),
        name="merge_blocks",
    )(start, pick, features, served, slabs, crossed, last)


def finish(start, up, features, served, left, last, merged, total, context, own_weight, base):
    count = last.shape[0]
    depth, cols = served.shape
    width = depth // start.shape[1]
    smalls = [base.shape, context.shape]
    return pl.pallas_call(
        final_kernel,
        out_shape=[
            jax.ShapeDtypeStruct(shape, jnp.bfloat16) for shape in [(depth, cols), *smalls]
        ],
        in_specs=[VMEM] * 6 + [HBM] + [VMEM] * 4,
        out_specs=[HBM] * 3,
        input_output_aliases={6: 0},
        scratch_shapes=[
            pltpu.VMEM((count, width, cols), jnp.bfloat16),
            pltpu.SemaphoreType.DMA((count + left.shape[0],)),
        ]
        + [pltpu.VMEM(shape, jnp.bfloat16) for shape in smalls]
        + [pltpu.SemaphoreType.DMA((2,))],
        compiler_params=pltpu.CompilerParams(vmem_limit_bytes=12 * 2**20),
        cost_estimate=pl.CostEstimate(
            flops=2 * count * width * cols * up.shape[0],
            bytes_accessed=4 * count * width * cols,
            transcendentals=0,
        ),
        name="finish_rows",
    )(start, up, features, served, left, last, merged, total, context, own_weight, base)


def panels(x):
    return [x[:, i : i + PANEL] for i in range(0, x.shape[1], PANEL)]


def body(
    hidden_in,
    queries,
    stored_keys,
    stored_values,
    fresh_token_key,
    lengths,
    served_value_weight,
    adapter_in,
    adapter_out,
    owner_rank,
):
    n = lax.axis_size("replica")
    replica = lax.axis_index("replica")
    core = lax.axis_index("tensor")
    swap = [(0, 1), (1, 0)]
    full = adapter_in.shape[1]
    width = full // 2
    rows = queries.shape[0]
    per, cols = adapter_out.shape
    rank = n * per

    bits = [n >> i for i in range(1, n.bit_length())]
    ways = [bits, bits[:-2] + bits[:-3:-1]]

    def exchange(x, *steps):
        pairs = [
            (2 * i + c, 2 * (i ^ sum(ways[c][step] for step in steps)) + c)
            for i in range(n)
            for c in range(2)
        ]
        return lax.ppermute(x, ("replica", "tensor"), pairs)

    below = jnp.concatenate(panels(adapter_out), axis=0)
    below = jnp.pad(below, ((0, -below.shape[0] % 8), (0, 0)))
    block = lax.dynamic_slice_in_dim(adapter_in, core * width, width, axis=1)
    block, below = lax.optimization_barrier((block, below))
    slabs = jnp.concatenate([*panels(block), below], axis=0)[None]

    given = in_hbm(lengths, queries, fresh_token_key, stored_keys, stored_values)
    *early, first, second, third = range(len(bits))
    for step in early:
        slabs = jnp.concatenate([slabs, exchange(slabs, step)], axis=0)

    split = rows // 2
    hid_other = lax.ppermute(hidden_in, "tensor", swap)
    came = exchange(slabs, first)
    part = attend(range(split), given, after=[slabs])
    came, part = lax.optimization_barrier((came, part))
    parts = [part]
    slabs = jnp.concatenate([slabs, came], axis=0)
    last = exchange(slabs, second, third)
    images = exchange(slabs, third)
    came = exchange(slabs, second)
    *part, served = attend(range(split, rows), given, *in_hbm(served_value_weight), [slabs])
    came, part, hid_other, owner_rank = lax.optimization_barrier(
        (came, part, hid_other, owner_rank)
    )
    parts.append(part)
    slabs = jnp.concatenate([slabs, came], axis=0)
    features = jnp.concatenate([hidden_in, hid_other], axis=1)
    features = jnp.where(core == 0, features, jnp.concatenate([hid_other, hidden_in], axis=1))

    slab = jnp.arange(n, dtype=jnp.int32)
    sources = []
    for way in ways:
        source = replica
        for step, bit in enumerate(way):
            source = source ^ (((slab >> step) & 1) * bit)
        sources.append(source)
    mine = jnp.where(core == 0, sources[0], sources[1])
    theirs = jnp.where(core == 0, sources[1], sources[0])
    source = jnp.concatenate([mine, theirs])
    half = jnp.concatenate([jnp.full((n,), core), jnp.full((n,), 1 - core)])
    place = jnp.sum(jnp.where(owner_rank[None, :] == source[:, None], slab[None, :], 0), axis=1)
    start = (place * full + half * width).astype(jnp.int32)[None]

    row = jnp.arange(rank, dtype=jnp.int32)
    row_source = replica
    for step in range(len(bits)):
        bit = jnp.where(core == 0, ways[0][step], ways[1][step])
        row_source = row_source ^ (((row // per >> step) & 1) * bit)
    pick = jnp.where(
        row[:, None] == (row_source * per + row % per)[None, :], ADAPTER_SCALE, 0.0
    ).astype(jnp.bfloat16)

    context, own_weight = (
        jnp.concatenate(pair, axis=0).reshape(queries.shape) for pair in zip(*parts)
    )
    crossed, start = lax.optimization_barrier((slabs, start))
    crossed = lax.ppermute(crossed, "tensor", swap)
    base = base_value(features, served, slabs)
    last, start, pick, context, own_weight, features, crossed, base = lax.optimization_barrier(
        (last, start, pick, context, own_weight, features, crossed, base)
    )
    last = jnp.concatenate([images, last], axis=0)
    last_crossed = lax.ppermute(last, "tensor", swap)
    merged, total, up, left = merge(per, start, pick, features, served, slabs, crossed, last)
    return tuple(
        finish(
            start, up, features, served, left, last_crossed, merged, total, context, own_weight,
            base,
        )
    )


def solution(mesh):
    in_specs = (
        P(("groups", "replica"), "tensor"),
        P(("groups", "replica"), "tensor"),
        P(("groups", "replica"), None, "tensor"),
        P(("groups", "replica"), None, "tensor"),
        P(("groups", "replica"), "tensor"),
        P(("groups", "replica")),
        P(None, "tensor"),
        P("groups", "replica"),
        P(("groups", "replica"), "tensor"),
        P("groups"),
    )
    out_specs = (
        P("groups", "tensor"),
        P(("groups", "replica"), "tensor"),
        P(("groups", "replica"), "tensor"),
    )
    return jax.shard_map(body, mesh=mesh, in_specs=in_specs, out_specs=out_specs, check_vma=False)
```

```python
import functools

import jax
import jax.numpy as jnp
from jax import lax
from jax.experimental import pallas as pl
from jax.experimental.pallas import tpu as pltpu
from jax.sharding import PartitionSpec as P

HEAD_SIZE = 128
ADAPTER_SCALE = 2.0
PANEL = 128

SMEM = pl.BlockSpec(memory_space=pltpu.SMEM)
VMEM = pl.BlockSpec(memory_space=pltpu.VMEM)
HBM = pl.BlockSpec(memory_space=pltpu.HBM)


def in_hbm(*arrays):
    return [pltpu.with_memory_space_constraint(x, pltpu.HBM) for x in arrays]


def attend_kernel(rows, fetch, lengths_hbm, q_hbm, own_k_hbm, k_hbm, v_hbm, *rest):
    rest = list(rest)
    if fetch:
        served_hbm, served_ref, served_sem = rest.pop(0), rest.pop(-10), rest.pop(-1)
    context_ref, own_weight_ref, lengths, q_ref, own_k_ref, k_buf, v_buf, small_sem, k_sem, v_sem = (
        rest[-10:]
    )
    smalls = [
        pltpu.make_async_copy(source, into, small_sem.at[i])
        for i, (source, into) in enumerate(
            [(lengths_hbm, lengths), (q_hbm, q_ref), (own_k_hbm, own_k_ref)]
        )
    ]
    for copy in smalls:
        copy.start()

    def copies(i, row):
        return (
            pltpu.make_async_copy(k_hbm.at[row], k_buf.at[i], k_sem.at[i]),
            pltpu.make_async_copy(v_hbm.at[row], v_buf.at[i], v_sem.at[i]),
        )

    for i, row in enumerate(rows):
        for copy in copies(i, row):
            copy.start()
    if fetch:
        get_served = pltpu.make_async_copy(served_hbm, served_ref, served_sem)
        get_served.start()
    for copy in smalls:
        copy.wait()
    queries = q_ref[...].astype(jnp.float32)
    own_keys = own_k_ref[...].astype(jnp.float32)
    heads = queries.shape[1] // HEAD_SIZE
    cache_len, width = k_buf.shape[1:]
    local_heads = width // HEAD_SIZE
    group = heads // local_heads
    scaling = 1.0 / HEAD_SIZE**0.5
    head_of = lax.broadcasted_iota(jnp.int32, (heads, HEAD_SIZE), 0) // group
    position = lax.broadcasted_iota(jnp.int32, (heads, cache_len), 1)
    for i, row in enumerate(rows):
        q = jnp.concatenate(
            [
                queries[row : row + 1, h * HEAD_SIZE : (h + 1) * HEAD_SIZE]
                for h in range(heads)
            ],
            axis=0,
        )
        spread = jnp.concatenate(
            [jnp.where(head_of == h, q, 0.0) for h in range(local_heads)], axis=1
        )
        own = jnp.sum(spread * own_keys[row : row + 1], axis=1, keepdims=True) * scaling
        get_keys, get_values = copies(i, row)
        get_keys.wait()
        scores = (
            lax.dot_general(
                spread.astype(jnp.bfloat16), k_buf[i], (((1,), (1,)), ((), ())),
                preferred_element_type=jnp.float32,
            )
            * scaling
        )
        valid = position < lengths[row]
        masked = jnp.where(valid, scores, -1e30)
        largest = jnp.maximum(jnp.max(masked, axis=1, keepdims=True), own)
        cached_exp = jnp.where(valid, jnp.exp(masked - largest), 0.0)
        own_exp = jnp.exp(own - largest)
        normaliser = jnp.sum(cached_exp, axis=1, keepdims=True) + own_exp
        weights = (cached_exp / normaliser).astype(jnp.bfloat16)
        weight_own = (own_exp / normaliser).astype(jnp.bfloat16).astype(jnp.float32)
        get_values.wait()
        wide = jnp.dot(weights, v_buf[i], preferred_element_type=jnp.float32)
        context = wide[:, :HEAD_SIZE]
        for h in range(1, local_heads):
            context = jnp.where(
                head_of == h, wide[:, h * HEAD_SIZE : (h + 1) * HEAD_SIZE], context
            )
        context_ref[i] = context
        own_weight_ref[i] = jnp.broadcast_to(weight_own, (heads, HEAD_SIZE))
    if fetch:
        get_served.wait()


def attend(rows, given, served=None, after=()):
    lengths, queries, own_key, stored_keys, stored_values = given
    fetch = served is not None
    cache_len, width = stored_keys.shape[1:]
    heads = queries.shape[1] // HEAD_SIZE
    count = len(rows)
    out_shape = [jax.ShapeDtypeStruct((count, heads, HEAD_SIZE), jnp.float32)] * 2
    if fetch:
        out_shape += [jax.ShapeDtypeStruct(served.shape, served.dtype)]
    return pl.pallas_call(
        functools.partial(attend_kernel, rows, fetch),
        out_shape=out_shape,
        in_specs=[HBM] * (5 + fetch) + [pl.BlockSpec(memory_space=pl.ANY)] * len(after),
        out_specs=[VMEM] * len(out_shape),
        scratch_shapes=[
            pltpu.SMEM(lengths.shape, jnp.int32),
            pltpu.VMEM(queries.shape, jnp.bfloat16),
            pltpu.VMEM(own_key.shape, jnp.bfloat16),
            pltpu.VMEM((count, cache_len, width), jnp.bfloat16),
            pltpu.VMEM((count, cache_len, width), jnp.bfloat16),
            pltpu.SemaphoreType.DMA((3,)),
            pltpu.SemaphoreType.DMA((count,)),
            pltpu.SemaphoreType.DMA((count,)),
        ]
        + [pltpu.SemaphoreType.DMA] * fetch,
        compiler_params=pltpu.CompilerParams(vmem_limit_bytes=12 * 2**20),
        cost_estimate=pl.CostEstimate(
            flops=4 * count * heads * cache_len * width,
            bytes_accessed=4 * count * cache_len * width,
            transcendentals=count * heads * cache_len,
        ),
        name="attend_cache",
    )(*given, *([served] if fetch else []), *after)


def base_kernel(features_ref, served_ref, after, base_ref):
    del after
    base_ref[...] = jnp.dot(
        features_ref[...], served_ref[...], preferred_element_type=jnp.float32
    )


def base_value(features, served, after):
    rows, depth = features.shape
    cols = served.shape[1]
    return pl.pallas_call(
        base_kernel,
        out_shape=jax.ShapeDtypeStruct((rows, cols), jnp.float32),
        in_specs=[VMEM, VMEM, pl.BlockSpec(memory_space=pl.ANY)],
        out_specs=VMEM,
        compiler_params=pltpu.CompilerParams(vmem_limit_bytes=12 * 2**20),
        cost_estimate=pl.CostEstimate(
            flops=2 * rows * depth * cols, bytes_accessed=0, transcendentals=0
        ),
        name="base_value",
    )(features, served, after)


class Merge:
    def __init__(self, start_ref, merged, out_sem, width):
        self.start, self.merged, self.out_sem, self.width = start_ref[...], merged, out_sem, width
        self.entry = lax.broadcasted_iota(jnp.int32, self.start.shape, 1)

    def rows_of(self, entry):
        first = jnp.sum(jnp.where(self.entry == entry, self.start, 0))
        return pl.ds(pl.multiple_of(first, self.width), self.width)

    def store(self, source, rows, at):
        return pltpu.make_async_copy(source, self.merged.at[rows], self.out_sem.at[at])

    def rows(self, slab, up, served_ref, features_ref, rows, total):
        rank = up.shape[0]
        block = jnp.concatenate(
            [slab[i * rank : (i + 1) * rank] for i in range(self.width // PANEL)], axis=1
        )
        update = lax.dot_general(
            block, up, (((0,), (0,)), ((), ())), preferred_element_type=jnp.float32
        )
        fold = (served_ref[rows, :].astype(jnp.float32) + update).astype(jnp.bfloat16)
        part = lax.dot_general(
            features_ref[:, rows], block, (((1,), (1,)), ((), ())),
            preferred_element_type=jnp.float32,
        )
        return fold, total + part


def merge_kernel(per, left, start_ref, pick_ref, features_ref, served_ref, slabs_ref, crossed_ref,
                 last_ref, merged, total_ref, up_ref, left_ref, m_buf, out_sem):
    width = m_buf.shape[1]
    rank, cols = up_ref.shape
    merge = Merge(start_ref, merged, out_sem, width)
    ups = []
    for ref in (slabs_ref, last_ref):
        for k in range(ref.shape[0]):
            below = ref[k, rank * (width // PANEL) :].astype(jnp.float32)
            ups.append(
                jnp.concatenate(
                    [below[i * per : (i + 1) * per] for i in range(cols // PANEL)], axis=1
                )
            )
    ups = jnp.concatenate(ups, axis=0).astype(jnp.bfloat16)
    up = jnp.dot(pick_ref[...], ups, preferred_element_type=jnp.float32).astype(jnp.bfloat16)
    up_ref[...] = up
    total = jnp.zeros(total_ref.shape, jnp.float32)
    refs = (slabs_ref, last_ref, crossed_ref)
    slabs = [ref.at[k] for ref in refs for k in range(ref.shape[0])]
    keep = len(slabs) - left
    stores = []
    for i, slab in enumerate(slabs):
        rows = merge.rows_of(i)
        fold, total = merge.rows(slab, up, served_ref, features_ref, rows, total)
        if i < keep:
            m_buf[i] = fold
            stores.append(merge.store(m_buf.at[i], rows, i))
            stores[-1].start()
        else:
            left_ref[i - keep] = fold
    total_ref[...] = total
    for store in stores:
        store.wait()


def final_kernel(start_ref, up_ref, features_ref, served_ref, left_ref, last_ref, merged_in,
                 total_ref, context_ref, own_weight_ref, base_ref, merged, fresh_hbm, attended_hbm, m_buf,
                 out_sem, fresh_ref, attended_ref, small_sem):
    del merged_in
    count, width = last_ref.shape[0], m_buf.shape[1]
    left = left_ref.shape[0]
    merge = Merge(start_ref, merged, out_sem, width)
    first = start_ref.shape[1] - count
    total = total_ref[...]
    stores = [
        merge.store(left_ref.at[k], merge.rows_of(first - left + k), count + k)
        for k in range(left)
    ]
    for store in stores:
        store.start()
    for i in range(count):
        rows = merge.rows_of(first + i)
        fold, total = merge.rows(last_ref.at[i], up_ref[...], served_ref, features_ref, rows, total)
        m_buf[i] = fold
        stores.append(merge.store(m_buf.at[i], rows, i))
        stores[-1].start()
    high = total.astype(jnp.bfloat16)
    low = (total - high.astype(jnp.float32)).astype(jnp.bfloat16)
    fresh = base_ref[...]
    for part in (low, high):
        fresh = fresh + jnp.dot(part, up_ref[...], preferred_element_type=jnp.float32)
    fresh = fresh.astype(jnp.bfloat16)
    fresh_ref[...] = fresh
    put_fresh = pltpu.make_async_copy(fresh_ref, fresh_hbm, small_sem.at[0])
    put_fresh.start()
    value = fresh.astype(jnp.float32)
    heads = attended_ref.shape[1] // HEAD_SIZE
    group = heads // (fresh_ref.shape[1] // HEAD_SIZE)
    for h in range(heads):
        cols = slice(h * HEAD_SIZE, (h + 1) * HEAD_SIZE)
        at = (h // group) * HEAD_SIZE
        attended_ref[:, cols] = (
            context_ref[:, cols] + own_weight_ref[:, cols] * value[:, at : at + HEAD_SIZE]
        ).astype(jnp.bfloat16)
    put_attended = pltpu.make_async_copy(attended_ref, attended_hbm, small_sem.at[1])
    put_attended.start()
    for store in stores:
        store.wait()
    put_fresh.wait()
    put_attended.wait()


def merge(per, start, pick, features, served, slabs, crossed, last):
    left = 1
    count = slabs.shape[0] + crossed.shape[0] + last.shape[0]
    rank = pick.shape[0]
    depth, cols = served.shape
    width = depth // start.shape[1]
    return pl.pallas_call(
        functools.partial(merge_kernel, per, left),
        out_shape=(
            jax.ShapeDtypeStruct((depth, cols), jnp.bfloat16),
            jax.ShapeDtypeStruct((features.shape[0], rank), jnp.float32),
            jax.ShapeDtypeStruct((rank, cols), jnp.bfloat16),
            jax.ShapeDtypeStruct((left, width, cols), jnp.bfloat16),
        ),
        in_specs=[VMEM] * 7,
        out_specs=(HBM, VMEM, VMEM, VMEM),
        scratch_shapes=[
            pltpu.VMEM((count - left, width, cols), jnp.bfloat16),
            pltpu.SemaphoreType.DMA((count - left,)),
        ],
        compiler_params=pltpu.CompilerParams(vmem_limit_bytes=12 * 2**20),
        cost_estimate=pl.CostEstimate(
            flops=2 * count * width * cols * rank,
            bytes_accessed=4 * count * width * cols,
            transcendentals=0,
        ),
        name="merge_blocks",
    )(start, pick, features, served, slabs, crossed, last)


def finish(start, up, features, served, left, last, merged, total, context, own_weight, base):
    count = last.shape[0]
    depth, cols = served.shape
    width = depth // start.shape[1]
    smalls = [base.shape, context.shape]
    return pl.pallas_call(
        final_kernel,
        out_shape=[
            jax.ShapeDtypeStruct(shape, jnp.bfloat16) for shape in [(depth, cols), *smalls]
        ],
        in_specs=[VMEM] * 6 + [HBM] + [VMEM] * 4,
        out_specs=[HBM] * 3,
        input_output_aliases={6: 0},
        scratch_shapes=[
            pltpu.VMEM((count, width, cols), jnp.bfloat16),
            pltpu.SemaphoreType.DMA((count + left.shape[0],)),
        ]
        + [pltpu.VMEM(shape, jnp.bfloat16) for shape in smalls]
        + [pltpu.SemaphoreType.DMA((2,))],
        compiler_params=pltpu.CompilerParams(vmem_limit_bytes=12 * 2**20),
        cost_estimate=pl.CostEstimate(
            flops=2 * count * width * cols * up.shape[0],
            bytes_accessed=4 * count * width * cols,
            transcendentals=0,
        ),
        name="finish_rows",
    )(start, up, features, served, left, last, merged, total, context, own_weight, base)


def panels(x):
    return [x[:, i : i + PANEL] for i in range(0, x.shape[1], PANEL)]


def body(
    hidden_in,
    queries,
    stored_keys,
    stored_values,
    fresh_token_key,
    lengths,
    served_value_weight,
    adapter_in,
    adapter_out,
    owner_rank,
):
    n = lax.axis_size("replica")
    replica = lax.axis_index("replica")
    core = lax.axis_index("tensor")
    swap = [(0, 1), (1, 0)]
    full = adapter_in.shape[1]
    width = full // 2
    rows = queries.shape[0]
    per, cols = adapter_out.shape
    rank = n * per

    bits = [n >> i for i in range(1, n.bit_length())]
    ways = [bits, bits[:-2] + bits[:-3:-1]]

    def exchange(x, *steps):
        pairs = [
            (2 * i + c, 2 * (i ^ sum(ways[c][step] for step in steps)) + c)
            for i in range(n)
            for c in range(2)
        ]
        return lax.ppermute(x, ("replica", "tensor"), pairs)

    below = jnp.concatenate(panels(adapter_out), axis=0)
    below = jnp.pad(below, ((0, -below.shape[0] % 8), (0, 0)))
    block = lax.dynamic_slice_in_dim(adapter_in, core * width, width, axis=1)
    block, below = lax.optimization_barrier((block, below))
    slabs = jnp.concatenate([*panels(block), below], axis=0)[None]

    given = in_hbm(lengths, queries, fresh_token_key, stored_keys, stored_values)
    *early, first, second, third = range(len(bits))
    for step in early:
        slabs = jnp.concatenate([slabs, exchange(slabs, step)], axis=0)

    split = rows // 2
    hid_other = lax.ppermute(hidden_in, "tensor", swap)
    came = exchange(slabs, first)
    part = attend(range(split), given, after=[slabs])
    came, part = lax.optimization_barrier((came, part))
    parts = [part]
    slabs = jnp.concatenate([slabs, came], axis=0)
    last = exchange(slabs, second, third)
    images = exchange(slabs, third)
    came = exchange(slabs, second)
    *part, served = attend(range(split, rows), given, *in_hbm(served_value_weight), [slabs])
    came, part, hid_other, owner_rank = lax.optimization_barrier(
        (came, part, hid_other, owner_rank)
    )
    parts.append(part)
    slabs = jnp.concatenate([slabs, came], axis=0)
    features = jnp.concatenate([hidden_in, hid_other], axis=1)
    features = jnp.where(core == 0, features, jnp.concatenate([hid_other, hidden_in], axis=1))

    slab = jnp.arange(n, dtype=jnp.int32)
    sources = []
    for way in ways:
        source = replica
        for step, bit in enumerate(way):
            source = source ^ (((slab >> step) & 1) * bit)
        sources.append(source)
    mine = jnp.where(core == 0, sources[0], sources[1])
    theirs = jnp.where(core == 0, sources[1], sources[0])
    source = jnp.concatenate([mine, theirs])
    half = jnp.concatenate([jnp.full((n,), core), jnp.full((n,), 1 - core)])
    place = jnp.sum(jnp.where(owner_rank[None, :] == source[:, None], slab[None, :], 0), axis=1)
    start = (place * full + half * width).astype(jnp.int32)[None]

    row = jnp.arange(rank, dtype=jnp.int32)
    row_source = replica
    for step in range(len(bits)):
        bit = jnp.where(core == 0, ways[0][step], ways[1][step])
        row_source = row_source ^ (((row // per >> step) & 1) * bit)
    pick = jnp.where(
        row[:, None] == (row_source * per + row % per)[None, :], ADAPTER_SCALE, 0.0
    ).astype(jnp.bfloat16)

    context, own_weight = (
        jnp.concatenate(pair, axis=0).reshape(queries.shape) for pair in zip(*parts)
    )
    crossed, start = lax.optimization_barrier((slabs, start))
    crossed = lax.ppermute(crossed, "tensor", swap)
    base = base_value(features, served, slabs)
    last, start, pick, context, own_weight, features, crossed, base = lax.optimization_barrier(
        (last, start, pick, context, own_weight, features, crossed, base)
    )
    last = jnp.concatenate([images, last], axis=0)
    last_crossed = lax.ppermute(last, "tensor", swap)
    merged, total, up, left = merge(per, start, pick, features, served, slabs, crossed, last)
    return tuple(
        finish(
            start, up, features, served, left, last_crossed, merged, total, context, own_weight,
            base,
        )
    )


def solution(mesh):
    in_specs = (
        P(("groups", "replica"), "tensor"),
        P(("groups", "replica"), "tensor"),
        P(("groups", "replica"), None, "tensor"),
        P(("groups", "replica"), None, "tensor"),
        P(("groups", "replica"), "tensor"),
        P(("groups", "replica")),
        P(None, "tensor"),
        P("groups", "replica"),
        P(("groups", "replica"), "tensor"),
        P("groups"),
    )
    out_specs = (
        P("groups", "tensor"),
        P(("groups", "replica"), "tensor"),
        P(("groups", "replica"), "tensor"),
    )
    return jax.shard_map(body, mesh=mesh, in_specs=in_specs, out_specs=out_specs, check_vma=False)
```

```python
import functools

import jax
import jax.numpy as jnp
from jax import lax
from jax.experimental import pallas as pl
from jax.experimental.pallas import tpu as pltpu
from jax.sharding import PartitionSpec as P

HEAD_SIZE = 128
ADAPTER_SCALE = 2.0
PANEL = 128

SMEM = pl.BlockSpec(memory_space=pltpu.SMEM)
VMEM = pl.BlockSpec(memory_space=pltpu.VMEM)
HBM = pl.BlockSpec(memory_space=pltpu.HBM)


def in_hbm(*arrays):
    return [pltpu.with_memory_space_constraint(x, pltpu.HBM) for x in arrays]


def attend_kernel(rows, fetch, lengths_hbm, q_hbm, own_k_hbm, k_hbm, v_hbm, *rest):
    rest = list(rest)
    if fetch:
        served_hbm, served_ref, served_sem = rest.pop(0), rest.pop(-10), rest.pop(-1)
    context_ref, own_weight_ref, lengths, q_ref, own_k_ref, k_buf, v_buf, small_sem, k_sem, v_sem = (
        rest[-10:]
    )
    smalls = [
        pltpu.make_async_copy(source, into, small_sem.at[i])
        for i, (source, into) in enumerate(
            [(lengths_hbm, lengths), (q_hbm, q_ref), (own_k_hbm, own_k_ref)]
        )
    ]
    for copy in smalls:
        copy.start()

    def copies(i, row):
        return (
            pltpu.make_async_copy(k_hbm.at[row], k_buf.at[i], k_sem.at[i]),
            pltpu.make_async_copy(v_hbm.at[row], v_buf.at[i], v_sem.at[i]),
        )

    for i, row in enumerate(rows):
        for copy in copies(i, row):
            copy.start()
    if fetch:
        get_served = pltpu.make_async_copy(served_hbm, served_ref, served_sem)
        get_served.start()
    for copy in smalls:
        copy.wait()
    queries = q_ref[...].astype(jnp.float32)
    own_keys = own_k_ref[...].astype(jnp.float32)
    heads = queries.shape[1] // HEAD_SIZE
    cache_len, width = k_buf.shape[1:]
    local_heads = width // HEAD_SIZE
    group = heads // local_heads
    scaling = 1.0 / HEAD_SIZE**0.5
    head_of = lax.broadcasted_iota(jnp.int32, (heads, HEAD_SIZE), 0) // group
    position = lax.broadcasted_iota(jnp.int32, (heads, cache_len), 1)
    for i, row in enumerate(rows):
        q = jnp.concatenate(
            [
                queries[row : row + 1, h * HEAD_SIZE : (h + 1) * HEAD_SIZE]
                for h in range(heads)
            ],
            axis=0,
        )
        spread = jnp.concatenate(
            [jnp.where(head_of == h, q, 0.0) for h in range(local_heads)], axis=1
        )
        own = jnp.sum(spread * own_keys[row : row + 1], axis=1, keepdims=True) * scaling
        get_keys, get_values = copies(i, row)
        get_keys.wait()
        scores = (
            lax.dot_general(
                spread.astype(jnp.bfloat16), k_buf[i], (((1,), (1,)), ((), ())),
                preferred_element_type=jnp.float32,
            )
            * scaling
        )
        valid = position < lengths[row]
        masked = jnp.where(valid, scores, -1e30)
        largest = jnp.maximum(jnp.max(masked, axis=1, keepdims=True), own)
        cached_exp = jnp.where(valid, jnp.exp(masked - largest), 0.0)
        own_exp = jnp.exp(own - largest)
        normaliser = jnp.sum(cached_exp, axis=1, keepdims=True) + own_exp
        weights = (cached_exp / normaliser).astype(jnp.bfloat16)
        weight_own = (own_exp / normaliser).astype(jnp.bfloat16).astype(jnp.float32)
        get_values.wait()
        wide = jnp.dot(weights, v_buf[i], preferred_element_type=jnp.float32)
        context = wide[:, :HEAD_SIZE]
        for h in range(1, local_heads):
            context = jnp.where(
                head_of == h, wide[:, h * HEAD_SIZE : (h + 1) * HEAD_SIZE], context
            )
        context_ref[i] = context
        own_weight_ref[i] = jnp.broadcast_to(weight_own, (heads, HEAD_SIZE))
    if fetch:
        get_served.wait()


def attend(rows, given, served=None, after=()):
    lengths, queries, own_key, stored_keys, stored_values = given
    fetch = served is not None
    cache_len, width = stored_keys.shape[1:]
    heads = queries.shape[1] // HEAD_SIZE
    count = len(rows)
    out_shape = [jax.ShapeDtypeStruct((count, heads, HEAD_SIZE), jnp.float32)] * 2
    if fetch:
        out_shape += [jax.ShapeDtypeStruct(served.shape, served.dtype)]
    return pl.pallas_call(
        functools.partial(attend_kernel, rows, fetch),
        out_shape=out_shape,
        in_specs=[HBM] * (5 + fetch) + [pl.BlockSpec(memory_space=pl.ANY)] * len(after),
        out_specs=[VMEM] * len(out_shape),
        scratch_shapes=[
            pltpu.SMEM(lengths.shape, jnp.int32),
            pltpu.VMEM(queries.shape, jnp.bfloat16),
            pltpu.VMEM(own_key.shape, jnp.bfloat16),
            pltpu.VMEM((count, cache_len, width), jnp.bfloat16),
            pltpu.VMEM((count, cache_len, width), jnp.bfloat16),
            pltpu.SemaphoreType.DMA((3,)),
            pltpu.SemaphoreType.DMA((count,)),
            pltpu.SemaphoreType.DMA((count,)),
        ]
        + [pltpu.SemaphoreType.DMA] * fetch,
        compiler_params=pltpu.CompilerParams(vmem_limit_bytes=12 * 2**20),
        cost_estimate=pl.CostEstimate(
            flops=4 * count * heads * cache_len * width,
            bytes_accessed=4 * count * cache_len * width,
            transcendentals=count * heads * cache_len,
        ),
        name="attend_cache",
    )(*given, *([served] if fetch else []), *after)


def base_kernel(features_ref, served_ref, after, base_ref):
    del after
    base_ref[...] = jnp.dot(
        features_ref[...], served_ref[...], preferred_element_type=jnp.float32
    )


def base_value(features, served, after):
    rows, depth = features.shape
    cols = served.shape[1]
    return pl.pallas_call(
        base_kernel,
        out_shape=jax.ShapeDtypeStruct((rows, cols), jnp.float32),
        in_specs=[VMEM, VMEM, pl.BlockSpec(memory_space=pl.ANY)],
        out_specs=VMEM,
        compiler_params=pltpu.CompilerParams(vmem_limit_bytes=12 * 2**20),
        cost_estimate=pl.CostEstimate(
            flops=2 * rows * depth * cols, bytes_accessed=0, transcendentals=0
        ),
        name="base_value",
    )(features, served, after)


class Merge:
    def __init__(self, start_ref, merged, out_sem, width):
        self.start, self.merged, self.out_sem, self.width = start_ref[...], merged, out_sem, width
        self.entry = lax.broadcasted_iota(jnp.int32, self.start.shape, 1)

    def rows_of(self, entry):
        first = jnp.sum(jnp.where(self.entry == entry, self.start, 0))
        return pl.ds(pl.multiple_of(first, self.width), self.width)

    def store(self, source, rows, at):
        return pltpu.make_async_copy(source, self.merged.at[rows], self.out_sem.at[at])

    def rows(self, slab, up, served_ref, features_ref, rows, total):
        rank = up.shape[0]
        block = jnp.concatenate(
            [slab[i * rank : (i + 1) * rank] for i in range(self.width // PANEL)], axis=1
        )
        update = lax.dot_general(
            block, up, (((0,), (0,)), ((), ())), preferred_element_type=jnp.float32
        )
        fold = (served_ref[rows, :].astype(jnp.float32) + update).astype(jnp.bfloat16)
        part = lax.dot_general(
            features_ref[:, rows], block, (((1,), (1,)), ((), ())),
            preferred_element_type=jnp.float32,
        )
        return fold, total + part


def merge_kernel(per, left, start_ref, pick_ref, features_ref, served_ref, slabs_ref, crossed_ref,
                 last_ref, merged, total_ref, up_ref, left_ref, m_buf, out_sem):
    width = m_buf.shape[1]
    rank, cols = up_ref.shape
    merge = Merge(start_ref, merged, out_sem, width)
    ups = []
    for ref in (slabs_ref, last_ref):
        for k in range(ref.shape[0]):
            below = ref[k, rank * (width // PANEL) :].astype(jnp.float32)
            ups.append(
                jnp.concatenate(
                    [below[i * per : (i + 1) * per] for i in range(cols // PANEL)], axis=1
                )
            )
    ups = jnp.concatenate(ups, axis=0).astype(jnp.bfloat16)
    up = jnp.dot(pick_ref[...], ups, preferred_element_type=jnp.float32).astype(jnp.bfloat16)
    up_ref[...] = up
    total = jnp.zeros(total_ref.shape, jnp.float32)
    refs = (slabs_ref, last_ref, crossed_ref)
    slabs = [ref.at[k] for ref in refs for k in range(ref.shape[0])]
    keep = len(slabs) - left
    stores = []
    for i, slab in enumerate(slabs):
        rows = merge.rows_of(i)
        fold, total = merge.rows(slab, up, served_ref, features_ref, rows, total)
        if i < keep:
            m_buf[i] = fold
            stores.append(merge.store(m_buf.at[i], rows, i))
            stores[-1].start()
        else:
            left_ref[i - keep] = fold
    total_ref[...] = total
    for store in stores:
        store.wait()


def final_kernel(start_ref, up_ref, features_ref, served_ref, left_ref, last_ref, merged_in,
                 total_ref, context_ref, own_weight_ref, base_ref, merged, fresh_hbm, attended_hbm, m_buf,
                 out_sem, fresh_ref, attended_ref, small_sem):
    del merged_in
    count, width = last_ref.shape[0], m_buf.shape[1]
    left = left_ref.shape[0]
    merge = Merge(start_ref, merged, out_sem, width)
    first = start_ref.shape[1] - count
    total = total_ref[...]
    stores = [
        merge.store(left_ref.at[k], merge.rows_of(first - left + k), count + k)
        for k in range(left)
    ]
    for store in stores:
        store.start()
    for i in range(count):
        rows = merge.rows_of(first + i)
        fold, total = merge.rows(last_ref.at[i], up_ref[...], served_ref, features_ref, rows, total)
        m_buf[i] = fold
        stores.append(merge.store(m_buf.at[i], rows, i))
        stores[-1].start()
    high = total.astype(jnp.bfloat16)
    low = (total - high.astype(jnp.float32)).astype(jnp.bfloat16)
    fresh = base_ref[...]
    for part in (low, high):
        fresh = fresh + jnp.dot(part, up_ref[...], preferred_element_type=jnp.float32)
    fresh = fresh.astype(jnp.bfloat16)
    fresh_ref[...] = fresh
    put_fresh = pltpu.make_async_copy(fresh_ref, fresh_hbm, small_sem.at[0])
    put_fresh.start()
    value = fresh.astype(jnp.float32)
    heads = attended_ref.shape[1] // HEAD_SIZE
    group = heads // (fresh_ref.shape[1] // HEAD_SIZE)
    for h in range(heads):
        cols = slice(h * HEAD_SIZE, (h + 1) * HEAD_SIZE)
        at = (h // group) * HEAD_SIZE
        attended_ref[:, cols] = (
            context_ref[:, cols] + own_weight_ref[:, cols] * value[:, at : at + HEAD_SIZE]
        ).astype(jnp.bfloat16)
    put_attended = pltpu.make_async_copy(attended_ref, attended_hbm, small_sem.at[1])
    put_attended.start()
    for store in stores:
        store.wait()
    put_fresh.wait()
    put_attended.wait()


def merge(per, start, pick, features, served, slabs, crossed, last):
    left = 6
    count = slabs.shape[0] + crossed.shape[0] + last.shape[0]
    rank = pick.shape[0]
    depth, cols = served.shape
    width = depth // start.shape[1]
    return pl.pallas_call(
        functools.partial(merge_kernel, per, left),
        out_shape=(
            jax.ShapeDtypeStruct((depth, cols), jnp.bfloat16),
            jax.ShapeDtypeStruct((features.shape[0], rank), jnp.float32),
            jax.ShapeDtypeStruct((rank, cols), jnp.bfloat16),
            jax.ShapeDtypeStruct((left, width, cols), jnp.bfloat16),
        ),
        in_specs=[VMEM] * 7,
        out_specs=(HBM, VMEM, VMEM, VMEM),
        scratch_shapes=[
            pltpu.VMEM((count - left, width, cols), jnp.bfloat16),
            pltpu.SemaphoreType.DMA((count - left,)),
        ],
        compiler_params=pltpu.CompilerParams(vmem_limit_bytes=12 * 2**20),
        cost_estimate=pl.CostEstimate(
            flops=2 * count * width * cols * rank,
            bytes_accessed=4 * count * width * cols,
            transcendentals=0,
        ),
        name="merge_blocks",
    )(start, pick, features, served, slabs, crossed, last)


def finish(start, up, features, served, left, last, merged, total, context, own_weight, base):
    count = last.shape[0]
    depth, cols = served.shape
    width = depth // start.shape[1]
    smalls = [base.shape, context.shape]
    return pl.pallas_call(
        final_kernel,
        out_shape=[
            jax.ShapeDtypeStruct(shape, jnp.bfloat16) for shape in [(depth, cols), *smalls]
        ],
        in_specs=[VMEM] * 6 + [HBM] + [VMEM] * 4,
        out_specs=[HBM] * 3,
        input_output_aliases={6: 0},
        scratch_shapes=[
            pltpu.VMEM((count, width, cols), jnp.bfloat16),
            pltpu.SemaphoreType.DMA((count + left.shape[0],)),
        ]
        + [pltpu.VMEM(shape, jnp.bfloat16) for shape in smalls]
        + [pltpu.SemaphoreType.DMA((2,))],
        compiler_params=pltpu.CompilerParams(vmem_limit_bytes=12 * 2**20),
        cost_estimate=pl.CostEstimate(
            flops=2 * count * width * cols * up.shape[0],
            bytes_accessed=4 * count * width * cols,
            transcendentals=0,
        ),
        name="finish_rows",
    )(start, up, features, served, left, last, merged, total, context, own_weight, base)


def panels(x):
    return [x[:, i : i + PANEL] for i in range(0, x.shape[1], PANEL)]


def body(
    hidden_in,
    queries,
    stored_keys,
    stored_values,
    fresh_token_key,
    lengths,
    served_value_weight,
    adapter_in,
    adapter_out,
    owner_rank,
):
    n = lax.axis_size("replica")
    replica = lax.axis_index("replica")
    core = lax.axis_index("tensor")
    swap = [(0, 1), (1, 0)]
    full = adapter_in.shape[1]
    width = full // 2
    rows = queries.shape[0]
    per, cols = adapter_out.shape
    rank = n * per

    bits = [n >> i for i in range(1, n.bit_length())]
    ways = [bits, bits[:-2] + bits[:-3:-1]]

    def exchange(x, *steps):
        pairs = [
            (2 * i + c, 2 * (i ^ sum(ways[c][step] for step in steps)) + c)
            for i in range(n)
            for c in range(2)
        ]
        return lax.ppermute(x, ("replica", "tensor"), pairs)

    below = jnp.concatenate(panels(adapter_out), axis=0)
    below = jnp.pad(below, ((0, -below.shape[0] % 8), (0, 0)))
    block = lax.dynamic_slice_in_dim(adapter_in, core * width, width, axis=1)
    block, below = lax.optimization_barrier((block, below))
    slabs = jnp.concatenate([*panels(block), below], axis=0)[None]

    given = in_hbm(lengths, queries, fresh_token_key, stored_keys, stored_values)
    *early, first, second, third = range(len(bits))
    for step in early:
        slabs = jnp.concatenate([slabs, exchange(slabs, step)], axis=0)

    split = rows // 2
    hid_other = lax.ppermute(hidden_in, "tensor", swap)
    came = exchange(slabs, first)
    part = attend(range(split), given, after=[slabs])
    came, part = lax.optimization_barrier((came, part))
    parts = [part]
    slabs = jnp.concatenate([slabs, came], axis=0)
    last = exchange(slabs, second, third)
    images = exchange(slabs, third)
    came = exchange(slabs, second)
    *part, served = attend(range(split, rows), given, *in_hbm(served_value_weight), [slabs])
    came, part, hid_other, owner_rank = lax.optimization_barrier(
        (came, part, hid_other, owner_rank)
    )
    parts.append(part)
    slabs = jnp.concatenate([slabs, came], axis=0)
    features = jnp.concatenate([hidden_in, hid_other], axis=1)
    features = jnp.where(core == 0, features, jnp.concatenate([hid_other, hidden_in], axis=1))

    slab = jnp.arange(n, dtype=jnp.int32)
    sources = []
    for way in ways:
        source = replica
        for step, bit in enumerate(way):
            source = source ^ (((slab >> step) & 1) * bit)
        sources.append(source)
    mine = jnp.where(core == 0, sources[0], sources[1])
    theirs = jnp.where(core == 0, sources[1], sources[0])
    source = jnp.concatenate([mine, theirs])
    half = jnp.concatenate([jnp.full((n,), core), jnp.full((n,), 1 - core)])
    place = jnp.sum(jnp.where(owner_rank[None, :] == source[:, None], slab[None, :], 0), axis=1)
    start = (place * full + half * width).astype(jnp.int32)[None]

    row = jnp.arange(rank, dtype=jnp.int32)
    row_source = replica
    for step in range(len(bits)):
        bit = jnp.where(core == 0, ways[0][step], ways[1][step])
        row_source = row_source ^ (((row // per >> step) & 1) * bit)
    pick = jnp.where(
        row[:, None] == (row_source * per + row % per)[None, :], ADAPTER_SCALE, 0.0
    ).astype(jnp.bfloat16)

    context, own_weight = (
        jnp.concatenate(pair, axis=0).reshape(queries.shape) for pair in zip(*parts)
    )
    crossed, start = lax.optimization_barrier((slabs, start))
    crossed = lax.ppermute(crossed, "tensor", swap)
    base = base_value(features, served, slabs)
    last, start, pick, context, own_weight, features, crossed, base = lax.optimization_barrier(
        (last, start, pick, context, own_weight, features, crossed, base)
    )
    last = jnp.concatenate([images, last], axis=0)
    last_crossed = lax.ppermute(last, "tensor", swap)
    merged, total, up, left = merge(per, start, pick, features, served, slabs, crossed, last)
    return tuple(
        finish(
            start, up, features, served, left, last_crossed, merged, total, context, own_weight,
            base,
        )
    )


def solution(mesh):
    in_specs = (
        P(("groups", "replica"), "tensor"),
        P(("groups", "replica"), "tensor"),
        P(("groups", "replica"), None, "tensor"),
        P(("groups", "replica"), None, "tensor"),
        P(("groups", "replica"), "tensor"),
        P(("groups", "replica")),
        P(None, "tensor"),
        P("groups", "replica"),
        P(("groups", "replica"), "tensor"),
        P("groups"),
    )
    out_specs = (
        P("groups", "tensor"),
        P(("groups", "replica"), "tensor"),
        P(("groups", "replica"), "tensor"),
    )
    return jax.shard_map(body, mesh=mesh, in_specs=in_specs, out_specs=out_specs, check_vma=False)
```
